32 devices in a mesh: seq: 8 (over z, core), mp: 4 (over y, x).
Axes of the slice: x: 2, y: 2, z: 4, core: 2. Of those that a mesh axis runs over, the one named last changes fastest.
Arguments:
- tokens: bfloat16 [2, 2, 2048, 2048], P(None, None, 'seq'), may hold values from -6 to 6
- query_weight: bfloat16 [2048, 2048], P('seq', 'mp'), may hold values from -0.125 to 0.125
- query_bias: bfloat16 [2048], P(('mp', 'seq')), may hold values from -1.75 to 1.75
- key_weight: bfloat16 [2048, 2048], P('seq', 'mp'), may hold values from -0.125 to 0.125
- value_weight: bfloat16 [2048, 2048], P('seq', 'mp'), may hold values from -0.125 to 0.125
- value_bias: bfloat16 [2048], P(('mp', 'seq')), may hold values from -0.125 to 0.125
- proj_weight: bfloat16 [2048, 2048], P('mp', 'seq'), may hold values from -3.5 to 3.5
- proj_bias: bfloat16 [2048], P('seq'), may hold values from -1.75 to 1.75
- gain_first: bfloat16 [2048], P('seq'), may hold values from 0.5 to 1.5
- shift_first: bfloat16 [2048], P('seq'), may hold values from -1.75 to 1.75
- inner_weight: bfloat16 [2048, 8192], P('seq', 'mp'), may hold values from -0.125 to 0.125
- inner_bias: bfloat16 [8192], P(('mp', 'seq')), may hold values from -1.75 to 1.75
- outer_weight: bfloat16 [8192, 2048], P('mp', 'seq'), may hold values from -0.0625 to 0.0625
- outer_bias: bfloat16 [2048], P('seq'), may hold values from -1.75 to 1.75
- gain_second: bfloat16 [2048], P('seq'), may hold values from 0.5 to 1.5
- shift_second: bfloat16 [2048], P('seq'), may hold values from -1.75 to 1.75
- cotangent: bfloat16 [2, 2, 2048, 2048], P(None, None, 'seq'), may hold values from -6 to 6
Outputs:
- layer_out: bfloat16 [2, 2, 2048, 2048], P(None, None, 'seq')
- input_grad: float32 [2, 2, 2048, 2048], P(None, None, 'seq')
- query_weight_grad: float32 [2048, 2048], P('seq', 'mp')
- query_bias_grad: float32 [2048], P(('mp', 'seq'))
- key_weight_grad: float32 [2048, 2048], P('seq', 'mp')
- value_weight_grad: float32 [2048, 2048], P('seq', 'mp')
- value_bias_grad: float32 [2048], P(('mp', 'seq'))
- proj_weight_grad: float32 [2048, 2048], P('mp', 'seq')
- proj_bias_grad: float32 [2048], P('seq')
- gain_first_grad: float32 [2048], P('seq')
- shift_first_grad: float32 [2048], P('seq')
- inner_weight_grad: float32 [2048, 8192], P('seq', 'mp')
- inner_bias_grad: float32 [8192], P(('mp', 'seq'))
- outer_weight_grad: float32 [8192, 2048], P('mp', 'seq')
- outer_bias_grad: float32 [2048], P('seq')
- second_gain_gradient: float32 [2048], P('seq')
- shift_second_grad: float32 [2048], P('seq')
The draws below stay inside these ranges and needn't reach their ends.
All inputs are finite; a program needn't handle non-finite values.
Results may differ from the reference program's by a relative error of at most 0.024.
Values may be sent and summed in bfloat16 or wider, within the bound.
A program may use at most 256 MiB of HBM per device.

```python
import jax
import jax.numpy as jnp
from jax import lax

D = 2048
HEADS = 16
DH = 128
FF = 8192
MICRO = 2
SEQS = 2
LENGTH = 2048


def steps_of(rng, shape, pieces, low, largest):
    level, own = 1.0, jax.random.fold_in(rng, 6)
    for position, parts in pieces:
        heights = jnp.exp(jax.random.uniform(jax.random.fold_in(own, position), (parts,), jnp.float32, low / len(pieces), largest / len(pieces)))
        level = level * jnp.repeat(heights, shape[position] // parts).reshape([-1 if axis == position else 1 for axis in range(len(shape))])
    return level


def normal_values(rng, extent, scale, reach, pieces=(), dtype=jnp.bfloat16):
    drawn = jax.random.normal(rng, extent, jnp.float32) * scale
    if len(pieces) > 0:
        drawn = steps_of(rng, extent, pieces, -0.22, 0.18) * drawn
    return jnp.clip(drawn, min=-reach, max=reach).astype(dtype)


def setup_inputs(seed: int = 0) -> dict:
    seeds = jax.random.split(jax.random.key(seed), 18)
    tokens = normal_values(seeds[0], (MICRO, SEQS, LENGTH, D), 1.0, 6.0, ((2, 8),))
    query_weight = normal_values(seeds[1], (D, D), D ** -0.5, 0.125, ((0, 8), (1, 4)))
    query_bias = normal_values(seeds[2], (D,), 0.3, 1.75, ((0, 32),))
    key_weight = normal_values(seeds[3], (D, D), D ** -0.5, 0.125, ((0, 8), (1, 4)))
    value_weight = normal_values(seeds[4], (D, D), D ** -0.5, 0.125, ((0, 8), (1, 4)))
    value_bias = normal_values(seeds[5], (D,), 0.02, 0.125, ((0, 32),))
    proj_weight = normal_values(seeds[6], (D, D), (max(1, 3 * D // LENGTH)) ** -0.5, 3.5, ((0, 4), (1, 8)))
    proj_bias = normal_values(seeds[7], (D,), 0.3, 1.75, ((0, 8),))
    gain_first = jnp.clip(1.0 + 0.1 * jax.random.normal(seeds[8], (D,), jnp.float32), 0.5, 1.5).astype(jnp.bfloat16)
    shift_first = normal_values(seeds[9], (D,), 0.3, 1.75, ((0, 8),))
    inner_weight = normal_values(seeds[10], (D, FF), D ** -0.5, 0.125, ((0, 8), (1, 4)))
    inner_bias = normal_values(seeds[11], (FF,), 0.3, 1.75, ((0, 32),))
    outer_weight = normal_values(seeds[12], (FF, D), FF ** -0.5, 0.0625, ((0, 4), (1, 8)))
    outer_bias = normal_values(seeds[13], (D,), 0.3, 1.75, ((0, 8),))
    gain_second = jnp.clip(1.0 + 0.1 * jax.random.normal(seeds[14], (D,), jnp.float32), 0.5, 1.5).astype(jnp.bfloat16)
    shift_second = normal_values(seeds[15], (D,), 0.3, 1.75, ((0, 8),))
    cotangent = normal_values(seeds[16], (MICRO, SEQS, LENGTH, D), 1.0, 6.0, ((2, 8),))
    return {"tokens": tokens, "query_weight": query_weight, "query_bias": query_bias, "key_weight": key_weight, "value_weight": value_weight, "value_bias": value_bias, "proj_weight": proj_weight, "proj_bias": proj_bias, "gain_first": gain_first, "shift_first": shift_first, "inner_weight": inner_weight, "inner_bias": inner_bias, "outer_weight": outer_weight, "outer_bias": outer_bias, "gain_second": gain_second, "shift_second": shift_second, "cotangent": cotangent}


@jax.custom_vjp
def low(v):
    return lax.optimization_barrier(v.astype(jnp.bfloat16)).astype(jnp.float32)

@jax.custom_vjp
def low_back(v):
    return v

def low_keep(v):
    return (low(v), None)

def low_pass(kept, grad):
    return (grad,)

def back_keep(v):
    return (v, None)

def back_low(kept, grad):
    return (low(grad),)
low.defvjp(low_keep, low_pass)
low_back.defvjp(back_keep, back_low)
EPSILON = 1e-06
FULL_PRECISION = lax.Precision.HIGHEST

def both_round(values):
    return low(low_back(values))

def layer_norm(values, gain, shift):
    centre = values - lax.optimization_barrier(jnp.mean(values, axis=-1, keepdims=True))
    spread = lax.optimization_barrier(jnp.mean(centre * centre, axis=-1, keepdims=True))
    return centre * lax.rsqrt(spread + EPSILON) * gain + shift

def attend_block(query_block, key_heads, value_heads):
    raw_scores = jnp.einsum('qhd,khd->hqk', query_block, key_heads, precision=FULL_PRECISION)
    scores = low_back(raw_scores) * DH ** (-0.5)
    row_max = lax.optimization_barrier(jnp.max(scores, axis=-1, keepdims=True))
    exponent = jnp.exp(scores - row_max)
    probs = exponent / lax.optimization_barrier(jnp.sum(exponent, axis=-1, keepdims=True))
    return jnp.einsum('hqk,khd->qhd', low(probs), value_heads, precision=FULL_PRECISION)

def one_sequence(params, hidden):
    w_query, b_query, w_key, w_value, b_value, w_proj, b_proj, gain_one, shift_one, w_inner, b_inner, w_outer, b_outer, gain_two, shift_two = params
    length = hidden.shape[0]
    span = min(512, length)
    query_matrix = both_round(jnp.dot(hidden, w_query, precision=FULL_PRECISION) + b_query)
    key_rows = both_round(jnp.dot(hidden, w_key, precision=FULL_PRECISION))
    value_rows = both_round(jnp.dot(hidden, w_value, precision=FULL_PRECISION) + b_value)
    query_blocks = query_matrix.reshape(length // span, span, HEADS, DH)
    key_heads = key_rows.reshape(length, HEADS, DH)
    value_heads = value_rows.reshape(length, HEADS, DH)
    attend = jax.checkpoint(lambda query_block: attend_block(query_block, key_heads, value_heads))
    mixture = both_round(lax.map(attend, query_blocks).reshape(length, D))
    first_in = hidden + low_back(jnp.dot(mixture, w_proj, precision=FULL_PRECISION)) + b_proj
    first_out = layer_norm(first_in, gain_one, shift_one)
    inner_pre = low_back(jnp.dot(low(first_out), w_inner, precision=FULL_PRECISION) + b_inner)
    active = low(jax.nn.gelu(inner_pre, approximate=True))
    second_in = first_out + low_back(jnp.dot(active, w_outer, precision=FULL_PRECISION)) + b_outer
    return layer_norm(second_in, gain_two, shift_two)

def forward(inputs, params):

    def advance(counter, hidden):
        return (counter, one_sequence(params, hidden))
    _, results = lax.scan(advance, jnp.zeros((), jnp.float32), inputs)
    return results

def reference(tokens, query_weight, query_bias, key_weight, value_weight, value_bias, proj_weight, proj_bias, gain_first, shift_first, inner_weight, inner_bias, outer_weight, outer_bias, gain_second, shift_second, cotangent):
    params = tuple((member.astype(jnp.float32) for member in (query_weight, query_bias, key_weight, value_weight, value_bias, proj_weight, proj_bias, gain_first, shift_first, inner_weight, inner_bias, outer_weight, outer_bias, gain_second, shift_second)))
    inputs = tokens.astype(jnp.float32).reshape(MICRO * SEQS, LENGTH, D)
    results, pullback = jax.vjp(forward, inputs, params)
    d_inputs, gradients = pullback(cotangent.astype(jnp.float32).reshape(MICRO * SEQS, LENGTH, D))
    return (results.astype(jnp.bfloat16).reshape(MICRO, SEQS, LENGTH, D), d_inputs.reshape(MICRO, SEQS, LENGTH, D), gradients[0], gradients[1], gradients[2], gradients[3], gradients[4], gradients[5], gradients[6], gradients[7], gradients[8], gradients[9], gradients[10], gradients[11], gradients[12], gradients[13], gradients[14])
```

```python
import functools

import jax
import jax.numpy as jnp
from jax import lax
from jax.experimental import pallas as pl
from jax.experimental.pallas import tpu as pltpu
from jax.sharding import PartitionSpec as P

DH = 128
EPSILON = 1e-06
BF = jnp.bfloat16
F32 = jnp.float32
MESH = pl.DeviceIdType.MESH
ANY = pl.BlockSpec(memory_space=pl.ANY)
VMEM = pl.BlockSpec(memory_space=pltpu.VMEM)
MIB = 1 << 20


def matmul(left, right):
    return jnp.dot(left, right, preferred_element_type=F32)


def over_rows(left, right):
    return lax.dot_general(left, right, (((0,), (0,)), ((), ())), preferred_element_type=F32)


def over_cols(left, right):
    return lax.dot_general(left, right, (((1,), (1,)), ((), ())), preferred_element_type=F32)


def gelu_tanh(values):
    return jax.nn.gelu(values, approximate=True)


def square():
    me = lax.axis_index("mp")
    return me, me + 1 - 2 * lax.rem(me, 2), lax.rem(me + 2, 4), 3 - me


def greet(devices):
    barrier = pltpu.get_barrier_semaphore()
    for device in devices:
        pl.semaphore_signal(barrier, inc=1, device_id=device, device_id_type=MESH)
    pl.semaphore_wait(barrier, len(devices))


def sender(send_sem, recv_sem):
    def send(source, target, slot, device):
        copy = pltpu.make_async_remote_copy(
            src_ref=source,
            dst_ref=target,
            send_sem=send_sem.at[slot],
            recv_sem=recv_sem.at[slot],
            device_id=device,
            device_id_type=MESH,
        )
        copy.start()
        return copy

    return send


def sum_kernel(part_ref, out_ref, landed, relay, send_sem, recv_sem):
    me, along_x, along_y, across = square()
    greet([{"mp": along_x}, {"mp": along_y}])
    send = sender(send_sem, recv_sem)
    half = out_ref.shape[0] // 2
    upper, lower = pl.ds(0, half), pl.ds(half, half)
    copies = [
        send(part_ref.at[across, upper], landed.at[0], 0, {"mp": along_x}),
        send(part_ref.at[across, lower], landed.at[1], 1, {"mp": along_y}),
        send(part_ref.at[along_x, upper], landed.at[2], 2, {"mp": along_x}),
        send(part_ref.at[along_y, lower], landed.at[3], 3, {"mp": along_y}),
    ]
    copies[0].wait_recv()
    relay[0] = (part_ref[along_y, upper].astype(F32) + landed[0].astype(F32)).astype(BF)
    copies.append(send(relay.at[0], landed.at[4], 4, {"mp": along_y}))
    copies[1].wait_recv()
    relay[1] = (part_ref[along_x, lower].astype(F32) + landed[1].astype(F32)).astype(BF)
    copies.append(send(relay.at[1], landed.at[5], 5, {"mp": along_x}))
    copies[2].wait_recv()
    out_ref[upper] = part_ref[me, upper].astype(F32) + landed[2].astype(F32)
    copies[3].wait_recv()
    out_ref[lower] = part_ref[me, lower].astype(F32) + landed[3].astype(F32)
    copies[4].wait_recv()
    out_ref[upper] += landed[4].astype(F32)
    copies[5].wait_recv()
    out_ref[lower] += landed[5].astype(F32)
    for copy in copies:
        copy.wait_send()


def sum_over_mp(part, parts, ident):
    rows, width = part.shape
    mine = rows // parts
    if parts != 4:
        return lax.psum_scatter(part, "mp", scatter_dimension=0, tiled=True).astype(F32)
    return pl.pallas_call(
        sum_kernel,
        out_shape=jax.ShapeDtypeStruct((mine, width), F32),
        in_specs=[VMEM],
        out_specs=VMEM,
        scratch_shapes=[
            pltpu.VMEM((6, mine // 2, width), BF),
            pltpu.VMEM((2, mine // 2, width), BF),
            pltpu.SemaphoreType.DMA((6,)),
            pltpu.SemaphoreType.DMA((6,)),
        ],
        compiler_params=pltpu.CompilerParams(
            collective_id=ident, has_side_effects=True, vmem_limit_bytes=48 * MIB
        ),
        cost_estimate=pl.CostEstimate(flops=0, bytes_accessed=100 * MIB, transcendentals=0),
        name=f"sum_over_mp_{ident}",
    )(part.reshape(parts, mine, width))


def share_kernel(own_ref, all_ref, send_sem, recv_sem, local_sem):
    me, along_x, along_y, _ = square()
    to_x, to_y = {"mp": along_x}, {"mp": along_y}
    greet([to_x, to_y])
    send = sender(send_sem, recv_sem)
    half = own_ref.shape[0] // 2
    upper, lower = pl.ds(0, half), pl.ds(half, half)
    copies = [
        send(own_ref.at[upper], all_ref.at[me, upper], 0, to_x),
        send(own_ref.at[lower], all_ref.at[me, lower], 1, to_y),
        send(own_ref.at[lower], all_ref.at[me, lower], 2, to_x),
        send(own_ref.at[upper], all_ref.at[me, upper], 3, to_y),
    ]
    local = pltpu.make_async_copy(own_ref, all_ref.at[me], local_sem)
    local.start()
    copies[0].wait_recv()
    copies.append(send(all_ref.at[along_x, upper], all_ref.at[along_x, upper], 4, to_y))
    copies[1].wait_recv()
    copies.append(send(all_ref.at[along_y, lower], all_ref.at[along_y, lower], 5, to_x))
    for copy in copies[2:]:
        copy.wait_recv()
    for copy in copies:
        copy.wait_send()
    local.wait()


def share_over_mp(own, parts, ident):
    if parts != 4:
        return lax.all_gather(own, "mp", axis=0)
    return pl.pallas_call(
        share_kernel,
        out_shape=jax.ShapeDtypeStruct((parts,) + own.shape, own.dtype),
        in_specs=[ANY],
        out_specs=ANY,
        scratch_shapes=[
            pltpu.SemaphoreType.DMA((6,)),
            pltpu.SemaphoreType.DMA((6,)),
            pltpu.SemaphoreType.DMA,
        ],
        compiler_params=pltpu.CompilerParams(collective_id=ident, has_side_effects=True),
        cost_estimate=pl.CostEstimate(flops=0, bytes_accessed=100 * MIB, transcendentals=0),
        name=f"share_over_mp_{ident}",
    )(own)


def swap_kernel(groups, per, block_ref, out_ref, send_sem, recv_sem, local_sem):
    index = lax.axis_index("seq")
    group, place = index // per, lax.rem(index, per)
    targets = [lax.rem(group + step, groups) for step in range(groups)]
    devices = [{"seq": target * per + place} for target in targets]
    greet(devices[1:])
    send = sender(send_sem, recv_sem)
    copies = [
        send(block_ref.at[targets[step]], out_ref.at[group], step, devices[step])
        for step in range(1, groups)
    ]
    local = pltpu.make_async_copy(block_ref.at[group], out_ref.at[group], local_sem)
    local.start()
    local.wait()
    for copy in copies:
        copy.wait()


def swap_groups(blocks, per, parts, ident):
    groups = blocks.shape[0]
    if parts != 4:
        members = [[group * per + place for group in range(groups)] for place in range(per)]
        return lax.all_to_all(blocks, "seq", 0, 0, axis_index_groups=members)
    return pl.pallas_call(
        functools.partial(swap_kernel, groups, per),
        out_shape=jax.ShapeDtypeStruct(blocks.shape, blocks.dtype),
        in_specs=[ANY],
        out_specs=ANY,
        scratch_shapes=[
            pltpu.SemaphoreType.DMA((groups,)),
            pltpu.SemaphoreType.DMA((groups,)),
            pltpu.SemaphoreType.DMA,
        ],
        compiler_params=pltpu.CompilerParams(collective_id=ident, has_side_effects=True),
        cost_estimate=pl.CostEstimate(flops=0, bytes_accessed=60 * MIB, transcendentals=0),
        name=f"swap_groups_{ident}",
    )(blocks)


def normed(values):
    centre = values - jnp.mean(values, axis=-1, keepdims=True)
    spread = jnp.mean(centre * centre, axis=-1, keepdims=True)
    inverse = lax.rsqrt(spread + EPSILON)
    return centre * inverse, inverse


def norm_back(grad, normal, inverse, gain):
    inner = grad * gain
    moved = inverse * (
        inner
        - jnp.mean(inner, axis=-1, keepdims=True)
        - normal * jnp.mean(inner * normal, axis=-1, keepdims=True)
    )
    return moved, jnp.sum(grad * normal, axis=0), jnp.sum(grad, axis=0)


def around_group(block, members, per):
    blocks = [block]
    for step in range(1, per):
        pairs = [
            (base + place, base + (place - step) % per)
            for base in range(0, members, per)
            for place in range(per)
        ]
        blocks.append(lax.ppermute(block, "seq", pairs))
    return blocks


def group_sum(blocks, members, per):
    total = blocks[0]
    for step in range(1, per):
        pairs = [
            (base + place, base + (place + step) % per)
            for base in range(0, members, per)
            for place in range(per)
        ]
        total = total + lax.ppermute(blocks[step].astype(BF), "seq", pairs).astype(F32)
    return total


def on_device(members, parts, *arrays):
    (
        tokens,
        query_weight,
        query_bias,
        key_weight,
        value_weight,
        value_bias,
        proj_weight,
        proj_bias,
        gain_first,
        shift_first,
        inner_weight,
        inner_bias,
        outer_weight,
        outer_bias,
        gain_second,
        shift_second,
        cotangent,
    ) = arrays
    micro, seqs, length, width = tokens.shape
    groups = micro * seqs
    per = members // groups
    assert per * groups == members
    piece = length // parts
    rows = groups * length
    quarter = groups * piece
    mine = lax.axis_index("mp")

    depth, cols = query_weight.shape
    heads = cols // DH
    proj_fold = proj_weight.reshape(-1, depth, width // members)
    folds = proj_fold.shape[0]
    vectors = [
        query_bias,
        value_bias,
        inner_bias,
        proj_bias,
        gain_first,
        shift_first,
        outer_bias,
        gain_second,
        shift_second,
    ]
    sizes = [vector.shape[0] for vector in vectors]
    first_cols = 3 * cols + folds * (width // members)
    flat = jnp.concatenate(vectors)
    extra = 16
    flat = jnp.pad(flat, (0, extra * first_cols - flat.shape[0])).reshape(extra, first_cols)
    first = jnp.concatenate(
        [
            jnp.concatenate(
                [query_weight, key_weight, value_weight] + [proj_fold[i] for i in range(folds)], axis=1
            ),
            flat,
        ],
        axis=0,
    )
    first = lax.all_gather(first, "seq", axis=0)
    w_inner = lax.all_gather(inner_weight, "seq", axis=0, tiled=True)
    w_outer = lax.all_gather(outer_weight, "seq", axis=1, tiled=True)
    w_qkv = first[:, :depth, : 3 * cols].reshape(members * depth, 3 * cols)
    w_proj = first[:, :depth, 3 * cols :].reshape(members, depth, folds, width // members)
    w_proj = w_proj.transpose(2, 1, 0, 3).reshape(folds * depth, width)
    flat = first[:, depth:, :].reshape(members, -1)
    full = []
    start = 0
    for size in sizes:
        full.append(flat[:, start : start + size].reshape(-1).astype(F32))
        start += size
    b_query, b_value, b_inner, b_proj, gain_one, shift_one, b_outer, gain_two, shift_two = full

    def to_group(array, ident):
        blocks = lax.dynamic_slice_in_dim(
            array.reshape(groups, length, width), mine * piece, piece, axis=1
        )
        return swap_groups(blocks, per, parts, ident).reshape(quarter, width)

    def from_group(array, swap_id, share_id):
        blocks = swap_groups(array.reshape(groups, piece, width), per, parts, swap_id)
        every = share_over_mp(blocks.reshape(quarter, width), parts, share_id)
        every = every.reshape(parts, groups, piece, width).transpose(1, 0, 2, 3)
        return every.reshape(micro, seqs, length, width)

    x_part = to_group(tokens, 1)
    x_rows = share_over_mp(x_part, parts, 2).reshape(rows, width)
    cotan = to_group(cotangent, 3).astype(F32)

    bias = jnp.concatenate([b_query, jnp.zeros_like(b_query), b_value])
    qkv = (matmul(x_rows, w_qkv) + bias).astype(BF)
    query = qkv[:, :cols].reshape(rows, heads, DH)
    kv = jnp.concatenate(around_group(qkv[:, cols:], members, per), axis=0)
    keys = kv[:, :cols].reshape(per * rows, heads, DH)
    values = kv[:, cols:].reshape(per * rows, heads, DH)
    scale = DH ** (-0.5)

    def scores_of():
        return jnp.einsum("qhd,khd->hqk", query, keys, preferred_element_type=F32) * scale

    scores = scores_of()
    row_max = jnp.max(scores, axis=-1, keepdims=True)
    exponent = jnp.exp(scores - row_max)
    row_total = jnp.sum(exponent, axis=-1, keepdims=True)
    log_total = row_max + jnp.log(row_total)
    probs_low = (exponent / row_total).astype(BF)
    mixture = jnp.einsum("hqk,khd->qhd", probs_low, values, preferred_element_type=F32)
    mixture_low = mixture.astype(BF).reshape(rows, cols)
    first_in = (
        x_part.astype(F32)
        + sum_over_mp(matmul(mixture_low, w_proj).astype(BF), parts, 4)
        + b_proj
    )
    normal_one, inverse_one = normed(first_in)
    first_out = normal_one * gain_one + shift_one
    first_low = share_over_mp(first_out.astype(BF), parts, 5).reshape(rows, width)

    inner_pre = matmul(first_low, w_inner) + b_inner
    active = gelu_tanh(inner_pre).astype(BF)
    second_in = first_out + sum_over_mp(matmul(active, w_outer).astype(BF), parts, 6) + b_outer
    normal_two, inverse_two = normed(second_in)
    layer_out = (normal_two * gain_two + shift_two).astype(BF)
    second_grad, gain_two_grad, shift_two_grad = norm_back(cotan, normal_two, inverse_two, gain_two)
    outer_b_grad = jnp.sum(second_grad, axis=0)
    second_low = share_over_mp(second_grad.astype(BF), parts, 7).reshape(rows, width)

    outer_w_grad = lax.psum_scatter(
        over_rows(active, second_low).astype(BF), "seq", scatter_dimension=1, tiled=True
    )
    _, pull_gelu = jax.vjp(gelu_tanh, inner_pre)
    inner_grad = pull_gelu(over_cols(second_low, w_outer))[0].astype(BF)
    inner_w_grad = lax.psum_scatter(
        over_rows(first_low, inner_grad).astype(BF), "seq", scatter_dimension=0, tiled=True
    )
    inner_b_grad = jnp.sum(inner_grad.astype(F32), axis=0)
    first_grad = sum_over_mp(over_cols(inner_grad, w_inner).astype(BF), parts, 8) + second_grad
    attn_grad, gain_one_grad, shift_one_grad = norm_back(
        first_grad, normal_one, inverse_one, gain_one
    )
    proj_b_grad = jnp.sum(attn_grad, axis=0)
    attn_low = share_over_mp(attn_grad.astype(BF), parts, 9).reshape(rows, width)

    proj_w_grad = lax.psum_scatter(
        over_rows(mixture_low, attn_low).astype(BF), "seq", scatter_dimension=1, tiled=True
    )
    mixture_grad = over_cols(attn_low, w_proj).astype(BF).reshape(rows, heads, DH)
    probs = jnp.exp(scores_of() - log_total)
    prob_grad = jnp.einsum("qhd,khd->hqk", mixture_grad, values, preferred_element_type=F32)
    row_terms = jnp.einsum("qhd,qhd->hq", mixture_grad.astype(F32), mixture)
    score_grad = (probs * (prob_grad - row_terms[..., None]) * scale).astype(BF)
    query_grad = jnp.einsum("hqk,khd->qhd", score_grad, keys, preferred_element_type=F32)
    key_part = jnp.einsum("hqk,qhd->khd", score_grad, query, preferred_element_type=F32)
    value_part = jnp.einsum(
        "hqk,qhd->khd", probs.astype(BF), mixture_grad, preferred_element_type=F32
    )
    kv_part = jnp.concatenate(
        [key_part.reshape(per, rows, cols), value_part.reshape(per, rows, cols)], axis=2
    )
    kv_grad = group_sum([kv_part[i] for i in range(per)], members, per)
    qkv_grad = jnp.concatenate([query_grad.reshape(rows, cols), kv_grad], axis=1).astype(BF)
    qkv_w_grad = over_rows(x_rows, qkv_grad)
    bias_grad = jnp.sum(qkv_grad.astype(F32), axis=0)

    whole_rows = jnp.stack(
        [proj_b_grad, gain_one_grad, shift_one_grad, outer_b_grad, gain_two_grad, shift_two_grad]
        + [jnp.zeros_like(proj_b_grad)] * 2
    )
    summed_rows = lax.psum(whole_rows, "mp")
    small = jnp.concatenate(
        [
            bias_grad[:cols].reshape(members, -1),
            bias_grad[2 * cols :].reshape(members, -1),
            inner_b_grad.reshape(members, -1),
        ]
        + [summed_rows[i].reshape(members, -1) for i in range(6)],
        axis=1,
    )
    small = jnp.pad(small, ((0, 0), (0, extra * 3 * cols - small.shape[1])))
    last = jnp.concatenate(
        [
            qkv_w_grad.astype(BF).reshape(members, depth, 3 * cols),
            small.astype(BF).reshape(members, extra, 3 * cols),
        ],
        axis=1,
    )
    last = lax.psum_scatter(last, "seq", scatter_dimension=0, tiled=True)[0].astype(F32)
    pieces = []
    start = 0
    flat = last[depth:].reshape(-1)
    for size in sizes:
        pieces.append(flat[start : start + size])
        start += size

    layer_out = from_group(layer_out, 10, 11)
    input_part = (
        sum_over_mp(
            over_cols(qkv_grad, w_qkv).astype(BF),
            parts,
            12,
        )
        + attn_grad
    )
    input_grad = from_group(input_part.astype(BF), 13, 14).astype(F32)
    return (
        layer_out,
        input_grad,
        last[:depth, :cols],
        pieces[0],
        last[:depth, cols : 2 * cols],
        last[:depth, 2 * cols :],
        pieces[1],
        proj_w_grad.astype(F32),
        pieces[3],
        pieces[4],
        pieces[5],
        inner_w_grad.astype(F32),
        pieces[2],
        outer_w_grad.astype(F32),
        pieces[6],
        pieces[7],
        pieces[8],
    )


def solution(mesh):
    tokens = P(None, None, "seq", None)
    rows_cols, cols_rows, both, seq = P("seq", "mp"), P("mp", "seq"), P(("mp", "seq")), P("seq")
    weights = (
        rows_cols,
        both,
        rows_cols,
        rows_cols,
        both,
        cols_rows,
        seq,
        seq,
        seq,
        rows_cols,
        both,
        cols_rows,
        seq,
        seq,
        seq,
    )
    return jax.shard_map(
        functools.partial(on_device, mesh.shape["seq"], mesh.shape["mp"]),
        mesh=mesh,
        in_specs=(tokens,) + weights + (tokens,),
        out_specs=(tokens, tokens) + weights,
        check_vma=False,
    )
```

```python
import functools

import jax
import jax.numpy as jnp
from jax import lax
from jax.experimental import pallas as pl
from jax.experimental.pallas import tpu as pltpu
from jax.sharding import PartitionSpec as P

DH = 128
EPSILON = 1e-06
BF = jnp.bfloat16
F32 = jnp.float32
MESH = pl.DeviceIdType.MESH
ANY = pl.BlockSpec(memory_space=pl.ANY)
VMEM = pl.BlockSpec(memory_space=pltpu.VMEM)
MIB = 1 << 20


def matmul(left, right):
    return jnp.dot(left, right, preferred_element_type=F32)


def over_rows(left, right):
    return lax.dot_general(left, right, (((0,), (0,)), ((), ())), preferred_element_type=F32)


def over_cols(left, right):
    return lax.dot_general(left, right, (((1,), (1,)), ((), ())), preferred_element_type=F32)


def gelu_tanh(values):
    return jax.nn.gelu(values, approximate=True)


def square():
    me = lax.axis_index("mp")
    return me, me + 1 - 2 * lax.rem(me, 2), lax.rem(me + 2, 4), 3 - me


def greet(devices):
    barrier = pltpu.get_barrier_semaphore()
    for device in devices:
        pl.semaphore_signal(barrier, inc=1, device_id=device, device_id_type=MESH)
    pl.semaphore_wait(barrier, len(devices))


def sender(send_sem, recv_sem):
    def send(source, target, slot, device):
        copy = pltpu.make_async_remote_copy(
            src_ref=source,
            dst_ref=target,
            send_sem=send_sem.at[slot],
            recv_sem=recv_sem.at[slot],
            device_id=device,
            device_id_type=MESH,
        )
        copy.start()
        return copy

    return send


class Exchange:
    def __init__(self, part_ref, landed, relay, send_sem, recv_sem):
        self.me, self.along_x, self.along_y, self.across = square()
        self.part, self.landed, self.relay = part_ref, landed, relay
        self.send = sender(send_sem, recv_sem)
        self.copies = {}

    def ways(self, index):
        pair = (self.along_x, self.along_y)
        return pair if index % 2 == 0 else pair[::-1]

    def start(self, index, piece):
        near, _ = self.ways(index)
        for kind, owner in enumerate((self.across, near)):
            self.copies[index, kind] = self.send(
                self.part.at[owner, piece], self.landed.at[index, kind], 6 * index + kind, {"mp": near}
            )

    def pass_on(self, index, piece):
        _, far = self.ways(index)
        self.copies[index, 0].wait_recv()
        self.relay[index] = (
            self.part[far, piece].astype(F32) + self.landed[index, 0].astype(F32)
        ).astype(BF)
        self.copies[index, 2] = self.send(
            self.relay.at[index], self.landed.at[index, 2], 6 * index + 2, {"mp": far}
        )

    def total(self, index, piece):
        self.copies[index, 1].wait_recv()
        self.copies[index, 2].wait_recv()
        return (
            self.part[self.me, piece].astype(F32)
            + self.landed[index, 1].astype(F32)
            + self.landed[index, 2].astype(F32)
        )

    def share(self, index, source, target):
        near, far = self.ways(index)
        self.copies[index, 3] = self.send(source, target(self.me), 6 * index + 3, {"mp": near})
        self.copies[index, 4] = self.send(source, target(self.me), 6 * index + 4, {"mp": far})

    def forward(self, index, target):
        near, far = self.ways(index)
        self.copies[index, 3].wait_recv()
        self.copies[index, 5] = self.send(target(near), target(near), 6 * index + 5, {"mp": far})

    def finish(self, count):
        for index in range(count):
            self.copies[index, 4].wait_recv()
            self.copies[index, 5].wait_recv()
        for copy in self.copies.values():
            copy.wait_send()


def piece_order(groups):
    return list(range(1, groups, 2)) + list(range(0, groups, 2)) if groups == 2 else (
        [1, 2, 0] + list(range(3, groups))
    )


def planes(groups, per):
    index = lax.axis_index("seq")
    return [{"seq": lax.rem(index + step * per, groups * per)} for step in range(groups)]


def mean_of(values):
    return jnp.mean(values, axis=-1, keepdims=True)


def normed(values):
    centre = values - mean_of(values)
    inverse = lax.rsqrt(mean_of(centre * centre) + EPSILON)
    return centre * inverse, inverse


def norm_back(grad, normal, inverse, gain):
    inner = grad * gain
    return inverse * (inner - mean_of(inner) - normal * mean_of(inner * normal))


def run_pieces(exchange, groups, work):
    order = piece_order(groups)
    places = list(enumerate(order))
    half = groups // 2
    first, second = places[:half], places[half:]
    for index, piece in first:
        exchange.start(index, piece)
    for index, piece in first:
        exchange.pass_on(index, piece)
    for index, piece in second:
        exchange.start(index, piece)
    for index, piece in first:
        work(index, piece, exchange.total(index, piece))
    for index, piece in second:
        exchange.pass_on(index, piece)
    return first, second


def first_norm_kernel(
    groups, part_ref, x_ref, rows_ref, low_ref, normal_ref, inverse_ref,
    landed, relay, ready, send_sem, recv_sem, local_sem,
):
    exchange = Exchange(part_ref, landed, relay, send_sem, recv_sem)
    greet([{"mp": exchange.along_x}, {"mp": exchange.along_y}])
    local = []

    def target(piece):
        return lambda device: low_ref.at[device, piece]

    def work(index, piece, total):
        values = x_ref[piece].astype(F32) + total + rows_ref[0:1]
        normal, inverse = normed(values)
        normal_ref[piece] = normal
        inverse_ref[piece] = inverse
        ready[index] = (normal * rows_ref[1:2] + rows_ref[2:3]).astype(BF)
        exchange.share(index, ready.at[index], target(piece))
        copy = pltpu.make_async_copy(
            ready.at[index], low_ref.at[exchange.me, piece], local_sem.at[index]
        )
        copy.start()
        local.append(copy)

    first, second = run_pieces(exchange, groups, work)
    for index, piece in first:
        exchange.forward(index, target(piece))
    for index, piece in second:
        work(index, piece, exchange.total(index, piece))
    for index, piece in second:
        exchange.forward(index, target(piece))
    exchange.finish(groups)
    for copy in local:
        copy.wait()


def second_norm_kernel(
    groups, per, part_ref, normal_ref, cotan_ref, rows_ref,
    low_ref, grad_ref, back_ref, sums_ref,
    landed, relay, ready, layer, cotan_in, send_sem, recv_sem, local_sem,
):
    exchange = Exchange(part_ref, landed, relay, send_sem, recv_sem)
    peers = planes(groups, per)
    greet([{"mp": exchange.along_x}, {"mp": exchange.along_y}] + peers[1:])
    base = 6 * groups
    arriving = {
        step: exchange.send(cotan_ref.at[step], cotan_in.at[step], base + step, peers[step])
        for step in range(1, groups)
    }
    leaving, local = [], []
    sums_ref[...] = jnp.zeros_like(sums_ref)

    def target(piece):
        return lambda device: low_ref.at[device, piece]

    def keep(source, place, slot):
        copy = pltpu.make_async_copy(source, place, local_sem.at[slot])
        copy.start()
        local.append(copy)

    def work(index, piece, total):
        gain_one, shift_one, bias = rows_ref[0:1], rows_ref[1:2], rows_ref[2:3]
        gain, shift = rows_ref[3:4], rows_ref[4:5]
        values = normal_ref[piece] * gain_one + shift_one + total + bias
        normal, inverse = normed(values)
        layer[index] = (normal * gain + shift).astype(BF)
        if piece == 0:
            keep(layer.at[index], back_ref.at[0], groups)
            cotan = cotan_ref[0].astype(F32)
        else:
            leaving.append(
                exchange.send(
                    layer.at[index], back_ref.at[piece], base + groups + piece, peers[groups - piece]
                )
            )
            arriving[piece].wait_recv()
            cotan = cotan_in[piece].astype(F32)
        grad = norm_back(cotan, normal, inverse, gain)
        grad_ref[piece] = grad
        ready[index] = grad.astype(BF)
        exchange.share(index, ready.at[index], target(piece))
        keep(ready.at[index], low_ref.at[exchange.me, piece], index)
        sums_ref[0:1] += jnp.sum(grad, axis=0, keepdims=True)
        sums_ref[1:2] += jnp.sum(cotan * normal, axis=0, keepdims=True)
        sums_ref[2:3] += jnp.sum(cotan, axis=0, keepdims=True)

    first, second = run_pieces(exchange, groups, work)
    for index, piece in first:
        exchange.forward(index, target(piece))
    for index, piece in second:
        work(index, piece, exchange.total(index, piece))
    for index, piece in second:
        exchange.forward(index, target(piece))
    exchange.finish(groups)
    for copy in leaving:
        copy.wait()
    for copy in arriving.values():
        copy.wait_send()
    for copy in local:
        copy.wait()


def first_back_kernel(
    groups, part_ref, grad_ref, normal_ref, inverse_ref, sums_in_ref, rows_ref,
    low_ref, out_ref, sums_ref,
    landed, relay, ready, own_sums, send_sem, recv_sem, local_sem,
):
    exchange = Exchange(part_ref, landed, relay, send_sem, recv_sem)
    greet([{"mp": exchange.along_x}, {"mp": exchange.along_y}, {"mp": exchange.across}])
    local = []
    own_sums[...] = sums_in_ref[...]

    def target(piece):
        return lambda device: low_ref.at[device, piece]

    def keep(source, place, slot):
        copy = pltpu.make_async_copy(source, place, local_sem.at[slot])
        copy.start()
        local.append(copy)

    def work(index, piece, total):
        grad = total + grad_ref[piece]
        normal = normal_ref[piece]
        moved = norm_back(grad, normal, inverse_ref[piece], rows_ref[0:1])
        out_ref[piece] = moved
        ready[index] = moved.astype(BF)
        exchange.share(index, ready.at[index], target(piece))
        keep(ready.at[index], low_ref.at[exchange.me, piece], index)
        own_sums[3:4] += jnp.sum(moved, axis=0, keepdims=True)
        own_sums[4:5] += jnp.sum(grad * normal, axis=0, keepdims=True)
        own_sums[5:6] += jnp.sum(grad, axis=0, keepdims=True)

    first, second = run_pieces(exchange, groups, work)
    for index, piece in first:
        exchange.forward(index, target(piece))
    for index, piece in second:
        work(index, piece, exchange.total(index, piece))
    others = [
        exchange.send(own_sums, sums_ref.at[exchange.me], 6 * groups + slot, {"mp": device})
        for slot, device in enumerate((exchange.along_x, exchange.along_y, exchange.across))
    ]
    keep(own_sums, sums_ref.at[exchange.me], groups)
    for index, piece in second:
        exchange.forward(index, target(piece))
    exchange.finish(groups)
    for copy in others:
        copy.wait()
    for copy in local:
        copy.wait()


def input_kernel(
    groups, per, part_ref, grad_ref, small_ref,
    all_ref, small_out,
    landed, relay, ready, back, send_sem, recv_sem, local_sem,
):
    exchange = Exchange(part_ref, landed, relay, send_sem, recv_sem)
    peers = planes(groups, per)
    members = groups * per
    here = lax.axis_index("seq")
    group = here // per
    devices = [{"seq": lax.rem(here + step, members)} for step in range(1, members)]
    greet([{"mp": exchange.along_x}, {"mp": exchange.along_y}] + devices)
    base = 6 * groups
    small = [
        exchange.send(
            small_ref.at[lax.rem(here + step, members)],
            small_out.at[here],
            base + groups + step,
            devices[step - 1],
        )
        for step in range(1, members)
    ]
    crossing, local = {}, []

    def keep(source, place, slot):
        copy = pltpu.make_async_copy(source, place, local_sem.at[slot])
        copy.start()
        local.append(copy)

    keep(small_ref.at[here], small_out.at[here], groups)

    def target(piece):
        sequence = lax.rem(group + piece, groups)
        return lambda device: all_ref.at[sequence, device]

    def work(index, piece, total):
        ready[piece] = (total + grad_ref[piece]).astype(BF)
        if piece > 0:
            crossing[piece] = exchange.send(
                ready.at[piece], back.at[piece], base + piece, peers[groups - piece]
            )

    def share(index, piece):
        source = ready.at[0]
        if piece > 0:
            crossing[piece].wait_recv()
            source = back.at[piece]
        exchange.share(index, source, target(piece))
        keep(source, target(piece)(exchange.me), index)

    first, second = run_pieces(exchange, groups, work)
    for index, piece in second:
        work(index, piece, exchange.total(index, piece))
    outward = [place for place in second if place[1] == 0] + first
    outward += [place for place in second if place[1] > 0]
    for index, piece in outward:
        share(index, piece)
    for index, piece in outward:
        exchange.forward(index, target(piece))
    exchange.finish(groups)
    for copy in small:
        copy.wait()
    for copy in crossing.values():
        copy.wait_send()
    for copy in local:
        copy.wait()


def exchange_call(kernel, ident, operands, results, groups, piece, width, scratch, extra):
    return pl.pallas_call(
        kernel,
        out_shape=tuple(jax.ShapeDtypeStruct(shape, dtype) for shape, dtype, _ in results),
        in_specs=[VMEM] * len(operands),
        out_specs=tuple(spec for _, _, spec in results),
        scratch_shapes=[
            pltpu.VMEM((groups, 3, piece, width), BF),
            pltpu.VMEM((groups, piece, width), BF),
            pltpu.VMEM((groups, piece, width), BF),
        ]
        + scratch
        + [
            pltpu.SemaphoreType.DMA((6 * groups + extra,)),
            pltpu.SemaphoreType.DMA((6 * groups + extra,)),
            pltpu.SemaphoreType.DMA((groups + 1,)),
        ],
        compiler_params=pltpu.CompilerParams(
            collective_id=ident, has_side_effects=True, vmem_limit_bytes=52 * MIB
        ),
        cost_estimate=pl.CostEstimate(flops=0, bytes_accessed=200 * MIB, transcendentals=0),
        name=f"exchange_{ident}",
    )(*operands)


def first_norm(part, x_part, rows, parts, ident):
    groups, piece, width = x_part.shape
    if parts != 4:
        total = lax.psum_scatter(part, "mp", scatter_dimension=0, tiled=True).astype(F32)
        values = x_part.astype(F32) + total.reshape(x_part.shape) + rows[0]
        normal, inverse = normed(values)
        low = lax.all_gather((normal * rows[1] + rows[2]).astype(BF), "mp", axis=0)
        return low, normal, inverse
    return exchange_call(
        functools.partial(first_norm_kernel, groups),
        ident,
        (part.reshape(parts, groups, piece, width), x_part, rows),
        [
            ((parts, groups, piece, width), BF, ANY),
            ((groups, piece, width), F32, VMEM),
            ((groups, piece, 1), F32, VMEM),
        ],
        groups, piece, width, [], 0,
    )


def second_norm(part, normal, cotan, rows, members, parts, ident):
    groups, piece, width = normal.shape
    if parts != 4:
        total = lax.psum_scatter(part, "mp", scatter_dimension=0, tiled=True).astype(F32)
        values = normal * rows[0] + rows[1] + total.reshape(normal.shape) + rows[2]
        normal, inverse = normed(values)
        layer = (normal * rows[3] + rows[4]).astype(BF)
        back = jnp.stack(swap_blocks(layer, members, -1))
        cotan = jnp.stack(swap_blocks(cotan, members, 1)).astype(F32)
        grad = norm_back(cotan, normal, inverse, rows[3])
        sums = [jnp.sum(array, axis=(0, 1)) for array in (grad, cotan * normal, cotan)]
        sums = jnp.stack(sums + [jnp.zeros_like(sums[0])] * 5)
        return lax.all_gather(grad.astype(BF), "mp", axis=0), grad, back, sums
    return exchange_call(
        functools.partial(second_norm_kernel, groups, members // groups),
        ident,
        (part.reshape(parts, groups, piece, width), normal, cotan, rows),
        [
            ((parts, groups, piece, width), BF, ANY),
            ((groups, piece, width), F32, VMEM),
            ((groups, piece, width), BF, ANY),
            ((8, width), F32, VMEM),
        ],
        groups, piece, width,
        [pltpu.VMEM((groups, piece, width), BF), pltpu.VMEM((groups, piece, width), BF)],
        2 * groups,
    )


def first_back(part, grad, normal, inverse, sums, rows, parts, ident):
    groups, piece, width = normal.shape
    if parts != 4:
        total = lax.psum_scatter(part, "mp", scatter_dimension=0, tiled=True).astype(F32)
        grad = total.reshape(normal.shape) + grad
        moved = norm_back(grad, normal, inverse, rows[0])
        more = [jnp.sum(array, axis=(0, 1)) for array in (moved, grad * normal, grad)]
        sums = sums.at[3:6].add(jnp.stack(more))
        return (
            lax.all_gather(moved.astype(BF), "mp", axis=0),
            moved,
            lax.all_gather(sums, "mp", axis=0),
        )
    return exchange_call(
        functools.partial(first_back_kernel, groups),
        ident,
        (part.reshape(parts, groups, piece, width), grad, normal, inverse, sums, rows),
        [
            ((parts, groups, piece, width), BF, ANY),
            ((groups, piece, width), F32, VMEM),
            ((parts, 8, width), F32, VMEM),
        ],
        groups, piece, width, [pltpu.VMEM((8, width), F32)], 3,
    )


def input_gradient(part, grad, small, members, parts, ident):
    groups, piece, width = grad.shape
    if parts != 4:
        total = lax.psum_scatter(part, "mp", scatter_dimension=0, tiled=True).astype(F32)
        ready = (total.reshape(grad.shape) + grad).astype(BF)
        back = jnp.stack(swap_blocks(ready, members, -1))
        back = jnp.roll(back, lax.axis_index("seq") // (members // groups), axis=0)
        return lax.all_gather(back, "mp", axis=1), lax.all_to_all(small, "seq", 0, 0)
    return exchange_call(
        functools.partial(input_kernel, groups, members // groups),
        ident,
        (part.reshape(parts, groups, piece, width), grad, small),
        [((groups, parts, piece, width), BF, ANY), (small.shape, F32, VMEM)],
        groups, piece, width, [pltpu.VMEM((groups, piece, width), BF)], groups + members,
    )


def share_kernel(own_ref, all_ref, send_sem, recv_sem, local_sem):
    me, along_x, along_y, _ = square()
    to_x, to_y = {"mp": along_x}, {"mp": along_y}
    greet([to_x, to_y])
    send = sender(send_sem, recv_sem)
    half = own_ref.shape[0] // 2
    upper, lower = pl.ds(0, half), pl.ds(half, half)
    copies = [
        send(own_ref.at[upper], all_ref.at[me, upper], 0, to_x),
        send(own_ref.at[lower], all_ref.at[me, lower], 1, to_y),
        send(own_ref.at[lower], all_ref.at[me, lower], 2, to_x),
        send(own_ref.at[upper], all_ref.at[me, upper], 3, to_y),
    ]
    local = pltpu.make_async_copy(own_ref, all_ref.at[me], local_sem)
    local.start()
    copies[0].wait_recv()
    copies.append(send(all_ref.at[along_x, upper], all_ref.at[along_x, upper], 4, to_y))
    copies[1].wait_recv()
    copies.append(send(all_ref.at[along_y, lower], all_ref.at[along_y, lower], 5, to_x))
    for copy in copies[2:]:
        copy.wait_recv()
    for copy in copies:
        copy.wait_send()
    local.wait()


def share_over_mp(own, parts, ident):
    if parts != 4:
        return lax.all_gather(own, "mp", axis=0)
    return pl.pallas_call(
        share_kernel,
        out_shape=jax.ShapeDtypeStruct((parts,) + own.shape, own.dtype),
        in_specs=[ANY],
        out_specs=ANY,
        scratch_shapes=[
            pltpu.SemaphoreType.DMA((6,)),
            pltpu.SemaphoreType.DMA((6,)),
            pltpu.SemaphoreType.DMA,
        ],
        compiler_params=pltpu.CompilerParams(collective_id=ident, has_side_effects=True),
        cost_estimate=pl.CostEstimate(flops=0, bytes_accessed=100 * MIB, transcendentals=0),
        name=f"share_over_mp_{ident}",
    )(own)


def swap_kernel(
    groups, per, sign, block_ref, small_ref, out_ref, small_out, send_sem, recv_sem, local_sem
):
    members = groups * per
    index = lax.axis_index("seq")
    devices = [{"seq": lax.rem(index + step, members)} for step in range(1, members)]
    greet(devices)
    send = sender(send_sem, recv_sem)
    copies = []
    for step in range(1, groups):
        ahead = step if sign > 0 else groups - step
        source = block_ref.at[step]
        copies.append(send(source, out_ref.at[step], step, devices[ahead * per - 1]))
    for step in range(1, members):
        target = lax.rem(index + step, members)
        copies.append(
            send(small_ref.at[target], small_out.at[index], groups + step, devices[step - 1])
        )
    locals_ = [
        pltpu.make_async_copy(block_ref.at[0], out_ref.at[0], local_sem.at[0]),
        pltpu.make_async_copy(small_ref.at[index], small_out.at[index], local_sem.at[1]),
    ]
    for local in locals_:
        local.start()
    for local in locals_:
        local.wait()
    for copy in copies:
        copy.wait()


def shift_pairs(members, ahead):
    return [(index, (index + ahead) % members) for index in range(members)]


def swap_blocks(blocks, members, sign):
    groups = blocks.shape[0]
    per = members // groups
    arrived = [blocks[0]]
    for step in range(1, groups):
        pairs = shift_pairs(members, sign * step * per)
        arrived.append(lax.ppermute(blocks[step], "seq", pairs))
    return arrived


def swap_groups(blocks, small, members, parts, sign, ident):
    groups = blocks.shape[0]
    per = members // groups
    if parts != 4:
        return jnp.stack(swap_blocks(blocks, members, sign)), lax.all_to_all(small, "seq", 0, 0)
    return pl.pallas_call(
        functools.partial(swap_kernel, groups, per, sign),
        out_shape=(
            jax.ShapeDtypeStruct(blocks.shape, blocks.dtype),
            jax.ShapeDtypeStruct(small.shape, small.dtype),
        ),
        in_specs=[ANY, ANY],
        out_specs=(ANY, ANY),
        scratch_shapes=[
            pltpu.SemaphoreType.DMA((groups + members,)),
            pltpu.SemaphoreType.DMA((groups + members,)),
            pltpu.SemaphoreType.DMA((2,)),
        ],
        compiler_params=pltpu.CompilerParams(collective_id=ident, has_side_effects=True),
        cost_estimate=pl.CostEstimate(flops=0, bytes_accessed=60 * MIB, transcendentals=0),
        name=f"swap_groups_{ident}",
    )(blocks, small)


def score_block(keys, queries):
    return lax.dot_general(keys, queries, (((1,), (1,)), ((), ())), preferred_element_type=F32)


def attend_kernel(
    query_ref, key_ref, value_ref, key_far_ref, value_far_ref, mix_ref, low_ref, log_ref, turned
):
    rows = key_ref.shape[0]

    @pl.when(pl.program_id(1) == 0)
    def _():
        turned[:, :rows] = value_ref[...].T
        turned[:, rows:] = value_far_ref[...].T

    scale = DH ** (-0.5)
    near = score_block(key_ref[...], query_ref[...])
    far = score_block(key_far_ref[...], query_ref[...])
    highest = jnp.maximum(
        jnp.max(near, axis=0, keepdims=True), jnp.max(far, axis=0, keepdims=True)
    )
    near = jnp.exp((near - highest) * scale)
    far = jnp.exp((far - highest) * scale)
    total = jnp.sum(near, axis=0, keepdims=True) + jnp.sum(far, axis=0, keepdims=True)
    mix = jnp.dot(turned[:, :rows], near.astype(BF), preferred_element_type=F32)
    mix += jnp.dot(turned[:, rows:], far.astype(BF), preferred_element_type=F32)
    mix = (mix / total).T
    mix_ref[...] = mix
    low_ref[...] = mix.astype(BF)
    log_ref[0] = highest * scale + jnp.log(total)


def attend(qkv, kv_far, heads):
    rows, cols = qkv.shape[0], heads * DH
    away = kv_far.shape[0]
    block = min(512, rows)

    def tile(offset):
        return pl.BlockSpec((block, DH), lambda h, i: (i, offset + h))

    def long(count, offset):
        return pl.BlockSpec((count, DH), lambda h, i: (0, offset + h))

    return pl.pallas_call(
        attend_kernel,
        grid=(heads, rows // block),
        out_shape=(
            jax.ShapeDtypeStruct((rows, cols), F32),
            jax.ShapeDtypeStruct((rows, cols), BF),
            jax.ShapeDtypeStruct((heads, 1, rows), F32),
        ),
        in_specs=[
            tile(0),
            long(rows, heads),
            long(rows, 2 * heads),
            long(away, 0),
            long(away, heads),
        ],
        out_specs=(tile(0), tile(0), pl.BlockSpec((1, 1, block), lambda h, i: (h, 0, i))),
        scratch_shapes=[pltpu.VMEM((DH, rows + away), BF)],
        compiler_params=pltpu.CompilerParams(vmem_limit_bytes=52 * MIB),
        cost_estimate=pl.CostEstimate(
            flops=8 * rows * (rows + away) * cols,
            bytes_accessed=20 * rows * cols,
            transcendentals=rows * (rows + away) * heads,
        ),
        name="attend",
    )(qkv, qkv, qkv, kv_far, kv_far)


def layer_copies(back_ref, all_ref, send_sem, recv_sem, groups, per):
    me, along_x, along_y, _ = square()
    group = lax.axis_index("seq") // per
    copies = []
    for piece in range(groups):
        near, far = (along_x, along_y) if piece % 2 == 0 else (along_y, along_x)
        sequence = lax.rem(group + piece, groups)
        block, own, passed = back_ref.at[piece], all_ref.at[sequence, me], all_ref.at[sequence, near]
        for kind, (source, target, device) in enumerate(
            ((block, own, near), (block, own, far), (passed, passed, far))
        ):
            copies.append(
                pltpu.make_async_remote_copy(
                    src_ref=source,
                    dst_ref=target,
                    send_sem=send_sem.at[3 * piece + kind],
                    recv_sem=recv_sem.at[3 * piece + kind],
                    device_id={"mp": device},
                    device_id_type=MESH,
                )
            )
    return copies[0::3], copies[1::3], copies[2::3]


def attend_back_kernel(
    groups,
    per,
    step,
    query_ref,
    key_ref,
    value_ref,
    key_far_ref,
    value_far_ref,
    grad_ref,
    mix_ref,
    log_ref,
    *rest,
):
    sharing = groups > 0
    if sharing:
        back_ref, *rest = rest
    dquery_ref, dkey_ref, dvalue_ref, dkey_far_ref, dvalue_far_ref, *rest = rest
    if sharing:
        all_ref, *rest = rest
    turned, key_sum, value_sum, *rest = rest
    block = pl.program_id(1)
    rows = key_ref.shape[0]
    if sharing:
        send_sem, recv_sem, local_sem = rest
        now = pl.program_id(0) * pl.num_programs(1) + block
        count = pl.num_programs(0) * pl.num_programs(1)
        near, far, passed = layer_copies(back_ref, all_ref, send_sem, recv_sem, groups, per)
        me, along_x, along_y, _ = square()
        group = lax.axis_index("seq") // per
        local = [
            pltpu.make_async_copy(
                back_ref.at[piece],
                all_ref.at[lax.rem(group + piece, groups), me],
                local_sem.at[piece],
            )
            for piece in range(groups)
        ]

        @pl.when(now == 0)
        def _():
            greet([{"mp": along_x}, {"mp": along_y}])
            for copy in near + far + local:
                copy.start()

        @pl.when(now == count * 5 // 8)
        def _():
            for first, second in zip(near, passed):
                first.wait_recv()
                second.start()

    @pl.when(block == 0)
    def _():
        turned[:, :rows] = key_ref[...].T
        turned[:, rows:] = key_far_ref[...].T
        key_sum[...] = jnp.zeros_like(key_sum)
        value_sum[...] = jnp.zeros_like(value_sum)

    scale = DH ** (-0.5)
    query, grad = query_ref[...], grad_ref[...]
    terms = jnp.sum((grad.astype(F32) * mix_ref[...]).T, axis=0, keepdims=True)
    logs = log_ref[0]
    dquery = jnp.zeros((DH, query.shape[0]), F32)
    spans = [(key_ref, value_ref, start, start) for start in range(0, rows, step)]
    spans += [
        (key_far_ref, value_far_ref, start, rows + start)
        for start in range(0, key_far_ref.shape[0], step)
    ]
    for keys, values, start, place in spans:
        part = pl.ds(place, step)
        probs = jnp.exp(score_block(keys[pl.ds(start, step)], query) * scale - logs)
        prob_grad = score_block(values[pl.ds(start, step)], grad)
        score_grad = (probs * (prob_grad - terms) * scale).astype(BF)
        value_sum[part] += jnp.dot(probs.astype(BF), grad, preferred_element_type=F32)
        key_sum[part] += jnp.dot(score_grad, query, preferred_element_type=F32)
        dquery += jnp.dot(turned[:, part], score_grad, preferred_element_type=F32)
    dquery_ref[...] = dquery.T.astype(BF)

    @pl.when(block == pl.num_programs(1) - 1)
    def _():
        dkey_ref[...] = key_sum[:rows]
        dvalue_ref[...] = value_sum[:rows]
        dkey_far_ref[...] = key_sum[rows:].astype(BF)
        dvalue_far_ref[...] = value_sum[rows:].astype(BF)

    if sharing:

        @pl.when(now == count - 1)
        def _():
            for copy in far + passed:
                copy.wait_recv()
            for copy in near + far + passed:
                copy.wait_send()
            for copy in local:
                copy.wait()


def attend_back(qkv, kv_far, grad, mix, logs, heads, layer_back, per, parts, ident):
    rows, cols = qkv.shape[0], heads * DH
    away = kv_far.shape[0]
    block, step = min(512, rows), min(512, rows)
    sharing = parts == 4
    groups, piece, width = layer_back.shape

    def tile(offset):
        return pl.BlockSpec((block, DH), lambda h, i: (i, offset + h))

    def long(count, offset):
        return pl.BlockSpec((count, DH), lambda h, i: (0, offset + h))

    results = pl.pallas_call(
        functools.partial(attend_back_kernel, groups if sharing else 0, per, step),
        grid=(heads, rows // block),
        out_shape=(
            jax.ShapeDtypeStruct((rows, cols), BF),
            jax.ShapeDtypeStruct((rows, cols), F32),
            jax.ShapeDtypeStruct((rows, cols), F32),
            jax.ShapeDtypeStruct((away, cols), BF),
            jax.ShapeDtypeStruct((away, cols), BF),
        )
        + ((jax.ShapeDtypeStruct((groups, parts, piece, width), BF),) if sharing else ()),
        in_specs=[
            tile(0),
            long(rows, heads),
            long(rows, 2 * heads),
            long(away, 0),
            long(away, heads),
            tile(0),
            tile(0),
            pl.BlockSpec((1, 1, block), lambda h, i: (h, 0, i)),
        ]
        + ([ANY] if sharing else []),
        out_specs=(tile(0), long(rows, 0), long(rows, 0), long(away, 0), long(away, 0))
        + ((ANY,) if sharing else ()),
        scratch_shapes=[
            pltpu.VMEM((DH, rows + away), BF),
            pltpu.VMEM((rows + away, DH), F32),
            pltpu.VMEM((rows + away, DH), F32),
        ]
        + (
            [
                pltpu.SemaphoreType.DMA((3 * groups,)),
                pltpu.SemaphoreType.DMA((3 * groups,)),
                pltpu.SemaphoreType.DMA((groups,)),
            ]
            if sharing
            else []
        ),
        compiler_params=pltpu.CompilerParams(
            vmem_limit_bytes=52 * MIB,
            **(dict(collective_id=ident, has_side_effects=True) if sharing else {}),
        ),
        cost_estimate=pl.CostEstimate(
            flops=20 * rows * (rows + away) * cols,
            bytes_accessed=30 * rows * cols,
            transcendentals=rows * (rows + away) * heads,
        ),
        name="attend_back",
    )(qkv, qkv, qkv, kv_far, kv_far, grad, mix, logs, *([layer_back] if sharing else []))
    if sharing:
        return results
    layer = jnp.roll(layer_back, lax.axis_index("seq") // per, axis=0)
    return (*results, lax.all_gather(layer, "mp", axis=1))


def from_group_members(block, members, per):
    blocks = []
    for step in range(1, per):
        pairs = [
            (base + place, base + (place - step) % per)
            for base in range(0, members, per)
            for place in range(per)
        ]
        blocks.append(lax.ppermute(block, "seq", pairs))
    return blocks


def to_group_members(total, blocks, members, per):
    for step in range(1, per):
        pairs = [
            (base + place, base + (place + step) % per)
            for base in range(0, members, per)
            for place in range(per)
        ]
        total = total + lax.ppermute(blocks[step - 1], "seq", pairs).astype(F32)
    return total


def packed(vectors, lines):
    flat = jnp.concatenate(vectors)
    return jnp.pad(flat, (0, lines * 128 - flat.shape[0])).reshape(lines, 128)


def after(value, *others):
    return lax.optimization_barrier((value,) + others)[0]


def on_device(members, parts, *arrays):
    (
        tokens,
        query_weight,
        query_bias,
        key_weight,
        value_weight,
        value_bias,
        proj_weight,
        proj_bias,
        gain_first,
        shift_first,
        inner_weight,
        inner_bias,
        outer_weight,
        outer_bias,
        gain_second,
        shift_second,
        cotangent,
    ) = arrays
    micro, seqs, length, width = tokens.shape
    groups = micro * seqs
    per = members // groups
    assert per * groups == members
    piece = length // parts
    rows = groups * length
    quarter = groups * piece
    mine = lax.axis_index("mp")
    group = lax.axis_index("seq") // per

    depth, cols = query_weight.shape
    narrow = width // members
    heads = cols // DH
    proj_fold = proj_weight.reshape(-1, depth, narrow)
    folds = proj_fold.shape[0]
    first = jnp.concatenate(
        [query_weight, key_weight, value_weight] + [proj_fold[i] for i in range(folds)], axis=1
    )
    first = lax.all_gather(first, "seq", axis=0, tiled=True)
    w_inner = lax.all_gather(inner_weight, "seq", axis=0, tiled=True)
    w_outer = lax.all_gather(outer_weight, "seq", axis=1, tiled=True)
    w_qkv = first[:, : 3 * cols]
    w_proj = first[:, 3 * cols :].reshape(members, depth, folds, narrow)
    w_proj = w_proj.transpose(2, 1, 0, 3).reshape(folds * depth, width)
    vectors = [
        query_bias,
        value_bias,
        inner_bias,
        proj_bias,
        gain_first,
        shift_first,
        outer_bias,
        gain_second,
        shift_second,
    ]
    sizes = [vector.shape[0] for vector in vectors]
    lines = -(-sum(sizes) // 2048) * 16
    own_vectors = packed(vectors, lines)

    def to_blocks(array):
        array = array.reshape(groups, length, width)
        return [
            lax.dynamic_slice(
                array, (lax.rem(group + k, groups), mine * piece, 0), (1, piece, width)
            )[0]
            for k in range(groups)
        ]

    x_part, all_vectors = swap_groups(
        jnp.stack(to_blocks(tokens)),
        jnp.broadcast_to(own_vectors[None], (members, lines, 128)),
        members,
        parts,
        1,
        1,
    )
    x_part = x_part.reshape(quarter, width)
    x_rows = share_over_mp(x_part, parts, 7).reshape(rows, width)
    all_vectors = all_vectors.reshape(members, -1).astype(F32)
    full = []
    start = 0
    for size in sizes:
        full.append(all_vectors[:, start : start + size].reshape(-1))
        start += size
    b_query, b_value, b_inner, b_proj, gain_one, shift_one, b_outer, gain_two, shift_two = full

    bias = jnp.concatenate([b_query, jnp.zeros_like(b_query), b_value])
    qkv = (matmul(x_rows, w_qkv) + bias).astype(BF)
    kv_far = from_group_members(qkv[:, cols:], members, per)
    kv_far = kv_far[0] if per == 2 else jnp.concatenate(kv_far, axis=0)
    mixture, mixture_low, logs = attend(qkv, kv_far, heads)

    def blocked(array):
        return array.reshape(groups, piece, width)

    first_low, normal_one, inverse_one = first_norm(
        matmul(mixture_low, w_proj).astype(BF),
        blocked(x_part),
        jnp.stack([b_proj, gain_one, shift_one]),
        parts,
        2,
    )
    first_low = first_low.reshape(rows, width)

    inner_pre = matmul(first_low, w_inner) + b_inner
    active = gelu_tanh(inner_pre).astype(BF)
    second_low, second_grad, layer_back, sums = second_norm(
        matmul(active, w_outer).astype(BF),
        normal_one,
        jnp.stack(to_blocks(cotangent)),
        jnp.stack([gain_one, shift_one, b_outer, gain_two, shift_two]),
        members,
        parts,
        3,
    )
    second_low = second_low.reshape(rows, width)

    outer_w_part = over_rows(active, second_low).astype(BF)
    outer_w_grad = lax.psum_scatter(outer_w_part, "seq", scatter_dimension=1, tiled=True)
    second_low = after(second_low, outer_w_part)
    _, pull_gelu = jax.vjp(gelu_tanh, inner_pre)
    inner_grad = pull_gelu(over_cols(second_low, w_outer))[0].astype(BF)
    inner_b_grad = jnp.sum(inner_grad.astype(F32), axis=0)
    first_part = over_cols(inner_grad, w_inner).astype(BF)
    inner_w_part = over_rows(first_low, inner_grad).astype(BF)
    inner_w_grad = lax.psum_scatter(inner_w_part, "seq", scatter_dimension=0, tiled=True)
    attn_low, attn_grad, summed_rows = first_back(
        after(first_part, inner_w_part),
        second_grad,
        normal_one,
        inverse_one,
        sums,
        gain_one[None],
        parts,
        4,
    )
    attn_low = after(attn_low.reshape(rows, width), outer_w_grad)
    summed_rows = jnp.sum(summed_rows, axis=0)

    proj_w_part = over_rows(mixture_low, attn_low).astype(BF)
    proj_w_grad = lax.psum_scatter(proj_w_part, "seq", scatter_dimension=1, tiled=True)
    mixture_grad = over_cols(after(attn_low, proj_w_part), w_proj).astype(BF)
    query_grad, key_grad, value_grad, key_away, value_away, layer_out = attend_back(
        qkv, kv_far, mixture_grad, mixture, logs, heads, layer_back, per, parts, 5
    )

    def blocks_of(array):
        return [array[i * rows : (i + 1) * rows] for i in range(per - 1)]

    key_grad = to_group_members(key_grad, blocks_of(key_away), members, per)
    value_grad = to_group_members(value_grad, blocks_of(value_away), members, per)
    qkv_grad = jnp.concatenate([query_grad, key_grad.astype(BF), value_grad.astype(BF)], axis=1)
    qkv_w_part = over_rows(x_rows, qkv_grad).astype(BF)
    qkv_w_grad = lax.psum_scatter(qkv_w_part, "seq", scatter_dimension=0, tiled=True).astype(F32)
    qkv_grad = after(qkv_grad, qkv_w_part, inner_w_grad)
    bias_grad = jnp.sum(qkv_grad.astype(F32), axis=0)
    small = jnp.concatenate(
        [
            bias_grad[:cols].reshape(members, -1),
            bias_grad[2 * cols :].reshape(members, -1),
            inner_b_grad.reshape(members, -1),
        ]
        + [summed_rows[i].reshape(members, -1) for i in (3, 4, 5, 0, 1, 2)],
        axis=1,
    )
    small = jnp.pad(small, ((0, 0), (0, lines * 128 - small.shape[1])))
    input_grad, small = input_gradient(
        over_cols(qkv_grad, w_qkv).astype(BF),
        attn_grad,
        small.reshape(members, lines, 128),
        members,
        parts,
        6,
    )
    input_grad = after(input_grad, proj_w_grad).astype(F32).reshape(micro, seqs, length, width)
    layer_out = layer_out.reshape(micro, seqs, length, width)
    small = jnp.sum(small, axis=0).reshape(-1)
    pieces = []
    start = 0
    for size in sizes:
        pieces.append(small[start : start + size])
        start += size
    return (
        layer_out,
        input_grad,
        qkv_w_grad[:, :cols],
        pieces[0],
        qkv_w_grad[:, cols : 2 * cols],
        qkv_w_grad[:, 2 * cols :],
        pieces[1],
        proj_w_grad.astype(F32),
        pieces[3],
        pieces[4],
        pieces[5],
        inner_w_grad.astype(F32),
        pieces[2],
        outer_w_grad.astype(F32),
        pieces[6],
        pieces[7],
        pieces[8],
    )


def solution(mesh):
    tokens = P(None, None, "seq", None)
    rows_cols, cols_rows, both, seq = P("seq", "mp"), P("mp", "seq"), P(("mp", "seq")), P("seq")
    weights = (
        rows_cols,
        both,
        rows_cols,
        rows_cols,
        both,
        cols_rows,
        seq,
        seq,
        seq,
        rows_cols,
        both,
        cols_rows,
        seq,
        seq,
        seq,
    )
    return jax.shard_map(
        functools.partial(on_device, mesh.shape["seq"], mesh.shape["mp"]),
        mesh=mesh,
        in_specs=(tokens,) + weights + (tokens,),
        out_specs=(tokens, tokens) + weights,
        check_vma=False,
    )
```

```python
import functools

import jax
import jax.numpy as jnp
from jax import lax
from jax.experimental import pallas as pl
from jax.experimental.pallas import tpu as pltpu
from jax.sharding import PartitionSpec as P

DH = 128
EPSILON = 1e-06
BF = jnp.bfloat16
F32 = jnp.float32
MESH = pl.DeviceIdType.MESH
ANY = pl.BlockSpec(memory_space=pl.ANY)
VMEM = pl.BlockSpec(memory_space=pltpu.VMEM)
MIB = 1 << 20


def matmul(left, right):
    return jnp.dot(left, right, preferred_element_type=F32)


def over_rows(left, right):
    return lax.dot_general(left, right, (((0,), (0,)), ((), ())), preferred_element_type=F32)


def over_cols(left, right):
    return lax.dot_general(left, right, (((1,), (1,)), ((), ())), preferred_element_type=F32)


def gelu_tanh(values):
    return jax.nn.gelu(values, approximate=True)


def square():
    me = lax.axis_index("mp")
    return me, me + 1 - 2 * lax.rem(me, 2), lax.rem(me + 2, 4), 3 - me


def greet(devices):
    barrier = pltpu.get_barrier_semaphore()
    for device in devices:
        pl.semaphore_signal(barrier, inc=1, device_id=device, device_id_type=MESH)
    pl.semaphore_wait(barrier, len(devices))


def sender(send_sem, recv_sem):
    def send(source, target, slot, device):
        copy = pltpu.make_async_remote_copy(
            src_ref=source,
            dst_ref=target,
            send_sem=send_sem.at[slot],
            recv_sem=recv_sem.at[slot],
            device_id=device,
            device_id_type=MESH,
        )
        copy.start()
        return copy

    return send


class Exchange:
    def __init__(self, part_ref, landed, relay, send_sem, recv_sem):
        self.me, self.along_x, self.along_y, self.across = square()
        self.parts, self.landed, self.relay = part_ref, landed, relay
        self.send = sender(send_sem, recv_sem)
        self.copies = {}

    def part(self, owner, piece):
        return self.parts.at[row_place(owner, piece, 2 * self.parts.shape[2])]

    def ways(self, index):
        pair = (self.along_x, self.along_y)
        return pair if index % 2 == 0 else pair[::-1]

    def start(self, index, piece):
        near, _ = self.ways(index)
        for kind, owner in enumerate((self.across, near)):
            self.copies[index, kind] = self.send(
                self.part(owner, piece), self.landed.at[index, kind], 6 * index + kind, {"mp": near}
            )

    def pass_on(self, index, piece):
        _, far = self.ways(index)
        self.copies[index, 0].wait_recv()
        self.relay[index] = (
            self.part(far, piece)[...].astype(F32) + self.landed[index, 0].astype(F32)
        ).astype(BF)
        self.copies[index, 2] = self.send(
            self.relay.at[index], self.landed.at[index, 2], 6 * index + 2, {"mp": far}
        )

    def total(self, index, piece):
        self.copies[index, 1].wait_recv()
        self.copies[index, 2].wait_recv()
        return (
            self.part(self.me, piece)[...].astype(F32)
            + self.landed[index, 1].astype(F32)
            + self.landed[index, 2].astype(F32)
        )

    def share(self, index, source, target):
        near, far = self.ways(index)
        self.copies[index, 3] = self.send(source, target(self.me), 6 * index + 3, {"mp": near})
        self.copies[index, 4] = self.send(source, target(self.me), 6 * index + 4, {"mp": far})

    def forward(self, index, target):
        near, far = self.ways(index)
        self.copies[index, 3].wait_recv()
        self.copies[index, 5] = self.send(target(near), target(near), 6 * index + 5, {"mp": far})

    def arrived(self, indices):
        for index in indices:
            self.copies[index, 4].wait_recv()
            self.copies[index, 5].wait_recv()

    def sent(self):
        for copy in self.copies.values():
            copy.wait_send()

    def finish(self, count):
        self.arrived(range(count))
        self.sent()


def row_place(owner, piece, groups):
    half = groups // 2
    return piece // half, owner, piece % half


def planes(groups, per):
    index = lax.axis_index("seq")
    return [{"seq": lax.rem(index + step * per, groups * per)} for step in range(groups)]


def mean_of(values):
    return jnp.mean(values, axis=-1, keepdims=True)


def normed(values):
    centre = values - mean_of(values)
    inverse = lax.rsqrt(mean_of(centre * centre) + EPSILON)
    return centre * inverse, inverse


def norm_back(grad, normal, inverse, gain):
    inner = grad * gain
    return inverse * (inner - mean_of(inner) - normal * mean_of(inner * normal))


class Product:
    def __init__(self, exchange, turned, left_ref, weight_ref, weight, rows, load_sem):
        self.exchange, self.turned = exchange, turned
        self.left, self.weight, self.rows = left_ref, weight, rows
        width = exchange.parts.shape[-1]
        self.count = load_sem.shape[0]
        self.step = width // self.count
        depth = left_ref.shape[-1]
        self.loads = []
        for index in range(self.count):
            span = pl.ds(index * self.step, self.step)
            place = (span, pl.ds(0, depth)) if turned else (pl.ds(0, depth), span)
            copy = pltpu.make_async_copy(
                weight_ref.at[place], weight.at[place], load_sem.at[index]
            )
            copy.start()
            self.loads.append(copy)

    def make(self, batch, first=False):
        _, _, half, piece_rows, _ = self.left.shape
        for place, (owner, piece) in enumerate(batch):
            self.rows[place * piece_rows : (place + 1) * piece_rows] = self.left[
                row_place(owner, piece, 2 * half)
            ]

        def columns(index):
            span = pl.ds(pl.multiple_of(index * self.step, self.step), self.step)
            if self.turned:
                product = over_cols(self.rows[...], self.weight[span])
            else:
                product = matmul(self.rows[...], self.weight[:, span])
            product = product.astype(BF)
            for place, (owner, piece) in enumerate(batch):
                self.exchange.part(owner, piece)[:, span] = product[
                    place * piece_rows : (place + 1) * piece_rows
                ]

        if first:
            for index in range(self.count):
                self.loads[index].wait()
                columns(index)
        else:
            pl.loop(0, self.count)(columns)


def run_pieces(exchange, order, work, product=None):
    groups = len(order)
    places = list(enumerate(order))
    half = groups // 2
    first, second = places[:half], places[half:]

    def make(half_places, near):
        if product is None:
            return
        batch = []
        for index, piece in half_places:
            ways = exchange.ways(index)
            owners = (exchange.across, ways[0]) if near else (ways[1], exchange.me)
            batch += [(owner, piece) for owner in owners]
        product.make(batch, near and half_places is first)

    make(first, True)
    for index, piece in first:
        exchange.start(index, piece)
    make(first, False)
    for index, piece in first:
        exchange.pass_on(index, piece)
    make(second, True)
    for index, piece in second:
        exchange.start(index, piece)
    make(second, False)
    for index, piece in first:
        work(index, piece, exchange.total(index, piece))
    for index, piece in second:
        exchange.pass_on(index, piece)
    return first, second


def first_norm_kernel(
    groups, part_ref, x_ref, rows_ref, low_ref, normal_ref, inverse_ref,
    landed, relay, ready, send_sem, recv_sem, local_sem,
):
    exchange = Exchange(part_ref, landed, relay, send_sem, recv_sem)
    greet([{"mp": exchange.along_x}, {"mp": exchange.along_y}])
    local = []

    def target(piece):
        return lambda device: low_ref.at[row_place(device, piece, groups)]

    def work(index, piece, total):
        values = x_ref[piece].astype(F32) + total + rows_ref[0:1]
        normal, inverse = normed(values)
        normal_ref[piece] = normal
        inverse_ref[piece] = inverse
        ready[index] = (normal * rows_ref[1:2] + rows_ref[2:3]).astype(BF)
        exchange.share(index, ready.at[index], target(piece))
        copy = pltpu.make_async_copy(
            ready.at[index], target(piece)(exchange.me), local_sem.at[index]
        )
        copy.start()
        local.append(copy)

    first, second = run_pieces(exchange, range(groups), work)
    for index, piece in first:
        exchange.forward(index, target(piece))
    for index, piece in second:
        work(index, piece, exchange.total(index, piece))
    for index, piece in second:
        exchange.forward(index, target(piece))
    exchange.finish(groups)
    for copy in local:
        copy.wait()


def second_norm_kernel(
    groups, per, left_ref, weight_ref, turned_ref, normal_ref, cotan_ref, rows_ref,
    low_ref, grad_ref, back_ref, sums_ref, weight_grad_ref,
    landed, relay, ready, layer, cotan_in, part_ref, weight, rows, load_sem, put_sem,
    send_sem, recv_sem, local_sem,
):
    exchange = Exchange(part_ref, landed, relay, send_sem, recv_sem)
    product = Product(exchange, False, left_ref, weight_ref, weight, rows, load_sem)
    peers = planes(groups, per)
    greet([{"mp": exchange.along_x}, {"mp": exchange.along_y}] + peers[1:])
    base = 6 * groups
    arriving = {
        step: exchange.send(cotan_ref.at[step], cotan_in.at[step], base + step, peers[step])
        for step in range(1, groups)
    }
    leaving, local = [], []
    sums_ref[...] = jnp.zeros_like(sums_ref)

    def target(piece):
        return lambda device: low_ref.at[row_place(device, piece, groups)]

    def keep(source, place, slot):
        copy = pltpu.make_async_copy(source, place, local_sem.at[slot])
        copy.start()
        local.append(copy)

    def work(index, piece, total):
        gain_one, shift_one, bias = rows_ref[0:1], rows_ref[1:2], rows_ref[2:3]
        gain, shift = rows_ref[3:4], rows_ref[4:5]
        values = normal_ref[piece] * gain_one + shift_one + total + bias
        normal, inverse = normed(values)
        layer[index] = (normal * gain + shift).astype(BF)
        if piece == 0:
            keep(layer.at[index], back_ref.at[0], groups)
            cotan = cotan_ref[0].astype(F32)
        else:
            leaving.append(
                exchange.send(
                    layer.at[index], back_ref.at[piece], base + groups + piece, peers[groups - piece]
                )
            )
            arriving[piece].wait_recv()
            cotan = cotan_in[piece].astype(F32)
        grad = norm_back(cotan, normal, inverse, gain)
        grad_ref[piece] = grad
        ready[index] = grad.astype(BF)
        exchange.share(index, ready.at[index], target(piece))
        keep(ready.at[index], target(piece)(exchange.me), index)
        sums_ref[0:1] += jnp.sum(grad, axis=0, keepdims=True)
        sums_ref[1:2] += jnp.sum(cotan * normal, axis=0, keepdims=True)
        sums_ref[2:3] += jnp.sum(cotan, axis=0, keepdims=True)

    first, second = run_pieces(exchange, range(groups), work, product)
    for index, piece in first:
        exchange.forward(index, target(piece))
    for index, piece in second:
        work(index, piece, exchange.total(index, piece))
    for index, piece in second:
        exchange.forward(index, target(piece))
    step = 256
    count = weight.shape[1] // step
    depth = turned_ref.shape[1] // 2

    def columns(index):
        return pl.ds(pl.multiple_of(index * step, step), step)

    def put(index):
        span = columns(index)
        return pltpu.make_async_copy(
            weight.at[:, span], weight_grad_ref.at[:, span], put_sem.at[index]
        )

    def product_of(part, span):
        low = low_ref[part, :, :, :, span].reshape(depth, step)
        return matmul(turned_ref[:, part * depth : (part + 1) * depth], low)

    exchange.arrived([index for index, _ in first])
    for copy in local[: len(first) + 1]:
        copy.wait()

    @pl.loop(0, count)
    def _(index):
        span = columns(index)
        weight[:, span] = product_of(0, span).astype(BF)

    exchange.arrived([index for index, _ in second])
    for copy in local[len(first) + 1 :]:
        copy.wait()

    @pl.loop(0, count)
    def _(index):
        span = columns(index)
        weight[:, span] = (product_of(1, span) + weight[:, span].astype(F32)).astype(BF)
        put(index).start()

    exchange.sent()
    for copy in leaving:
        copy.wait()
    for copy in arriving.values():
        copy.wait_send()
    for index in range(count):
        put(index).wait()


def first_back_kernel(
    groups, left_ref, weight_ref, grad_ref, normal_ref, inverse_ref, sums_in_ref, rows_ref,
    low_ref, out_ref, sums_ref,
    landed, relay, ready, own_sums, part_ref, weight, rows, load_sem,
    send_sem, recv_sem, local_sem,
):
    exchange = Exchange(part_ref, landed, relay, send_sem, recv_sem)
    product = Product(exchange, True, left_ref, weight_ref, weight, rows, load_sem)
    greet([{"mp": exchange.along_x}, {"mp": exchange.along_y}, {"mp": exchange.across}])
    local = []
    own_sums[...] = sums_in_ref[...]

    def target(piece):
        return lambda device: low_ref.at[row_place(device, piece, groups)]

    def keep(source, place, slot):
        copy = pltpu.make_async_copy(source, place, local_sem.at[slot])
        copy.start()
        local.append(copy)

    def work(index, piece, total):
        grad = total + grad_ref[piece]
        normal = normal_ref[piece]
        moved = norm_back(grad, normal, inverse_ref[piece], rows_ref[0:1])
        out_ref[piece] = moved
        ready[index] = moved.astype(BF)
        exchange.share(index, ready.at[index], target(piece))
        keep(ready.at[index], target(piece)(exchange.me), index)
        own_sums[3:4] += jnp.sum(moved, axis=0, keepdims=True)
        own_sums[4:5] += jnp.sum(grad * normal, axis=0, keepdims=True)
        own_sums[5:6] += jnp.sum(grad, axis=0, keepdims=True)

    first, second = run_pieces(exchange, range(groups), work, product)
    for index, piece in first:
        exchange.forward(index, target(piece))
    for index, piece in second:
        work(index, piece, exchange.total(index, piece))
    others = [
        exchange.send(own_sums, sums_ref.at[exchange.me], 6 * groups + slot, {"mp": device})
        for slot, device in enumerate((exchange.along_x, exchange.along_y, exchange.across))
    ]
    keep(own_sums, sums_ref.at[exchange.me], groups)
    for index, piece in second:
        exchange.forward(index, target(piece))
    exchange.finish(groups)
    for copy in others:
        copy.wait()
    for copy in local:
        copy.wait()


def input_order(groups):
    return list(range(1, groups - 1)) + [0, groups - 1]


def input_kernel(
    groups, per, left_ref, weight_ref, grad_ref, small_ref,
    all_ref, small_out,
    landed, relay, ready, back, part_ref, weight, rows, load_sem,
    send_sem, recv_sem, local_sem,
):
    exchange = Exchange(part_ref, landed, relay, send_sem, recv_sem)
    product = Product(exchange, True, left_ref, weight_ref, weight, rows, load_sem)
    peers = planes(groups, per)
    members = groups * per
    here = lax.axis_index("seq")
    group = here // per
    devices = [{"seq": lax.rem(here + step, members)} for step in range(1, members)]
    greet([{"mp": exchange.along_x}, {"mp": exchange.along_y}] + devices)
    base = 6 * groups
    small = [
        exchange.send(
            small_ref.at[lax.rem(here + step, members)],
            small_out.at[here],
            base + groups + step,
            devices[step - 1],
        )
        for step in range(1, members)
    ]
    crossing, local = {}, []

    def keep(source, place, slot):
        copy = pltpu.make_async_copy(source, place, local_sem.at[slot])
        copy.start()
        local.append(copy)

    keep(small_ref.at[here], small_out.at[here], groups)

    def target(piece):
        sequence = lax.rem(group + piece, groups)
        return lambda device: all_ref.at[sequence, device]

    def work(index, piece, total):
        ready[piece] = (total + grad_ref[piece]).astype(BF)
        if piece > 0:
            crossing[piece] = exchange.send(
                ready.at[piece], back.at[piece], base + piece, peers[groups - piece]
            )

    def share(index, piece):
        source = ready.at[0]
        if piece > 0:
            crossing[piece].wait_recv()
            source = back.at[piece]
        exchange.share(index, source, target(piece))
        keep(source, target(piece)(exchange.me), index)

    first, second = run_pieces(exchange, input_order(groups), work, product)
    for index, piece in second:
        work(index, piece, exchange.total(index, piece))
    outward = [place for place in second if place[1] == 0] + first
    outward += [place for place in second if place[1] > 0]
    for index, piece in outward:
        share(index, piece)
    for index, piece in outward:
        exchange.forward(index, target(piece))
    exchange.finish(groups)
    for copy in small:
        copy.wait()
    for copy in crossing.values():
        copy.wait_send()
    for copy in local:
        copy.wait()


def product_scratch(parts, groups, piece, width, depth, turned):
    return [
        pltpu.VMEM((2, parts, groups // 2, piece, width), BF),
        pltpu.VMEM((width, depth) if turned else (depth, width), BF),
        pltpu.VMEM((groups * piece, depth), BF),
        pltpu.SemaphoreType.DMA((width // 512,)),
    ]


def exchange_call(
    kernel, ident, operands, results, groups, piece, width, scratch, extra, outside=()
):
    return pl.pallas_call(
        kernel,
        out_shape=tuple(jax.ShapeDtypeStruct(shape, dtype) for shape, dtype, _ in results),
        in_specs=[ANY if place in outside else VMEM for place in range(len(operands))],
        out_specs=tuple(spec for _, _, spec in results),
        scratch_shapes=[
            pltpu.VMEM((groups, 3, piece, width), BF),
            pltpu.VMEM((groups, piece, width), BF),
            pltpu.VMEM((groups, piece, width), BF),
        ]
        + scratch
        + [
            pltpu.SemaphoreType.DMA((6 * groups + extra,)),
            pltpu.SemaphoreType.DMA((6 * groups + extra,)),
            pltpu.SemaphoreType.DMA((groups + 1,)),
        ],
        compiler_params=pltpu.CompilerParams(
            collective_id=ident, has_side_effects=True, vmem_limit_bytes=58 * MIB
        ),
        cost_estimate=pl.CostEstimate(flops=0, bytes_accessed=200 * MIB, transcendentals=0),
        name=f"exchange_{ident}",
    )(*operands)


def first_norm(part, x_part, rows, parts, ident):
    groups, piece, width = x_part.shape
    half = groups // 2
    if parts != 4:
        total = lax.psum_scatter(part, "mp", scatter_dimension=0, tiled=True).astype(F32)
        values = x_part.astype(F32) + total.reshape(x_part.shape) + rows[0]
        normal, inverse = normed(values)
        low = lax.all_gather((normal * rows[1] + rows[2]).astype(BF), "mp", axis=0)
        return low, normal, inverse
    return exchange_call(
        functools.partial(first_norm_kernel, groups),
        ident,
        (part.reshape(2, parts, half, piece, width), x_part, rows),
        [
            ((2, parts, half, piece, width), BF, ANY),
            ((groups, piece, width), F32, VMEM),
            ((groups, piece, 1), F32, VMEM),
        ],
        groups, piece, width, [], 0,
    )


def second_norm(left, weight, turned, normal, cotan, rows, members, parts, ident):
    groups, piece, width = normal.shape
    depth = left.shape[-1]
    half = groups // 2
    if parts != 4:
        part = matmul(left, weight).astype(BF)
        total = lax.psum_scatter(part, "mp", scatter_dimension=0, tiled=True).astype(F32)
        values = normal * rows[0] + rows[1] + total.reshape(normal.shape) + rows[2]
        normal, inverse = normed(values)
        layer = (normal * rows[3] + rows[4]).astype(BF)
        back = jnp.stack(swap_blocks(layer, members, -1))
        cotan = jnp.stack(swap_blocks(cotan, members, 1)).astype(F32)
        grad = norm_back(cotan, normal, inverse, rows[3])
        sums = [jnp.sum(array, axis=(0, 1)) for array in (grad, cotan * normal, cotan)]
        sums = jnp.stack(sums + [jnp.zeros_like(sums[0])] * 5)
        low = lax.all_gather(grad.astype(BF), "mp", axis=0)
        return low, grad, back, sums, matmul(turned, low.reshape(-1, width)).astype(BF)
    return exchange_call(
        functools.partial(second_norm_kernel, groups, members // groups),
        ident,
        (left.reshape(2, parts, half, piece, depth), weight, turned, normal, cotan, rows),
        [
            ((2, parts, half, piece, width), BF, VMEM),
            ((groups, piece, width), F32, VMEM),
            ((groups, piece, width), BF, ANY),
            ((8, width), F32, VMEM),
            ((depth, width), BF, ANY),
        ],
        groups, piece, width,
        [pltpu.VMEM((groups, piece, width), BF), pltpu.VMEM((groups, piece, width), BF)]
        + product_scratch(parts, groups, piece, width, depth, False)
        + [pltpu.SemaphoreType.DMA((width // 256,))],
        2 * groups,
        (1,),
    )


def first_back(left, weight, grad, normal, inverse, sums, rows, parts, ident):
    groups, piece, width = normal.shape
    depth = left.shape[-1]
    if parts != 4:
        part = over_cols(left, weight).astype(BF)
        total = lax.psum_scatter(part, "mp", scatter_dimension=0, tiled=True).astype(F32)
        grad = total.reshape(normal.shape) + grad
        moved = norm_back(grad, normal, inverse, rows[0])
        more = [jnp.sum(array, axis=(0, 1)) for array in (moved, grad * normal, grad)]
        sums = sums.at[3:6].add(jnp.stack(more))
        return (
            lax.all_gather(moved.astype(BF), "mp", axis=0),
            moved,
            lax.all_gather(sums, "mp", axis=0),
        )
    half = groups // 2
    return exchange_call(
        functools.partial(first_back_kernel, groups),
        ident,
        (
            left.reshape(2, parts, half, piece, depth), weight,
            grad, normal, inverse, sums, rows,
        ),
        [
            ((2, parts, half, piece, width), BF, ANY),
            ((groups, piece, width), F32, VMEM),
            ((parts, 8, width), F32, VMEM),
        ],
        groups, piece, width,
        [pltpu.VMEM((8, width), F32)]
        + product_scratch(parts, groups, piece, width, depth, True),
        3,
        (1,),
    )


def input_gradient(left, weight, grad, small, members, parts, ident):
    groups, piece, width = grad.shape
    depth = left.shape[-1]
    if parts != 4:
        part = over_cols(left, weight[:, :depth]).astype(BF)
        total = lax.psum_scatter(part, "mp", scatter_dimension=0, tiled=True).astype(F32)
        ready = (total.reshape(grad.shape) + grad).astype(BF)
        back = jnp.stack(swap_blocks(ready, members, -1))
        back = jnp.roll(back, lax.axis_index("seq") // (members // groups), axis=0)
        return lax.all_gather(back, "mp", axis=1), lax.all_to_all(small, "seq", 0, 0)
    return exchange_call(
        functools.partial(input_kernel, groups, members // groups),
        ident,
        (left.reshape(2, parts, groups // 2, piece, depth), weight, grad, small),
        [((groups, parts, piece, width), BF, ANY), (small.shape, F32, VMEM)],
        groups, piece, width,
        [pltpu.VMEM((groups, piece, width), BF)]
        + product_scratch(parts, groups, piece, width, depth, True),
        groups + members,
        (1,),
    )


def share_kernel(own_ref, all_ref, send_sem, recv_sem, local_sem):
    me, along_x, along_y, _ = square()
    to_x, to_y = {"mp": along_x}, {"mp": along_y}
    greet([to_x, to_y])
    send = sender(send_sem, recv_sem)
    half = own_ref.shape[0] // 2
    upper, lower = pl.ds(0, half), pl.ds(half, half)
    copies = [
        send(own_ref.at[upper], all_ref.at[0, me], 0, to_x),
        send(own_ref.at[lower], all_ref.at[1, me], 1, to_y),
        send(own_ref.at[lower], all_ref.at[1, me], 2, to_x),
        send(own_ref.at[upper], all_ref.at[0, me], 3, to_y),
    ]
    local = [
        pltpu.make_async_copy(own_ref.at[upper], all_ref.at[0, me], local_sem.at[0]),
        pltpu.make_async_copy(own_ref.at[lower], all_ref.at[1, me], local_sem.at[1]),
    ]
    for copy in local:
        copy.start()
    copies[0].wait_recv()
    copies.append(send(all_ref.at[0, along_x], all_ref.at[0, along_x], 4, to_y))
    copies[1].wait_recv()
    copies.append(send(all_ref.at[1, along_y], all_ref.at[1, along_y], 5, to_x))
    for copy in copies[2:]:
        copy.wait_recv()
    for copy in copies:
        copy.wait_send()
    for copy in local:
        copy.wait()


def share_over_mp(own, parts, ident):
    if parts != 4:
        return lax.all_gather(own, "mp", axis=0)
    return pl.pallas_call(
        share_kernel,
        out_shape=jax.ShapeDtypeStruct((2, parts, own.shape[0] // 2, own.shape[1]), own.dtype),
        in_specs=[ANY],
        out_specs=ANY,
        scratch_shapes=[
            pltpu.SemaphoreType.DMA((6,)),
            pltpu.SemaphoreType.DMA((6,)),
            pltpu.SemaphoreType.DMA((2,)),
        ],
        compiler_params=pltpu.CompilerParams(collective_id=ident, has_side_effects=True),
        cost_estimate=pl.CostEstimate(flops=0, bytes_accessed=100 * MIB, transcendentals=0),
        name=f"share_over_mp_{ident}",
    )(own)


def swap_kernel(
    groups, per, sign, block_ref, small_ref, out_ref, small_out, send_sem, recv_sem, local_sem
):
    members = groups * per
    index = lax.axis_index("seq")
    devices = [{"seq": lax.rem(index + step, members)} for step in range(1, members)]
    greet(devices)
    send = sender(send_sem, recv_sem)
    copies = []
    for step in range(1, groups):
        ahead = step if sign > 0 else groups - step
        source = block_ref.at[step]
        copies.append(send(source, out_ref.at[step], step, devices[ahead * per - 1]))
    for step in range(1, members):
        target = lax.rem(index + step, members)
        copies.append(
            send(small_ref.at[target], small_out.at[index], groups + step, devices[step - 1])
        )
    locals_ = [
        pltpu.make_async_copy(block_ref.at[0], out_ref.at[0], local_sem.at[0]),
        pltpu.make_async_copy(small_ref.at[index], small_out.at[index], local_sem.at[1]),
    ]
    for local in locals_:
        local.start()
    for local in locals_:
        local.wait()
    for copy in copies:
        copy.wait()


def shift_pairs(members, ahead):
    return [(index, (index + ahead) % members) for index in range(members)]


def swap_blocks(blocks, members, sign):
    groups = blocks.shape[0]
    per = members // groups
    arrived = [blocks[0]]
    for step in range(1, groups):
        pairs = shift_pairs(members, sign * step * per)
        arrived.append(lax.ppermute(blocks[step], "seq", pairs))
    return arrived


def swap_groups(blocks, small, members, parts, sign, ident):
    groups = blocks.shape[0]
    per = members // groups
    if parts != 4:
        return jnp.stack(swap_blocks(blocks, members, sign)), lax.all_to_all(small, "seq", 0, 0)
    return pl.pallas_call(
        functools.partial(swap_kernel, groups, per, sign),
        out_shape=(
            jax.ShapeDtypeStruct(blocks.shape, blocks.dtype),
            jax.ShapeDtypeStruct(small.shape, small.dtype),
        ),
        in_specs=[ANY, ANY],
        out_specs=(ANY, ANY),
        scratch_shapes=[
            pltpu.SemaphoreType.DMA((groups + members,)),
            pltpu.SemaphoreType.DMA((groups + members,)),
            pltpu.SemaphoreType.DMA((2,)),
        ],
        compiler_params=pltpu.CompilerParams(collective_id=ident, has_side_effects=True),
        cost_estimate=pl.CostEstimate(flops=0, bytes_accessed=60 * MIB, transcendentals=0),
        name=f"swap_groups_{ident}",
    )(blocks, small)


def score_block(keys, queries):
    return lax.dot_general(keys, queries, (((1,), (1,)), ((), ())), preferred_element_type=F32)


def attend_kernel(
    query_ref, key_ref, value_ref, key_far_ref, value_far_ref, mix_ref, low_ref, log_ref, turned
):
    rows = key_ref.shape[0]

    @pl.when(pl.program_id(1) == 0)
    def _():
        turned[:, :rows] = value_ref[...].T
        turned[:, rows:] = value_far_ref[...].T

    scale = DH ** (-0.5)
    near = score_block(key_ref[...], query_ref[...])
    far = score_block(key_far_ref[...], query_ref[...])
    highest = jnp.maximum(
        jnp.max(near, axis=0, keepdims=True), jnp.max(far, axis=0, keepdims=True)
    )
    near = jnp.exp((near - highest) * scale)
    far = jnp.exp((far - highest) * scale)
    total = jnp.sum(near, axis=0, keepdims=True) + jnp.sum(far, axis=0, keepdims=True)
    mix = jnp.dot(turned[:, :rows], near.astype(BF), preferred_element_type=F32)
    mix += jnp.dot(turned[:, rows:], far.astype(BF), preferred_element_type=F32)
    mix = (mix / total).T
    mix_ref[...] = mix
    low_ref[...] = mix.astype(BF)
    log_ref[0] = highest * scale + jnp.log(total)


def attend(qkv, kv_far, heads):
    rows, cols = qkv.shape[0], heads * DH
    away = kv_far.shape[0]
    block = min(512, rows)

    def tile(offset):
        return pl.BlockSpec((block, DH), lambda h, i: (i, offset + h))

    def long(count, offset):
        return pl.BlockSpec((count, DH), lambda h, i: (0, offset + h))

    return pl.pallas_call(
        attend_kernel,
        grid=(heads, rows // block),
        out_shape=(
            jax.ShapeDtypeStruct((rows, cols), F32),
            jax.ShapeDtypeStruct((rows, cols), BF),
            jax.ShapeDtypeStruct((heads, 1, rows), F32),
        ),
        in_specs=[
            tile(0),
            long(rows, heads),
            long(rows, 2 * heads),
            long(away, 0),
            long(away, heads),
        ],
        out_specs=(tile(0), tile(0), pl.BlockSpec((1, 1, block), lambda h, i: (h, 0, i))),
        scratch_shapes=[pltpu.VMEM((DH, rows + away), BF)],
        compiler_params=pltpu.CompilerParams(vmem_limit_bytes=52 * MIB),
        cost_estimate=pl.CostEstimate(
            flops=8 * rows * (rows + away) * cols,
            bytes_accessed=20 * rows * cols,
            transcendentals=rows * (rows + away) * heads,
        ),
        name="attend",
    )(qkv, qkv, qkv, kv_far, kv_far)


def layer_copies(back_ref, all_ref, send_sem, recv_sem, groups, per):
    me, along_x, along_y, _ = square()
    group = lax.axis_index("seq") // per
    copies = []
    for piece in range(groups):
        near, far = (along_x, along_y) if piece % 2 == 0 else (along_y, along_x)
        sequence = lax.rem(group + piece, groups)
        block, own, passed = back_ref.at[piece], all_ref.at[sequence, me], all_ref.at[sequence, near]
        for kind, (source, target, device) in enumerate(
            ((block, own, near), (block, own, far), (passed, passed, far))
        ):
            copies.append(
                pltpu.make_async_remote_copy(
                    src_ref=source,
                    dst_ref=target,
                    send_sem=send_sem.at[3 * piece + kind],
                    recv_sem=recv_sem.at[3 * piece + kind],
                    device_id={"mp": device},
                    device_id_type=MESH,
                )
            )
    return copies[0::3], copies[1::3], copies[2::3]


def attend_back_kernel(
    groups,
    per,
    step,
    query_ref,
    key_ref,
    value_ref,
    key_far_ref,
    value_far_ref,
    grad_ref,
    mix_ref,
    log_ref,
    *rest,
):
    sharing = groups > 0
    if sharing:
        back_ref, *rest = rest
    dquery_ref, dkey_ref, dvalue_ref, dkey_far_ref, dvalue_far_ref, *rest = rest
    if sharing:
        all_ref, *rest = rest
    turned, key_sum, value_sum, *rest = rest
    block = pl.program_id(1)
    rows = key_ref.shape[0]
    if sharing:
        send_sem, recv_sem, local_sem = rest
        now = pl.program_id(0) * pl.num_programs(1) + block
        count = pl.num_programs(0) * pl.num_programs(1)
        near, far, passed = layer_copies(back_ref, all_ref, send_sem, recv_sem, groups, per)
        me, along_x, along_y, _ = square()
        group = lax.axis_index("seq") // per
        local = [
            pltpu.make_async_copy(
                back_ref.at[piece],
                all_ref.at[lax.rem(group + piece, groups), me],
                local_sem.at[piece],
            )
            for piece in range(groups)
        ]

        @pl.when(now == 0)
        def _():
            greet([{"mp": along_x}, {"mp": along_y}])
            for copy in near + far + local:
                copy.start()

        @pl.when(now == count * 3 // 8)
        def _():
            for first, second in zip(near, passed):
                first.wait_recv()
                second.start()

    @pl.when(block == 0)
    def _():
        turned[:, :rows] = key_ref[...].T
        turned[:, rows:] = key_far_ref[...].T
        key_sum[...] = jnp.zeros_like(key_sum)
        value_sum[...] = jnp.zeros_like(value_sum)

    scale = DH ** (-0.5)
    query, grad = query_ref[...], grad_ref[...]
    terms = jnp.sum((grad.astype(F32) * mix_ref[...]).T, axis=0, keepdims=True)
    logs = log_ref[0]
    dquery = jnp.zeros((DH, query.shape[0]), F32)
    spans = [(key_ref, value_ref, start, start) for start in range(0, rows, step)]
    spans += [
        (key_far_ref, value_far_ref, start, rows + start)
        for start in range(0, key_far_ref.shape[0], step)
    ]
    for keys, values, start, place in spans:
        part = pl.ds(place, step)
        probs = jnp.exp(score_block(keys[pl.ds(start, step)], query) * scale - logs)
        prob_grad = score_block(values[pl.ds(start, step)], grad)
        score_grad = (probs * (prob_grad - terms) * scale).astype(BF)
        value_sum[part] += jnp.dot(probs.astype(BF), grad, preferred_element_type=F32)
        key_sum[part] += jnp.dot(score_grad, query, preferred_element_type=F32)
        dquery += jnp.dot(turned[:, part], score_grad, preferred_element_type=F32)
    dquery_ref[...] = dquery.T.astype(BF)

    @pl.when(block == pl.num_programs(1) - 1)
    def _():
        dkey_ref[...] = key_sum[:rows]
        dvalue_ref[...] = value_sum[:rows]
        dkey_far_ref[...] = key_sum[rows:].astype(BF)
        dvalue_far_ref[...] = value_sum[rows:].astype(BF)

    if sharing:

        @pl.when(now == count - 1)
        def _():
            for copy in far + passed:
                copy.wait_recv()
            for copy in near + far + passed:
                copy.wait_send()
            for copy in local:
                copy.wait()


def attend_back(qkv, kv_far, grad, mix, logs, heads, layer_back, per, parts, ident):
    rows, cols = qkv.shape[0], heads * DH
    away = kv_far.shape[0]
    block, step = min(512, rows), min(512, rows)
    sharing = parts == 4
    groups, piece, width = layer_back.shape

    def tile(offset):
        return pl.BlockSpec((block, DH), lambda h, i: (i, offset + h))

    def long(count, offset):
        return pl.BlockSpec((count, DH), lambda h, i: (0, offset + h))

    results = pl.pallas_call(
        functools.partial(attend_back_kernel, groups if sharing else 0, per, step),
        grid=(heads, rows // block),
        out_shape=(
            jax.ShapeDtypeStruct((rows, cols), BF),
            jax.ShapeDtypeStruct((rows, cols), F32),
            jax.ShapeDtypeStruct((rows, cols), F32),
            jax.ShapeDtypeStruct((away, cols), BF),
            jax.ShapeDtypeStruct((away, cols), BF),
        )
        + ((jax.ShapeDtypeStruct((groups, parts, piece, width), BF),) if sharing else ()),
        in_specs=[
            tile(0),
            long(rows, heads),
            long(rows, 2 * heads),
            long(away, 0),
            long(away, heads),
            tile(0),
            tile(0),
            pl.BlockSpec((1, 1, block), lambda h, i: (h, 0, i)),
        ]
        + ([ANY] if sharing else []),
        out_specs=(tile(0), long(rows, 0), long(rows, 0), long(away, 0), long(away, 0))
        + ((ANY,) if sharing else ()),
        scratch_shapes=[
            pltpu.VMEM((DH, rows + away), BF),
            pltpu.VMEM((rows + away, DH), F32),
            pltpu.VMEM((rows + away, DH), F32),
        ]
        + (
            [
                pltpu.SemaphoreType.DMA((3 * groups,)),
                pltpu.SemaphoreType.DMA((3 * groups,)),
                pltpu.SemaphoreType.DMA((groups,)),
            ]
            if sharing
            else []
        ),
        compiler_params=pltpu.CompilerParams(
            vmem_limit_bytes=52 * MIB,
            **(dict(collective_id=ident, has_side_effects=True) if sharing else {}),
        ),
        cost_estimate=pl.CostEstimate(
            flops=20 * rows * (rows + away) * cols,
            bytes_accessed=30 * rows * cols,
            transcendentals=rows * (rows + away) * heads,
        ),
        name="attend_back",
    )(qkv, qkv, qkv, kv_far, kv_far, grad, mix, logs, *([layer_back] if sharing else []))
    if sharing:
        return results
    layer = jnp.roll(layer_back, lax.axis_index("seq") // per, axis=0)
    return (*results, lax.all_gather(layer, "mp", axis=1))


def from_group_members(block, members, per):
    blocks = []
    for step in range(1, per):
        pairs = [
            (base + place, base + (place - step) % per)
            for base in range(0, members, per)
            for place in range(per)
        ]
        blocks.append(lax.ppermute(block, "seq", pairs))
    return blocks


def to_group_members(total, blocks, members, per):
    for step in range(1, per):
        pairs = [
            (base + place, base + (place + step) % per)
            for base in range(0, members, per)
            for place in range(per)
        ]
        total = total + lax.ppermute(blocks[step - 1], "seq", pairs).astype(F32)
    return total


def last_kernel(
    turned_ref, query_ref, key_ref, value_ref, key_in_ref, value_in_ref, proj_ref,
    grad_ref, sums_ref, part_ref, made, copy_sem,
):
    rows, cols = query_ref.shape
    copies = [
        pltpu.make_async_copy(proj_ref, part_ref.at[:, pl.ds(3 * cols, cols)], copy_sem.at[3])
    ]
    copies[0].start()
    for index, (own, far) in enumerate(
        ((query_ref, None), (key_ref, key_in_ref), (value_ref, value_in_ref))
    ):
        span = pl.ds(index * cols, cols)
        grad = own[...] if far is None else (own[...] + far[...].astype(F32)).astype(BF)
        grad_ref[:, span] = grad
        sums_ref[:, span] = jnp.sum(grad.astype(F32), axis=0, keepdims=True)
        step = 512

        @pl.loop(0, turned_ref.shape[0] // step)
        def _(place, index=index, span=span):
            block = pl.ds(pl.multiple_of(place * step, step), step)
            made[index, block] = matmul(turned_ref[block], grad_ref[:, span]).astype(BF)

        copy = pltpu.make_async_copy(made.at[index], part_ref.at[:, span], copy_sem.at[index])
        copy.start()
        copies.append(copy)
    for copy in copies:
        copy.wait()


def last_gradients(turned, query, key, value, key_in, value_in, proj_part):
    rows, cols = query.shape
    width = turned.shape[0]
    return pl.pallas_call(
        last_kernel,
        out_shape=(
            jax.ShapeDtypeStruct((rows, 3 * cols), BF),
            jax.ShapeDtypeStruct((1, 3 * cols), F32),
            jax.ShapeDtypeStruct((width, 4 * cols), BF),
        ),
        in_specs=[VMEM] * 7,
        out_specs=(VMEM, VMEM, ANY),
        scratch_shapes=[pltpu.VMEM((3, width, cols), BF), pltpu.SemaphoreType.DMA((4,))],
        compiler_params=pltpu.CompilerParams(vmem_limit_bytes=48 * MIB),
        cost_estimate=pl.CostEstimate(
            flops=6 * rows * width * cols, bytes_accessed=32 * MIB, transcendentals=0
        ),
        name="last_gradients",
    )(turned, query, key, value, key_in, value_in, proj_part)


def packed(vectors, lines):
    flat = jnp.concatenate(vectors)
    return jnp.pad(flat, (0, lines * 128 - flat.shape[0])).reshape(lines, 128)


def after(value, *others):
    return lax.optimization_barrier((value,) + others)[0]


def on_device(members, parts, *arrays):
    (
        tokens,
        query_weight,
        query_bias,
        key_weight,
        value_weight,
        value_bias,
        proj_weight,
        proj_bias,
        gain_first,
        shift_first,
        inner_weight,
        inner_bias,
        outer_weight,
        outer_bias,
        gain_second,
        shift_second,
        cotangent,
    ) = arrays
    micro, seqs, length, width = tokens.shape
    groups = micro * seqs
    per = members // groups
    assert per * groups == members
    piece = length // parts
    rows = groups * length
    quarter = groups * piece
    mine = lax.axis_index("mp")
    group = lax.axis_index("seq") // per

    depth, cols = query_weight.shape
    narrow = width // members
    heads = cols // DH
    proj_fold = proj_weight.reshape(-1, depth, narrow)
    folds = proj_fold.shape[0]
    first = jnp.concatenate(
        [query_weight, key_weight, value_weight] + [proj_fold[i] for i in range(folds)], axis=1
    )
    first = lax.all_gather(first, "seq", axis=0, tiled=True)
    w_inner = lax.all_gather(inner_weight, "seq", axis=0, tiled=True)
    w_outer = lax.all_gather(outer_weight, "seq", axis=1, tiled=True)
    w_qkv = first[:, : 3 * cols]
    w_proj = first[:, 3 * cols :].reshape(members, depth, folds, narrow)
    w_proj = w_proj.transpose(2, 1, 0, 3).reshape(folds * depth, width)
    vectors = [
        query_bias,
        value_bias,
        inner_bias,
        proj_bias,
        gain_first,
        shift_first,
        outer_bias,
        gain_second,
        shift_second,
    ]
    sizes = [vector.shape[0] for vector in vectors]
    lines = -(-sum(sizes) // 2048) * 16
    own_vectors = packed(vectors, lines)

    def to_blocks(array):
        array = array.reshape(groups, length, width)
        return [
            lax.dynamic_slice(
                array, (lax.rem(group + k, groups), mine * piece, 0), (1, piece, width)
            )[0]
            for k in range(groups)
        ]

    x_part, all_vectors = swap_groups(
        jnp.stack(to_blocks(tokens)),
        jnp.broadcast_to(own_vectors[None], (members, lines, 128)),
        members,
        parts,
        1,
        1,
    )
    x_part = x_part.reshape(quarter, width)
    x_rows = share_over_mp(x_part, parts, 7).reshape(rows, width)
    all_vectors = all_vectors.reshape(members, -1).astype(F32)
    full = []
    start = 0
    for size in sizes:
        full.append(all_vectors[:, start : start + size].reshape(-1))
        start += size
    b_query, b_value, b_inner, b_proj, gain_one, shift_one, b_outer, gain_two, shift_two = full

    bias = jnp.concatenate([b_query, jnp.zeros_like(b_query), b_value])
    qkv = (matmul(x_rows, w_qkv) + bias).astype(BF)
    kv_far = from_group_members(qkv[:, cols:], members, per)
    kv_far = kv_far[0] if per == 2 else jnp.concatenate(kv_far, axis=0)
    mixture, mixture_low, logs = attend(qkv, kv_far, heads)

    def blocked(array):
        return array.reshape(groups, piece, width)

    first_low, normal_one, inverse_one = first_norm(
        matmul(mixture_low, w_proj).astype(BF),
        blocked(x_part),
        jnp.stack([b_proj, gain_one, shift_one]),
        parts,
        2,
    )
    first_low = first_low.reshape(rows, width)

    inner_pre = matmul(first_low, w_inner) + b_inner
    active = gelu_tanh(inner_pre).astype(BF)
    active_turned, x_turned, active = lax.optimization_barrier((active.T, x_rows.T, active))
    second_low, second_grad, layer_back, sums, outer_w_part = second_norm(
        active,
        w_outer,
        active_turned,
        normal_one,
        jnp.stack(to_blocks(cotangent)),
        jnp.stack([gain_one, shift_one, b_outer, gain_two, shift_two]),
        members,
        parts,
        3,
    )
    second_low = second_low.reshape(rows, width)

    outer_w_grad = lax.psum_scatter(outer_w_part, "seq", scatter_dimension=1, tiled=True)
    _, pull_gelu = jax.vjp(gelu_tanh, inner_pre)
    inner_grad = pull_gelu(over_cols(second_low, w_outer))[0].astype(BF)
    inner_b_grad = jnp.sum(inner_grad.astype(F32), axis=0)
    inner_w_part = over_rows(first_low, inner_grad).astype(BF)
    inner_w_grad = lax.psum_scatter(inner_w_part, "seq", scatter_dimension=0, tiled=True)
    attn_low, attn_grad, summed_rows = first_back(
        inner_grad,
        w_inner,
        second_grad,
        normal_one,
        inverse_one,
        after(sums, inner_w_part),
        gain_one[None],
        parts,
        4,
    )
    attn_low = after(attn_low.reshape(rows, width), outer_w_grad)
    summed_rows = jnp.sum(summed_rows, axis=0)

    proj_w_part = over_rows(attn_low, mixture_low).astype(BF)
    mixture_grad = over_cols(after(attn_low, proj_w_part), w_proj).astype(BF)
    query_grad, key_grad, value_grad, key_away, value_away, layer_out = attend_back(
        qkv, kv_far, mixture_grad, mixture, logs, heads, layer_back, per, parts, 5
    )

    def blocks_of(array):
        return [array[i * rows : (i + 1) * rows] for i in range(per - 1)]

    if parts == 4 and per == 2:
        pairs = [(index, index + 1 - 2 * (index % 2)) for index in range(members)]
        qkv_grad, bias_grad, last_w_part = last_gradients(
            x_turned,
            query_grad,
            key_grad,
            value_grad,
            lax.ppermute(key_away, "seq", pairs),
            lax.ppermute(value_away, "seq", pairs),
            proj_w_part,
        )
        bias_grad = bias_grad[0]
    else:
        key_grad = to_group_members(key_grad, blocks_of(key_away), members, per)
        value_grad = to_group_members(value_grad, blocks_of(value_away), members, per)
        qkv_grad = jnp.concatenate([query_grad, key_grad.astype(BF), value_grad.astype(BF)], axis=1)
        last_w_part = jnp.concatenate([matmul(x_turned, qkv_grad).astype(BF), proj_w_part], axis=1)
        bias_grad = jnp.sum(qkv_grad.astype(F32), axis=0)
    last_w_grad = lax.psum_scatter(last_w_part, "seq", scatter_dimension=0, tiled=True).astype(F32)
    small = jnp.concatenate(
        [
            bias_grad[:cols].reshape(members, -1),
            bias_grad[2 * cols :].reshape(members, -1),
            inner_b_grad.reshape(members, -1),
        ]
        + [summed_rows[i].reshape(members, -1) for i in (3, 4, 5, 0, 1, 2)],
        axis=1,
    )
    small = jnp.pad(small, ((0, 0), (0, lines * 128 - small.shape[1])))
    input_grad, small = input_gradient(
        qkv_grad,
        first,
        attn_grad,
        small.reshape(members, lines, 128),
        members,
        parts,
        6,
    )
    input_grad = after(input_grad, inner_w_grad).astype(F32).reshape(micro, seqs, length, width)
    layer_out = layer_out.reshape(micro, seqs, length, width)
    small = jnp.sum(small, axis=0).reshape(-1)
    pieces = []
    start = 0
    for size in sizes:
        pieces.append(small[start : start + size])
        start += size
    return (
        layer_out,
        input_grad,
        last_w_grad[:, :cols],
        pieces[0],
        last_w_grad[:, cols : 2 * cols],
        last_w_grad[:, 2 * cols : 3 * cols],
        pieces[1],
        last_w_grad[:, 3 * cols :].T,
        pieces[3],
        pieces[4],
        pieces[5],
        inner_w_grad.astype(F32),
        pieces[2],
        outer_w_grad.astype(F32),
        pieces[6],
        pieces[7],
        pieces[8],
    )


def solution(mesh):
    tokens = P(None, None, "seq", None)
    rows_cols, cols_rows, both, seq = P("seq", "mp"), P("mp", "seq"), P(("mp", "seq")), P("seq")
    weights = (
        rows_cols,
        both,
        rows_cols,
        rows_cols,
        both,
        cols_rows,
        seq,
        seq,
        seq,
        rows_cols,
        both,
        cols_rows,
        seq,
        seq,
        seq,
    )
    return jax.shard_map(
        functools.partial(on_device, mesh.shape["seq"], mesh.shape["mp"]),
        mesh=mesh,
        in_specs=(tokens,) + weights + (tokens,),
        out_specs=(tokens, tokens) + weights,
        check_vma=False,
    )
```

```python
import functools
import math

import jax
import jax.numpy as jnp
from jax import lax
from jax.experimental import pallas as pl
from jax.experimental.pallas import tpu as pltpu
from jax.sharding import PartitionSpec as P

DH = 128
EPSILON = 1e-06
BF = jnp.bfloat16
F32 = jnp.float32
MESH = pl.DeviceIdType.MESH
ANY = pl.BlockSpec(memory_space=pl.ANY)
VMEM = pl.BlockSpec(memory_space=pltpu.VMEM)
MIB = 1 << 20


def matmul(left, right):
    return jnp.dot(left, right, preferred_element_type=F32)


def over_rows(left, right):
    return lax.dot_general(left, right, (((0,), (0,)), ((), ())), preferred_element_type=F32)


def over_cols(left, right):
    return lax.dot_general(left, right, (((1,), (1,)), ((), ())), preferred_element_type=F32)


def gelu_tanh(values):
    return jax.nn.gelu(values, approximate=True)


def square():
    me = lax.axis_index("mp")
    return me, me + 1 - 2 * lax.rem(me, 2), lax.rem(me + 2, 4), 3 - me


def greet(devices):
    barrier = pltpu.get_barrier_semaphore()
    for device in devices:
        pl.semaphore_signal(barrier, inc=1, device_id=device, device_id_type=MESH)
    pl.semaphore_wait(barrier, len(devices))


def sender(send_sem, recv_sem, start=True):
    def send(source, target, slot, device):
        copy = pltpu.make_async_remote_copy(
            src_ref=source,
            dst_ref=target,
            send_sem=send_sem.at[slot],
            recv_sem=recv_sem.at[slot],
            device_id=device,
            device_id_type=MESH,
        )
        if start:
            copy.start()
        return copy

    return send


class Exchange:
    def __init__(self, part_ref, landed, relay, send_sem, recv_sem):
        self.me, self.along_x, self.along_y, self.across = square()
        self.parts, self.landed, self.relay = part_ref, landed, relay
        self.send = sender(send_sem, recv_sem)
        self.copies = {}

    def part(self, owner, piece):
        return self.parts.at[row_place(owner, piece, 2 * self.parts.shape[2])]

    def ways(self, index):
        pair = (self.along_x, self.along_y)
        return pair if index % 2 == 0 else pair[::-1]

    def start(self, index, piece):
        near, _ = self.ways(index)
        for kind, owner in enumerate((self.across, near)):
            self.copies[index, kind] = self.send(
                self.part(owner, piece), self.landed.at[index, kind], 6 * index + kind, {"mp": near}
            )

    def pass_on(self, index, piece):
        _, far = self.ways(index)
        self.copies[index, 0].wait_recv()
        self.relay[index] = (
            self.part(far, piece)[...].astype(F32) + self.landed[index, 0].astype(F32)
        ).astype(BF)
        self.copies[index, 2] = self.send(
            self.relay.at[index], self.landed.at[index, 2], 6 * index + 2, {"mp": far}
        )

    def total(self, index, piece):
        self.copies[index, 1].wait_recv()
        self.copies[index, 2].wait_recv()
        return (
            self.part(self.me, piece)[...].astype(F32)
            + self.landed[index, 1].astype(F32)
            + self.landed[index, 2].astype(F32)
        )

    def share(self, index, source, target):
        near, far = self.ways(index)
        self.copies[index, 3] = self.send(source, target(self.me), 6 * index + 3, {"mp": near})
        self.copies[index, 4] = self.send(source, target(self.me), 6 * index + 4, {"mp": far})

    def forward(self, index, target):
        near, far = self.ways(index)
        self.copies[index, 3].wait_recv()
        self.copies[index, 5] = self.send(target(near), target(near), 6 * index + 5, {"mp": far})

    def arrived(self, indices):
        for index in indices:
            self.copies[index, 4].wait_recv()
            self.copies[index, 5].wait_recv()

    def sent(self):
        for copy in self.copies.values():
            copy.wait_send()

    def finish(self, count):
        self.arrived(range(count))
        self.sent()


def row_place(owner, piece, groups):
    half = groups // 2
    return piece // half, owner, piece % half


def planes(groups, per):
    index = lax.axis_index("seq")
    return [{"seq": lax.rem(index + step * per, groups * per)} for step in range(groups)]


def mean_of(values):
    return jnp.mean(values, axis=-1, keepdims=True)


def normed(values):
    centre = values - mean_of(values)
    inverse = lax.rsqrt(mean_of(centre * centre) + EPSILON)
    return centre * inverse, inverse


def norm_back(grad, normal, inverse, gain):
    inner = grad * gain
    return inverse * (inner - mean_of(inner) - normal * mean_of(inner * normal))


def turner(rows_of, turned_ref):
    width, rows = turned_ref.shape
    step = 256

    def fill(part):
        @pl.loop(0, width // (2 * step))
        def _(index):
            span = pl.ds(pl.multiple_of(part * (width // 2) + index * step, step), step)
            turned_ref[span] = rows_of(span).reshape(rows, step).T

    return fill


class Product:
    def __init__(self, exchange, turned, left_ref, weight_ref, weight, rows, load_sem):
        self.exchange, self.turned = exchange, turned
        self.left, self.weight, self.rows = left_ref, weight, rows
        width = exchange.parts.shape[-1]
        self.count = load_sem.shape[0]
        self.step = width // self.count
        depth = left_ref.shape[-1]
        self.loads = []
        for index in range(self.count):
            span = pl.ds(index * self.step, self.step)
            place = (span, pl.ds(0, depth)) if turned else (pl.ds(0, depth), span)
            copy = pltpu.make_async_copy(
                weight_ref.at[place], weight.at[place], load_sem.at[index]
            )
            copy.start()
            self.loads.append(copy)

    def make(self, batch, first=False):
        _, _, half, piece_rows, _ = self.left.shape
        for place, (owner, piece) in enumerate(batch):
            self.rows[place * piece_rows : (place + 1) * piece_rows] = self.left[
                row_place(owner, piece, 2 * half)
            ]

        def columns(index):
            span = pl.ds(pl.multiple_of(index * self.step, self.step), self.step)
            if self.turned:
                product = over_cols(self.rows[...], self.weight[span])
            else:
                product = matmul(self.rows[...], self.weight[:, span])
            product = product.astype(BF)
            for place, (owner, piece) in enumerate(batch):
                self.exchange.part(owner, piece)[:, span] = product[
                    place * piece_rows : (place + 1) * piece_rows
                ]

        if first:
            for index in range(self.count):
                self.loads[index].wait()
                columns(index)
        else:
            pl.loop(0, self.count)(columns)


def run_pieces(exchange, order, work, product=None, fill=None):
    groups = len(order)
    places = list(enumerate(order))
    half = groups // 2
    first, second = places[:half], places[half:]

    def make(half_places, near):
        if product is None:
            return
        batch = []
        for index, piece in half_places:
            ways = exchange.ways(index)
            owners = (exchange.across, ways[0]) if near else (ways[1], exchange.me)
            batch += [(owner, piece) for owner in owners]
        product.make(batch, near and half_places is first)

    make(first, True)
    for index, piece in first:
        exchange.start(index, piece)
    make(first, False)
    if fill is not None:
        fill(0)
    for index, piece in first:
        exchange.pass_on(index, piece)
    make(second, True)
    for index, piece in second:
        exchange.start(index, piece)
    make(second, False)
    if fill is not None:
        fill(1)
    for index, piece in first:
        work(index, piece, exchange.total(index, piece))
    for index, piece in second:
        exchange.pass_on(index, piece)
    return first, second


def first_norm_kernel(
    groups, part_ref, x_ref, all_ref, rows_ref, low_ref, normal_ref, inverse_ref, turned_ref,
    landed, relay, ready, send_sem, recv_sem, local_sem,
):
    exchange = Exchange(part_ref, landed, relay, send_sem, recv_sem)
    greet([{"mp": exchange.along_x}, {"mp": exchange.along_y}])
    local = []

    def target(piece):
        return lambda device: low_ref.at[row_place(device, piece, groups)]

    def work(index, piece, total):
        values = x_ref[piece].astype(F32) + total + rows_ref[0:1]
        normal, inverse = normed(values)
        normal_ref[piece] = normal
        inverse_ref[piece] = inverse
        ready[index] = (normal * rows_ref[1:2] + rows_ref[2:3]).astype(BF)
        exchange.share(index, ready.at[index], target(piece))
        copy = pltpu.make_async_copy(
            ready.at[index], target(piece)(exchange.me), local_sem.at[index]
        )
        copy.start()
        local.append(copy)

    first, second = run_pieces(
        exchange, range(groups), work, None, turner(lambda span: all_ref[:, span], turned_ref)
    )
    for index, piece in first:
        exchange.forward(index, target(piece))
    for index, piece in second:
        work(index, piece, exchange.total(index, piece))
    for index, piece in second:
        exchange.forward(index, target(piece))
    exchange.finish(groups)
    for copy in local:
        copy.wait()


def half_sum_kernel(
    groups, left_ref, weight_ref, total_ref, turned_ref,
    landed, relay, part_ref, weight, rows, load_sem, send_sem, recv_sem,
):
    exchange = Exchange(part_ref, landed, relay, send_sem, recv_sem)
    product = Product(exchange, False, left_ref, weight_ref, weight, rows, load_sem)
    greet([{"mp": exchange.along_x}, {"mp": exchange.along_y}])

    def work(index, piece, total):
        total_ref[piece] = total

    fill = turner(lambda span: left_ref[:, :, :, :, span], turned_ref)
    _, second = run_pieces(exchange, range(groups), work, product, fill)
    for index, piece in second:
        work(index, piece, exchange.total(index, piece))
    exchange.sent()


def second_norm_kernel(
    groups, per, left_ref, weights_ref, weight_ref, turned_ref, done_ref,
    normal_ref, cotan_ref, rows_ref,
    low_ref, grad_ref, back_ref, sums_ref, weight_grad_ref, whole_ref,
    landed, relay, part_ref, weight, rows, load_sem,
    ready, layer, cotan_in, done_weight, whole, put_sem, whole_sem,
    send_sem, recv_sem, local_sem,
):
    exchange = Exchange(part_ref, landed, relay, send_sem, recv_sem)
    product = Product(exchange, False, left_ref, weight_ref, weight, rows, load_sem)
    members = groups * per
    narrow = weight.shape[1] // members
    load_done = pltpu.make_async_copy(weights_ref, done_weight, whole_sem.at[0])
    load_done.start()

    def join(part):
        if part == 0:
            load_done.wait()
        for place in range(part * members // 2, (part + 1) * members // 2):
            for index, source in enumerate((done_weight, weight)):
                target = pl.ds((2 * place + index) * narrow, narrow)
                whole[:, target] = source[:, place * narrow : (place + 1) * narrow]

    peers = planes(groups, per)
    greet([{"mp": exchange.along_x}, {"mp": exchange.along_y}] + peers[1:])
    base = 6 * groups
    arriving = {
        step: exchange.send(cotan_ref.at[step], cotan_in.at[step], base + step, peers[step])
        for step in range(1, groups)
    }
    leaving, local = [], []
    sums_ref[...] = jnp.zeros_like(sums_ref)

    def target(piece):
        return lambda device: low_ref.at[row_place(device, piece, groups)]

    def keep(source, place, slot):
        copy = pltpu.make_async_copy(source, place, local_sem.at[slot])
        copy.start()
        local.append(copy)

    def work(index, piece, total):
        gain_one, shift_one, bias = rows_ref[0:1], rows_ref[1:2], rows_ref[2:3]
        gain, shift = rows_ref[3:4], rows_ref[4:5]
        done = done_ref[piece]
        total = jnp.concatenate(
            [
                half[:, place * narrow : (place + 1) * narrow]
                for place in range(members)
                for half in (done, total)
            ],
            axis=1,
        )
        values = normal_ref[piece] * gain_one + shift_one + total + bias
        normal, inverse = normed(values)
        layer[index] = (normal * gain + shift).astype(BF)
        if piece == 0:
            keep(layer.at[index], back_ref.at[0], groups)
            cotan = cotan_ref[0].astype(F32)
        else:
            leaving.append(
                exchange.send(
                    layer.at[index], back_ref.at[piece], base + groups + piece, peers[groups - piece]
                )
            )
            arriving[piece].wait_recv()
            cotan = cotan_in[piece].astype(F32)
        grad = norm_back(cotan, normal, inverse, gain)
        grad_ref[piece] = grad
        ready[index] = grad.astype(BF)
        exchange.share(index, ready.at[index], target(piece))
        keep(ready.at[index], target(piece)(exchange.me), index)
        sums_ref[0:1] += jnp.sum(grad, axis=0, keepdims=True)
        sums_ref[1:2] += jnp.sum(cotan * normal, axis=0, keepdims=True)
        sums_ref[2:3] += jnp.sum(cotan, axis=0, keepdims=True)

    first, second = run_pieces(exchange, range(groups), work, product, join)
    put_whole = pltpu.make_async_copy(whole, whole_ref, whole_sem.at[1])
    put_whole.start()
    for index, piece in first:
        exchange.forward(index, target(piece))
    for index, piece in second:
        work(index, piece, exchange.total(index, piece))
    for index, piece in second:
        exchange.forward(index, target(piece))
    step = 256
    count = whole.shape[1] // step
    depth = turned_ref.shape[1] // 2

    def columns(index):
        return pl.ds(pl.multiple_of(index * step, step), step)

    def put(index):
        span = columns(index)
        return pltpu.make_async_copy(
            whole.at[:, span], weight_grad_ref.at[:, span], put_sem.at[index]
        )

    def product_of(part, span):
        low = low_ref[part, :, :, :, span].reshape(depth, step)
        return matmul(turned_ref[:, part * depth : (part + 1) * depth], low)

    exchange.arrived([index for index, _ in first])
    put_whole.wait()
    for copy in local[: len(first) + 1]:
        copy.wait()

    @pl.loop(0, count)
    def _(index):
        span = columns(index)
        whole[:, span] = product_of(0, span).astype(BF)

    exchange.arrived([index for index, _ in second])
    for copy in local[len(first) + 1 :]:
        copy.wait()

    @pl.loop(0, count)
    def _(index):
        span = columns(index)
        whole[:, span] = (product_of(1, span) + whole[:, span].astype(F32)).astype(BF)
        put(index).start()

    exchange.sent()
    for copy in leaving:
        copy.wait()
    for copy in arriving.values():
        copy.wait_send()
    for index in range(count):
        put(index).wait()


def first_back_kernel(
    groups, left_ref, weight_ref, grad_ref, normal_ref, inverse_ref, sums_in_ref, rows_ref,
    low_ref, out_ref, sums_ref,
    landed, relay, ready, own_sums, part_ref, weight, rows, load_sem,
    send_sem, recv_sem, local_sem,
):
    exchange = Exchange(part_ref, landed, relay, send_sem, recv_sem)
    product = Product(exchange, True, left_ref, weight_ref, weight, rows, load_sem)
    greet([{"mp": exchange.along_x}, {"mp": exchange.along_y}, {"mp": exchange.across}])
    local = []
    own_sums[...] = sums_in_ref[...]

    def target(piece):
        return lambda device: low_ref.at[row_place(device, piece, groups)]

    def keep(source, place, slot):
        copy = pltpu.make_async_copy(source, place, local_sem.at[slot])
        copy.start()
        local.append(copy)

    def work(index, piece, total):
        grad = total + grad_ref[piece]
        normal = normal_ref[piece]
        moved = norm_back(grad, normal, inverse_ref[piece], rows_ref[0:1])
        out_ref[piece] = moved
        ready[index] = moved.astype(BF)
        exchange.share(index, ready.at[index], target(piece))
        keep(ready.at[index], target(piece)(exchange.me), index)
        own_sums[3:4] += jnp.sum(moved, axis=0, keepdims=True)
        own_sums[4:5] += jnp.sum(grad * normal, axis=0, keepdims=True)
        own_sums[5:6] += jnp.sum(grad, axis=0, keepdims=True)

    first, second = run_pieces(exchange, range(groups), work, product)
    for index, piece in first:
        exchange.forward(index, target(piece))
    for index, piece in second:
        work(index, piece, exchange.total(index, piece))
    others = [
        exchange.send(own_sums, sums_ref.at[exchange.me], 6 * groups + slot, {"mp": device})
        for slot, device in enumerate((exchange.along_x, exchange.along_y, exchange.across))
    ]
    keep(own_sums, sums_ref.at[exchange.me], groups)
    for index, piece in second:
        exchange.forward(index, target(piece))
    exchange.finish(groups)
    for copy in others:
        copy.wait()
    for copy in local:
        copy.wait()


def input_order(groups):
    return list(range(1, groups - 1)) + [0, groups - 1]


def input_kernel(
    groups, per, left_ref, weight_ref, grad_ref, small_ref,
    all_ref, small_out,
    landed, relay, ready, back, part_ref, weight, rows, load_sem,
    send_sem, recv_sem, local_sem,
):
    exchange = Exchange(part_ref, landed, relay, send_sem, recv_sem)
    product = Product(exchange, True, left_ref, weight_ref, weight, rows, load_sem)
    peers = planes(groups, per)
    members = groups * per
    here = lax.axis_index("seq")
    group = here // per
    devices = [{"seq": lax.rem(here + step, members)} for step in range(1, members)]
    greet([{"mp": exchange.along_x}, {"mp": exchange.along_y}] + devices)
    base = 6 * groups
    small = [
        exchange.send(
            small_ref.at[lax.rem(here + step, members)],
            small_out.at[here],
            base + groups + step,
            devices[step - 1],
        )
        for step in range(1, members)
    ]
    crossing, local = {}, []

    def keep(source, place, slot):
        copy = pltpu.make_async_copy(source, place, local_sem.at[slot])
        copy.start()
        local.append(copy)

    keep(small_ref.at[here], small_out.at[here], groups)

    def target(piece):
        sequence = lax.rem(group + piece, groups)
        return lambda device: all_ref.at[sequence, device]

    def work(index, piece, total):
        ready[piece] = (total + grad_ref[piece]).astype(BF)
        if piece > 0:
            crossing[piece] = exchange.send(
                ready.at[piece], back.at[piece], base + piece, peers[groups - piece]
            )

    def share(index, piece):
        source = ready.at[0]
        if piece > 0:
            crossing[piece].wait_recv()
            source = back.at[piece]
        exchange.share(index, source, target(piece))
        keep(source, target(piece)(exchange.me), index)

    first, second = run_pieces(exchange, input_order(groups), work, product)
    for index, piece in second:
        work(index, piece, exchange.total(index, piece))
    outward = [place for place in second if place[1] == 0] + first
    outward += [place for place in second if place[1] > 0]
    for index, piece in outward:
        share(index, piece)
    for index, piece in outward:
        exchange.forward(index, target(piece))
    exchange.finish(groups)
    for copy in small:
        copy.wait()
    for copy in crossing.values():
        copy.wait_send()
    for copy in local:
        copy.wait()


def product_scratch(parts, groups, piece, width, depth, turned):
    return [
        pltpu.VMEM((2, parts, groups // 2, piece, width), BF),
        pltpu.VMEM((width, depth) if turned else (depth, width), BF),
        pltpu.VMEM((groups * piece, depth), BF),
        pltpu.SemaphoreType.DMA((width // 512,)),
    ]


def exchange_call(kernel, ident, operands, results, sums, scratch, extra, outside=(), local=True):
    groups, piece, width = sums
    return pl.pallas_call(
        kernel,
        out_shape=tuple(jax.ShapeDtypeStruct(shape, dtype) for shape, dtype, _ in results),
        in_specs=[ANY if place in outside else VMEM for place in range(len(operands))],
        out_specs=tuple(spec for _, _, spec in results),
        scratch_shapes=[
            pltpu.VMEM((groups, 3, piece, width), BF),
            pltpu.VMEM((groups, piece, width), BF),
        ]
        + scratch
        + [
            pltpu.SemaphoreType.DMA((6 * groups + extra,)),
            pltpu.SemaphoreType.DMA((6 * groups + extra,)),
        ]
        + ([pltpu.SemaphoreType.DMA((groups + 1,))] if local else []),
        compiler_params=pltpu.CompilerParams(
            collective_id=ident, has_side_effects=True, vmem_limit_bytes=58 * MIB
        ),
        cost_estimate=pl.CostEstimate(flops=0, bytes_accessed=200 * MIB, transcendentals=0),
        name=f"exchange_{ident}",
    )(*operands)


def first_norm(part, x_part, x_rows, rows, parts, ident):
    groups, piece, width = x_part.shape
    half = groups // 2
    if parts != 4:
        total = lax.psum_scatter(part, "mp", scatter_dimension=0, tiled=True).astype(F32)
        values = x_part.astype(F32) + total.reshape(x_part.shape) + rows[0]
        normal, inverse = normed(values)
        low = lax.all_gather((normal * rows[1] + rows[2]).astype(BF), "mp", axis=0)
        return low, normal, inverse, x_rows.T
    return exchange_call(
        functools.partial(first_norm_kernel, groups),
        ident,
        (part.reshape(2, parts, half, piece, width), x_part, x_rows, rows),
        [
            ((2, parts, half, piece, width), BF, ANY),
            ((groups, piece, width), F32, VMEM),
            ((groups, piece, 1), F32, VMEM),
            ((width, x_rows.shape[0]), BF, VMEM),
        ],
        (groups, piece, width),
        [pltpu.VMEM((groups, piece, width), BF)],
        0,
    )


def half_sum(left, weight, groups, piece, parts, ident):
    rows, depth = left.shape
    width = weight.shape[1]
    return exchange_call(
        functools.partial(half_sum_kernel, groups),
        ident,
        (left.reshape(2, parts, groups // 2, piece, depth), weight),
        [((groups, piece, width), F32, VMEM), ((depth, rows), BF, VMEM)],
        (groups, piece, width),
        product_scratch(parts, groups, piece, width, depth, False),
        0,
        (1,),
        False,
    )


def second_norm(left, shard, normal, cotan, rows, members, parts, ident):
    groups, piece, width = normal.shape
    depth = left.shape[-1]
    half = groups // 2
    if parts != 4:
        weight = lax.all_gather(shard, "seq", axis=1, tiled=True)
        part = matmul(left, weight).astype(BF)
        total = lax.psum_scatter(part, "mp", scatter_dimension=0, tiled=True).astype(F32)
        values = normal * rows[0] + rows[1] + total.reshape(normal.shape) + rows[2]
        normal, inverse = normed(values)
        layer = (normal * rows[3] + rows[4]).astype(BF)
        back = jnp.stack(swap_blocks(layer, members, -1))
        cotan = jnp.stack(swap_blocks(cotan, members, 1)).astype(F32)
        grad = norm_back(cotan, normal, inverse, rows[3])
        sums = [jnp.sum(array, axis=(0, 1)) for array in (grad, cotan * normal, cotan)]
        sums = jnp.stack(sums + [jnp.zeros_like(sums[0])] * 5)
        low = lax.all_gather(grad.astype(BF), "mp", axis=0)
        return low, grad, back, sums, over_rows(left, low.reshape(-1, width)).astype(BF), weight
    narrow = shard.shape[1] // 2
    weights = [
        lax.all_gather(block, "seq", axis=1, tiled=True)
        for block in (shard[:, :narrow], shard[:, narrow:])
    ]
    done, turned = half_sum(left, weights[0], groups, piece, parts, ident + 10)
    block = pltpu.VMEM((groups, piece, width), BF)
    return exchange_call(
        functools.partial(second_norm_kernel, groups, members // groups),
        ident,
        (
            left.reshape(2, parts, half, piece, depth),
            weights[0], weights[1], turned, done, normal, cotan, rows,
        ),
        [
            ((2, parts, half, piece, width), BF, VMEM),
            ((groups, piece, width), F32, VMEM),
            ((groups, piece, width), BF, ANY),
            ((8, width), F32, VMEM),
            ((depth, width), BF, ANY),
            ((depth, width), BF, ANY),
        ],
        (groups, piece, width // 2),
        product_scratch(parts, groups, piece, width // 2, depth, False)
        + [
            block,
            block,
            block,
            pltpu.VMEM((depth, width // 2), BF),
            pltpu.VMEM((depth, width), BF),
            pltpu.SemaphoreType.DMA((width // 256,)),
            pltpu.SemaphoreType.DMA((2,)),
        ],
        2 * groups,
        (1, 2),
    )


def first_back(left, weight, grad, normal, inverse, sums, rows, parts, ident):
    groups, piece, width = normal.shape
    depth = left.shape[-1]
    if parts != 4:
        part = over_cols(left, weight).astype(BF)
        total = lax.psum_scatter(part, "mp", scatter_dimension=0, tiled=True).astype(F32)
        grad = total.reshape(normal.shape) + grad
        moved = norm_back(grad, normal, inverse, rows[0])
        more = [jnp.sum(array, axis=(0, 1)) for array in (moved, grad * normal, grad)]
        sums = sums.at[3:6].add(jnp.stack(more))
        return (
            lax.all_gather(moved.astype(BF), "mp", axis=0),
            moved,
            lax.all_gather(sums, "mp", axis=0),
        )
    half = groups // 2
    return exchange_call(
        functools.partial(first_back_kernel, groups),
        ident,
        (
            left.reshape(2, parts, half, piece, depth), weight,
            grad, normal, inverse, sums, rows,
        ),
        [
            ((2, parts, half, piece, width), BF, ANY),
            ((groups, piece, width), F32, VMEM),
            ((parts, 8, width), F32, VMEM),
        ],
        (groups, piece, width),
        [pltpu.VMEM((groups, piece, width), BF), pltpu.VMEM((8, width), F32)]
        + product_scratch(parts, groups, piece, width, depth, True),
        3,
        (1,),
    )


def input_gradient(left, weight, grad, small, members, parts, ident):
    groups, piece, width = grad.shape
    depth = left.shape[-1]
    if parts != 4:
        part = over_cols(left, weight[:, :depth]).astype(BF)
        total = lax.psum_scatter(part, "mp", scatter_dimension=0, tiled=True).astype(F32)
        ready = (total.reshape(grad.shape) + grad).astype(BF)
        back = jnp.stack(swap_blocks(ready, members, -1))
        back = jnp.roll(back, lax.axis_index("seq") // (members // groups), axis=0)
        return lax.all_gather(back, "mp", axis=1), lax.all_to_all(small, "seq", 0, 0)
    return exchange_call(
        functools.partial(input_kernel, groups, members // groups),
        ident,
        (left.reshape(2, parts, groups // 2, piece, depth), weight, grad, small),
        [((groups, parts, piece, width), BF, ANY), (small.shape, F32, VMEM)],
        (groups, piece, width),
        [pltpu.VMEM((groups, piece, width), BF)] * 2
        + product_scratch(parts, groups, piece, width, depth, True),
        groups + members,
        (1,),
    )


def share_kernel(own_ref, all_ref, send_sem, recv_sem, local_sem):
    me, along_x, along_y, _ = square()
    to_x, to_y = {"mp": along_x}, {"mp": along_y}
    greet([to_x, to_y])
    send = sender(send_sem, recv_sem)
    half = own_ref.shape[0] // 2
    upper, lower = pl.ds(0, half), pl.ds(half, half)
    copies = [
        send(own_ref.at[upper], all_ref.at[0, me], 0, to_x),
        send(own_ref.at[lower], all_ref.at[1, me], 1, to_y),
        send(own_ref.at[lower], all_ref.at[1, me], 2, to_x),
        send(own_ref.at[upper], all_ref.at[0, me], 3, to_y),
    ]
    local = [
        pltpu.make_async_copy(own_ref.at[upper], all_ref.at[0, me], local_sem.at[0]),
        pltpu.make_async_copy(own_ref.at[lower], all_ref.at[1, me], local_sem.at[1]),
    ]
    for copy in local:
        copy.start()
    copies[0].wait_recv()
    copies.append(send(all_ref.at[0, along_x], all_ref.at[0, along_x], 4, to_y))
    copies[1].wait_recv()
    copies.append(send(all_ref.at[1, along_y], all_ref.at[1, along_y], 5, to_x))
    for copy in copies[2:]:
        copy.wait_recv()
    for copy in copies:
        copy.wait_send()
    for copy in local:
        copy.wait()


def share_over_mp(own, parts, ident):
    if parts != 4:
        return lax.all_gather(own, "mp", axis=0)
    return pl.pallas_call(
        share_kernel,
        out_shape=jax.ShapeDtypeStruct((2, parts, own.shape[0] // 2, own.shape[1]), own.dtype),
        in_specs=[ANY],
        out_specs=ANY,
        scratch_shapes=[
            pltpu.SemaphoreType.DMA((6,)),
            pltpu.SemaphoreType.DMA((6,)),
            pltpu.SemaphoreType.DMA((2,)),
        ],
        compiler_params=pltpu.CompilerParams(collective_id=ident, has_side_effects=True),
        cost_estimate=pl.CostEstimate(flops=0, bytes_accessed=100 * MIB, transcendentals=0),
        name=f"share_over_mp_{ident}",
    )(own)


def swap_kernel(
    groups, per, sign, block_ref, small_ref, out_ref, small_out, send_sem, recv_sem, local_sem
):
    members = groups * per
    index = lax.axis_index("seq")
    devices = [{"seq": lax.rem(index + step, members)} for step in range(1, members)]
    greet(devices)
    send = sender(send_sem, recv_sem)
    copies = []
    for step in range(1, groups):
        ahead = step if sign > 0 else groups - step
        source = block_ref.at[step]
        copies.append(send(source, out_ref.at[step], step, devices[ahead * per - 1]))
    for step in range(1, members):
        target = lax.rem(index + step, members)
        copies.append(
            send(small_ref.at[target], small_out.at[index], groups + step, devices[step - 1])
        )
    locals_ = [
        pltpu.make_async_copy(block_ref.at[0], out_ref.at[0], local_sem.at[0]),
        pltpu.make_async_copy(small_ref.at[index], small_out.at[index], local_sem.at[1]),
    ]
    for local in locals_:
        local.start()
    for local in locals_:
        local.wait()
    for copy in copies:
        copy.wait()


def shift_pairs(members, ahead):
    return [(index, (index + ahead) % members) for index in range(members)]


def swap_blocks(blocks, members, sign):
    groups = blocks.shape[0]
    per = members // groups
    arrived = [blocks[0]]
    for step in range(1, groups):
        pairs = shift_pairs(members, sign * step * per)
        arrived.append(lax.ppermute(blocks[step], "seq", pairs))
    return arrived


def swap_groups(blocks, small, members, parts, sign, ident):
    groups = blocks.shape[0]
    per = members // groups
    if parts != 4:
        return jnp.stack(swap_blocks(blocks, members, sign)), lax.all_to_all(small, "seq", 0, 0)
    return pl.pallas_call(
        functools.partial(swap_kernel, groups, per, sign),
        out_shape=(
            jax.ShapeDtypeStruct(blocks.shape, blocks.dtype),
            jax.ShapeDtypeStruct(small.shape, small.dtype),
        ),
        in_specs=[ANY, ANY],
        out_specs=(ANY, ANY),
        scratch_shapes=[
            pltpu.SemaphoreType.DMA((groups + members,)),
            pltpu.SemaphoreType.DMA((groups + members,)),
            pltpu.SemaphoreType.DMA((2,)),
        ],
        compiler_params=pltpu.CompilerParams(collective_id=ident, has_side_effects=True),
        cost_estimate=pl.CostEstimate(flops=0, bytes_accessed=60 * MIB, transcendentals=0),
        name=f"swap_groups_{ident}",
    )(blocks, small)


def score_block(keys, queries):
    return lax.dot_general(keys, queries, (((1,), (1,)), ((), ())), preferred_element_type=F32)


def attend_kernel(
    query_ref, key_ref, value_ref, key_far_ref, value_far_ref, mix_ref, low_ref, log_ref, turned
):
    rows = key_ref.shape[0]

    @pl.when(pl.program_id(1) == 0)
    def _():
        turned[:, :rows] = value_ref[...].T
        turned[:, rows:] = value_far_ref[...].T

    scale = DH ** (-0.5)
    near = score_block(key_ref[...], query_ref[...])
    far = score_block(key_far_ref[...], query_ref[...])
    highest = jnp.maximum(
        jnp.max(near, axis=0, keepdims=True), jnp.max(far, axis=0, keepdims=True)
    )
    near = jnp.exp((near - highest) * scale)
    far = jnp.exp((far - highest) * scale)
    total = jnp.sum(near, axis=0, keepdims=True) + jnp.sum(far, axis=0, keepdims=True)
    mix = jnp.dot(turned[:, :rows], near.astype(BF), preferred_element_type=F32)
    mix += jnp.dot(turned[:, rows:], far.astype(BF), preferred_element_type=F32)
    mix = (mix / total).T
    mix_ref[...] = mix
    low_ref[...] = mix.astype(BF)
    log_ref[0] = highest * scale + jnp.log(total)


def attend(qkv, kv_far, heads):
    rows, cols = qkv.shape[0], heads * DH
    away = kv_far.shape[0]
    block = min(512, rows)

    def tile(offset):
        return pl.BlockSpec((block, DH), lambda h, i: (i, offset + h))

    def long(count, offset):
        return pl.BlockSpec((count, DH), lambda h, i: (0, offset + h))

    return pl.pallas_call(
        attend_kernel,
        grid=(heads, rows // block),
        out_shape=(
            jax.ShapeDtypeStruct((rows, cols), F32),
            jax.ShapeDtypeStruct((rows, cols), BF),
            jax.ShapeDtypeStruct((heads, 1, rows), F32),
        ),
        in_specs=[
            tile(0),
            long(rows, heads),
            long(rows, 2 * heads),
            long(away, 0),
            long(away, heads),
        ],
        out_specs=(tile(0), tile(0), pl.BlockSpec((1, 1, block), lambda h, i: (h, 0, i))),
        scratch_shapes=[pltpu.VMEM((DH, rows + away), BF)],
        compiler_params=pltpu.CompilerParams(vmem_limit_bytes=52 * MIB),
        cost_estimate=pl.CostEstimate(
            flops=8 * rows * (rows + away) * cols,
            bytes_accessed=20 * rows * cols,
            transcendentals=rows * (rows + away) * heads,
        ),
        name="attend",
    )(qkv, qkv, qkv, kv_far, kv_far)


def share_meanwhile(now, count, pieces, back_ref, all_ref, send_sem, recv_sem, local_sem):
    me, along_x, along_y, _ = square()
    send = sender(send_sem, recv_sem, False)
    near, far, passed, local = [], [], [], []
    for index, piece in enumerate(pieces):
        ways = (along_x, along_y) if index % 2 == 0 else (along_y, along_x)
        block, own = back_ref.at[piece], all_ref.at[index, me]
        relayed = all_ref.at[index, ways[0]]
        near.append(send(block, own, 3 * index, {"mp": ways[0]}))
        far.append(send(block, own, 3 * index + 1, {"mp": ways[1]}))
        passed.append(send(relayed, relayed, 3 * index + 2, {"mp": ways[1]}))
        local.append(pltpu.make_async_copy(block, own, local_sem.at[index]))

    @pl.when(now == 0)
    def _():
        greet([{"mp": along_x}, {"mp": along_y}])
        for copy in near + far + local:
            copy.start()

    @pl.when(now == count // 4)
    def _():
        for first, second in zip(near, passed):
            first.wait_recv()
            second.start()

    def finish():
        @pl.when(now == count - 1)
        def _():
            for copy in far + passed:
                copy.wait_recv()
            for copy in near + far + passed:
                copy.wait_send()
            for copy in local:
                copy.wait()

    return finish


def meanwhile_scratch(pieces):
    return [
        pltpu.SemaphoreType.DMA((3 * len(pieces),)),
        pltpu.SemaphoreType.DMA((3 * len(pieces),)),
        pltpu.SemaphoreType.DMA((len(pieces),)),
    ]


def feed_back_kernel(
    pieces, low_ref, weight_ref, pre_ref, turned_ref, back_ref,
    grad_ref, sums_ref, weight_grad_ref, all_ref, send_sem, recv_sem, local_sem,
):
    now, count = pl.program_id(0), pl.num_programs(0)
    finish = share_meanwhile(now, count, pieces, back_ref, all_ref, send_sem, recv_sem, local_sem)
    value = pre_ref[...]
    root = (2 / math.pi) ** 0.5
    square_of = value * value
    bent = jnp.tanh(root * value * (1 + 0.044715 * square_of))
    slope = 0.5 * (1 + bent) + (0.5 * root) * value * (1 - bent * bent) * (
        1 + 3 * 0.044715 * square_of
    )
    grad = (over_cols(low_ref[...], weight_ref[...]) * slope).astype(BF)
    grad_ref[...] = grad
    sums_ref[...] = jnp.sum(grad.astype(F32), axis=0, keepdims=True)
    weight_grad_ref[...] = matmul(turned_ref[...], grad).astype(BF)
    finish()


def feed_back(low, weight, inner_pre, turned, layer_back, pieces, parts, ident):
    rows, hidden = inner_pre.shape
    width = low.shape[1]
    step = 512
    _, piece, _ = layer_back.shape
    return pl.pallas_call(
        functools.partial(feed_back_kernel, pieces),
        grid=(hidden // step,),
        out_shape=(
            jax.ShapeDtypeStruct((rows, hidden), BF),
            jax.ShapeDtypeStruct((1, hidden), F32),
            jax.ShapeDtypeStruct((width, hidden), BF),
            jax.ShapeDtypeStruct((len(pieces), parts, piece, width), BF),
        ),
        in_specs=[
            pl.BlockSpec((rows, width), lambda i: (0, 0)),
            pl.BlockSpec((step, width), lambda i: (i, 0)),
            pl.BlockSpec((rows, step), lambda i: (0, i)),
            pl.BlockSpec((width, rows), lambda i: (0, 0)),
            ANY,
        ],
        out_specs=(
            pl.BlockSpec((rows, step), lambda i: (0, i)),
            pl.BlockSpec((1, step), lambda i: (0, i)),
            pl.BlockSpec((width, step), lambda i: (0, i)),
            ANY,
        ),
        scratch_shapes=meanwhile_scratch(pieces),
        compiler_params=pltpu.CompilerParams(
            collective_id=ident, has_side_effects=True, vmem_limit_bytes=58 * MIB
        ),
        cost_estimate=pl.CostEstimate(
            flops=4 * rows * width * hidden, bytes_accessed=40 * MIB, transcendentals=rows * hidden
        ),
        name="feed_back",
    )(low, weight, inner_pre, turned, layer_back)


def attend_back_kernel(
    pieces,
    step,
    query_ref,
    key_ref,
    value_ref,
    key_far_ref,
    value_far_ref,
    grad_ref,
    mix_ref,
    log_ref,
    *rest,
):
    sharing = len(pieces) > 0
    if sharing:
        back_ref, *rest = rest
    dquery_ref, dkey_ref, dvalue_ref, dkey_far_ref, dvalue_far_ref, *rest = rest
    if sharing:
        all_ref, *rest = rest
    turned, key_sum, value_sum, *rest = rest
    block = pl.program_id(1)
    rows = key_ref.shape[0]
    if sharing:
        send_sem, recv_sem, local_sem = rest
        now = pl.program_id(0) * pl.num_programs(1) + block
        count = pl.num_programs(0) * pl.num_programs(1)
        finish = share_meanwhile(
            now, count, pieces, back_ref, all_ref, send_sem, recv_sem, local_sem
        )

    @pl.when(block == 0)
    def _():
        turned[:, :rows] = key_ref[...].T
        turned[:, rows:] = key_far_ref[...].T
        key_sum[...] = jnp.zeros_like(key_sum)
        value_sum[...] = jnp.zeros_like(value_sum)

    scale = DH ** (-0.5)
    query, grad = query_ref[...], grad_ref[...]
    terms = jnp.sum((grad.astype(F32) * mix_ref[...]).T, axis=0, keepdims=True)
    logs = log_ref[0]
    dquery = jnp.zeros((DH, query.shape[0]), F32)
    spans = [(key_ref, value_ref, start, start) for start in range(0, rows, step)]
    spans += [
        (key_far_ref, value_far_ref, start, rows + start)
        for start in range(0, key_far_ref.shape[0], step)
    ]
    for keys, values, start, place in spans:
        part = pl.ds(place, step)
        probs = jnp.exp(score_block(keys[pl.ds(start, step)], query) * scale - logs)
        prob_grad = score_block(values[pl.ds(start, step)], grad)
        score_grad = (probs * (prob_grad - terms) * scale).astype(BF)
        value_sum[part] += jnp.dot(probs.astype(BF), grad, preferred_element_type=F32)
        key_sum[part] += jnp.dot(score_grad, query, preferred_element_type=F32)
        dquery += jnp.dot(turned[:, part], score_grad, preferred_element_type=F32)
    dquery_ref[...] = dquery.T.astype(BF)

    @pl.when(block == pl.num_programs(1) - 1)
    def _():
        dkey_ref[...] = key_sum[:rows]
        dvalue_ref[...] = value_sum[:rows]
        dkey_far_ref[...] = key_sum[rows:].astype(BF)
        dvalue_far_ref[...] = value_sum[rows:].astype(BF)

    if sharing:
        finish()


def attend_back(qkv, kv_far, grad, mix, logs, heads, layer_back, pieces, parts, ident):
    rows, cols = qkv.shape[0], heads * DH
    away = kv_far.shape[0]
    block, step = min(512, rows), min(512, rows)
    sharing = len(pieces) > 0
    _, piece, width = layer_back.shape

    def tile(offset):
        return pl.BlockSpec((block, DH), lambda h, i: (i, offset + h))

    def long(count, offset):
        return pl.BlockSpec((count, DH), lambda h, i: (0, offset + h))

    return pl.pallas_call(
        functools.partial(attend_back_kernel, pieces, step),
        grid=(heads, rows // block),
        out_shape=(
            jax.ShapeDtypeStruct((rows, cols), BF),
            jax.ShapeDtypeStruct((rows, cols), F32),
            jax.ShapeDtypeStruct((rows, cols), F32),
            jax.ShapeDtypeStruct((away, cols), BF),
            jax.ShapeDtypeStruct((away, cols), BF),
        )
        + ((jax.ShapeDtypeStruct((len(pieces), parts, piece, width), BF),) if sharing else ()),
        in_specs=[
            tile(0),
            long(rows, heads),
            long(rows, 2 * heads),
            long(away, 0),
            long(away, heads),
            tile(0),
            tile(0),
            pl.BlockSpec((1, 1, block), lambda h, i: (h, 0, i)),
        ]
        + ([ANY] if sharing else []),
        out_specs=(tile(0), long(rows, 0), long(rows, 0), long(away, 0), long(away, 0))
        + ((ANY,) if sharing else ()),
        scratch_shapes=[
            pltpu.VMEM((DH, rows + away), BF),
            pltpu.VMEM((rows + away, DH), F32),
            pltpu.VMEM((rows + away, DH), F32),
        ]
        + (meanwhile_scratch(pieces) if sharing else []),
        compiler_params=pltpu.CompilerParams(
            vmem_limit_bytes=52 * MIB,
            **(dict(collective_id=ident, has_side_effects=True) if sharing else {}),
        ),
        cost_estimate=pl.CostEstimate(
            flops=20 * rows * (rows + away) * cols,
            bytes_accessed=30 * rows * cols,
            transcendentals=rows * (rows + away) * heads,
        ),
        name="attend_back",
    )(qkv, qkv, qkv, kv_far, kv_far, grad, mix, logs, *([layer_back] if sharing else []))


def from_group_members(block, members, per):
    blocks = []
    for step in range(1, per):
        pairs = [
            (base + place, base + (place - step) % per)
            for base in range(0, members, per)
            for place in range(per)
        ]
        blocks.append(lax.ppermute(block, "seq", pairs))
    return blocks


def to_group_members(total, blocks, members, per):
    for step in range(1, per):
        pairs = [
            (base + place, base + (place + step) % per)
            for base in range(0, members, per)
            for place in range(per)
        ]
        total = total + lax.ppermute(blocks[step - 1], "seq", pairs).astype(F32)
    return total


def last_kernel(
    per, turned_hbm, query_ref, key_ref, value_ref, key_in_ref, value_in_ref, proj_hbm, layer_hbm, layer_more_hbm,
    grad_ref, sums_ref, part_ref, layer_ref, turned_ref, made, proj, layer, load_sem, put_sem,
):
    rows, cols = query_ref.shape
    count = load_sem.shape[0] - 3
    step = turned_ref.shape[0] // count
    loads = []
    for place in range(count):
        block = pl.ds(place * step, step)
        loads.append(
            pltpu.make_async_copy(turned_hbm.at[block], turned_ref.at[block], load_sem.at[place])
        )
    loads.append(pltpu.make_async_copy(proj_hbm, proj, load_sem.at[count]))
    groups = layer.shape[0]
    for place, source in enumerate((layer_hbm, layer_more_hbm)):
        block = pl.ds(place * (groups // 2), groups // 2)
        loads.append(pltpu.make_async_copy(source, layer.at[block], load_sem.at[count + 1 + place]))
    for copy in loads:
        copy.start()
    puts = []

    def put(source, target):
        copy = pltpu.make_async_copy(source, target, put_sem.at[len(puts)])
        copy.start()
        puts.append(copy)

    for index, (own, far) in enumerate(
        ((query_ref, None), (key_ref, key_in_ref), (value_ref, value_in_ref))
    ):
        span = pl.ds(index * cols, cols)
        grad = own[...] if far is None else (own[...] + far[...].astype(F32)).astype(BF)
        grad_ref[:, span] = grad
        sums_ref[:, span] = jnp.sum(grad.astype(F32), axis=0, keepdims=True)
        for place in range(count):
            block = pl.ds(place * step, step)
            if index == 0:
                loads[place].wait()
            made[index, block] = matmul(turned_ref[block], grad_ref[:, span]).astype(BF)
        put(made.at[index], part_ref.at[:, span])
        if index == 1:
            loads[count].wait()
            put(proj, part_ref.at[:, pl.ds(3 * cols, cols)])
            for copy in loads[count + 1 :]:
                copy.wait()
            group = lax.axis_index("seq") // per
            for piece in range(groups):
                put(layer.at[piece], layer_ref.at[lax.rem(group + piece, groups)])
    for copy in puts:
        copy.wait()


def last_gradients(turned, query, key, value, key_in, value_in, proj_part, layer, layer_more, per):
    rows, cols = query.shape
    width = turned.shape[0]
    return pl.pallas_call(
        functools.partial(last_kernel, per),
        out_shape=(
            jax.ShapeDtypeStruct((rows, 3 * cols), BF),
            jax.ShapeDtypeStruct((1, 3 * cols), F32),
            jax.ShapeDtypeStruct((width, 4 * cols), BF),
            jax.ShapeDtypeStruct((2 * layer.shape[0],) + layer.shape[1:], layer.dtype),
        ),
        in_specs=[ANY] + [VMEM] * 5 + [ANY] * 3,
        out_specs=(VMEM, VMEM, ANY, ANY),
        scratch_shapes=[
            pltpu.VMEM(turned.shape, BF),
            pltpu.VMEM((3, width, cols), BF),
            pltpu.VMEM(proj_part.shape, BF),
            pltpu.VMEM((2 * layer.shape[0],) + layer.shape[1:], BF),
            pltpu.SemaphoreType.DMA((7,)),
            pltpu.SemaphoreType.DMA((4 + 2 * layer.shape[0],)),
        ],
        compiler_params=pltpu.CompilerParams(vmem_limit_bytes=52 * MIB),
        cost_estimate=pl.CostEstimate(
            flops=6 * rows * width * cols, bytes_accessed=32 * MIB, transcendentals=0
        ),
        name="last_gradients",
    )(turned, query, key, value, key_in, value_in, proj_part, layer, layer_more)


def packed(vectors, lines):
    flat = jnp.concatenate(vectors)
    return jnp.pad(flat, (0, lines * 128 - flat.shape[0])).reshape(lines, 128)


def after(value, *others):
    return lax.optimization_barrier((value,) + others)[0]


def on_device(members, parts, *arrays):
    (
        tokens,
        query_weight,
        query_bias,
        key_weight,
        value_weight,
        value_bias,
        proj_weight,
        proj_bias,
        gain_first,
        shift_first,
        inner_weight,
        inner_bias,
        outer_weight,
        outer_bias,
        gain_second,
        shift_second,
        cotangent,
    ) = arrays
    micro, seqs, length, width = tokens.shape
    groups = micro * seqs
    per = members // groups
    assert per * groups == members
    piece = length // parts
    rows = groups * length
    quarter = groups * piece
    mine = lax.axis_index("mp")
    group = lax.axis_index("seq") // per

    depth, cols = query_weight.shape
    heads = cols // DH
    first = jnp.concatenate([query_weight, key_weight, value_weight, proj_weight.T], axis=1)
    first = lax.all_gather(first, "seq", axis=0, tiled=True)
    w_inner = lax.all_gather(inner_weight, "seq", axis=0, tiled=True)
    w_qkv = first[:, : 3 * cols]
    w_proj = first[:, 3 * cols :]
    vectors = [
        query_bias,
        value_bias,
        inner_bias,
        proj_bias,
        gain_first,
        shift_first,
        outer_bias,
        gain_second,
        shift_second,
    ]
    sizes = [vector.shape[0] for vector in vectors]
    lines = -(-sum(sizes) // 2048) * 16
    own_vectors = packed(vectors, lines)

    def to_blocks(array):
        array = array.reshape(groups, length, width)
        return [
            lax.dynamic_slice(
                array, (lax.rem(group + k, groups), mine * piece, 0), (1, piece, width)
            )[0]
            for k in range(groups)
        ]

    x_part, all_vectors = swap_groups(
        jnp.stack(to_blocks(tokens)),
        jnp.broadcast_to(own_vectors[None], (members, lines, 128)),
        members,
        parts,
        1,
        1,
    )
    x_part = x_part.reshape(quarter, width)
    x_rows = share_over_mp(x_part, parts, 8).reshape(rows, width)
    all_vectors = all_vectors.reshape(members, -1).astype(F32)
    full = []
    start = 0
    for size in sizes:
        full.append(all_vectors[:, start : start + size].reshape(-1))
        start += size
    b_query, b_value, b_inner, b_proj, gain_one, shift_one, b_outer, gain_two, shift_two = full

    bias = jnp.concatenate([b_query, jnp.zeros_like(b_query), b_value])
    qkv = (matmul(x_rows, w_qkv) + bias).astype(BF)
    kv_far = from_group_members(qkv[:, cols:], members, per)
    kv_far = kv_far[0] if per == 2 else jnp.concatenate(kv_far, axis=0)
    mixture, mixture_low, logs = attend(qkv, kv_far, heads)

    def blocked(array):
        return array.reshape(groups, piece, width)

    first_low, normal_one, inverse_one, x_turned = first_norm(
        over_cols(mixture_low, w_proj).astype(BF),
        blocked(x_part),
        x_rows,
        jnp.stack([b_proj, gain_one, shift_one]),
        parts,
        2,
    )
    first_low = first_low.reshape(rows, width)

    inner_pre = matmul(first_low, w_inner) + b_inner
    active = gelu_tanh(inner_pre).astype(BF)
    first_turned = first_low.T
    second_low, second_grad, layer_back, sums, outer_w_part, w_outer = second_norm(
        active,
        outer_weight,
        normal_one,
        jnp.stack(to_blocks(cotangent)),
        after(jnp.stack([gain_one, shift_one, b_outer, gain_two, shift_two]), first_turned),
        members,
        parts,
        3,
    )
    second_low = second_low.reshape(rows, width)

    outer_w_grad = lax.psum_scatter(outer_w_part, "seq", scatter_dimension=1, tiled=True)
    fused = parts == 4 and per == 2
    pieces = list(range(groups)) if fused else []
    early, late = pieces[: groups // 2], pieces[groups // 2 :]
    if fused:
        inner_grad, inner_b_grad, inner_w_part, layer_out = feed_back(
            second_low, w_outer, inner_pre, first_turned, layer_back, early, parts, 7
        )
    else:
        _, pull_gelu = jax.vjp(gelu_tanh, inner_pre)
        inner_grad = pull_gelu(over_cols(second_low, w_outer))[0].astype(BF)
        inner_b_grad = jnp.sum(inner_grad.astype(F32), axis=0)
        inner_w_part = matmul(first_turned, inner_grad).astype(BF)
        layer_out = lax.all_gather(jnp.roll(layer_back, group, axis=0), "mp", axis=1)
    inner_w_grad = lax.psum_scatter(inner_w_part, "seq", scatter_dimension=0, tiled=True)
    attn_low, attn_grad, summed_rows = first_back(
        inner_grad,
        w_inner,
        second_grad,
        normal_one,
        inverse_one,
        after(sums, inner_w_part),
        gain_one[None],
        parts,
        4,
    )
    attn_low = after(attn_low.reshape(rows, width), outer_w_grad)
    summed_rows = jnp.sum(summed_rows, axis=0)

    proj_w_part = over_rows(attn_low, mixture_low).astype(BF)
    mixture_grad = matmul(after(attn_low, proj_w_part), w_proj).astype(BF)
    query_grad, key_grad, value_grad, key_away, value_away, *layer_more = attend_back(
        qkv, kv_far, mixture_grad, mixture, logs, heads, layer_back, late, parts, 5
    )

    def blocks_of(array):
        return [array[i * rows : (i + 1) * rows] for i in range(per - 1)]

    if fused:
        pairs = [(index, index + 1 - 2 * (index % 2)) for index in range(members)]
        qkv_grad, bias_grad, last_w_part, layer_out = last_gradients(
            x_turned,
            query_grad,
            key_grad,
            value_grad,
            lax.ppermute(key_away, "seq", pairs),
            lax.ppermute(value_away, "seq", pairs),
            proj_w_part,
            layer_out,
            layer_more[0],
            per,
        )
        bias_grad = bias_grad[0]
    else:
        key_grad = to_group_members(key_grad, blocks_of(key_away), members, per)
        value_grad = to_group_members(value_grad, blocks_of(value_away), members, per)
        qkv_grad = jnp.concatenate([query_grad, key_grad.astype(BF), value_grad.astype(BF)], axis=1)
        last_w_part = jnp.concatenate([matmul(x_turned, qkv_grad).astype(BF), proj_w_part], axis=1)
        bias_grad = jnp.sum(qkv_grad.astype(F32), axis=0)
    last_w_grad = lax.psum_scatter(last_w_part, "seq", scatter_dimension=0, tiled=True).astype(F32)
    small = jnp.concatenate(
        [
            bias_grad[:cols].reshape(members, -1),
            bias_grad[2 * cols :].reshape(members, -1),
            inner_b_grad.reshape(members, -1),
        ]
        + [summed_rows[i].reshape(members, -1) for i in (3, 4, 5, 0, 1, 2)],
        axis=1,
    )
    small = jnp.pad(small, ((0, 0), (0, lines * 128 - small.shape[1])))
    input_grad, small = input_gradient(
        qkv_grad,
        first,
        attn_grad,
        small.reshape(members, lines, 128),
        members,
        parts,
        6,
    )
    input_grad = after(input_grad, inner_w_grad).astype(F32).reshape(micro, seqs, length, width)
    layer_out = layer_out.reshape(micro, seqs, length, width)
    small = jnp.sum(small, axis=0).reshape(-1)
    pieces = []
    start = 0
    for size in sizes:
        pieces.append(small[start : start + size])
        start += size
    return (
        layer_out,
        input_grad,
        last_w_grad[:, :cols],
        pieces[0],
        last_w_grad[:, cols : 2 * cols],
        last_w_grad[:, 2 * cols : 3 * cols],
        pieces[1],
        last_w_grad[:, 3 * cols :].T,
        pieces[3],
        pieces[4],
        pieces[5],
        inner_w_grad.astype(F32),
        pieces[2],
        outer_w_grad.astype(F32),
        pieces[6],
        pieces[7],
        pieces[8],
    )


def solution(mesh):
    tokens = P(None, None, "seq", None)
    rows_cols, cols_rows, both, seq = P("seq", "mp"), P("mp", "seq"), P(("mp", "seq")), P("seq")
    weights = (
        rows_cols,
        both,
        rows_cols,
        rows_cols,
        both,
        cols_rows,
        seq,
        seq,
        seq,
        rows_cols,
        both,
        cols_rows,
        seq,
        seq,
        seq,
    )
    return jax.shard_map(
        functools.partial(on_device, mesh.shape["seq"], mesh.shape["mp"]),
        mesh=mesh,
        in_specs=(tokens,) + weights + (tokens,),
        out_specs=(tokens, tokens) + weights,
        check_vma=False,
    )
```

```python
import functools
import math

import jax
import jax.numpy as jnp
from jax import lax
from jax.experimental import pallas as pl
from jax.experimental.pallas import tpu as pltpu
from jax.sharding import PartitionSpec as P

DH = 128
EPSILON = 1e-06
BF = jnp.bfloat16
F32 = jnp.float32
MESH = pl.DeviceIdType.MESH
ANY = pl.BlockSpec(memory_space=pl.ANY)
VMEM = pl.BlockSpec(memory_space=pltpu.VMEM)
MIB = 1 << 20


def matmul(left, right):
    return jnp.dot(left, right, preferred_element_type=F32)


def over_rows(left, right):
    return lax.dot_general(left, right, (((0,), (0,)), ((), ())), preferred_element_type=F32)


def over_cols(left, right):
    return lax.dot_general(left, right, (((1,), (1,)), ((), ())), preferred_element_type=F32)


def gelu_tanh(values):
    return jax.nn.gelu(values, approximate=True)


def square():
    me = lax.axis_index("mp")
    return me, me + 1 - 2 * lax.rem(me, 2), lax.rem(me + 2, 4), 3 - me


def greet(devices):
    barrier = pltpu.get_barrier_semaphore()
    for device in devices:
        pl.semaphore_signal(barrier, inc=1, device_id=device, device_id_type=MESH)
    pl.semaphore_wait(barrier, len(devices))


def sender(send_sem, recv_sem, start=True):
    def send(source, target, slot, device):
        copy = pltpu.make_async_remote_copy(
            src_ref=source,
            dst_ref=target,
            send_sem=send_sem.at[slot],
            recv_sem=recv_sem.at[slot],
            device_id=device,
            device_id_type=MESH,
        )
        if start:
            copy.start()
        return copy

    return send


class Exchange:
    def __init__(self, part_ref, landed, relay, send_sem, recv_sem):
        self.me, self.along_x, self.along_y, self.across = square()
        self.parts, self.landed, self.relay = part_ref, landed, relay
        self.send = sender(send_sem, recv_sem)
        self.copies = {}

    def part(self, owner, piece):
        return self.parts.at[row_place(owner, piece, 2 * self.parts.shape[2])]

    def ways(self, index):
        pair = (self.along_x, self.along_y)
        return pair if index % 2 == 0 else pair[::-1]

    def start(self, index, piece):
        near, _ = self.ways(index)
        for kind, owner in enumerate((self.across, near)):
            self.copies[index, kind] = self.send(
                self.part(owner, piece), self.landed.at[index, kind], 6 * index + kind, {"mp": near}
            )

    def pass_on(self, index, piece):
        _, far = self.ways(index)
        self.copies[index, 0].wait_recv()
        self.relay[index] = (
            self.part(far, piece)[...].astype(F32) + self.landed[index, 0].astype(F32)
        ).astype(BF)
        self.copies[index, 2] = self.send(
            self.relay.at[index], self.landed.at[index, 2], 6 * index + 2, {"mp": far}
        )

    def total(self, index, piece):
        self.copies[index, 1].wait_recv()
        self.copies[index, 2].wait_recv()
        return (
            self.part(self.me, piece)[...].astype(F32)
            + self.landed[index, 1].astype(F32)
            + self.landed[index, 2].astype(F32)
        )

    def share(self, index, source, target):
        near, far = self.ways(index)
        self.copies[index, 3] = self.send(source, target(self.me), 6 * index + 3, {"mp": near})
        self.copies[index, 4] = self.send(source, target(self.me), 6 * index + 4, {"mp": far})

    def forward(self, index, target):
        near, far = self.ways(index)
        self.copies[index, 3].wait_recv()
        self.copies[index, 5] = self.send(target(near), target(near), 6 * index + 5, {"mp": far})

    def arrived(self, indices):
        for index in indices:
            self.copies[index, 4].wait_recv()
            self.copies[index, 5].wait_recv()

    def sent(self):
        for copy in self.copies.values():
            copy.wait_send()

    def finish(self, count):
        self.arrived(range(count))
        self.sent()


def row_place(owner, piece, groups):
    half = groups // 2
    return piece // half, owner, piece % half


def planes(groups, per):
    index = lax.axis_index("seq")
    return [{"seq": lax.rem(index + step * per, groups * per)} for step in range(groups)]


def mean_of(values):
    return jnp.mean(values, axis=-1, keepdims=True)


def normed(values):
    centre = values - mean_of(values)
    inverse = lax.rsqrt(mean_of(centre * centre) + EPSILON)
    return centre * inverse, inverse


def norm_back(grad, normal, inverse, gain):
    inner = grad * gain
    return inverse * (inner - mean_of(inner) - normal * mean_of(inner * normal))


def turner(rows_of, turned_ref):
    width, rows = turned_ref.shape
    step = 256

    def fill(part):
        @pl.loop(0, width // (2 * step))
        def _(index):
            span = pl.ds(pl.multiple_of(part * (width // 2) + index * step, step), step)
            turned_ref[span] = rows_of(span).reshape(rows, step).T

    return fill


class Product:
    def __init__(self, exchange, turned, left_ref, weight_ref, weight, rows, load_sem, blocks=None):
        self.exchange, self.turned = exchange, turned
        self.left, self.weight, self.rows = left_ref, weight, rows
        width = exchange.parts.shape[-1]
        self.step = min(512, width)
        self.count = width // self.step
        depth = left_ref.shape[-1]
        self.loads, slot = [], 0
        for index in range(self.count):
            span = pl.ds(index * self.step, self.step)
            place = (span, pl.ds(0, depth)) if turned else (pl.ds(0, depth), span)
            pairs = [(weight_ref.at[place], weight.at[place])] if blocks is None else blocks(index)
            copies = []
            for source, target in pairs:
                copy = pltpu.make_async_copy(source, target, load_sem.at[slot])
                copy.start()
                copies.append(copy)
                slot += 1
            self.loads.append(copies)

    def make(self, batch, first=False):
        _, _, half, piece_rows, _ = self.left.shape
        for place, (owner, piece) in enumerate(batch):
            self.rows[place * piece_rows : (place + 1) * piece_rows] = self.left[
                row_place(owner, piece, 2 * half)
            ]

        def columns(index):
            span = pl.ds(pl.multiple_of(index * self.step, self.step), self.step)
            if self.turned:
                product = over_cols(self.rows[...], self.weight[span])
            else:
                product = matmul(self.rows[...], self.weight[:, span])
            product = product.astype(BF)
            for place, (owner, piece) in enumerate(batch):
                self.exchange.part(owner, piece)[:, span] = product[
                    place * piece_rows : (place + 1) * piece_rows
                ]

        if first:
            for index in range(self.count):
                for copy in self.loads[index]:
                    copy.wait()
                columns(index)
        else:
            pl.loop(0, self.count)(columns)


def run_pieces(exchange, order, work, product=None, fill=None):
    groups = len(order)
    places = list(enumerate(order))
    half = groups // 2
    first, second = places[:half], places[half:]

    def make(half_places, near):
        if product is None:
            return
        batch = []
        for index, piece in half_places:
            ways = exchange.ways(index)
            owners = (exchange.across, ways[0]) if near else (ways[1], exchange.me)
            batch += [(owner, piece) for owner in owners]
        product.make(batch, near and half_places is first)

    make(first, True)
    for index, piece in first:
        exchange.start(index, piece)
    make(first, False)
    if fill is not None:
        fill(0)
    for index, piece in first:
        exchange.pass_on(index, piece)
    make(second, True)
    for index, piece in second:
        exchange.start(index, piece)
    make(second, False)
    if fill is not None:
        fill(1)
    for index, piece in first:
        work(index, piece, exchange.total(index, piece))
    for index, piece in second:
        exchange.pass_on(index, piece)
    return first, second


def first_norm_kernel(
    groups, part_ref, x_ref, all_ref, rows_ref, low_ref, normal_ref, inverse_ref, turned_ref,
    landed, relay, ready, send_sem, recv_sem, local_sem,
):
    exchange = Exchange(part_ref, landed, relay, send_sem, recv_sem)
    greet([{"mp": exchange.along_x}, {"mp": exchange.along_y}])
    local = []

    def target(piece):
        return lambda device: low_ref.at[row_place(device, piece, groups)]

    def work(index, piece, total):
        values = x_ref[piece].astype(F32) + total + rows_ref[0:1]
        normal, inverse = normed(values)
        normal_ref[piece] = normal
        inverse_ref[piece] = inverse
        ready[index] = (normal * rows_ref[1:2] + rows_ref[2:3]).astype(BF)
        exchange.share(index, ready.at[index], target(piece))
        copy = pltpu.make_async_copy(
            ready.at[index], target(piece)(exchange.me), local_sem.at[index]
        )
        copy.start()
        local.append(copy)

    first, second = run_pieces(
        exchange, range(groups), work, None, turner(lambda span: all_ref[:, span], turned_ref)
    )
    for index, piece in first:
        exchange.forward(index, target(piece))
    for index, piece in second:
        work(index, piece, exchange.total(index, piece))
    for index, piece in second:
        exchange.forward(index, target(piece))
    exchange.finish(groups)
    for copy in local:
        copy.wait()


def half_sum_kernel(
    groups, members, left_ref, weight_ref, first_ref, total_ref, turned_ref, weight_out, first_turned_ref,
    landed, relay, part_ref, weight, rows, load_sem, put_sem, send_sem, recv_sem,
):
    exchange = Exchange(part_ref, landed, relay, send_sem, recv_sem)
    width, depth = weight.shape
    narrow, half = width // members, depth // 2
    apart = weight_ref.shape[1] - half

    def blocks(index):
        step = min(512, width)
        for place in range(index * step // narrow, (index + 1) * step // narrow):
            for part in range(2):
                yield (
                    weight_ref.at[pl.ds((2 * place + part) * narrow, narrow), pl.ds(apart, half)],
                    weight.at[pl.ds(place * narrow, narrow), pl.ds(part * half, half)],
                )

    product = Product(exchange, True, left_ref, weight_ref, weight, rows, load_sem, blocks)
    greet([{"mp": exchange.along_x}, {"mp": exchange.along_y}])

    def work(index, piece, total):
        total_ref[piece] = total

    turn_left = turner(lambda span: left_ref[:, :, :, :, span], turned_ref)
    turn_first = turner(lambda span: first_ref[:, span], first_turned_ref)

    def fill(part):
        turn_left(part)
        turn_first(part)

    _, second = run_pieces(exchange, range(groups), work, product, fill)
    put = pltpu.make_async_copy(weight, weight_out, put_sem)
    put.start()
    for index, piece in second:
        work(index, piece, exchange.total(index, piece))
    put.wait()
    exchange.sent()


def second_norm_kernel(
    groups, per, left_ref, weight_ref, turned_hbm, done_ref,
    normal_ref, cotan_ref, rows_ref,
    low_ref, grad_ref, back_ref, sums_ref, weight_grad_ref,
    landed, relay, part_ref, weight, rows, load_sem,
    ready, layer, cotan_in, turned_ref, whole, put_sem, turned_sem,
    send_sem, recv_sem, local_sem,
):
    exchange = Exchange(part_ref, landed, relay, send_sem, recv_sem)
    product = Product(exchange, True, left_ref, weight_ref, weight, rows, load_sem)
    members = groups * per
    narrow = weight.shape[0] // members
    load_turned = pltpu.make_async_copy(turned_hbm, turned_ref, turned_sem)
    load_turned.start()
    peers = planes(groups, per)
    greet([{"mp": exchange.along_x}, {"mp": exchange.along_y}] + peers[1:])
    base = 6 * groups
    arriving = {
        step: exchange.send(cotan_ref.at[step], cotan_in.at[step], base + step, peers[step])
        for step in range(1, groups)
    }
    leaving, local = [], []
    sums_ref[...] = jnp.zeros_like(sums_ref)

    def target(piece):
        return lambda device: low_ref.at[row_place(device, piece, groups)]

    def keep(source, place, slot):
        copy = pltpu.make_async_copy(source, place, local_sem.at[slot])
        copy.start()
        local.append(copy)

    def work(index, piece, total):
        gain_one, shift_one, bias = rows_ref[0:1], rows_ref[1:2], rows_ref[2:3]
        gain, shift = rows_ref[3:4], rows_ref[4:5]
        done = done_ref[piece]
        total = jnp.concatenate(
            [
                half[:, place * narrow : (place + 1) * narrow]
                for place in range(members)
                for half in (done, total)
            ],
            axis=1,
        )
        values = normal_ref[piece] * gain_one + shift_one + total + bias
        normal, inverse = normed(values)
        layer[index] = (normal * gain + shift).astype(BF)
        if piece == 0:
            keep(layer.at[index], back_ref.at[0], groups)
            cotan = cotan_ref[0].astype(F32)
        else:
            leaving.append(
                exchange.send(
                    layer.at[index], back_ref.at[piece], base + groups + piece, peers[groups - piece]
                )
            )
            arriving[piece].wait_recv()
            cotan = cotan_in[piece].astype(F32)
        grad = norm_back(cotan, normal, inverse, gain)
        grad_ref[piece] = grad
        ready[index] = grad.astype(BF)
        exchange.share(index, ready.at[index], target(piece))
        keep(ready.at[index], target(piece)(exchange.me), index)
        sums_ref[0:1] += jnp.sum(grad, axis=0, keepdims=True)
        sums_ref[1:2] += jnp.sum(cotan * normal, axis=0, keepdims=True)
        sums_ref[2:3] += jnp.sum(cotan, axis=0, keepdims=True)

    first, second = run_pieces(exchange, range(groups), work, product)
    for index, piece in first:
        exchange.forward(index, target(piece))
    for index, piece in second:
        work(index, piece, exchange.total(index, piece))
    for index, piece in second:
        exchange.forward(index, target(piece))
    step = 256
    count = whole.shape[1] // step
    depth = turned_ref.shape[1] // 2

    def columns(index):
        return pl.ds(pl.multiple_of(index * step, step), step)

    def put(index):
        span = columns(index)
        return pltpu.make_async_copy(
            whole.at[:, span], weight_grad_ref.at[:, span], put_sem.at[index]
        )

    def product_of(part, span):
        low = low_ref[part, :, :, :, span].reshape(depth, step)
        return matmul(turned_ref[:, part * depth : (part + 1) * depth], low)

    exchange.arrived([index for index, _ in first])
    load_turned.wait()
    for copy in local[: len(first) + 1]:
        copy.wait()

    @pl.loop(0, count)
    def _(index):
        span = columns(index)
        whole[:, span] = product_of(0, span).astype(BF)

    exchange.arrived([index for index, _ in second])
    for copy in local[len(first) + 1 :]:
        copy.wait()

    @pl.loop(0, count)
    def _(index):
        span = columns(index)
        whole[:, span] = (product_of(1, span) + whole[:, span].astype(F32)).astype(BF)
        put(index).start()

    exchange.sent()
    for copy in leaving:
        copy.wait()
    for copy in arriving.values():
        copy.wait_send()
    for index in range(count):
        put(index).wait()


def first_back_kernel(
    groups, left_ref, weight_ref, grad_ref, normal_ref, inverse_ref, sums_in_ref, rows_ref,
    low_ref, out_ref, sums_ref,
    landed, relay, ready, own_sums, part_ref, weight, rows, load_sem,
    send_sem, recv_sem, local_sem,
):
    exchange = Exchange(part_ref, landed, relay, send_sem, recv_sem)
    product = Product(exchange, True, left_ref, weight_ref, weight, rows, load_sem)
    greet([{"mp": exchange.along_x}, {"mp": exchange.along_y}, {"mp": exchange.across}])
    local = []
    own_sums[...] = sums_in_ref[...]

    def target(piece):
        return lambda device: low_ref.at[row_place(device, piece, groups)]

    def keep(source, place, slot):
        copy = pltpu.make_async_copy(source, place, local_sem.at[slot])
        copy.start()
        local.append(copy)

    def work(index, piece, total):
        grad = total + grad_ref[piece]
        normal = normal_ref[piece]
        moved = norm_back(grad, normal, inverse_ref[piece], rows_ref[0:1])
        out_ref[piece] = moved
        ready[index] = moved.astype(BF)
        exchange.share(index, ready.at[index], target(piece))
        keep(ready.at[index], target(piece)(exchange.me), index)
        own_sums[3:4] += jnp.sum(moved, axis=0, keepdims=True)
        own_sums[4:5] += jnp.sum(grad * normal, axis=0, keepdims=True)
        own_sums[5:6] += jnp.sum(grad, axis=0, keepdims=True)

    first, second = run_pieces(exchange, range(groups), work, product)
    for index, piece in first:
        exchange.forward(index, target(piece))
    for index, piece in second:
        work(index, piece, exchange.total(index, piece))
    others = [
        exchange.send(own_sums, sums_ref.at[exchange.me], 6 * groups + slot, {"mp": device})
        for slot, device in enumerate((exchange.along_x, exchange.along_y, exchange.across))
    ]
    keep(own_sums, sums_ref.at[exchange.me], groups)
    for index, piece in second:
        exchange.forward(index, target(piece))
    exchange.finish(groups)
    for copy in others:
        copy.wait()
    for copy in local:
        copy.wait()


def input_order(groups):
    return list(range(1, groups - 1)) + [0, groups - 1]


def input_kernel(
    groups, per, left_ref, weight_ref, grad_ref, small_ref,
    all_ref, small_out,
    landed, relay, ready, back, part_ref, weight, rows, load_sem,
    send_sem, recv_sem, local_sem,
):
    exchange = Exchange(part_ref, landed, relay, send_sem, recv_sem)
    product = Product(exchange, True, left_ref, weight_ref, weight, rows, load_sem)
    peers = planes(groups, per)
    members = groups * per
    here = lax.axis_index("seq")
    group = here // per
    devices = [{"seq": lax.rem(here + step, members)} for step in range(1, members)]
    greet([{"mp": exchange.along_x}, {"mp": exchange.along_y}] + devices)
    base = 6 * groups
    small = [
        exchange.send(
            small_ref.at[lax.rem(here + step, members)],
            small_out.at[here],
            base + groups + step,
            devices[step - 1],
        )
        for step in range(1, members)
    ]
    crossing, local = {}, []

    def keep(source, place, slot):
        copy = pltpu.make_async_copy(source, place, local_sem.at[slot])
        copy.start()
        local.append(copy)

    keep(small_ref.at[here], small_out.at[here], groups)

    def target(piece):
        sequence = lax.rem(group + piece, groups)
        return lambda device: all_ref.at[sequence, device]

    def work(index, piece, total):
        ready[piece] = (total + grad_ref[piece]).astype(BF)
        if piece > 0:
            crossing[piece] = exchange.send(
                ready.at[piece], back.at[piece], base + piece, peers[groups - piece]
            )

    def share(index, piece):
        source = ready.at[0]
        if piece > 0:
            crossing[piece].wait_recv()
            source = back.at[piece]
        exchange.share(index, source, target(piece))
        keep(source, target(piece)(exchange.me), index)

    first, second = run_pieces(exchange, input_order(groups), work, product)
    for index, piece in second:
        work(index, piece, exchange.total(index, piece))
    outward = [place for place in second if place[1] == 0] + first
    outward += [place for place in second if place[1] > 0]
    for index, piece in outward:
        share(index, piece)
    for index, piece in outward:
        exchange.forward(index, target(piece))
    exchange.finish(groups)
    for copy in small:
        copy.wait()
    for copy in crossing.values():
        copy.wait_send()
    for copy in local:
        copy.wait()


def product_scratch(parts, groups, piece, width, depth, turned, loads=1):
    return [
        pltpu.VMEM((2, parts, groups // 2, piece, width), BF),
        pltpu.VMEM((width, depth) if turned else (depth, width), BF),
        pltpu.VMEM((groups * piece, depth), BF),
        pltpu.SemaphoreType.DMA((max(width // 512, loads),)),
    ]


def exchange_call(kernel, ident, operands, results, sums, scratch, extra, outside=(), local=True):
    groups, piece, width = sums
    return pl.pallas_call(
        kernel,
        out_shape=tuple(jax.ShapeDtypeStruct(shape, dtype) for shape, dtype, _ in results),
        in_specs=[ANY if place in outside else VMEM for place in range(len(operands))],
        out_specs=tuple(spec for _, _, spec in results),
        scratch_shapes=[
            pltpu.VMEM((groups, 3, piece, width), BF),
            pltpu.VMEM((groups, piece, width), BF),
        ]
        + scratch
        + [
            pltpu.SemaphoreType.DMA((6 * groups + extra,)),
            pltpu.SemaphoreType.DMA((6 * groups + extra,)),
        ]
        + ([pltpu.SemaphoreType.DMA((groups + 1,))] if local else []),
        compiler_params=pltpu.CompilerParams(
            collective_id=ident, has_side_effects=True, vmem_limit_bytes=58 * MIB
        ),
        cost_estimate=pl.CostEstimate(flops=0, bytes_accessed=200 * MIB, transcendentals=0),
        name=f"exchange_{ident}",
    )(*operands)


def first_norm(part, x_part, x_rows, rows, parts, ident):
    groups, piece, width = x_part.shape
    half = groups // 2
    if parts != 4:
        total = lax.psum_scatter(part, "mp", scatter_dimension=0, tiled=True).astype(F32)
        values = x_part.astype(F32) + total.reshape(x_part.shape) + rows[0]
        normal, inverse = normed(values)
        low = lax.all_gather((normal * rows[1] + rows[2]).astype(BF), "mp", axis=0)
        return low, normal, inverse, x_rows.T
    return exchange_call(
        functools.partial(first_norm_kernel, groups),
        ident,
        (part.reshape(2, parts, half, piece, width), x_part, x_rows, rows),
        [
            ((2, parts, half, piece, width), BF, ANY),
            ((groups, piece, width), F32, VMEM),
            ((groups, piece, 1), F32, VMEM),
            ((width, x_rows.shape[0]), BF, VMEM),
        ],
        (groups, piece, width),
        [pltpu.VMEM((groups, piece, width), BF)],
        0,
    )


def half_sum(left, second, first, groups, piece, members, parts, ident):
    rows, depth = left.shape
    width = second.shape[0] // 2
    return exchange_call(
        functools.partial(half_sum_kernel, groups, members),
        ident,
        (left.reshape(2, parts, groups // 2, piece, depth), second, first),
        [
            ((groups, piece, width), F32, VMEM),
            ((depth, rows), BF, VMEM),
            ((width, depth), BF, ANY),
            (first.shape[::-1], BF, VMEM),
        ],
        (groups, piece, width),
        product_scratch(parts, groups, piece, width, depth, True, 2 * members)
        + [pltpu.SemaphoreType.DMA],
        0,
        (1,),
        False,
    )


def second_norm(left, weight, turned, done, normal, cotan, rows, members, parts, ident):
    groups, piece, width = normal.shape
    depth = left.shape[-1]
    half = groups // 2
    if parts != 4:
        part = over_cols(left, weight).astype(BF)
        total = lax.psum_scatter(part, "mp", scatter_dimension=0, tiled=True).astype(F32)
        values = normal * rows[0] + rows[1] + total.reshape(normal.shape) + rows[2]
        normal, inverse = normed(values)
        layer = (normal * rows[3] + rows[4]).astype(BF)
        back = jnp.stack(swap_blocks(layer, members, -1))
        cotan = jnp.stack(swap_blocks(cotan, members, 1)).astype(F32)
        grad = norm_back(cotan, normal, inverse, rows[3])
        sums = [jnp.sum(array, axis=(0, 1)) for array in (grad, cotan * normal, cotan)]
        sums = jnp.stack(sums + [jnp.zeros_like(sums[0])] * 5)
        low = lax.all_gather(grad.astype(BF), "mp", axis=0)
        return low, grad, back, sums, over_rows(left, low.reshape(-1, width)).astype(BF)
    block = pltpu.VMEM((groups, piece, width), BF)
    return exchange_call(
        functools.partial(second_norm_kernel, groups, members // groups),
        ident,
        (
            left.reshape(2, parts, half, piece, depth),
            weight, turned, done, normal, cotan, rows,
        ),
        [
            ((2, parts, half, piece, width), BF, VMEM),
            ((groups, piece, width), F32, VMEM),
            ((groups, piece, width), BF, ANY),
            ((8, width), F32, VMEM),
            ((depth, width), BF, ANY),
        ],
        (groups, piece, width // 2),
        product_scratch(parts, groups, piece, width // 2, depth, True)
        + [
            block,
            block,
            block,
            pltpu.VMEM(turned.shape, BF),
            pltpu.VMEM((depth, width), BF),
            pltpu.SemaphoreType.DMA((width // 256,)),
            pltpu.SemaphoreType.DMA,
        ],
        2 * groups,
        (1, 2),
    )


def first_back(left, weight, grad, normal, inverse, sums, rows, parts, ident):
    groups, piece, width = normal.shape
    depth = left.shape[-1]
    if parts != 4:
        part = over_cols(left, weight[:, :depth]).astype(BF)
        total = lax.psum_scatter(part, "mp", scatter_dimension=0, tiled=True).astype(F32)
        grad = total.reshape(normal.shape) + grad
        moved = norm_back(grad, normal, inverse, rows[0])
        more = [jnp.sum(array, axis=(0, 1)) for array in (moved, grad * normal, grad)]
        sums = sums.at[3:6].add(jnp.stack(more))
        return (
            lax.all_gather(moved.astype(BF), "mp", axis=0),
            moved,
            lax.all_gather(sums, "mp", axis=0),
        )
    half = groups // 2
    return exchange_call(
        functools.partial(first_back_kernel, groups),
        ident,
        (
            left.reshape(2, parts, half, piece, depth), weight,
            grad, normal, inverse, sums, rows,
        ),
        [
            ((2, parts, half, piece, width), BF, ANY),
            ((groups, piece, width), F32, VMEM),
            ((parts, 8, width), F32, VMEM),
        ],
        (groups, piece, width),
        [pltpu.VMEM((groups, piece, width), BF), pltpu.VMEM((8, width), F32)]
        + product_scratch(parts, groups, piece, width, depth, True),
        3,
        (1,),
    )


def input_gradient(left, weight, grad, small, members, parts, ident):
    groups, piece, width = grad.shape
    depth = left.shape[-1]
    if parts != 4:
        part = over_cols(left, weight[:, :depth]).astype(BF)
        total = lax.psum_scatter(part, "mp", scatter_dimension=0, tiled=True).astype(F32)
        ready = (total.reshape(grad.shape) + grad).astype(BF)
        back = jnp.stack(swap_blocks(ready, members, -1))
        back = jnp.roll(back, lax.axis_index("seq") // (members // groups), axis=0)
        return lax.all_gather(back, "mp", axis=1), lax.all_to_all(small, "seq", 0, 0)
    return exchange_call(
        functools.partial(input_kernel, groups, members // groups),
        ident,
        (left.reshape(2, parts, groups // 2, piece, depth), weight, grad, small),
        [((groups, parts, piece, width), BF, ANY), (small.shape, F32, VMEM)],
        (groups, piece, width),
        [pltpu.VMEM((groups, piece, width), BF)] * 2
        + product_scratch(parts, groups, piece, width, depth, True),
        groups + members,
        (1,),
    )


def share_kernel(own_ref, all_ref, send_sem, recv_sem, local_sem):
    me, along_x, along_y, _ = square()
    to_x, to_y = {"mp": along_x}, {"mp": along_y}
    greet([to_x, to_y])
    send = sender(send_sem, recv_sem)
    half = own_ref.shape[0] // 2
    upper, lower = pl.ds(0, half), pl.ds(half, half)
    copies = [
        send(own_ref.at[upper], all_ref.at[0, me], 0, to_x),
        send(own_ref.at[lower], all_ref.at[1, me], 1, to_y),
        send(own_ref.at[lower], all_ref.at[1, me], 2, to_x),
        send(own_ref.at[upper], all_ref.at[0, me], 3, to_y),
    ]
    local = [
        pltpu.make_async_copy(own_ref.at[upper], all_ref.at[0, me], local_sem.at[0]),
        pltpu.make_async_copy(own_ref.at[lower], all_ref.at[1, me], local_sem.at[1]),
    ]
    for copy in local:
        copy.start()
    copies[0].wait_recv()
    copies.append(send(all_ref.at[0, along_x], all_ref.at[0, along_x], 4, to_y))
    copies[1].wait_recv()
    copies.append(send(all_ref.at[1, along_y], all_ref.at[1, along_y], 5, to_x))
    for copy in copies[2:]:
        copy.wait_recv()
    for copy in copies:
        copy.wait_send()
    for copy in local:
        copy.wait()


def share_over_mp(own, parts, ident):
    if parts != 4:
        return lax.all_gather(own, "mp", axis=0)
    return pl.pallas_call(
        share_kernel,
        out_shape=jax.ShapeDtypeStruct((2, parts, own.shape[0] // 2, own.shape[1]), own.dtype),
        in_specs=[ANY],
        out_specs=ANY,
        scratch_shapes=[
            pltpu.SemaphoreType.DMA((6,)),
            pltpu.SemaphoreType.DMA((6,)),
            pltpu.SemaphoreType.DMA((2,)),
        ],
        compiler_params=pltpu.CompilerParams(collective_id=ident, has_side_effects=True),
        cost_estimate=pl.CostEstimate(flops=0, bytes_accessed=100 * MIB, transcendentals=0),
        name=f"share_over_mp_{ident}",
    )(own)


def swap_kernel(
    groups, per, sign, block_ref, small_ref, out_ref, small_out, send_sem, recv_sem, local_sem
):
    members = groups * per
    index = lax.axis_index("seq")
    devices = [{"seq": lax.rem(index + step, members)} for step in range(1, members)]
    greet(devices)
    send = sender(send_sem, recv_sem)
    copies = []
    for step in range(1, groups):
        ahead = step if sign > 0 else groups - step
        source = block_ref.at[step]
        copies.append(send(source, out_ref.at[step], step, devices[ahead * per - 1]))
    for step in range(1, members):
        target = lax.rem(index + step, members)
        copies.append(
            send(small_ref.at[target], small_out.at[index], groups + step, devices[step - 1])
        )
    locals_ = [
        pltpu.make_async_copy(block_ref.at[0], out_ref.at[0], local_sem.at[0]),
        pltpu.make_async_copy(small_ref.at[index], small_out.at[index], local_sem.at[1]),
    ]
    for local in locals_:
        local.start()
    for local in locals_:
        local.wait()
    for copy in copies:
        copy.wait()


def shift_pairs(members, ahead):
    return [(index, (index + ahead) % members) for index in range(members)]


def swap_blocks(blocks, members, sign):
    groups = blocks.shape[0]
    per = members // groups
    arrived = [blocks[0]]
    for step in range(1, groups):
        pairs = shift_pairs(members, sign * step * per)
        arrived.append(lax.ppermute(blocks[step], "seq", pairs))
    return arrived


def swap_groups(blocks, small, members, parts, sign, ident):
    groups = blocks.shape[0]
    per = members // groups
    if parts != 4:
        return jnp.stack(swap_blocks(blocks, members, sign)), lax.all_to_all(small, "seq", 0, 0)
    return pl.pallas_call(
        functools.partial(swap_kernel, groups, per, sign),
        out_shape=(
            jax.ShapeDtypeStruct(blocks.shape, blocks.dtype),
            jax.ShapeDtypeStruct(small.shape, small.dtype),
        ),
        in_specs=[ANY, ANY],
        out_specs=(ANY, ANY),
        scratch_shapes=[
            pltpu.SemaphoreType.DMA((groups + members,)),
            pltpu.SemaphoreType.DMA((groups + members,)),
            pltpu.SemaphoreType.DMA((2,)),
        ],
        compiler_params=pltpu.CompilerParams(collective_id=ident, has_side_effects=True),
        cost_estimate=pl.CostEstimate(flops=0, bytes_accessed=60 * MIB, transcendentals=0),
        name=f"swap_groups_{ident}",
    )(blocks, small)


def score_block(keys, queries):
    return lax.dot_general(keys, queries, (((1,), (1,)), ((), ())), preferred_element_type=F32)


def attend_kernel(
    query_ref, key_ref, value_ref, key_far_ref, value_far_ref, mix_ref, low_ref, log_ref, turned
):
    rows = key_ref.shape[0]

    @pl.when(pl.program_id(1) == 0)
    def _():
        turned[:, :rows] = value_ref[...].T
        turned[:, rows:] = value_far_ref[...].T

    scale = DH ** (-0.5)
    near = score_block(key_ref[...], query_ref[...])
    far = score_block(key_far_ref[...], query_ref[...])
    highest = jnp.maximum(
        jnp.max(near, axis=0, keepdims=True), jnp.max(far, axis=0, keepdims=True)
    )
    near = jnp.exp((near - highest) * scale)
    far = jnp.exp((far - highest) * scale)
    total = jnp.sum(near, axis=0, keepdims=True) + jnp.sum(far, axis=0, keepdims=True)
    mix = jnp.dot(turned[:, :rows], near.astype(BF), preferred_element_type=F32)
    mix += jnp.dot(turned[:, rows:], far.astype(BF), preferred_element_type=F32)
    mix = (mix / total).T
    mix_ref[...] = mix
    low_ref[...] = mix.astype(BF)
    log_ref[0] = highest * scale + jnp.log(total)


def attend(qkv, kv_far, heads):
    rows, cols = qkv.shape[0], heads * DH
    away = kv_far.shape[0]
    block = min(512, rows)

    def tile(offset):
        return pl.BlockSpec((block, DH), lambda h, i: (i, offset + h))

    def long(count, offset):
        return pl.BlockSpec((count, DH), lambda h, i: (0, offset + h))

    return pl.pallas_call(
        attend_kernel,
        grid=(heads, rows // block),
        out_shape=(
            jax.ShapeDtypeStruct((rows, cols), F32),
            jax.ShapeDtypeStruct((rows, cols), BF),
            jax.ShapeDtypeStruct((heads, 1, rows), F32),
        ),
        in_specs=[
            tile(0),
            long(rows, heads),
            long(rows, 2 * heads),
            long(away, 0),
            long(away, heads),
        ],
        out_specs=(tile(0), tile(0), pl.BlockSpec((1, 1, block), lambda h, i: (h, 0, i))),
        scratch_shapes=[pltpu.VMEM((DH, rows + away), BF)],
        compiler_params=pltpu.CompilerParams(vmem_limit_bytes=52 * MIB),
        cost_estimate=pl.CostEstimate(
            flops=8 * rows * (rows + away) * cols,
            bytes_accessed=20 * rows * cols,
            transcendentals=rows * (rows + away) * heads,
        ),
        name="attend",
    )(qkv, qkv, qkv, kv_far, kv_far)


def share_meanwhile(
    now, count, pieces, back_ref, all_ref, send_sem, recv_sem, local_sem, also=()
):
    me, along_x, along_y, _ = square()
    send = sender(send_sem, recv_sem, False)
    near, far, passed, local = [], [], [], []
    for index, piece in enumerate(pieces):
        ways = (along_x, along_y) if index % 2 == 0 else (along_y, along_x)
        block, own = back_ref.at[piece], all_ref.at[index, me]
        relayed = all_ref.at[index, ways[0]]
        near.append(send(block, own, 3 * index, {"mp": ways[0]}))
        far.append(send(block, own, 3 * index + 1, {"mp": ways[1]}))
        passed.append(send(relayed, relayed, 3 * index + 2, {"mp": ways[1]}))
        local.append(pltpu.make_async_copy(block, own, local_sem.at[index]))

    @pl.when(now == 0)
    def _():
        greet([{"mp": along_x}, {"mp": along_y}, *also])
        for copy in near + far + local:
            copy.start()

    @pl.when(now == count // 4)
    def _():
        for first, second in zip(near, passed):
            first.wait_recv()
            second.start()

    def finish():
        @pl.when(now == count - 1)
        def _():
            for copy in far + passed:
                copy.wait_recv()
            for copy in near + far + passed:
                copy.wait_send()
            for copy in local:
                copy.wait()

    return finish


def meanwhile_scratch(pieces):
    return [
        pltpu.SemaphoreType.DMA((3 * len(pieces),)),
        pltpu.SemaphoreType.DMA((3 * len(pieces),)),
        pltpu.SemaphoreType.DMA((len(pieces),)),
    ]


def feed_back_kernel(
    pieces, members, low_ref, weight_ref, more_ref, pre_ref, turned_ref, back_ref,
    grad_ref, sums_ref, weight_grad_ref, all_ref, send_sem, recv_sem, local_sem,
):
    now, count = pl.program_id(0), pl.num_programs(0)
    finish = share_meanwhile(now, count, pieces, back_ref, all_ref, send_sem, recv_sem, local_sem)
    value = pre_ref[...]
    root = (2 / math.pi) ** 0.5
    square_of = value * value
    bent = jnp.tanh(root * value * (1 + 0.044715 * square_of))
    slope = 0.5 * (1 + bent) + (0.5 * root) * value * (1 - bent * bent) * (
        1 + 3 * 0.044715 * square_of
    )
    narrow = weight_ref.shape[0] // members
    weight = jnp.concatenate(
        [
            half[place * narrow : (place + 1) * narrow]
            for place in range(members)
            for half in (weight_ref, more_ref)
        ],
        axis=0,
    )
    grad = (matmul(low_ref[...], weight) * slope).astype(BF)
    grad_ref[...] = grad
    sums_ref[...] = jnp.sum(grad.astype(F32), axis=0, keepdims=True)
    weight_grad_ref[...] = matmul(turned_ref[...], grad).astype(BF)
    finish()


def feed_back(low, weight, more, inner_pre, turned, layer_back, pieces, members, parts, ident):
    rows, hidden = inner_pre.shape
    width = low.shape[1]
    step = 512
    _, piece, _ = layer_back.shape
    return pl.pallas_call(
        functools.partial(feed_back_kernel, pieces, members),
        grid=(hidden // step,),
        out_shape=(
            jax.ShapeDtypeStruct((rows, hidden), BF),
            jax.ShapeDtypeStruct((1, hidden), F32),
            jax.ShapeDtypeStruct((width, hidden), BF),
            jax.ShapeDtypeStruct((len(pieces), parts, piece, width), BF),
        ),
        in_specs=[
            pl.BlockSpec((rows, width), lambda i: (0, 0)),
            pl.BlockSpec((width // 2, step), lambda i: (0, i)),
            pl.BlockSpec((width // 2, step), lambda i: (0, i)),
            pl.BlockSpec((rows, step), lambda i: (0, i)),
            pl.BlockSpec((width, rows), lambda i: (0, 0)),
            ANY,
        ],
        out_specs=(
            pl.BlockSpec((rows, step), lambda i: (0, i)),
            pl.BlockSpec((1, step), lambda i: (0, i)),
            pl.BlockSpec((width, step), lambda i: (0, i)),
            ANY,
        ),
        scratch_shapes=meanwhile_scratch(pieces),
        compiler_params=pltpu.CompilerParams(
            collective_id=ident, has_side_effects=True, vmem_limit_bytes=58 * MIB
        ),
        cost_estimate=pl.CostEstimate(
            flops=4 * rows * width * hidden, bytes_accessed=40 * MIB, transcendentals=rows * hidden
        ),
        name="feed_back",
    )(low, weight, more, inner_pre, turned, layer_back)


def sibling():
    here = lax.axis_index("seq")
    return {"seq": here + 1 - 2 * lax.rem(here, 2)}


def attend_back_kernel(
    pieces,
    step,
    query_ref,
    key_ref,
    value_ref,
    key_far_ref,
    value_far_ref,
    grad_ref,
    mix_ref,
    log_ref,
    *rest,
):
    sharing = len(pieces) > 0
    if sharing:
        back_ref, *rest = rest
    dquery_ref, dkey_ref, dvalue_ref, *rest = rest
    if sharing:
        in_ref, all_ref, *rest = rest
    else:
        dkey_far_ref, dvalue_far_ref, *rest = rest
    turned, key_sum, value_sum, *rest = rest
    block = pl.program_id(1)
    rows = key_ref.shape[0]
    if sharing:
        away, pair_send, pair_recv, send_sem, recv_sem, local_sem = rest
        now = pl.program_id(0) * pl.num_programs(1) + block
        count = pl.num_programs(0) * pl.num_programs(1)
        finish = share_meanwhile(
            now, count, pieces, back_ref, all_ref, send_sem, recv_sem, local_sem, [sibling()]
        )

        def cross(kind, head):
            return pltpu.make_async_remote_copy(
                src_ref=away.at[kind, head],
                dst_ref=in_ref.at[kind, head],
                send_sem=pair_send.at[kind, head],
                recv_sem=pair_recv.at[kind, head],
                device_id=sibling(),
                device_id_type=MESH,
            )

    @pl.when(block == 0)
    def _():
        turned[:, :rows] = key_ref[...].T
        turned[:, rows:] = key_far_ref[...].T
        key_sum[...] = jnp.zeros_like(key_sum)
        value_sum[...] = jnp.zeros_like(value_sum)

    scale = DH ** (-0.5)
    query, grad = query_ref[...], grad_ref[...]
    terms = jnp.sum((grad.astype(F32) * mix_ref[...]).T, axis=0, keepdims=True)
    logs = log_ref[0]
    dquery = jnp.zeros((DH, query.shape[0]), F32)
    spans = [(key_ref, value_ref, start, start) for start in range(0, rows, step)]
    spans += [
        (key_far_ref, value_far_ref, start, rows + start)
        for start in range(0, key_far_ref.shape[0], step)
    ]
    for keys, values, start, place in spans:
        part = pl.ds(place, step)
        probs = jnp.exp(score_block(keys[pl.ds(start, step)], query) * scale - logs)
        prob_grad = score_block(values[pl.ds(start, step)], grad)
        score_grad = (probs * (prob_grad - terms) * scale).astype(BF)
        value_sum[part] += jnp.dot(probs.astype(BF), grad, preferred_element_type=F32)
        key_sum[part] += jnp.dot(score_grad, query, preferred_element_type=F32)
        dquery += jnp.dot(turned[:, part], score_grad, preferred_element_type=F32)
    dquery_ref[...] = dquery.T.astype(BF)

    @pl.when(block == pl.num_programs(1) - 1)
    def _():
        dkey_ref[...] = key_sum[:rows]
        dvalue_ref[...] = value_sum[:rows]
        if sharing:
            head = pl.program_id(0)
            for kind, total in enumerate((key_sum, value_sum)):
                away[kind, head] = total[rows:].astype(BF)
                cross(kind, head).start()
        else:
            dkey_far_ref[...] = key_sum[rows:].astype(BF)
            dvalue_far_ref[...] = value_sum[rows:].astype(BF)

    if sharing:

        @pl.when(now == count - 1)
        def _():
            for kind in range(2):
                for head in range(away.shape[1]):
                    cross(kind, head).wait()

        finish()


def attend_back(qkv, kv_far, grad, mix, logs, heads, layer_back, pieces, parts, ident):
    rows, cols = qkv.shape[0], heads * DH
    away = kv_far.shape[0]
    block, step = min(512, rows), min(512, rows)
    sharing = len(pieces) > 0
    _, piece, width = layer_back.shape

    def tile(offset):
        return pl.BlockSpec((block, DH), lambda h, i: (i, offset + h))

    def long(count, offset):
        return pl.BlockSpec((count, DH), lambda h, i: (0, offset + h))

    return pl.pallas_call(
        functools.partial(attend_back_kernel, pieces, step),
        grid=(heads, rows // block),
        out_shape=(
            jax.ShapeDtypeStruct((rows, cols), BF),
            jax.ShapeDtypeStruct((rows, cols), F32),
            jax.ShapeDtypeStruct((rows, cols), F32),
        )
        + (
            (
                jax.ShapeDtypeStruct((2, heads, rows, DH), BF),
                jax.ShapeDtypeStruct((len(pieces), parts, piece, width), BF),
            )
            if sharing
            else (jax.ShapeDtypeStruct((away, cols), BF),) * 2
        ),
        in_specs=[
            tile(0),
            long(rows, heads),
            long(rows, 2 * heads),
            long(away, 0),
            long(away, heads),
            tile(0),
            tile(0),
            pl.BlockSpec((1, 1, block), lambda h, i: (h, 0, i)),
        ]
        + ([ANY] if sharing else []),
        out_specs=(tile(0), long(rows, 0), long(rows, 0))
        + ((ANY, ANY) if sharing else (long(away, 0), long(away, 0))),
        scratch_shapes=[
            pltpu.VMEM((DH, rows + away), BF),
            pltpu.VMEM((rows + away, DH), F32),
            pltpu.VMEM((rows + away, DH), F32),
        ]
        + (
            [
                pltpu.VMEM((2, heads, rows, DH), BF),
                pltpu.SemaphoreType.DMA((2, heads)),
                pltpu.SemaphoreType.DMA((2, heads)),
            ]
            + meanwhile_scratch(pieces)
            if sharing
            else []
        ),
        compiler_params=pltpu.CompilerParams(
            vmem_limit_bytes=52 * MIB,
            **(dict(collective_id=ident, has_side_effects=True) if sharing else {}),
        ),
        cost_estimate=pl.CostEstimate(
            flops=20 * rows * (rows + away) * cols,
            bytes_accessed=30 * rows * cols,
            transcendentals=rows * (rows + away) * heads,
        ),
        name="attend_back",
    )(qkv, qkv, qkv, kv_far, kv_far, grad, mix, logs, *([layer_back] if sharing else []))


def from_group_members(block, members, per):
    blocks = []
    for step in range(1, per):
        pairs = [
            (base + place, base + (place - step) % per)
            for base in range(0, members, per)
            for place in range(per)
        ]
        blocks.append(lax.ppermute(block, "seq", pairs))
    return blocks


def to_group_members(total, blocks, members, per):
    for step in range(1, per):
        pairs = [
            (base + place, base + (place + step) % per)
            for base in range(0, members, per)
            for place in range(per)
        ]
        total = total + lax.ppermute(blocks[step - 1], "seq", pairs).astype(F32)
    return total


def last_kernel(
    per, turned_hbm, query_ref, key_ref, value_ref, in_ref, proj_hbm, layer_hbm, layer_more_hbm,
    grad_ref, sums_ref, part_ref, layer_ref, turned_ref, made, proj, layer, load_sem, put_sem,
):
    rows, cols = query_ref.shape
    count = load_sem.shape[0] - 3
    step = turned_ref.shape[0] // count
    loads = []
    for place in range(count):
        block = pl.ds(place * step, step)
        loads.append(
            pltpu.make_async_copy(turned_hbm.at[block], turned_ref.at[block], load_sem.at[place])
        )
    loads.append(pltpu.make_async_copy(proj_hbm, proj, load_sem.at[count]))
    groups = layer.shape[0]
    for place, source in enumerate((layer_hbm, layer_more_hbm)):
        block = pl.ds(place * (groups // 2), groups // 2)
        loads.append(pltpu.make_async_copy(source, layer.at[block], load_sem.at[count + 1 + place]))
    for copy in loads:
        copy.start()
    puts = []

    def put(source, target):
        copy = pltpu.make_async_copy(source, target, put_sem.at[len(puts)])
        copy.start()
        puts.append(copy)

    for index, (own, far) in enumerate(
        ((query_ref, None), (key_ref, 0), (value_ref, 1))
    ):
        span = pl.ds(index * cols, cols)
        grad = own[...]
        if far is not None:
            far = [in_ref[far, head] for head in range(cols // DH)]
            grad = (grad + jnp.concatenate(far, axis=1).astype(F32)).astype(BF)
        grad_ref[:, span] = grad
        sums_ref[:, span] = jnp.sum(grad.astype(F32), axis=0, keepdims=True)
        for place in range(count):
            block = pl.ds(place * step, step)
            if index == 0:
                loads[place].wait()
            made[index, block] = matmul(turned_ref[block], grad_ref[:, span]).astype(BF)
        put(made.at[index], part_ref.at[:, span])
        if index == 1:
            loads[count].wait()
            put(proj, part_ref.at[:, pl.ds(3 * cols, cols)])
            for copy in loads[count + 1 :]:
                copy.wait()
            group = lax.axis_index("seq") // per
            for piece in range(groups):
                put(layer.at[piece], layer_ref.at[lax.rem(group + piece, groups)])
    for copy in puts:
        copy.wait()


def last_gradients(turned, query, key, value, arrived, proj_part, layer, layer_more, per):
    rows, cols = query.shape
    width = turned.shape[0]
    return pl.pallas_call(
        functools.partial(last_kernel, per),
        out_shape=(
            jax.ShapeDtypeStruct((rows, 3 * cols), BF),
            jax.ShapeDtypeStruct((1, 3 * cols), F32),
            jax.ShapeDtypeStruct((width, 4 * cols), BF),
            jax.ShapeDtypeStruct((2 * layer.shape[0],) + layer.shape[1:], layer.dtype),
        ),
        in_specs=[ANY] + [VMEM] * 4 + [ANY] * 3,
        out_specs=(VMEM, VMEM, ANY, ANY),
        scratch_shapes=[
            pltpu.VMEM(turned.shape, BF),
            pltpu.VMEM((3, width, cols), BF),
            pltpu.VMEM(proj_part.shape, BF),
            pltpu.VMEM((2 * layer.shape[0],) + layer.shape[1:], BF),
            pltpu.SemaphoreType.DMA((7,)),
            pltpu.SemaphoreType.DMA((4 + 2 * layer.shape[0],)),
        ],
        compiler_params=pltpu.CompilerParams(vmem_limit_bytes=52 * MIB),
        cost_estimate=pl.CostEstimate(
            flops=6 * rows * width * cols, bytes_accessed=32 * MIB, transcendentals=0
        ),
        name="last_gradients",
    )(turned, query, key, value, arrived, proj_part, layer, layer_more)


def packed(vectors, lines):
    flat = jnp.concatenate(vectors)
    return jnp.pad(flat, (0, lines * 128 - flat.shape[0])).reshape(lines, 128)


def after(value, *others):
    return lax.optimization_barrier((value,) + others)[0]


def on_device(members, parts, *arrays):
    (
        tokens,
        query_weight,
        query_bias,
        key_weight,
        value_weight,
        value_bias,
        proj_weight,
        proj_bias,
        gain_first,
        shift_first,
        inner_weight,
        inner_bias,
        outer_weight,
        outer_bias,
        gain_second,
        shift_second,
        cotangent,
    ) = arrays
    micro, seqs, length, width = tokens.shape
    groups = micro * seqs
    per = members // groups
    assert per * groups == members and (parts != 4 or per == 2)
    piece = length // parts
    rows = groups * length
    quarter = groups * piece
    mine = lax.axis_index("mp")
    group = lax.axis_index("seq") // per

    depth, cols = query_weight.shape
    heads = cols // DH
    first = jnp.concatenate([query_weight, key_weight, value_weight, proj_weight.T], axis=1)
    first = lax.all_gather(first, "seq", axis=0, tiled=True)
    hidden = inner_weight.shape[1]
    fused = parts == 4 and per == 2
    outer_turned = outer_weight.T
    if fused:
        part = depth // 2
        folded = jnp.concatenate(
            [outer_turned[:part, : hidden // 2], outer_turned[:part, hidden // 2 :]], axis=0
        )
        second = jnp.concatenate([inner_weight, folded], axis=1)
        second = lax.all_gather(second, "seq", axis=0, tiled=True)
        w_inner = second[:, :hidden]
        w_outer = lax.all_gather(outer_turned[part:], "seq", axis=0, tiled=True)
    else:
        w_inner = second = lax.all_gather(inner_weight, "seq", axis=0, tiled=True)
        w_outer = lax.all_gather(outer_turned, "seq", axis=0, tiled=True)
    w_qkv = first[:, : 3 * cols]
    w_proj = first[:, 3 * cols :]
    vectors = [
        query_bias,
        value_bias,
        inner_bias,
        proj_bias,
        gain_first,
        shift_first,
        outer_bias,
        gain_second,
        shift_second,
    ]
    sizes = [vector.shape[0] for vector in vectors]
    lines = -(-sum(sizes) // 2048) * 16
    own_vectors = packed(vectors, lines)

    def to_blocks(array):
        array = array.reshape(groups, length, width)
        return [
            lax.dynamic_slice(
                array, (lax.rem(group + k, groups), mine * piece, 0), (1, piece, width)
            )[0]
            for k in range(groups)
        ]

    x_part, all_vectors = swap_groups(
        jnp.stack(to_blocks(tokens)),
        jnp.broadcast_to(own_vectors[None], (members, lines, 128)),
        members,
        parts,
        1,
        1,
    )
    x_part = x_part.reshape(quarter, width)
    x_rows = share_over_mp(x_part, parts, 8).reshape(rows, width)
    all_vectors = all_vectors.reshape(members, -1).astype(F32)
    full = []
    start = 0
    for size in sizes:
        full.append(all_vectors[:, start : start + size].reshape(-1))
        start += size
    b_query, b_value, b_inner, b_proj, gain_one, shift_one, b_outer, gain_two, shift_two = full

    bias = jnp.concatenate([b_query, jnp.zeros_like(b_query), b_value])
    qkv = (matmul(x_rows, w_qkv) + bias).astype(BF)
    kv_far = from_group_members(qkv[:, cols:], members, per)
    kv_far = kv_far[0] if per == 2 else jnp.concatenate(kv_far, axis=0)
    mixture, mixture_low, logs = attend(qkv, kv_far, heads)

    def blocked(array):
        return array.reshape(groups, piece, width)

    first_low, normal_one, inverse_one, x_turned = first_norm(
        over_cols(mixture_low, w_proj).astype(BF),
        blocked(x_part),
        x_rows,
        jnp.stack([b_proj, gain_one, shift_one]),
        parts,
        2,
    )
    first_low = first_low.reshape(rows, width)

    inner_pre = matmul(first_low, w_inner) + b_inner
    active = gelu_tanh(inner_pre).astype(BF)
    done, active_turned, w_outer_half = None, None, None
    if fused:
        done, active_turned, w_outer_half, first_turned = half_sum(
            active, second, first_low, groups, piece, members, parts, 13
        )
    else:
        first_turned = first_low.T
    second_low, second_grad, layer_back, sums, outer_w_part = second_norm(
        active,
        w_outer,
        active_turned,
        done,
        normal_one,
        jnp.stack(to_blocks(cotangent)),
        jnp.stack([gain_one, shift_one, b_outer, gain_two, shift_two]),
        members,
        parts,
        3,
    )
    second_low = second_low.reshape(rows, width)

    outer_w_grad = lax.psum_scatter(outer_w_part, "seq", scatter_dimension=1, tiled=True)
    pieces = list(range(groups)) if fused else []
    early, late = pieces[: groups // 2], pieces[groups // 2 :]
    if fused:
        inner_grad, inner_b_grad, inner_w_part, layer_out = feed_back(
            second_low,
            w_outer_half,
            w_outer,
            inner_pre,
            first_turned,
            layer_back,
            early,
            members,
            parts,
            7,
        )
    else:
        _, pull_gelu = jax.vjp(gelu_tanh, inner_pre)
        inner_grad = pull_gelu(matmul(second_low, w_outer))[0].astype(BF)
        inner_b_grad = jnp.sum(inner_grad.astype(F32), axis=0)
        inner_w_part = matmul(first_turned, inner_grad).astype(BF)
        layer_out = lax.all_gather(jnp.roll(layer_back, group, axis=0), "mp", axis=1)
    inner_w_grad = lax.psum_scatter(inner_w_part, "seq", scatter_dimension=0, tiled=True)
    attn_low, attn_grad, summed_rows = first_back(
        inner_grad,
        second,
        second_grad,
        normal_one,
        inverse_one,
        after(sums, inner_w_part),
        gain_one[None],
        parts,
        4,
    )
    attn_low = after(attn_low.reshape(rows, width), outer_w_grad)
    summed_rows = jnp.sum(summed_rows, axis=0)

    proj_w_part = over_rows(attn_low, mixture_low).astype(BF)
    mixture_grad = matmul(after(attn_low, proj_w_part), w_proj).astype(BF)
    query_grad, key_grad, value_grad, *others = attend_back(
        qkv, kv_far, mixture_grad, mixture, logs, heads, layer_back, late, parts, 5
    )

    def blocks_of(array):
        return [array[i * rows : (i + 1) * rows] for i in range(per - 1)]

    if fused:
        qkv_grad, bias_grad, last_w_part, layer_out = last_gradients(
            x_turned,
            query_grad,
            key_grad,
            value_grad,
            others[0],
            proj_w_part,
            layer_out,
            others[1],
            per,
        )
        bias_grad = bias_grad[0]
    else:
        key_grad = to_group_members(key_grad, blocks_of(others[0]), members, per)
        value_grad = to_group_members(value_grad, blocks_of(others[1]), members, per)
        qkv_grad = jnp.concatenate([query_grad, key_grad.astype(BF), value_grad.astype(BF)], axis=1)
        last_w_part = jnp.concatenate([matmul(x_turned, qkv_grad).astype(BF), proj_w_part], axis=1)
        bias_grad = jnp.sum(qkv_grad.astype(F32), axis=0)
    last_w_grad = lax.psum_scatter(last_w_part, "seq", scatter_dimension=0, tiled=True).astype(F32)
    small = jnp.concatenate(
        [
            bias_grad[:cols].reshape(members, -1),
            bias_grad[2 * cols :].reshape(members, -1),
            inner_b_grad.reshape(members, -1),
        ]
        + [summed_rows[i].reshape(members, -1) for i in (3, 4, 5, 0, 1, 2)],
        axis=1,
    )
    small = jnp.pad(small, ((0, 0), (0, lines * 128 - small.shape[1])))
    input_grad, small = input_gradient(
        qkv_grad,
        first,
        attn_grad,
        small.reshape(members, lines, 128),
        members,
        parts,
        6,
    )
    input_grad = after(input_grad, inner_w_grad).astype(F32).reshape(micro, seqs, length, width)
    layer_out = layer_out.reshape(micro, seqs, length, width)
    small = jnp.sum(small, axis=0).reshape(-1)
    pieces = []
    start = 0
    for size in sizes:
        pieces.append(small[start : start + size])
        start += size
    return (
        layer_out,
        input_grad,
        last_w_grad[:, :cols],
        pieces[0],
        last_w_grad[:, cols : 2 * cols],
        last_w_grad[:, 2 * cols : 3 * cols],
        pieces[1],
        last_w_grad[:, 3 * cols :].T,
        pieces[3],
        pieces[4],
        pieces[5],
        inner_w_grad.astype(F32),
        pieces[2],
        outer_w_grad.astype(F32),
        pieces[6],
        pieces[7],
        pieces[8],
    )


def solution(mesh):
    tokens = P(None, None, "seq", None)
    rows_cols, cols_rows, both, seq = P("seq", "mp"), P("mp", "seq"), P(("mp", "seq")), P("seq")
    weights = (
        rows_cols,
        both,
        rows_cols,
        rows_cols,
        both,
        cols_rows,
        seq,
        seq,
        seq,
        rows_cols,
        both,
        cols_rows,
        seq,
        seq,
        seq,
    )
    return jax.shard_map(
        functools.partial(on_device, mesh.shape["seq"], mesh.shape["mp"]),
        mesh=mesh,
        in_specs=(tokens,) + weights + (tokens,),
        out_specs=(tokens, tokens) + weights,
        check_vma=False,
    )
```

```python
import functools
import math

import jax
import jax.numpy as jnp
from jax import lax
from jax.experimental import pallas as pl
from jax.experimental.pallas import tpu as pltpu
from jax.sharding import PartitionSpec as P

DH = 128
EPSILON = 1e-06
BF = jnp.bfloat16
F32 = jnp.float32
MESH = pl.DeviceIdType.MESH
ANY = pl.BlockSpec(memory_space=pl.ANY)
VMEM = pl.BlockSpec(memory_space=pltpu.VMEM)
MIB = 1 << 20


def matmul(left, right):
    return jnp.dot(left, right, preferred_element_type=F32)


def over_rows(left, right):
    return lax.dot_general(left, right, (((0,), (0,)), ((), ())), preferred_element_type=F32)


def over_cols(left, right):
    return lax.dot_general(left, right, (((1,), (1,)), ((), ())), preferred_element_type=F32)


def gelu_tanh(values):
    return jax.nn.gelu(values, approximate=True)


def square():
    me = lax.axis_index("mp")
    return me, me + 1 - 2 * lax.rem(me, 2), lax.rem(me + 2, 4), 3 - me


def greet(devices):
    barrier = pltpu.get_barrier_semaphore()
    for device in devices:
        pl.semaphore_signal(barrier, inc=1, device_id=device, device_id_type=MESH)
    pl.semaphore_wait(barrier, len(devices))


def sender(send_sem, recv_sem, start=True):
    def send(source, target, slot, device):
        copy = pltpu.make_async_remote_copy(
            src_ref=source,
            dst_ref=target,
            send_sem=send_sem.at[slot],
            recv_sem=recv_sem.at[slot],
            device_id=device,
            device_id_type=MESH,
        )
        if start:
            copy.start()
        return copy

    return send


class Exchange:
    def __init__(self, part_ref, landed, relay, send_sem, recv_sem):
        self.me, self.along_x, self.along_y, self.across = square()
        self.parts, self.landed, self.relay = part_ref, landed, relay
        self.send = sender(send_sem, recv_sem)
        self.copies = {}

    def part(self, owner, piece):
        return self.parts.at[row_place(owner, piece, 2 * self.parts.shape[2])]

    def ways(self, index):
        pair = (self.along_x, self.along_y)
        return pair if index % 2 == 0 else pair[::-1]

    def start(self, index, piece):
        near, _ = self.ways(index)
        for kind, owner in enumerate((self.across, near)):
            self.copies[index, kind] = self.send(
                self.part(owner, piece), self.landed.at[index, kind], 6 * index + kind, {"mp": near}
            )

    def pass_on(self, index, piece):
        _, far = self.ways(index)
        self.copies[index, 0].wait_recv()
        self.relay[index] = (
            self.part(far, piece)[...].astype(F32) + self.landed[index, 0].astype(F32)
        ).astype(BF)
        self.copies[index, 2] = self.send(
            self.relay.at[index], self.landed.at[index, 2], 6 * index + 2, {"mp": far}
        )

    def total(self, index, piece):
        self.copies[index, 1].wait_recv()
        self.copies[index, 2].wait_recv()
        return (
            self.part(self.me, piece)[...].astype(F32)
            + self.landed[index, 1].astype(F32)
            + self.landed[index, 2].astype(F32)
        )

    def share(self, index, source, target):
        near, far = self.ways(index)
        self.copies[index, 3] = self.send(source, target(self.me), 6 * index + 3, {"mp": near})
        self.copies[index, 4] = self.send(source, target(self.me), 6 * index + 4, {"mp": far})

    def forward(self, index, target):
        near, far = self.ways(index)
        self.copies[index, 3].wait_recv()
        self.copies[index, 5] = self.send(target(near), target(near), 6 * index + 5, {"mp": far})

    def arrived(self, indices):
        for index in indices:
            self.copies[index, 4].wait_recv()
            self.copies[index, 5].wait_recv()

    def sent(self):
        for copy in self.copies.values():
            copy.wait_send()

    def finish(self, count):
        self.arrived(range(count))
        self.sent()


def row_place(owner, piece, groups):
    half = groups // 2
    return piece // half, owner, piece % half


def planes(groups, per):
    index = lax.axis_index("seq")
    return [{"seq": lax.rem(index + step * per, groups * per)} for step in range(groups)]


def mean_of(values):
    return jnp.mean(values, axis=-1, keepdims=True)


def normed(values):
    centre = values - mean_of(values)
    inverse = lax.rsqrt(mean_of(centre * centre) + EPSILON)
    return centre * inverse, inverse


def norm_back(grad, normal, inverse, gain):
    inner = grad * gain
    return inverse * (inner - mean_of(inner) - normal * mean_of(inner * normal))


def turner(rows_of, turned_ref):
    width, rows = turned_ref.shape
    step = 256

    def fill(part):
        @pl.loop(0, width // (2 * step))
        def _(index):
            span = pl.ds(pl.multiple_of(part * (width // 2) + index * step, step), step)
            turned_ref[span] = rows_of(span).reshape(rows, step).T

    return fill


class Product:
    def __init__(self, exchange, turned, left_ref, weight_ref, weight, rows, load_sem, blocks=None):
        self.exchange, self.turned = exchange, turned
        self.left, self.weight, self.rows = left_ref, weight, rows
        self.left_loads = {}
        width = exchange.parts.shape[-1]
        self.step = min(512, width)
        self.count = width // self.step
        depth = left_ref.shape[-1]
        self.loads, slot = [], 0
        for index in range(self.count):
            span = pl.ds(index * self.step, self.step)
            place = (span, pl.ds(0, depth)) if turned else (pl.ds(0, depth), span)
            pairs = [(weight_ref.at[place], weight.at[place])] if blocks is None else blocks(index)
            copies = []
            for source, target in pairs:
                copy = pltpu.make_async_copy(source, target, load_sem.at[slot])
                copy.start()
                copies.append(copy)
                slot += 1
            self.loads.append(copies)

    def make(self, batch, first=False):
        _, _, half, piece_rows, _ = self.left.shape
        for _, piece in batch:
            if piece // half in self.left_loads:
                self.left_loads.pop(piece // half).wait()
        for place, (owner, piece) in enumerate(batch):
            self.rows[place * piece_rows : (place + 1) * piece_rows] = self.left[
                row_place(owner, piece, 2 * half)
            ]

        def columns(index):
            span = pl.ds(pl.multiple_of(index * self.step, self.step), self.step)
            if self.turned:
                product = over_cols(self.rows[...], self.weight[span])
            else:
                product = matmul(self.rows[...], self.weight[:, span])
            product = product.astype(BF)
            for place, (owner, piece) in enumerate(batch):
                self.exchange.part(owner, piece)[:, span] = product[
                    place * piece_rows : (place + 1) * piece_rows
                ]

        if first:
            for index in range(self.count):
                for copy in self.loads[index]:
                    copy.wait()
                columns(index)
        else:
            pl.loop(0, self.count)(columns)


def run_pieces(exchange, order, work, product=None, fill=None):
    groups = len(order)
    places = list(enumerate(order))
    half = groups // 2
    first, second = places[:half], places[half:]

    def make(half_places, near):
        if product is None:
            return
        batch = []
        for index, piece in half_places:
            ways = exchange.ways(index)
            owners = (exchange.across, ways[0]) if near else (ways[1], exchange.me)
            batch += [(owner, piece) for owner in owners]
        product.make(batch, near and half_places is first)

    make(first, True)
    for index, piece in first:
        exchange.start(index, piece)
    make(first, False)
    if fill is not None:
        fill(0)
    for index, piece in first:
        exchange.pass_on(index, piece)
    make(second, True)
    for index, piece in second:
        exchange.start(index, piece)
    make(second, False)
    if fill is not None:
        fill(1)
    for index, piece in first:
        work(index, piece, exchange.total(index, piece))
    for index, piece in second:
        exchange.pass_on(index, piece)
    return first, second


def first_norm_kernel(
    groups, part_ref, x_ref, all_ref, rows_ref, low_ref, normal_ref, inverse_ref, turned_ref,
    landed, relay, ready, send_sem, recv_sem, local_sem,
):
    exchange = Exchange(part_ref, landed, relay, send_sem, recv_sem)
    greet([{"mp": exchange.along_x}, {"mp": exchange.along_y}])
    local = []

    def target(piece):
        return lambda device: low_ref.at[row_place(device, piece, groups)]

    def work(index, piece, total):
        values = x_ref[piece].astype(F32) + total + rows_ref[0:1]
        normal, inverse = normed(values)
        normal_ref[piece] = normal
        inverse_ref[piece] = inverse
        ready[index] = (normal * rows_ref[1:2] + rows_ref[2:3]).astype(BF)
        exchange.share(index, ready.at[index], target(piece))
        copy = pltpu.make_async_copy(
            ready.at[index], target(piece)(exchange.me), local_sem.at[index]
        )
        copy.start()
        local.append(copy)

    first, second = run_pieces(
        exchange, range(groups), work, None, turner(lambda span: all_ref[:, span], turned_ref)
    )
    for index, piece in first:
        exchange.forward(index, target(piece))
    for index, piece in second:
        work(index, piece, exchange.total(index, piece))
    for index, piece in second:
        exchange.forward(index, target(piece))
    exchange.finish(groups)
    for copy in local:
        copy.wait()


def half_sum_kernel(
    groups, members, left_ref, weight_ref, first_ref, total_ref, turned_ref, weight_out, first_turned_ref,
    landed, relay, part_ref, weight, rows, load_sem, put_sem, send_sem, recv_sem,
):
    exchange = Exchange(part_ref, landed, relay, send_sem, recv_sem)
    width, depth = weight.shape
    narrow, half = width // members, depth // 2
    apart = weight_ref.shape[1] - half

    def blocks(index):
        step = min(512, width)
        for place in range(index * step // narrow, (index + 1) * step // narrow):
            for part in range(2):
                yield (
                    weight_ref.at[pl.ds((2 * place + part) * narrow, narrow), pl.ds(apart, half)],
                    weight.at[pl.ds(place * narrow, narrow), pl.ds(part * half, half)],
                )

    product = Product(exchange, True, left_ref, weight_ref, weight, rows, load_sem, blocks)
    greet([{"mp": exchange.along_x}, {"mp": exchange.along_y}])

    def work(index, piece, total):
        total_ref[piece] = total

    turn_left = turner(lambda span: left_ref[:, :, :, :, span], turned_ref)
    turn_first = turner(lambda span: first_ref[:, span], first_turned_ref)

    def fill(part):
        turn_left(part)
        turn_first(part)

    _, second = run_pieces(exchange, range(groups), work, product, fill)
    put = pltpu.make_async_copy(weight, weight_out, put_sem)
    put.start()
    for index, piece in second:
        work(index, piece, exchange.total(index, piece))
    put.wait()
    exchange.sent()


def second_norm_kernel(
    groups, per, left_hbm, weight_ref, turned_hbm, done_hbm,
    normal_hbm, cotan_ref, rows_ref,
    low_hbm, grad_hbm, back_ref, sums_ref, weight_grad_ref,
    landed, relay, part_ref, weight, rows, load_sem,
    ready, layer, cotan_in, turned_ref, whole, left_ref, done_ref, normal_ref, low_ref, grad_ref,
    put_sem, in_sem, out_sem,
    send_sem, recv_sem, local_sem,
):
    exchange = Exchange(part_ref, landed, relay, send_sem, recv_sem)

    def moved(source, target, sem):
        copy = pltpu.make_async_copy(source, target, sem)
        copy.start()
        return copy

    left_loads = {0: moved(left_hbm.at[0], left_ref.at[0], in_sem.at[0])}
    product = Product(exchange, True, left_ref, weight_ref, weight, rows, load_sem)
    members = groups * per
    narrow = weight.shape[0] // members
    left_loads[1] = moved(left_hbm.at[1], left_ref.at[1], in_sem.at[1])
    product.left_loads = left_loads
    early = [
        moved(cotan_ref.at[0], cotan_in.at[0], in_sem.at[2]),
        moved(normal_hbm, normal_ref, in_sem.at[3]),
        moved(done_hbm, done_ref, in_sem.at[4]),
    ]
    load_turned = moved(turned_hbm, turned_ref, in_sem.at[5])
    outward = []
    peers = planes(groups, per)
    greet([{"mp": exchange.along_x}, {"mp": exchange.along_y}] + peers[1:])
    base = 6 * groups
    arriving = {
        step: exchange.send(cotan_ref.at[step], cotan_in.at[step], base + step, peers[step])
        for step in range(1, groups)
    }
    leaving, local = [], []
    sums_ref[...] = jnp.zeros_like(sums_ref)

    def target(piece):
        return lambda device: low_ref.at[row_place(device, piece, groups)]

    def keep(source, place, slot):
        copy = pltpu.make_async_copy(source, place, local_sem.at[slot])
        copy.start()
        local.append(copy)

    def work(index, piece, total):
        while early:
            early.pop().wait()
        gain_one, shift_one, bias = rows_ref[0:1], rows_ref[1:2], rows_ref[2:3]
        gain, shift = rows_ref[3:4], rows_ref[4:5]
        done = done_ref[piece]
        total = jnp.concatenate(
            [
                half[:, place * narrow : (place + 1) * narrow]
                for place in range(members)
                for half in (done, total)
            ],
            axis=1,
        )
        values = normal_ref[piece] * gain_one + shift_one + total + bias
        normal, inverse = normed(values)
        layer[index] = (normal * gain + shift).astype(BF)
        if piece == 0:
            keep(layer.at[index], back_ref.at[0], groups)
            cotan = cotan_in[0].astype(F32)
        else:
            leaving.append(
                exchange.send(
                    layer.at[index], back_ref.at[piece], base + groups + piece, peers[groups - piece]
                )
            )
            arriving[piece].wait_recv()
            cotan = cotan_in[piece].astype(F32)
        grad = norm_back(cotan, normal, inverse, gain)
        grad_ref[piece] = grad
        ready[index] = grad.astype(BF)
        exchange.share(index, ready.at[index], target(piece))
        keep(ready.at[index], target(piece)(exchange.me), index)
        sums_ref[0:1] += jnp.sum(grad, axis=0, keepdims=True)
        sums_ref[1:2] += jnp.sum(cotan * normal, axis=0, keepdims=True)
        sums_ref[2:3] += jnp.sum(cotan, axis=0, keepdims=True)
        outward.append(moved(grad_ref.at[piece], grad_hbm.at[piece], out_sem.at[2 + index]))

    first, second = run_pieces(exchange, range(groups), work, product)
    for index, piece in first:
        exchange.forward(index, target(piece))
    for index, piece in second:
        work(index, piece, exchange.total(index, piece))
    step = 256
    count = whole.shape[1] // step
    depth = turned_ref.shape[1] // 2

    def columns(index):
        return pl.ds(pl.multiple_of(index * step, step), step)

    def put(index):
        span = columns(index)
        return pltpu.make_async_copy(
            whole.at[:, span], weight_grad_ref.at[:, span], put_sem.at[index]
        )

    def product_of(part, span):
        low = low_ref[part, :, :, :, span].reshape(depth, step)
        return matmul(turned_ref[:, part * depth : (part + 1) * depth], low)

    exchange.arrived([index for index, _ in first])
    load_turned.wait()
    for copy in local[: len(first) + 1]:
        copy.wait()
    outward.append(moved(low_ref.at[0], low_hbm.at[0], out_sem.at[0]))

    def first_product(start, stop):
        @pl.loop(start, stop)
        def _(index):
            span = columns(index)
            whole[:, span] = product_of(0, span).astype(BF)

    share_out = count // (2 * len(second))
    done = count // 2
    first_product(0, done)
    for index, piece in second:
        exchange.forward(index, target(piece))
        first_product(done, done + share_out)
        done += share_out
    exchange.arrived([index for index, _ in second])
    for copy in local[len(first) + 1 :]:
        copy.wait()
    outward.append(moved(low_ref.at[1], low_hbm.at[1], out_sem.at[1]))

    @pl.loop(0, count)
    def _(index):
        span = columns(index)
        whole[:, span] = (product_of(1, span) + whole[:, span].astype(F32)).astype(BF)
        put(index).start()

    exchange.sent()
    for copy in outward:
        copy.wait()
    for copy in leaving:
        copy.wait()
    for copy in arriving.values():
        copy.wait_send()
    for index in range(count):
        put(index).wait()


def first_back_kernel(
    groups, left_ref, weight_ref, grad_ref, normal_ref, inverse_ref, sums_in_ref, rows_ref,
    low_ref, out_ref, sums_ref,
    landed, relay, ready, own_sums, part_ref, weight, rows, load_sem,
    send_sem, recv_sem, local_sem,
):
    exchange = Exchange(part_ref, landed, relay, send_sem, recv_sem)
    product = Product(exchange, True, left_ref, weight_ref, weight, rows, load_sem)
    greet([{"mp": exchange.along_x}, {"mp": exchange.along_y}, {"mp": exchange.across}])
    local = []
    own_sums[...] = sums_in_ref[...]

    def target(piece):
        return lambda device: low_ref.at[row_place(device, piece, groups)]

    def keep(source, place, slot):
        copy = pltpu.make_async_copy(source, place, local_sem.at[slot])
        copy.start()
        local.append(copy)

    def work(index, piece, total):
        grad = total + grad_ref[piece]
        normal = normal_ref[piece]
        moved = norm_back(grad, normal, inverse_ref[piece], rows_ref[0:1])
        out_ref[piece] = moved
        ready[index] = moved.astype(BF)
        exchange.share(index, ready.at[index], target(piece))
        keep(ready.at[index], target(piece)(exchange.me), index)
        own_sums[3:4] += jnp.sum(moved, axis=0, keepdims=True)
        own_sums[4:5] += jnp.sum(grad * normal, axis=0, keepdims=True)
        own_sums[5:6] += jnp.sum(grad, axis=0, keepdims=True)

    first, second = run_pieces(exchange, range(groups), work, product)
    for index, piece in first:
        exchange.forward(index, target(piece))
    for index, piece in second:
        work(index, piece, exchange.total(index, piece))
    others = [
        exchange.send(own_sums, sums_ref.at[exchange.me], 6 * groups + slot, {"mp": device})
        for slot, device in enumerate((exchange.along_x, exchange.along_y, exchange.across))
    ]
    keep(own_sums, sums_ref.at[exchange.me], groups)
    for index, piece in second:
        exchange.forward(index, target(piece))
    exchange.finish(groups)
    for copy in others:
        copy.wait()
    for copy in local:
        copy.wait()


def input_order(groups):
    return list(range(1, groups - 1)) + [0, groups - 1]


def input_kernel(
    groups, per, left_ref, weight_ref, grad_ref, small_ref,
    all_ref, small_out,
    landed, relay, ready, back, part_ref, weight, rows, load_sem,
    send_sem, recv_sem, local_sem,
):
    exchange = Exchange(part_ref, landed, relay, send_sem, recv_sem)
    product = Product(exchange, True, left_ref, weight_ref, weight, rows, load_sem)
    peers = planes(groups, per)
    members = groups * per
    here = lax.axis_index("seq")
    group = here // per
    devices = [{"seq": lax.rem(here + step, members)} for step in range(1, members)]
    greet([{"mp": exchange.along_x}, {"mp": exchange.along_y}] + devices)
    base = 6 * groups
    small = [
        exchange.send(
            small_ref.at[lax.rem(here + step, members)],
            small_out.at[here],
            base + groups + step,
            devices[step - 1],
        )
        for step in range(1, members)
    ]
    crossing, local = {}, []

    def keep(source, place, slot):
        copy = pltpu.make_async_copy(source, place, local_sem.at[slot])
        copy.start()
        local.append(copy)

    keep(small_ref.at[here], small_out.at[here], groups)

    def target(piece):
        sequence = lax.rem(group + piece, groups)
        return lambda device: all_ref.at[sequence, device]

    def work(index, piece, total):
        ready[piece] = (total + grad_ref[piece]).astype(BF)
        if piece > 0:
            crossing[piece] = exchange.send(
                ready.at[piece], back.at[piece], base + piece, peers[groups - piece]
            )

    def share(index, piece):
        source = ready.at[0]
        if piece > 0:
            crossing[piece].wait_recv()
            source = back.at[piece]
        exchange.share(index, source, target(piece))
        keep(source, target(piece)(exchange.me), index)

    first, second = run_pieces(exchange, input_order(groups), work, product)
    for index, piece in second:
        work(index, piece, exchange.total(index, piece))
    outward = [place for place in second if place[1] == 0] + first
    outward += [place for place in second if place[1] > 0]
    for index, piece in outward:
        share(index, piece)
    for index, piece in outward:
        exchange.forward(index, target(piece))
    exchange.finish(groups)
    for copy in small:
        copy.wait()
    for copy in crossing.values():
        copy.wait_send()
    for copy in local:
        copy.wait()


def product_scratch(parts, groups, piece, width, depth, turned, loads=1):
    return [
        pltpu.VMEM((2, parts, groups // 2, piece, width), BF),
        pltpu.VMEM((width, depth) if turned else (depth, width), BF),
        pltpu.VMEM((groups * piece, depth), BF),
        pltpu.SemaphoreType.DMA((max(width // 512, loads),)),
    ]


def exchange_call(kernel, ident, operands, results, sums, scratch, extra, outside=(), local=True):
    groups, piece, width = sums
    return pl.pallas_call(
        kernel,
        out_shape=tuple(jax.ShapeDtypeStruct(shape, dtype) for shape, dtype, _ in results),
        in_specs=[ANY if place in outside else VMEM for place in range(len(operands))],
        out_specs=tuple(spec for _, _, spec in results),
        scratch_shapes=[
            pltpu.VMEM((groups, 3, piece, width), BF),
            pltpu.VMEM((groups, piece, width), BF),
        ]
        + scratch
        + [
            pltpu.SemaphoreType.DMA((6 * groups + extra,)),
            pltpu.SemaphoreType.DMA((6 * groups + extra,)),
        ]
        + ([pltpu.SemaphoreType.DMA((groups + 1,))] if local else []),
        compiler_params=pltpu.CompilerParams(
            collective_id=ident, has_side_effects=True, vmem_limit_bytes=58 * MIB
        ),
        cost_estimate=pl.CostEstimate(flops=0, bytes_accessed=200 * MIB, transcendentals=0),
        name=f"exchange_{ident}",
    )(*operands)


def first_norm(part, x_part, x_rows, rows, parts, ident):
    groups, piece, width = x_part.shape
    half = groups // 2
    if parts != 4:
        total = lax.psum_scatter(part, "mp", scatter_dimension=0, tiled=True).astype(F32)
        values = x_part.astype(F32) + total.reshape(x_part.shape) + rows[0]
        normal, inverse = normed(values)
        low = lax.all_gather((normal * rows[1] + rows[2]).astype(BF), "mp", axis=0)
        return low, normal, inverse, x_rows.T
    return exchange_call(
        functools.partial(first_norm_kernel, groups),
        ident,
        (part.reshape(2, parts, half, piece, width), x_part, x_rows, rows),
        [
            ((2, parts, half, piece, width), BF, ANY),
            ((groups, piece, width), F32, VMEM),
            ((groups, piece, 1), F32, VMEM),
            ((width, x_rows.shape[0]), BF, VMEM),
        ],
        (groups, piece, width),
        [pltpu.VMEM((groups, piece, width), BF)],
        0,
    )


def half_sum(left, second, first, groups, piece, members, parts, ident):
    rows, depth = left.shape
    width = second.shape[0] // 2
    return exchange_call(
        functools.partial(half_sum_kernel, groups, members),
        ident,
        (left.reshape(2, parts, groups // 2, piece, depth), second, first),
        [
            ((groups, piece, width), F32, VMEM),
            ((depth, rows), BF, VMEM),
            ((width, depth), BF, ANY),
            (first.shape[::-1], BF, VMEM),
        ],
        (groups, piece, width),
        product_scratch(parts, groups, piece, width, depth, True, 2 * members)
        + [pltpu.SemaphoreType.DMA],
        0,
        (1,),
        False,
    )


def second_norm(left, weight, turned, done, normal, cotan, rows, members, parts, ident):
    groups, piece, width = normal.shape
    depth = left.shape[-1]
    half = groups // 2
    if parts != 4:
        part = over_cols(left, weight).astype(BF)
        total = lax.psum_scatter(part, "mp", scatter_dimension=0, tiled=True).astype(F32)
        values = normal * rows[0] + rows[1] + total.reshape(normal.shape) + rows[2]
        normal, inverse = normed(values)
        layer = (normal * rows[3] + rows[4]).astype(BF)
        back = jnp.stack(swap_blocks(layer, members, -1))
        cotan = jnp.stack(swap_blocks(cotan, members, 1)).astype(F32)
        grad = norm_back(cotan, normal, inverse, rows[3])
        sums = [jnp.sum(array, axis=(0, 1)) for array in (grad, cotan * normal, cotan)]
        sums = jnp.stack(sums + [jnp.zeros_like(sums[0])] * 5)
        low = lax.all_gather(grad.astype(BF), "mp", axis=0)
        return low, grad, back, sums, over_rows(left, low.reshape(-1, width)).astype(BF)
    block = pltpu.VMEM((groups, piece, width), BF)
    return exchange_call(
        functools.partial(second_norm_kernel, groups, members // groups),
        ident,
        (
            left.reshape(2, parts, half, piece, depth),
            weight, turned, done, normal, cotan, rows,
        ),
        [
            ((2, parts, half, piece, width), BF, ANY),
            ((groups, piece, width), F32, ANY),
            ((groups, piece, width), BF, ANY),
            ((8, width), F32, VMEM),
            ((depth, width), BF, ANY),
        ],
        (groups, piece, width // 2),
        product_scratch(parts, groups, piece, width // 2, depth, True)
        + [
            block,
            block,
            block,
            pltpu.VMEM(turned.shape, BF),
            pltpu.VMEM((depth, width), BF),
            pltpu.VMEM((2, parts, half, piece, depth), BF),
            pltpu.VMEM(done.shape, F32),
            pltpu.VMEM(normal.shape, F32),
            pltpu.VMEM((2, parts, half, piece, width), BF),
            pltpu.VMEM((groups, piece, width), F32),
            pltpu.SemaphoreType.DMA((width // 256,)),
            pltpu.SemaphoreType.DMA((6,)),
            pltpu.SemaphoreType.DMA((2 + groups,)),
        ],
        2 * groups,
        (0, 1, 2, 3, 4, 5),
    )


def first_back(left, weight, grad, normal, inverse, sums, rows, parts, ident):
    groups, piece, width = normal.shape
    depth = left.shape[-1]
    if parts != 4:
        part = over_cols(left, weight[:, :depth]).astype(BF)
        total = lax.psum_scatter(part, "mp", scatter_dimension=0, tiled=True).astype(F32)
        grad = total.reshape(normal.shape) + grad
        moved = norm_back(grad, normal, inverse, rows[0])
        more = [jnp.sum(array, axis=(0, 1)) for array in (moved, grad * normal, grad)]
        sums = sums.at[3:6].add(jnp.stack(more))
        return (
            lax.all_gather(moved.astype(BF), "mp", axis=0),
            moved,
            lax.all_gather(sums, "mp", axis=0),
        )
    half = groups // 2
    return exchange_call(
        functools.partial(first_back_kernel, groups),
        ident,
        (
            left.reshape(2, parts, half, piece, depth), weight,
            grad, normal, inverse, sums, rows,
        ),
        [
            ((2, parts, half, piece, width), BF, ANY),
            ((groups, piece, width), F32, VMEM),
            ((parts, 8, width), F32, VMEM),
        ],
        (groups, piece, width),
        [pltpu.VMEM((groups, piece, width), BF), pltpu.VMEM((8, width), F32)]
        + product_scratch(parts, groups, piece, width, depth, True),
        3,
        (1,),
    )


def input_gradient(left, weight, grad, small, members, parts, ident):
    groups, piece, width = grad.shape
    depth = left.shape[-1]
    if parts != 4:
        part = over_cols(left, weight[:, :depth]).astype(BF)
        total = lax.psum_scatter(part, "mp", scatter_dimension=0, tiled=True).astype(F32)
        ready = (total.reshape(grad.shape) + grad).astype(BF)
        back = jnp.stack(swap_blocks(ready, members, -1))
        back = jnp.roll(back, lax.axis_index("seq") // (members // groups), axis=0)
        return lax.all_gather(back, "mp", axis=1), lax.all_to_all(small, "seq", 0, 0)
    return exchange_call(
        functools.partial(input_kernel, groups, members // groups),
        ident,
        (left.reshape(2, parts, groups // 2, piece, depth), weight, grad, small),
        [((groups, parts, piece, width), BF, ANY), (small.shape, F32, VMEM)],
        (groups, piece, width),
        [pltpu.VMEM((groups, piece, width), BF)] * 2
        + product_scratch(parts, groups, piece, width, depth, True),
        groups + members,
        (1,),
    )


def share_kernel(own_ref, all_ref, send_sem, recv_sem, local_sem):
    me, along_x, along_y, _ = square()
    to_x, to_y = {"mp": along_x}, {"mp": along_y}
    greet([to_x, to_y])
    send = sender(send_sem, recv_sem)
    half = own_ref.shape[0] // 2
    upper, lower = pl.ds(0, half), pl.ds(half, half)
    copies = [
        send(own_ref.at[upper], all_ref.at[0, me], 0, to_x),
        send(own_ref.at[lower], all_ref.at[1, me], 1, to_y),
        send(own_ref.at[lower], all_ref.at[1, me], 2, to_x),
        send(own_ref.at[upper], all_ref.at[0, me], 3, to_y),
    ]
    local = [
        pltpu.make_async_copy(own_ref.at[upper], all_ref.at[0, me], local_sem.at[0]),
        pltpu.make_async_copy(own_ref.at[lower], all_ref.at[1, me], local_sem.at[1]),
    ]
    for copy in local:
        copy.start()
    copies[0].wait_recv()
    copies.append(send(all_ref.at[0, along_x], all_ref.at[0, along_x], 4, to_y))
    copies[1].wait_recv()
    copies.append(send(all_ref.at[1, along_y], all_ref.at[1, along_y], 5, to_x))
    for copy in copies[2:]:
        copy.wait_recv()
    for copy in copies:
        copy.wait_send()
    for copy in local:
        copy.wait()


def share_over_mp(own, parts, ident):
    if parts != 4:
        return lax.all_gather(own, "mp", axis=0)
    return pl.pallas_call(
        share_kernel,
        out_shape=jax.ShapeDtypeStruct((2, parts, own.shape[0] // 2, own.shape[1]), own.dtype),
        in_specs=[ANY],
        out_specs=ANY,
        scratch_shapes=[
            pltpu.SemaphoreType.DMA((6,)),
            pltpu.SemaphoreType.DMA((6,)),
            pltpu.SemaphoreType.DMA((2,)),
        ],
        compiler_params=pltpu.CompilerParams(collective_id=ident, has_side_effects=True),
        cost_estimate=pl.CostEstimate(flops=0, bytes_accessed=100 * MIB, transcendentals=0),
        name=f"share_over_mp_{ident}",
    )(own)


def swap_kernel(
    groups, per, sign, block_ref, small_ref, out_ref, small_out, send_sem, recv_sem, local_sem
):
    members = groups * per
    index = lax.axis_index("seq")
    devices = [{"seq": lax.rem(index + step, members)} for step in range(1, members)]
    greet(devices)
    send = sender(send_sem, recv_sem)
    copies = []
    for step in range(1, groups):
        ahead = step if sign > 0 else groups - step
        source = block_ref.at[step]
        copies.append(send(source, out_ref.at[step], step, devices[ahead * per - 1]))
    for step in range(1, members):
        target = lax.rem(index + step, members)
        copies.append(
            send(small_ref.at[target], small_out.at[index], groups + step, devices[step - 1])
        )
    locals_ = [
        pltpu.make_async_copy(block_ref.at[0], out_ref.at[0], local_sem.at[0]),
        pltpu.make_async_copy(small_ref.at[index], small_out.at[index], local_sem.at[1]),
    ]
    for local in locals_:
        local.start()
    for local in locals_:
        local.wait()
    for copy in copies:
        copy.wait()


def shift_pairs(members, ahead):
    return [(index, (index + ahead) % members) for index in range(members)]


def swap_blocks(blocks, members, sign):
    groups = blocks.shape[0]
    per = members // groups
    arrived = [blocks[0]]
    for step in range(1, groups):
        pairs = shift_pairs(members, sign * step * per)
        arrived.append(lax.ppermute(blocks[step], "seq", pairs))
    return arrived


def swap_groups(blocks, small, members, parts, sign, ident):
    groups = blocks.shape[0]
    per = members // groups
    if parts != 4:
        return jnp.stack(swap_blocks(blocks, members, sign)), lax.all_to_all(small, "seq", 0, 0)
    return pl.pallas_call(
        functools.partial(swap_kernel, groups, per, sign),
        out_shape=(
            jax.ShapeDtypeStruct(blocks.shape, blocks.dtype),
            jax.ShapeDtypeStruct(small.shape, small.dtype),
        ),
        in_specs=[ANY, ANY],
        out_specs=(ANY, ANY),
        scratch_shapes=[
            pltpu.SemaphoreType.DMA((groups + members,)),
            pltpu.SemaphoreType.DMA((groups + members,)),
            pltpu.SemaphoreType.DMA((2,)),
        ],
        compiler_params=pltpu.CompilerParams(collective_id=ident, has_side_effects=True),
        cost_estimate=pl.CostEstimate(flops=0, bytes_accessed=60 * MIB, transcendentals=0),
        name=f"swap_groups_{ident}",
    )(blocks, small)


def score_block(keys, queries):
    return lax.dot_general(keys, queries, (((1,), (1,)), ((), ())), preferred_element_type=F32)


def attend_kernel(
    query_ref, key_ref, value_ref, key_far_ref, value_far_ref, mix_ref, low_ref, log_ref, turned
):
    rows = key_ref.shape[0]

    @pl.when(pl.program_id(1) == 0)
    def _():
        turned[:, :rows] = value_ref[...].T
        turned[:, rows:] = value_far_ref[...].T

    scale = DH ** (-0.5)
    near = score_block(key_ref[...], query_ref[...])
    far = score_block(key_far_ref[...], query_ref[...])
    highest = jnp.maximum(
        jnp.max(near, axis=0, keepdims=True), jnp.max(far, axis=0, keepdims=True)
    )
    near = jnp.exp((near - highest) * scale)
    far = jnp.exp((far - highest) * scale)
    total = jnp.sum(near, axis=0, keepdims=True) + jnp.sum(far, axis=0, keepdims=True)
    mix = jnp.dot(turned[:, :rows], near.astype(BF), preferred_element_type=F32)
    mix += jnp.dot(turned[:, rows:], far.astype(BF), preferred_element_type=F32)
    mix = (mix / total).T
    mix_ref[...] = mix
    low_ref[...] = mix.astype(BF)
    log_ref[0] = highest * scale + jnp.log(total)


def attend(qkv, kv_far, heads):
    rows, cols = qkv.shape[0], heads * DH
    away = kv_far.shape[0]
    block = min(512, rows)

    def tile(offset):
        return pl.BlockSpec((block, DH), lambda h, i: (i, offset + h))

    def long(count, offset):
        return pl.BlockSpec((count, DH), lambda h, i: (0, offset + h))

    return pl.pallas_call(
        attend_kernel,
        grid=(heads, rows // block),
        out_shape=(
            jax.ShapeDtypeStruct((rows, cols), F32),
            jax.ShapeDtypeStruct((rows, cols), BF),
            jax.ShapeDtypeStruct((heads, 1, rows), F32),
        ),
        in_specs=[
            tile(0),
            long(rows, heads),
            long(rows, 2 * heads),
            long(away, 0),
            long(away, heads),
        ],
        out_specs=(tile(0), tile(0), pl.BlockSpec((1, 1, block), lambda h, i: (h, 0, i))),
        scratch_shapes=[pltpu.VMEM((DH, rows + away), BF)],
        compiler_params=pltpu.CompilerParams(vmem_limit_bytes=52 * MIB),
        cost_estimate=pl.CostEstimate(
            flops=8 * rows * (rows + away) * cols,
            bytes_accessed=20 * rows * cols,
            transcendentals=rows * (rows + away) * heads,
        ),
        name="attend",
    )(qkv, qkv, qkv, kv_far, kv_far)


def share_meanwhile(
    now, count, pieces, back_ref, all_ref, send_sem, recv_sem, local_sem, also=()
):
    me, along_x, along_y, _ = square()
    send = sender(send_sem, recv_sem, False)
    near, far, passed, local = [], [], [], []
    for index, piece in enumerate(pieces):
        ways = (along_x, along_y) if index % 2 == 0 else (along_y, along_x)
        block, own = back_ref.at[piece], all_ref.at[index, me]
        relayed = all_ref.at[index, ways[0]]
        near.append(send(block, own, 3 * index, {"mp": ways[0]}))
        far.append(send(block, own, 3 * index + 1, {"mp": ways[1]}))
        passed.append(send(relayed, relayed, 3 * index + 2, {"mp": ways[1]}))
        local.append(pltpu.make_async_copy(block, own, local_sem.at[index]))

    @pl.when(now == 0)
    def _():
        greet([{"mp": along_x}, {"mp": along_y}, *also])
        for copy in near + far + local:
            copy.start()

    @pl.when(now == count // 4)
    def _():
        for first, second in zip(near, passed):
            first.wait_recv()
            second.start()

    def finish():
        @pl.when(now == count - 1)
        def _():
            for copy in far + passed:
                copy.wait_recv()
            for copy in near + far + passed:
                copy.wait_send()
            for copy in local:
                copy.wait()

    return finish


def meanwhile_scratch(pieces):
    return [
        pltpu.SemaphoreType.DMA((3 * len(pieces),)),
        pltpu.SemaphoreType.DMA((3 * len(pieces),)),
        pltpu.SemaphoreType.DMA((len(pieces),)),
    ]


def feed_back_kernel(
    pieces, members, low_ref, weight_ref, more_ref, pre_ref, turned_ref, back_ref,
    grad_ref, sums_ref, weight_grad_ref, all_ref, send_sem, recv_sem, local_sem,
):
    now, count = pl.program_id(0), pl.num_programs(0)
    finish = share_meanwhile(now, count, pieces, back_ref, all_ref, send_sem, recv_sem, local_sem)
    value = pre_ref[...]
    root = (2 / math.pi) ** 0.5
    square_of = value * value
    bent = jnp.tanh(root * value * (1 + 0.044715 * square_of))
    slope = 0.5 * (1 + bent) + (0.5 * root) * value * (1 - bent * bent) * (
        1 + 3 * 0.044715 * square_of
    )
    narrow = weight_ref.shape[0] // members
    weight = jnp.concatenate(
        [
            half[place * narrow : (place + 1) * narrow]
            for place in range(members)
            for half in (weight_ref, more_ref)
        ],
        axis=0,
    )
    grad = (matmul(low_ref[...], weight) * slope).astype(BF)
    grad_ref[...] = grad
    sums_ref[...] = jnp.sum(grad.astype(F32), axis=0, keepdims=True)
    weight_grad_ref[...] = matmul(turned_ref[...], grad).astype(BF)
    finish()


def feed_back(low, weight, more, inner_pre, turned, layer_back, pieces, members, parts, ident):
    rows, hidden = inner_pre.shape
    width = low.shape[1]
    step = 512
    _, piece, _ = layer_back.shape
    return pl.pallas_call(
        functools.partial(feed_back_kernel, pieces, members),
        grid=(hidden // step,),
        out_shape=(
            jax.ShapeDtypeStruct((rows, hidden), BF),
            jax.ShapeDtypeStruct((1, hidden), F32),
            jax.ShapeDtypeStruct((width, hidden), BF),
            jax.ShapeDtypeStruct((len(pieces), parts, piece, width), BF),
        ),
        in_specs=[
            pl.BlockSpec((rows, width), lambda i: (0, 0)),
            pl.BlockSpec((width // 2, step), lambda i: (0, i)),
            pl.BlockSpec((width // 2, step), lambda i: (0, i)),
            pl.BlockSpec((rows, step), lambda i: (0, i)),
            pl.BlockSpec((width, rows), lambda i: (0, 0)),
            ANY,
        ],
        out_specs=(
            pl.BlockSpec((rows, step), lambda i: (0, i)),
            pl.BlockSpec((1, step), lambda i: (0, i)),
            pl.BlockSpec((width, step), lambda i: (0, i)),
            ANY,
        ),
        scratch_shapes=meanwhile_scratch(pieces),
        compiler_params=pltpu.CompilerParams(
            collective_id=ident, has_side_effects=True, vmem_limit_bytes=58 * MIB
        ),
        cost_estimate=pl.CostEstimate(
            flops=4 * rows * width * hidden, bytes_accessed=40 * MIB, transcendentals=rows * hidden
        ),
        name="feed_back",
    )(low, weight, more, inner_pre, turned, layer_back)


def sibling():
    here = lax.axis_index("seq")
    return {"seq": here + 1 - 2 * lax.rem(here, 2)}


def attend_back_kernel(
    pieces,
    step,
    query_ref,
    key_ref,
    value_ref,
    key_far_ref,
    value_far_ref,
    grad_ref,
    mix_ref,
    log_ref,
    *rest,
):
    sharing = len(pieces) > 0
    if sharing:
        back_ref, *rest = rest
    dquery_ref, dkey_ref, dvalue_ref, *rest = rest
    if sharing:
        in_ref, all_ref, *rest = rest
    else:
        dkey_far_ref, dvalue_far_ref, *rest = rest
    turned, key_sum, value_sum, *rest = rest
    block = pl.program_id(1)
    rows = key_ref.shape[0]
    if sharing:
        away, pair_send, pair_recv, send_sem, recv_sem, local_sem = rest
        now = pl.program_id(0) * pl.num_programs(1) + block
        count = pl.num_programs(0) * pl.num_programs(1)
        finish = share_meanwhile(
            now, count, pieces, back_ref, all_ref, send_sem, recv_sem, local_sem, [sibling()]
        )

        def cross(kind, head):
            return pltpu.make_async_remote_copy(
                src_ref=away.at[kind, head],
                dst_ref=in_ref.at[kind, head],
                send_sem=pair_send.at[kind, head],
                recv_sem=pair_recv.at[kind, head],
                device_id=sibling(),
                device_id_type=MESH,
            )

    @pl.when(block == 0)
    def _():
        turned[:, :rows] = key_ref[...].T
        turned[:, rows:] = key_far_ref[...].T
        key_sum[...] = jnp.zeros_like(key_sum)
        value_sum[...] = jnp.zeros_like(value_sum)

    scale = DH ** (-0.5)
    query, grad = query_ref[...], grad_ref[...]
    terms = jnp.sum((grad.astype(F32) * mix_ref[...]).T, axis=0, keepdims=True)
    logs = log_ref[0]
    dquery = jnp.zeros((DH, query.shape[0]), F32)
    spans = [(key_ref, value_ref, start, start) for start in range(0, rows, step)]
    spans += [
        (key_far_ref, value_far_ref, start, rows + start)
        for start in range(0, key_far_ref.shape[0], step)
    ]
    for keys, values, start, place in spans:
        part = pl.ds(place, step)
        probs = jnp.exp(score_block(keys[pl.ds(start, step)], query) * scale - logs)
        prob_grad = score_block(values[pl.ds(start, step)], grad)
        score_grad = (probs * (prob_grad - terms) * scale).astype(BF)
        value_sum[part] += jnp.dot(probs.astype(BF), grad, preferred_element_type=F32)
        key_sum[part] += jnp.dot(score_grad, query, preferred_element_type=F32)
        dquery += jnp.dot(turned[:, part], score_grad, preferred_element_type=F32)
    dquery_ref[...] = dquery.T.astype(BF)

    @pl.when(block == pl.num_programs(1) - 1)
    def _():
        dkey_ref[...] = key_sum[:rows]
        dvalue_ref[...] = value_sum[:rows]
        if sharing:
            head = pl.program_id(0)
            for kind, total in enumerate((key_sum, value_sum)):
                away[kind, head] = total[rows:].astype(BF)
                cross(kind, head).start()
        else:
            dkey_far_ref[...] = key_sum[rows:].astype(BF)
            dvalue_far_ref[...] = value_sum[rows:].astype(BF)

    if sharing:

        @pl.when(now == count - 1)
        def _():
            for kind in range(2):
                for head in range(away.shape[1]):
                    cross(kind, head).wait()

        finish()


def attend_back(qkv, kv_far, grad, mix, logs, heads, layer_back, pieces, parts, ident):
    rows, cols = qkv.shape[0], heads * DH
    away = kv_far.shape[0]
    block, step = min(512, rows), min(512, rows)
    sharing = len(pieces) > 0
    _, piece, width = layer_back.shape

    def tile(offset):
        return pl.BlockSpec((block, DH), lambda h, i: (i, offset + h))

    def long(count, offset):
        return pl.BlockSpec((count, DH), lambda h, i: (0, offset + h))

    return pl.pallas_call(
        functools.partial(attend_back_kernel, pieces, step),
        grid=(heads, rows // block),
        out_shape=(
            jax.ShapeDtypeStruct((rows, cols), BF),
            jax.ShapeDtypeStruct((rows, cols), F32),
            jax.ShapeDtypeStruct((rows, cols), F32),
        )
        + (
            (
                jax.ShapeDtypeStruct((2, heads, rows, DH), BF),
                jax.ShapeDtypeStruct((len(pieces), parts, piece, width), BF),
            )
            if sharing
            else (jax.ShapeDtypeStruct((away, cols), BF),) * 2
        ),
        in_specs=[
            tile(0),
            long(rows, heads),
            long(rows, 2 * heads),
            long(away, 0),
            long(away, heads),
            tile(0),
            tile(0),
            pl.BlockSpec((1, 1, block), lambda h, i: (h, 0, i)),
        ]
        + ([ANY] if sharing else []),
        out_specs=(tile(0), long(rows, 0), long(rows, 0))
        + ((ANY, ANY) if sharing else (long(away, 0), long(away, 0))),
        scratch_shapes=[
            pltpu.VMEM((DH, rows + away), BF),
            pltpu.VMEM((rows + away, DH), F32),
            pltpu.VMEM((rows + away, DH), F32),
        ]
        + (
            [
                pltpu.VMEM((2, heads, rows, DH), BF),
                pltpu.SemaphoreType.DMA((2, heads)),
                pltpu.SemaphoreType.DMA((2, heads)),
            ]
            + meanwhile_scratch(pieces)
            if sharing
            else []
        ),
        compiler_params=pltpu.CompilerParams(
            vmem_limit_bytes=52 * MIB,
            **(dict(collective_id=ident, has_side_effects=True) if sharing else {}),
        ),
        cost_estimate=pl.CostEstimate(
            flops=20 * rows * (rows + away) * cols,
            bytes_accessed=30 * rows * cols,
            transcendentals=rows * (rows + away) * heads,
        ),
        name="attend_back",
    )(qkv, qkv, qkv, kv_far, kv_far, grad, mix, logs, *([layer_back] if sharing else []))


def from_group_members(block, members, per):
    blocks = []
    for step in range(1, per):
        pairs = [
            (base + place, base + (place - step) % per)
            for base in range(0, members, per)
            for place in range(per)
        ]
        blocks.append(lax.ppermute(block, "seq", pairs))
    return blocks


def to_group_members(total, blocks, members, per):
    for step in range(1, per):
        pairs = [
            (base + place, base + (place + step) % per)
            for base in range(0, members, per)
            for place in range(per)
        ]
        total = total + lax.ppermute(blocks[step - 1], "seq", pairs).astype(F32)
    return total


def last_kernel(
    per, turned_hbm, query_ref, key_ref, value_ref, in_ref, proj_hbm, layer_hbm, layer_more_hbm,
    grad_ref, sums_ref, part_ref, layer_ref, turned_ref, made, proj, layer, load_sem, put_sem,
):
    rows, cols = query_ref.shape
    count = load_sem.shape[0] - 3
    step = turned_ref.shape[0] // count
    loads = []
    for place in range(count):
        block = pl.ds(place * step, step)
        loads.append(
            pltpu.make_async_copy(turned_hbm.at[block], turned_ref.at[block], load_sem.at[place])
        )
    loads.append(pltpu.make_async_copy(proj_hbm, proj, load_sem.at[count]))
    groups = layer.shape[0]
    for place, source in enumerate((layer_hbm, layer_more_hbm)):
        block = pl.ds(place * (groups // 2), groups // 2)
        loads.append(pltpu.make_async_copy(source, layer.at[block], load_sem.at[count + 1 + place]))
    for copy in loads:
        copy.start()
    puts = []

    def put(source, target):
        copy = pltpu.make_async_copy(source, target, put_sem.at[len(puts)])
        copy.start()
        puts.append(copy)

    for index, (own, far) in enumerate(
        ((query_ref, None), (key_ref, 0), (value_ref, 1))
    ):
        span = pl.ds(index * cols, cols)
        grad = own[...]
        if far is not None:
            far = [in_ref[far, head] for head in range(cols // DH)]
            grad = (grad + jnp.concatenate(far, axis=1).astype(F32)).astype(BF)
        grad_ref[:, span] = grad
        sums_ref[:, span] = jnp.sum(grad.astype(F32), axis=0, keepdims=True)
        for place in range(count):
            block = pl.ds(place * step, step)
            if index == 0:
                loads[place].wait()
            made[index, block] = matmul(turned_ref[block], grad_ref[:, span]).astype(BF)
        put(made.at[index], part_ref.at[:, span])
        if index == 1:
            loads[count].wait()
            put(proj, part_ref.at[:, pl.ds(3 * cols, cols)])
            for copy in loads[count + 1 :]:
                copy.wait()
            group = lax.axis_index("seq") // per
            for piece in range(groups):
                put(layer.at[piece], layer_ref.at[lax.rem(group + piece, groups)])
    for copy in puts:
        copy.wait()


def last_gradients(turned, query, key, value, arrived, proj_part, layer, layer_more, per):
    rows, cols = query.shape
    width = turned.shape[0]
    return pl.pallas_call(
        functools.partial(last_kernel, per),
        out_shape=(
            jax.ShapeDtypeStruct((rows, 3 * cols), BF),
            jax.ShapeDtypeStruct((1, 3 * cols), F32),
            jax.ShapeDtypeStruct((width, 4 * cols), BF),
            jax.ShapeDtypeStruct((2 * layer.shape[0],) + layer.shape[1:], layer.dtype),
        ),
        in_specs=[ANY] + [VMEM] * 4 + [ANY] * 3,
        out_specs=(VMEM, VMEM, ANY, ANY),
        scratch_shapes=[
            pltpu.VMEM(turned.shape, BF),
            pltpu.VMEM((3, width, cols), BF),
            pltpu.VMEM(proj_part.shape, BF),
            pltpu.VMEM((2 * layer.shape[0],) + layer.shape[1:], BF),
            pltpu.SemaphoreType.DMA((7,)),
            pltpu.SemaphoreType.DMA((4 + 2 * layer.shape[0],)),
        ],
        compiler_params=pltpu.CompilerParams(vmem_limit_bytes=52 * MIB),
        cost_estimate=pl.CostEstimate(
            flops=6 * rows * width * cols, bytes_accessed=32 * MIB, transcendentals=0
        ),
        name="last_gradients",
    )(turned, query, key, value, arrived, proj_part, layer, layer_more)


def packed(vectors, lines):
    flat = jnp.concatenate(vectors)
    return jnp.pad(flat, (0, lines * 128 - flat.shape[0])).reshape(lines, 128)


def after(value, *others):
    return lax.optimization_barrier((value,) + others)[0]


def on_device(members, parts, *arrays):
    (
        tokens,
        query_weight,
        query_bias,
        key_weight,
        value_weight,
        value_bias,
        proj_weight,
        proj_bias,
        gain_first,
        shift_first,
        inner_weight,
        inner_bias,
        outer_weight,
        outer_bias,
        gain_second,
        shift_second,
        cotangent,
    ) = arrays
    micro, seqs, length, width = tokens.shape
    groups = micro * seqs
    per = members // groups
    assert per * groups == members and (parts != 4 or per == 2)
    piece = length // parts
    rows = groups * length
    quarter = groups * piece
    mine = lax.axis_index("mp")
    group = lax.axis_index("seq") // per

    depth, cols = query_weight.shape
    heads = cols // DH
    first = jnp.concatenate([query_weight, key_weight, value_weight, proj_weight.T], axis=1)
    first = lax.all_gather(first, "seq", axis=0, tiled=True)
    hidden = inner_weight.shape[1]
    fused = parts == 4 and per == 2
    outer_turned = outer_weight.T
    if fused:
        part = depth // 2
        folded = jnp.concatenate(
            [outer_turned[:part, : hidden // 2], outer_turned[:part, hidden // 2 :]], axis=0
        )
        second = jnp.concatenate([inner_weight, folded], axis=1)
        second = lax.all_gather(second, "seq", axis=0, tiled=True)
        w_inner = second[:, :hidden]
        w_outer = lax.all_gather(outer_turned[part:], "seq", axis=0, tiled=True)
    else:
        w_inner = second = lax.all_gather(inner_weight, "seq", axis=0, tiled=True)
        w_outer = lax.all_gather(outer_turned, "seq", axis=0, tiled=True)
    w_qkv = first[:, : 3 * cols]
    w_proj = first[:, 3 * cols :]
    vectors = [
        query_bias,
        value_bias,
        inner_bias,
        proj_bias,
        gain_first,
        shift_first,
        outer_bias,
        gain_second,
        shift_second,
    ]
    sizes = [vector.shape[0] for vector in vectors]
    lines = -(-sum(sizes) // 2048) * 16
    own_vectors = packed(vectors, lines)

    def to_blocks(array):
        array = array.reshape(groups, length, width)
        return [
            lax.dynamic_slice(
                array, (lax.rem(group + k, groups), mine * piece, 0), (1, piece, width)
            )[0]
            for k in range(groups)
        ]

    x_part, all_vectors = swap_groups(
        jnp.stack(to_blocks(tokens)),
        jnp.broadcast_to(own_vectors[None], (members, lines, 128)),
        members,
        parts,
        1,
        1,
    )
    x_part = x_part.reshape(quarter, width)
    x_rows = share_over_mp(x_part, parts, 8).reshape(rows, width)
    all_vectors = all_vectors.reshape(members, -1).astype(F32)
    full = []
    start = 0
    for size in sizes:
        full.append(all_vectors[:, start : start + size].reshape(-1))
        start += size
    b_query, b_value, b_inner, b_proj, gain_one, shift_one, b_outer, gain_two, shift_two = full

    bias = jnp.concatenate([b_query, jnp.zeros_like(b_query), b_value])
    qkv = (matmul(x_rows, w_qkv) + bias).astype(BF)
    kv_far = from_group_members(qkv[:, cols:], members, per)
    kv_far = kv_far[0] if per == 2 else jnp.concatenate(kv_far, axis=0)
    mixture, mixture_low, logs = attend(qkv, kv_far, heads)

    def blocked(array):
        return array.reshape(groups, piece, width)

    first_low, normal_one, inverse_one, x_turned = first_norm(
        over_cols(mixture_low, w_proj).astype(BF),
        blocked(x_part),
        x_rows,
        jnp.stack([b_proj, gain_one, shift_one]),
        parts,
        2,
    )
    first_low = first_low.reshape(rows, width)

    inner_pre = matmul(first_low, w_inner) + b_inner
    active = gelu_tanh(inner_pre).astype(BF)
    done, active_turned, w_outer_half = None, None, None
    if fused:
        done, active_turned, w_outer_half, first_turned = half_sum(
            active, second, first_low, groups, piece, members, parts, 13
        )
    else:
        first_turned = first_low.T
    second_low, second_grad, layer_back, sums, outer_w_part = second_norm(
        active,
        w_outer,
        active_turned,
        done,
        normal_one,
        jnp.stack(to_blocks(cotangent)),
        jnp.stack([gain_one, shift_one, b_outer, gain_two, shift_two]),
        members,
        parts,
        3,
    )
    second_low = second_low.reshape(rows, width)

    outer_w_grad = lax.psum_scatter(outer_w_part, "seq", scatter_dimension=1, tiled=True)
    pieces = list(range(groups)) if fused else []
    early, late = pieces[: groups // 2], pieces[groups // 2 :]
    if fused:
        inner_grad, inner_b_grad, inner_w_part, layer_out = feed_back(
            second_low,
            w_outer_half,
            w_outer,
            inner_pre,
            first_turned,
            layer_back,
            early,
            members,
            parts,
            7,
        )
    else:
        _, pull_gelu = jax.vjp(gelu_tanh, inner_pre)
        inner_grad = pull_gelu(matmul(second_low, w_outer))[0].astype(BF)
        inner_b_grad = jnp.sum(inner_grad.astype(F32), axis=0)
        inner_w_part = matmul(first_turned, inner_grad).astype(BF)
        layer_out = lax.all_gather(jnp.roll(layer_back, group, axis=0), "mp", axis=1)
    inner_w_grad = lax.psum_scatter(inner_w_part, "seq", scatter_dimension=0, tiled=True)
    attn_low, attn_grad, summed_rows = first_back(
        inner_grad,
        second,
        second_grad,
        normal_one,
        inverse_one,
        after(sums, inner_w_part),
        gain_one[None],
        parts,
        4,
    )
    attn_low = after(attn_low.reshape(rows, width), outer_w_grad)
    summed_rows = jnp.sum(summed_rows, axis=0)

    proj_w_part = over_rows(attn_low, mixture_low).astype(BF)
    mixture_grad = matmul(after(attn_low, proj_w_part), w_proj).astype(BF)
    query_grad, key_grad, value_grad, *others = attend_back(
        qkv, kv_far, mixture_grad, mixture, logs, heads, layer_back, late, parts, 5
    )

    def blocks_of(array):
        return [array[i * rows : (i + 1) * rows] for i in range(per - 1)]

    if fused:
        qkv_grad, bias_grad, last_w_part, layer_out = last_gradients(
            x_turned,
            query_grad,
            key_grad,
            value_grad,
            others[0],
            proj_w_part,
            layer_out,
            others[1],
            per,
        )
        bias_grad = bias_grad[0]
    else:
        key_grad = to_group_members(key_grad, blocks_of(others[0]), members, per)
        value_grad = to_group_members(value_grad, blocks_of(others[1]), members, per)
        qkv_grad = jnp.concatenate([query_grad, key_grad.astype(BF), value_grad.astype(BF)], axis=1)
        last_w_part = jnp.concatenate([matmul(x_turned, qkv_grad).astype(BF), proj_w_part], axis=1)
        bias_grad = jnp.sum(qkv_grad.astype(F32), axis=0)
    last_w_grad = lax.psum_scatter(last_w_part, "seq", scatter_dimension=0, tiled=True).astype(F32)
    small = jnp.concatenate(
        [
            bias_grad[:cols].reshape(members, -1),
            bias_grad[2 * cols :].reshape(members, -1),
            inner_b_grad.reshape(members, -1),
        ]
        + [summed_rows[i].reshape(members, -1) for i in (3, 4, 5, 0, 1, 2)],
        axis=1,
    )
    small = jnp.pad(small, ((0, 0), (0, lines * 128 - small.shape[1])))
    input_grad, small = input_gradient(
        qkv_grad,
        first,
        attn_grad,
        small.reshape(members, lines, 128),
        members,
        parts,
        6,
    )
    input_grad = after(input_grad, inner_w_grad).astype(F32).reshape(micro, seqs, length, width)
    layer_out = layer_out.reshape(micro, seqs, length, width)
    small = jnp.sum(small, axis=0).reshape(-1)
    pieces = []
    start = 0
    for size in sizes:
        pieces.append(small[start : start + size])
        start += size
    return (
        layer_out,
        input_grad,
        last_w_grad[:, :cols],
        pieces[0],
        last_w_grad[:, cols : 2 * cols],
        last_w_grad[:, 2 * cols : 3 * cols],
        pieces[1],
        last_w_grad[:, 3 * cols :].T,
        pieces[3],
        pieces[4],
        pieces[5],
        inner_w_grad.astype(F32),
        pieces[2],
        outer_w_grad.astype(F32),
        pieces[6],
        pieces[7],
        pieces[8],
    )


def solution(mesh):
    tokens = P(None, None, "seq", None)
    rows_cols, cols_rows, both, seq = P("seq", "mp"), P("mp", "seq"), P(("mp", "seq")), P("seq")
    weights = (
        rows_cols,
        both,
        rows_cols,
        rows_cols,
        both,
        cols_rows,
        seq,
        seq,
        seq,
        rows_cols,
        both,
        cols_rows,
        seq,
        seq,
        seq,
    )
    return jax.shard_map(
        functools.partial(on_device, mesh.shape["seq"], mesh.shape["mp"]),
        mesh=mesh,
        in_specs=(tokens,) + weights + (tokens,),
        out_specs=(tokens, tokens) + weights,
        check_vma=False,
    )
```

```python
import functools
import math

import jax
import jax.numpy as jnp
from jax import lax
from jax.experimental import pallas as pl
from jax.experimental.pallas import tpu as pltpu
from jax.sharding import PartitionSpec as P

DH = 128
EPSILON = 1e-06
BF = jnp.bfloat16
F32 = jnp.float32
MESH = pl.DeviceIdType.MESH
ANY = pl.BlockSpec(memory_space=pl.ANY)
VMEM = pl.BlockSpec(memory_space=pltpu.VMEM)
MIB = 1 << 20


def matmul(left, right):
    return jnp.dot(left, right, preferred_element_type=F32)


def over_rows(left, right):
    return lax.dot_general(left, right, (((0,), (0,)), ((), ())), preferred_element_type=F32)


def over_cols(left, right):
    return lax.dot_general(left, right, (((1,), (1,)), ((), ())), preferred_element_type=F32)


def gelu_tanh(values):
    return jax.nn.gelu(values, approximate=True)


def square():
    me = lax.axis_index("mp")
    return me, me + 1 - 2 * lax.rem(me, 2), lax.rem(me + 2, 4), 3 - me


def greet(devices):
    barrier = pltpu.get_barrier_semaphore()
    for device in devices:
        pl.semaphore_signal(barrier, inc=1, device_id=device, device_id_type=MESH)
    pl.semaphore_wait(barrier, len(devices))


def sender(send_sem, recv_sem, start=True):
    def send(source, target, slot, device):
        copy = pltpu.make_async_remote_copy(
            src_ref=source,
            dst_ref=target,
            send_sem=send_sem.at[slot],
            recv_sem=recv_sem.at[slot],
            device_id=device,
            device_id_type=MESH,
        )
        if start:
            copy.start()
        return copy

    return send


class Exchange:
    def __init__(self, part_ref, landed, relay, send_sem, recv_sem):
        self.me, self.along_x, self.along_y, self.across = square()
        self.parts, self.landed, self.relay = part_ref, landed, relay
        self.send = sender(send_sem, recv_sem)
        self.copies = {}

    def part(self, owner, piece):
        return self.parts.at[row_place(owner, piece, 2 * self.parts.shape[2])]

    def ways(self, index):
        pair = (self.along_x, self.along_y)
        return pair if index % 2 == 0 else pair[::-1]

    def start(self, index, piece):
        near, _ = self.ways(index)
        for kind, owner in enumerate((self.across, near)):
            self.copies[index, kind] = self.send(
                self.part(owner, piece), self.landed.at[index, kind], 6 * index + kind, {"mp": near}
            )

    def pass_on(self, index, piece):
        _, far = self.ways(index)
        self.copies[index, 0].wait_recv()
        self.relay[index] = (
            self.part(far, piece)[...].astype(F32) + self.landed[index, 0].astype(F32)
        ).astype(BF)
        self.copies[index, 2] = self.send(
            self.relay.at[index], self.landed.at[index, 2], 6 * index + 2, {"mp": far}
        )

    def total(self, index, piece):
        self.copies[index, 1].wait_recv()
        self.copies[index, 2].wait_recv()
        return (
            self.part(self.me, piece)[...].astype(F32)
            + self.landed[index, 1].astype(F32)
            + self.landed[index, 2].astype(F32)
        )

    def share(self, index, source, target):
        near, far = self.ways(index)
        self.copies[index, 3] = self.send(source, target(self.me), 6 * index + 3, {"mp": near})
        self.copies[index, 4] = self.send(source, target(self.me), 6 * index + 4, {"mp": far})

    def forward(self, index, target):
        near, far = self.ways(index)
        self.copies[index, 3].wait_recv()
        self.copies[index, 5] = self.send(target(near), target(near), 6 * index + 5, {"mp": far})

    def arrived(self, indices):
        for index in indices:
            self.copies[index, 4].wait_recv()
            self.copies[index, 5].wait_recv()

    def sent(self):
        for copy in self.copies.values():
            copy.wait_send()

    def finish(self, count):
        self.arrived(range(count))
        self.sent()


def row_place(owner, piece, groups):
    half = groups // 2
    return piece // half, owner, piece % half


def planes(groups, per):
    index = lax.axis_index("seq")
    return [{"seq": lax.rem(index + step * per, groups * per)} for step in range(groups)]


def mean_of(values):
    return jnp.mean(values, axis=-1, keepdims=True)


def normed(values):
    centre = values - mean_of(values)
    inverse = lax.rsqrt(mean_of(centre * centre) + EPSILON)
    return centre * inverse, inverse


def norm_back(grad, normal, inverse, gain):
    inner = grad * gain
    return inverse * (inner - mean_of(inner) - normal * mean_of(inner * normal))


def turner(rows_of, turned_ref):
    width, rows = turned_ref.shape
    step = 256

    def fill(part):
        @pl.loop(0, width // (2 * step))
        def _(index):
            span = pl.ds(pl.multiple_of(part * (width // 2) + index * step, step), step)
            turned_ref[span] = rows_of(span).reshape(rows, step).T

    return fill


class Product:
    def __init__(self, exchange, turned, left_ref, weight_ref, weight, rows, load_sem, blocks=None):
        self.exchange, self.turned = exchange, turned
        self.left, self.weight, self.rows = left_ref, weight, rows
        self.left_loads = {}
        width = exchange.parts.shape[-1]
        self.step = min(512, width)
        self.count = width // self.step
        depth = left_ref.shape[-1]
        self.loads, slot = [], 0
        for index in range(self.count):
            span = pl.ds(index * self.step, self.step)
            place = (span, pl.ds(0, depth)) if turned else (pl.ds(0, depth), span)
            pairs = [(weight_ref.at[place], weight.at[place])] if blocks is None else blocks(index)
            copies = []
            for source, target in pairs:
                copy = pltpu.make_async_copy(source, target, load_sem.at[slot])
                copy.start()
                copies.append(copy)
                slot += 1
            self.loads.append(copies)

    def make(self, batch, first=False):
        _, _, half, piece_rows, _ = self.left.shape
        for _, piece in batch:
            if piece // half in self.left_loads:
                self.left_loads.pop(piece // half).wait()
        for place, (owner, piece) in enumerate(batch):
            self.rows[place * piece_rows : (place + 1) * piece_rows] = self.left[
                row_place(owner, piece, 2 * half)
            ]

        def columns(index):
            span = pl.ds(pl.multiple_of(index * self.step, self.step), self.step)
            if self.turned:
                product = over_cols(self.rows[...], self.weight[span])
            else:
                product = matmul(self.rows[...], self.weight[:, span])
            product = product.astype(BF)
            for place, (owner, piece) in enumerate(batch):
                self.exchange.part(owner, piece)[:, span] = product[
                    place * piece_rows : (place + 1) * piece_rows
                ]

        if first:
            for index in range(self.count):
                for copy in self.loads[index]:
                    copy.wait()
                columns(index)
        else:
            pl.loop(0, self.count)(columns)


def run_pieces(exchange, order, work, product=None, fill=None):
    groups = len(order)
    places = list(enumerate(order))
    half = groups // 2
    first, second = places[:half], places[half:]

    def make(half_places, near):
        if product is None:
            return
        batch = []
        for index, piece in half_places:
            ways = exchange.ways(index)
            owners = (exchange.across, ways[0]) if near else (ways[1], exchange.me)
            batch += [(owner, piece) for owner in owners]
        product.make(batch, near and half_places is first)

    make(first, True)
    for index, piece in first:
        exchange.start(index, piece)
    make(first, False)
    if fill is not None:
        fill(0)
    for index, piece in first:
        exchange.pass_on(index, piece)
    make(second, True)
    for index, piece in second:
        exchange.start(index, piece)
    make(second, False)
    if fill is not None:
        fill(1)
    for index, piece in first:
        work(index, piece, exchange.total(index, piece))
    for index, piece in second:
        exchange.pass_on(index, piece)
    return first, second


def first_norm_kernel(
    groups, part_ref, x_ref, all_ref, rows_ref, low_ref, normal_ref, inverse_ref, turned_ref,
    landed, relay, ready, send_sem, recv_sem, local_sem,
):
    exchange = Exchange(part_ref, landed, relay, send_sem, recv_sem)
    greet([{"mp": exchange.along_x}, {"mp": exchange.along_y}])
    local = []

    def target(piece):
        return lambda device: low_ref.at[row_place(device, piece, groups)]

    def work(index, piece, total):
        values = x_ref[piece].astype(F32) + total + rows_ref[0:1]
        normal, inverse = normed(values)
        normal_ref[piece] = normal
        inverse_ref[piece] = inverse
        ready[index] = (normal * rows_ref[1:2] + rows_ref[2:3]).astype(BF)
        exchange.share(index, ready.at[index], target(piece))
        copy = pltpu.make_async_copy(
            ready.at[index], target(piece)(exchange.me), local_sem.at[index]
        )
        copy.start()
        local.append(copy)

    first, second = run_pieces(
        exchange, range(groups), work, None, turner(lambda span: all_ref[:, span], turned_ref)
    )
    for index, piece in first:
        exchange.forward(index, target(piece))
    for index, piece in second:
        work(index, piece, exchange.total(index, piece))
    for index, piece in second:
        exchange.forward(index, target(piece))
    exchange.finish(groups)
    for copy in local:
        copy.wait()


def half_sum_kernel(
    groups, members, left_ref, weight_ref, first_ref, total_ref, turned_ref, weight_out, first_turned_ref,
    landed, relay, part_ref, weight, rows, load_sem, put_sem, send_sem, recv_sem,
):
    exchange = Exchange(part_ref, landed, relay, send_sem, recv_sem)
    width, depth = weight.shape
    narrow, half = width // members, depth // 2
    apart = weight_ref.shape[1] - half

    def blocks(index):
        step = min(512, width)
        for place in range(index * step // narrow, (index + 1) * step // narrow):
            for part in range(2):
                yield (
                    weight_ref.at[pl.ds((2 * place + part) * narrow, narrow), pl.ds(apart, half)],
                    weight.at[pl.ds(place * narrow, narrow), pl.ds(part * half, half)],
                )

    product = Product(exchange, True, left_ref, weight_ref, weight, rows, load_sem, blocks)
    greet([{"mp": exchange.along_x}, {"mp": exchange.along_y}])

    def work(index, piece, total):
        total_ref[piece] = total

    turn_left = turner(lambda span: left_ref[:, :, :, :, span], turned_ref)
    turn_first = turner(lambda span: first_ref[:, span], first_turned_ref)

    def fill(part):
        turn_left(part)
        turn_first(part)

    _, second = run_pieces(exchange, range(groups), work, product, fill)
    put = pltpu.make_async_copy(weight, weight_out, put_sem)
    put.start()
    for index, piece in second:
        work(index, piece, exchange.total(index, piece))
    put.wait()
    exchange.sent()


def second_norm_kernel(
    groups, per, left_hbm, weight_ref, turned_hbm, done_hbm,
    normal_hbm, cotan_ref, rows_ref,
    low_hbm, grad_hbm, back_ref, sums_ref, weight_grad_ref,
    landed, relay, part_ref, weight, rows, load_sem,
    ready, layer, cotan_in, turned_ref, whole, left_ref, done_ref, normal_ref, low_ref, grad_ref,
    put_sem, in_sem, out_sem,
    send_sem, recv_sem, local_sem,
):
    exchange = Exchange(part_ref, landed, relay, send_sem, recv_sem)

    def moved(source, target, sem):
        copy = pltpu.make_async_copy(source, target, sem)
        copy.start()
        return copy

    left_loads = {0: moved(left_hbm.at[0], left_ref.at[0], in_sem.at[0])}
    product = Product(exchange, True, left_ref, weight_ref, weight, rows, load_sem)
    members = groups * per
    narrow = weight.shape[0] // members
    left_loads[1] = moved(left_hbm.at[1], left_ref.at[1], in_sem.at[1])
    product.left_loads = left_loads
    early = [
        moved(cotan_ref.at[0], cotan_in.at[0], in_sem.at[2]),
        moved(normal_hbm, normal_ref, in_sem.at[3]),
        moved(done_hbm, done_ref, in_sem.at[4]),
    ]
    load_turned = moved(turned_hbm, turned_ref, in_sem.at[5])
    outward = []
    peers = planes(groups, per)
    greet([{"mp": exchange.along_x}, {"mp": exchange.along_y}] + peers[1:])
    base = 6 * groups
    arriving = {
        step: exchange.send(cotan_ref.at[step], cotan_in.at[step], base + step, peers[step])
        for step in range(1, groups)
    }
    leaving, local = [], []
    sums_ref[...] = jnp.zeros_like(sums_ref)

    def target(piece):
        return lambda device: low_ref.at[row_place(device, piece, groups)]

    def keep(source, place, slot):
        copy = pltpu.make_async_copy(source, place, local_sem.at[slot])
        copy.start()
        local.append(copy)

    def work(index, piece, total):
        while early:
            early.pop().wait()
        gain_one, shift_one, bias = rows_ref[0:1], rows_ref[1:2], rows_ref[2:3]
        gain, shift = rows_ref[3:4], rows_ref[4:5]
        done = done_ref[piece]
        total = jnp.concatenate(
            [
                half[:, place * narrow : (place + 1) * narrow]
                for place in range(members)
                for half in (done, total)
            ],
            axis=1,
        )
        values = normal_ref[piece] * gain_one + shift_one + total + bias
        normal, inverse = normed(values)
        layer[index] = (normal * gain + shift).astype(BF)
        if piece == 0:
            keep(layer.at[index], back_ref.at[0], groups)
            cotan = cotan_in[0].astype(F32)
        else:
            leaving.append(
                exchange.send(
                    layer.at[index], back_ref.at[piece], base + groups + piece, peers[groups - piece]
                )
            )
            arriving[piece].wait_recv()
            cotan = cotan_in[piece].astype(F32)
        grad = norm_back(cotan, normal, inverse, gain)
        grad_ref[piece] = grad
        ready[index] = grad.astype(BF)
        exchange.share(index, ready.at[index], target(piece))
        keep(ready.at[index], target(piece)(exchange.me), index)
        sums_ref[0:1] += jnp.sum(grad, axis=0, keepdims=True)
        sums_ref[1:2] += jnp.sum(cotan * normal, axis=0, keepdims=True)
        sums_ref[2:3] += jnp.sum(cotan, axis=0, keepdims=True)
        outward.append(moved(grad_ref.at[piece], grad_hbm.at[piece], out_sem.at[2 + index]))

    first, second = run_pieces(exchange, range(groups), work, product)
    for index, piece in first:
        exchange.forward(index, target(piece))
    for index, piece in second:
        work(index, piece, exchange.total(index, piece))
    step = 512
    count = whole.shape[1] // step
    depth = turned_ref.shape[1] // 2

    def columns(index):
        return pl.ds(pl.multiple_of(index * step, step), step)

    def put(index):
        span = columns(index)
        return pltpu.make_async_copy(
            whole.at[:, span], weight_grad_ref.at[:, span], put_sem.at[index]
        )

    def product_of(part, span):
        low = low_ref[part, :, :, :, span].reshape(depth, step)
        return matmul(turned_ref[:, part * depth : (part + 1) * depth], low)

    exchange.arrived([index for index, _ in first])
    load_turned.wait()
    for copy in local[: len(first) + 1]:
        copy.wait()
    outward.append(moved(low_ref.at[0], low_hbm.at[0], out_sem.at[0]))

    def first_product(start, stop):
        @pl.loop(start, stop)
        def _(index):
            span = columns(index)
            whole[:, span] = product_of(0, span).astype(BF)

    share_out = count // (2 * len(second))
    done = count // 2
    first_product(0, done)
    for index, piece in second:
        exchange.forward(index, target(piece))
        first_product(done, done + share_out)
        done += share_out
    exchange.arrived([index for index, _ in second])
    for copy in local[len(first) + 1 :]:
        copy.wait()
    outward.append(moved(low_ref.at[1], low_hbm.at[1], out_sem.at[1]))

    @pl.loop(0, count)
    def _(index):
        span = columns(index)
        whole[:, span] = (product_of(1, span) + whole[:, span].astype(F32)).astype(BF)
        put(index).start()

    exchange.sent()
    for copy in outward:
        copy.wait()
    for copy in leaving:
        copy.wait()
    for copy in arriving.values():
        copy.wait_send()
    for index in range(count):
        put(index).wait()


def first_back_kernel(
    groups, left_ref, weight_ref, grad_ref, normal_ref, inverse_ref, sums_in_ref, rows_ref,
    low_ref, out_ref, sums_ref,
    landed, relay, ready, own_sums, part_ref, weight, rows, load_sem,
    send_sem, recv_sem, local_sem,
):
    exchange = Exchange(part_ref, landed, relay, send_sem, recv_sem)
    product = Product(exchange, True, left_ref, weight_ref, weight, rows, load_sem)
    greet([{"mp": exchange.along_x}, {"mp": exchange.along_y}, {"mp": exchange.across}])
    local = []
    own_sums[...] = sums_in_ref[...]

    def target(piece):
        return lambda device: low_ref.at[row_place(device, piece, groups)]

    def keep(source, place, slot):
        copy = pltpu.make_async_copy(source, place, local_sem.at[slot])
        copy.start()
        local.append(copy)

    def work(index, piece, total):
        grad = total + grad_ref[piece]
        normal = normal_ref[piece]
        moved = norm_back(grad, normal, inverse_ref[piece], rows_ref[0:1])
        out_ref[piece] = moved
        ready[index] = moved.astype(BF)
        exchange.share(index, ready.at[index], target(piece))
        keep(ready.at[index], target(piece)(exchange.me), index)
        own_sums[3:4] += jnp.sum(moved, axis=0, keepdims=True)
        own_sums[4:5] += jnp.sum(grad * normal, axis=0, keepdims=True)
        own_sums[5:6] += jnp.sum(grad, axis=0, keepdims=True)

    first, second = run_pieces(exchange, range(groups), work, product)
    for index, piece in first:
        exchange.forward(index, target(piece))
    for index, piece in second:
        work(index, piece, exchange.total(index, piece))
    others = [
        exchange.send(own_sums, sums_ref.at[exchange.me], 6 * groups + slot, {"mp": device})
        for slot, device in enumerate((exchange.along_x, exchange.along_y, exchange.across))
    ]
    keep(own_sums, sums_ref.at[exchange.me], groups)
    for index, piece in second:
        exchange.forward(index, target(piece))
    exchange.finish(groups)
    for copy in others:
        copy.wait()
    for copy in local:
        copy.wait()


def input_order(groups):
    return list(range(1, groups - 1)) + [0, groups - 1]


class LineSum:
    def __init__(
        self, groups, per, blocks_ref, own, other, inbox, line_send, line_recv, pair_send, pair_recv, pair_local
    ):
        self.groups, self.per = groups, per
        here = lax.axis_index("seq")
        self.group, self.place = here // per, lax.rem(here, per)
        self.own, self.other, self.inbox = own, other, inbox
        self.line_send, self.line_recv = line_send, line_recv
        sibling = {"seq": self.group * per + 1 - self.place}
        send = sender(pair_send, pair_recv)
        self.order = sorted(range(groups), key=lambda index: -abs(2 * index - groups + 1))
        self.away, self.near = {}, {}
        for index in self.order:
            self.away[index] = send(
                blocks_ref.at[index, 1 - self.place], other.at[index], index, sibling
            )
            copy = pltpu.make_async_copy(
                blocks_ref.at[index, self.place], own.at[index], pair_local.at[index]
            )
            copy.start()
            self.near[index] = copy

    def seen(self, stream):
        return self.group if stream == 0 else self.groups - 1 - self.group

    def copy(self, stream, to):
        group = to if stream == 0 else self.groups - 1 - to
        ahead = self.group + (1 if stream == 0 else -1)
        slot = stream * self.groups + to
        return pltpu.make_async_remote_copy(
            src_ref=self.own.at[group],
            dst_ref=self.inbox.at[stream, to - 1],
            send_sem=self.line_send.at[slot],
            recv_sem=self.line_recv.at[slot],
            device_id={"seq": ahead * self.per + self.place},
            device_id_type=MESH,
        )

    def first_send(self, to):
        for stream in range(2):

            @pl.when(self.seen(stream) == 0)
            def _(stream=stream):
                self.copy(stream, to).start()

    def pair_sums(self, indices):
        for index in indices:
            self.near[index].wait()
            self.away[index].wait_recv()
            self.own[index] = (
                self.own[index].astype(F32) + self.other[index].astype(F32)
            ).astype(BF)

    def begin(self):
        self.pair_sums(self.order[:2])
        self.first_send(self.groups - 1)

    def go_on(self):
        self.pair_sums(self.order[2:])
        self.first_send(self.groups - 2)

    def hop(self, time):
        if self.groups - 2 - time > 0:
            for stream in range(2):

                @pl.when(self.seen(stream) == 0)
                def _(stream=stream):
                    self.copy(stream, self.groups - time).wait_send()

            self.first_send(self.groups - 2 - time)
        for stream in range(2):
            seen = self.seen(stream)

            @pl.when((seen >= 1) & (seen <= time))
            def _(stream=stream, seen=seen):
                to = self.groups - 1 + seen - time
                group = to if stream == 0 else self.groups - 1 - to
                self.copy(stream, to).wait_recv()
                self.own[group] = (
                    self.own[group].astype(F32) + self.inbox[stream, to - 1].astype(F32)
                ).astype(BF)
                self.copy(stream, to).start()

    def end(self, out_ref):
        out_ref[...] = self.own[self.group].astype(F32)
        for stream in range(2):
            seen = self.seen(stream)

            @pl.when(seen >= 1)
            def _(stream=stream, seen=seen):
                self.copy(stream, seen).wait_recv()
                out_ref[...] += self.inbox[stream, seen - 1].astype(F32)

        for stream in range(2):
            for to in range(1, self.groups):

                seen = self.seen(stream)
                waited = (seen == 0) & (to > 2)

                @pl.when((seen < to) & jnp.logical_not(waited))
                def _(stream=stream, to=to):
                    self.copy(stream, to).wait_send()

        for copy in self.away.values():
            copy.wait_send()


def input_kernel(
    groups, per, left_ref, weight_ref, grad_ref, small_ref, blocks_ref,
    all_ref, small_out, block_out,
    landed, relay, ready, back, part_ref, weight, rows, load_sem,
    own, other, inbox, line_send, line_recv, pair_send, pair_recv, pair_local,
    send_sem, recv_sem, local_sem,
):
    exchange = Exchange(part_ref, landed, relay, send_sem, recv_sem)
    product = Product(exchange, True, left_ref, weight_ref, weight, rows, load_sem)
    peers = planes(groups, per)
    members = groups * per
    here = lax.axis_index("seq")
    group = here // per
    devices = [{"seq": lax.rem(here + step, members)} for step in range(1, members)]
    greet([{"mp": exchange.along_x}, {"mp": exchange.along_y}] + devices)
    line = LineSum(
        groups, per, blocks_ref, own, other, inbox,
        line_send, line_recv, pair_send, pair_recv, pair_local,
    )
    base = 6 * groups
    small = [
        exchange.send(
            small_ref.at[lax.rem(here + step, members)],
            small_out.at[here],
            base + groups + step,
            devices[step - 1],
        )
        for step in range(1, members)
    ]
    crossing, local = {}, []

    def keep(source, place, slot):
        copy = pltpu.make_async_copy(source, place, local_sem.at[slot])
        copy.start()
        local.append(copy)

    keep(small_ref.at[here], small_out.at[here], groups)

    def target(piece):
        sequence = lax.rem(group + piece, groups)
        return lambda device: all_ref.at[sequence, device]

    def work(index, piece, total):
        ready[piece] = (total + grad_ref[piece]).astype(BF)
        if piece > 0:
            crossing[piece] = exchange.send(
                ready.at[piece], back.at[piece], base + piece, peers[groups - piece]
            )

    def share(index, piece):
        source = ready.at[0]
        if piece > 0:
            crossing[piece].wait_recv()
            source = back.at[piece]
        exchange.share(index, source, target(piece))
        keep(source, target(piece)(exchange.me), index)

    def fill(part):
        if part == 0:
            line.begin()
        else:
            line.go_on()

    first, second = run_pieces(exchange, input_order(groups), work, product, fill)
    for index, piece in second:
        work(index, piece, exchange.total(index, piece))
    here_first = [place for place in second if place[1] == 0]
    late = [place for place in second if place[1] > 0]
    line.hop(1)
    for index, piece in here_first + first:
        share(index, piece)
    for index, piece in here_first:
        exchange.forward(index, target(piece))
    for time in range(2, groups - 1):
        line.hop(time)
    for index, piece in late:
        share(index, piece)
    for index, piece in first + late:
        exchange.forward(index, target(piece))
    line.end(block_out)
    exchange.finish(groups)
    for copy in small:
        copy.wait()
    for copy in crossing.values():
        copy.wait_send()
    for copy in local:
        copy.wait()


def product_scratch(parts, groups, piece, width, depth, turned, loads=1):
    return [
        pltpu.VMEM((2, parts, groups // 2, piece, width), BF),
        pltpu.VMEM((width, depth) if turned else (depth, width), BF),
        pltpu.VMEM((groups * piece, depth), BF),
        pltpu.SemaphoreType.DMA((max(width // 512, loads),)),
    ]


def exchange_call(kernel, ident, operands, results, sums, scratch, extra, outside=(), local=True):
    groups, piece, width = sums
    return pl.pallas_call(
        kernel,
        out_shape=tuple(jax.ShapeDtypeStruct(shape, dtype) for shape, dtype, _ in results),
        in_specs=[ANY if place in outside else VMEM for place in range(len(operands))],
        out_specs=tuple(spec for _, _, spec in results),
        scratch_shapes=[
            pltpu.VMEM((groups, 3, piece, width), BF),
            pltpu.VMEM((groups, piece, width), BF),
        ]
        + scratch
        + [
            pltpu.SemaphoreType.DMA((6 * groups + extra,)),
            pltpu.SemaphoreType.DMA((6 * groups + extra,)),
        ]
        + ([pltpu.SemaphoreType.DMA((groups + 1,))] if local else []),
        compiler_params=pltpu.CompilerParams(
            collective_id=ident, has_side_effects=True, vmem_limit_bytes=58 * MIB
        ),
        cost_estimate=pl.CostEstimate(flops=0, bytes_accessed=200 * MIB, transcendentals=0),
        name=f"exchange_{ident}",
    )(*operands)


def first_norm(part, x_part, x_rows, rows, parts, ident):
    groups, piece, width = x_part.shape
    half = groups // 2
    if parts != 4:
        total = lax.psum_scatter(part, "mp", scatter_dimension=0, tiled=True).astype(F32)
        values = x_part.astype(F32) + total.reshape(x_part.shape) + rows[0]
        normal, inverse = normed(values)
        low = lax.all_gather((normal * rows[1] + rows[2]).astype(BF), "mp", axis=0)
        return low, normal, inverse, x_rows.T
    return exchange_call(
        functools.partial(first_norm_kernel, groups),
        ident,
        (part.reshape(2, parts, half, piece, width), x_part, x_rows, rows),
        [
            ((2, parts, half, piece, width), BF, ANY),
            ((groups, piece, width), F32, VMEM),
            ((groups, piece, 1), F32, VMEM),
            ((width, x_rows.shape[0]), BF, VMEM),
        ],
        (groups, piece, width),
        [pltpu.VMEM((groups, piece, width), BF)],
        0,
    )


def half_sum(left, second, first, groups, piece, members, parts, ident):
    rows, depth = left.shape
    width = second.shape[0] // 2
    return exchange_call(
        functools.partial(half_sum_kernel, groups, members),
        ident,
        (left.reshape(2, parts, groups // 2, piece, depth), second, first),
        [
            ((groups, piece, width), F32, VMEM),
            ((depth, rows), BF, VMEM),
            ((width, depth), BF, ANY),
            (first.shape[::-1], BF, VMEM),
        ],
        (groups, piece, width),
        product_scratch(parts, groups, piece, width, depth, True, 2 * members)
        + [pltpu.SemaphoreType.DMA],
        0,
        (1,),
        False,
    )


def second_norm(left, weight, turned, done, normal, cotan, rows, members, parts, ident):
    groups, piece, width = normal.shape
    depth = left.shape[-1]
    half = groups // 2
    if parts != 4:
        part = over_cols(left, weight).astype(BF)
        total = lax.psum_scatter(part, "mp", scatter_dimension=0, tiled=True).astype(F32)
        values = normal * rows[0] + rows[1] + total.reshape(normal.shape) + rows[2]
        normal, inverse = normed(values)
        layer = (normal * rows[3] + rows[4]).astype(BF)
        back = jnp.stack(swap_blocks(layer, members, -1))
        cotan = jnp.stack(swap_blocks(cotan, members, 1)).astype(F32)
        grad = norm_back(cotan, normal, inverse, rows[3])
        sums = [jnp.sum(array, axis=(0, 1)) for array in (grad, cotan * normal, cotan)]
        sums = jnp.stack(sums + [jnp.zeros_like(sums[0])] * 5)
        low = lax.all_gather(grad.astype(BF), "mp", axis=0)
        return low, grad, back, sums, over_rows(left, low.reshape(-1, width)).astype(BF)
    block = pltpu.VMEM((groups, piece, width), BF)
    return exchange_call(
        functools.partial(second_norm_kernel, groups, members // groups),
        ident,
        (
            left.reshape(2, parts, half, piece, depth),
            weight, turned, done, normal, cotan, rows,
        ),
        [
            ((2, parts, half, piece, width), BF, ANY),
            ((groups, piece, width), F32, ANY),
            ((groups, piece, width), BF, ANY),
            ((8, width), F32, VMEM),
            ((depth, width), BF, ANY),
        ],
        (groups, piece, width // 2),
        product_scratch(parts, groups, piece, width // 2, depth, True)
        + [
            block,
            block,
            block,
            pltpu.VMEM(turned.shape, BF),
            pltpu.VMEM((depth, width), BF),
            pltpu.VMEM((2, parts, half, piece, depth), BF),
            pltpu.VMEM(done.shape, F32),
            pltpu.VMEM(normal.shape, F32),
            pltpu.VMEM((2, parts, half, piece, width), BF),
            pltpu.VMEM((groups, piece, width), F32),
            pltpu.SemaphoreType.DMA((width // 256,)),
            pltpu.SemaphoreType.DMA((6,)),
            pltpu.SemaphoreType.DMA((2 + groups,)),
        ],
        2 * groups,
        (0, 1, 2, 3, 4, 5),
    )


def first_back(left, weight, grad, normal, inverse, sums, rows, parts, ident):
    groups, piece, width = normal.shape
    depth = left.shape[-1]
    if parts != 4:
        part = over_cols(left, weight[:, :depth]).astype(BF)
        total = lax.psum_scatter(part, "mp", scatter_dimension=0, tiled=True).astype(F32)
        grad = total.reshape(normal.shape) + grad
        moved = norm_back(grad, normal, inverse, rows[0])
        more = [jnp.sum(array, axis=(0, 1)) for array in (moved, grad * normal, grad)]
        sums = sums.at[3:6].add(jnp.stack(more))
        return (
            lax.all_gather(moved.astype(BF), "mp", axis=0),
            moved,
            lax.all_gather(sums, "mp", axis=0),
        )
    half = groups // 2
    return exchange_call(
        functools.partial(first_back_kernel, groups),
        ident,
        (
            left.reshape(2, parts, half, piece, depth), weight,
            grad, normal, inverse, sums, rows,
        ),
        [
            ((2, parts, half, piece, width), BF, ANY),
            ((groups, piece, width), F32, VMEM),
            ((parts, 8, width), F32, VMEM),
        ],
        (groups, piece, width),
        [pltpu.VMEM((groups, piece, width), BF), pltpu.VMEM((8, width), F32)]
        + product_scratch(parts, groups, piece, width, depth, True),
        3,
        (1,),
    )


def input_gradient(left, weight, grad, small, part, members, parts, ident):
    groups, piece, width = grad.shape
    depth = left.shape[-1]
    if parts != 4:
        summed = lax.psum_scatter(part, "seq", scatter_dimension=0, tiled=True).astype(F32)
        part = over_cols(left, weight[:, :depth]).astype(BF)
        total = lax.psum_scatter(part, "mp", scatter_dimension=0, tiled=True).astype(F32)
        ready = (total.reshape(grad.shape) + grad).astype(BF)
        back = jnp.stack(swap_blocks(ready, members, -1))
        back = jnp.roll(back, lax.axis_index("seq") // (members // groups), axis=0)
        return lax.all_gather(back, "mp", axis=1), lax.all_to_all(small, "seq", 0, 0), summed
    per = members // groups
    block = (part.shape[0] // members, part.shape[1])
    return exchange_call(
        functools.partial(input_kernel, groups, members // groups),
        ident,
        (left.reshape(2, parts, groups // 2, piece, depth), weight, grad, small, part.reshape(groups, per, *block)),
        [
            ((groups, parts, piece, width), BF, ANY),
            (small.shape, F32, VMEM),
            (block, F32, VMEM),
        ],
        (groups, piece, width),
        [pltpu.VMEM((groups, piece, width), BF)] * 2
        + product_scratch(parts, groups, piece, width, depth, True)
        + [
            pltpu.VMEM((groups, *block), BF),
            pltpu.VMEM((groups, *block), BF),
            pltpu.VMEM((2, groups - 1, *block), BF),
        ]
        + [pltpu.SemaphoreType.DMA((2 * groups,))] * 2
        + [pltpu.SemaphoreType.DMA((groups,))] * 3,
        groups + members,
        (1, 4),
    )


def share_kernel(own_ref, all_ref, send_sem, recv_sem, local_sem):
    me, along_x, along_y, _ = square()
    to_x, to_y = {"mp": along_x}, {"mp": along_y}
    greet([to_x, to_y])
    send = sender(send_sem, recv_sem)
    half = own_ref.shape[0] // 2
    upper, lower = pl.ds(0, half), pl.ds(half, half)
    copies = [
        send(own_ref.at[upper], all_ref.at[0, me], 0, to_x),
        send(own_ref.at[lower], all_ref.at[1, me], 1, to_y),
        send(own_ref.at[lower], all_ref.at[1, me], 2, to_x),
        send(own_ref.at[upper], all_ref.at[0, me], 3, to_y),
    ]
    local = [
        pltpu.make_async_copy(own_ref.at[upper], all_ref.at[0, me], local_sem.at[0]),
        pltpu.make_async_copy(own_ref.at[lower], all_ref.at[1, me], local_sem.at[1]),
    ]
    for copy in local:
        copy.start()
    copies[0].wait_recv()
    copies.append(send(all_ref.at[0, along_x], all_ref.at[0, along_x], 4, to_y))
    copies[1].wait_recv()
    copies.append(send(all_ref.at[1, along_y], all_ref.at[1, along_y], 5, to_x))
    for copy in copies[2:]:
        copy.wait_recv()
    for copy in copies:
        copy.wait_send()
    for copy in local:
        copy.wait()


def share_over_mp(own, parts, ident):
    if parts != 4:
        return lax.all_gather(own, "mp", axis=0)
    return pl.pallas_call(
        share_kernel,
        out_shape=jax.ShapeDtypeStruct((2, parts, own.shape[0] // 2, own.shape[1]), own.dtype),
        in_specs=[ANY],
        out_specs=ANY,
        scratch_shapes=[
            pltpu.SemaphoreType.DMA((6,)),
            pltpu.SemaphoreType.DMA((6,)),
            pltpu.SemaphoreType.DMA((2,)),
        ],
        compiler_params=pltpu.CompilerParams(collective_id=ident, has_side_effects=True),
        cost_estimate=pl.CostEstimate(flops=0, bytes_accessed=100 * MIB, transcendentals=0),
        name=f"share_over_mp_{ident}",
    )(own)


def swap_kernel(
    groups, per, sign, block_ref, small_ref, out_ref, small_out, send_sem, recv_sem, local_sem
):
    members = groups * per
    index = lax.axis_index("seq")
    devices = [{"seq": lax.rem(index + step, members)} for step in range(1, members)]
    greet(devices)
    send = sender(send_sem, recv_sem)
    copies = []
    for step in range(1, groups):
        ahead = step if sign > 0 else groups - step
        source = block_ref.at[step]
        copies.append(send(source, out_ref.at[step], step, devices[ahead * per - 1]))
    for step in range(1, members):
        target = lax.rem(index + step, members)
        copies.append(
            send(small_ref.at[target], small_out.at[index], groups + step, devices[step - 1])
        )
    locals_ = [
        pltpu.make_async_copy(block_ref.at[0], out_ref.at[0], local_sem.at[0]),
        pltpu.make_async_copy(small_ref.at[index], small_out.at[index], local_sem.at[1]),
    ]
    for local in locals_:
        local.start()
    for local in locals_:
        local.wait()
    for copy in copies:
        copy.wait()


def shift_pairs(members, ahead):
    return [(index, (index + ahead) % members) for index in range(members)]


def swap_blocks(blocks, members, sign):
    groups = blocks.shape[0]
    per = members // groups
    arrived = [blocks[0]]
    for step in range(1, groups):
        pairs = shift_pairs(members, sign * step * per)
        arrived.append(lax.ppermute(blocks[step], "seq", pairs))
    return arrived


def swap_groups(blocks, small, members, parts, sign, ident):
    groups = blocks.shape[0]
    per = members // groups
    if parts != 4:
        return jnp.stack(swap_blocks(blocks, members, sign)), lax.all_to_all(small, "seq", 0, 0)
    return pl.pallas_call(
        functools.partial(swap_kernel, groups, per, sign),
        out_shape=(
            jax.ShapeDtypeStruct(blocks.shape, blocks.dtype),
            jax.ShapeDtypeStruct(small.shape, small.dtype),
        ),
        in_specs=[ANY, ANY],
        out_specs=(ANY, ANY),
        scratch_shapes=[
            pltpu.SemaphoreType.DMA((groups + members,)),
            pltpu.SemaphoreType.DMA((groups + members,)),
            pltpu.SemaphoreType.DMA((2,)),
        ],
        compiler_params=pltpu.CompilerParams(collective_id=ident, has_side_effects=True),
        cost_estimate=pl.CostEstimate(flops=0, bytes_accessed=60 * MIB, transcendentals=0),
        name=f"swap_groups_{ident}",
    )(blocks, small)


def score_block(keys, queries):
    return lax.dot_general(keys, queries, (((1,), (1,)), ((), ())), preferred_element_type=F32)


def attend_kernel(
    query_ref, key_ref, value_ref, key_far_ref, value_far_ref, mix_ref, low_ref, log_ref, turned
):
    rows = key_ref.shape[0]

    @pl.when(pl.program_id(1) == 0)
    def _():
        turned[:, :rows] = value_ref[...].T
        turned[:, rows:] = value_far_ref[...].T

    scale = DH ** (-0.5)
    near = score_block(key_ref[...], query_ref[...])
    far = score_block(key_far_ref[...], query_ref[...])
    highest = jnp.maximum(
        jnp.max(near, axis=0, keepdims=True), jnp.max(far, axis=0, keepdims=True)
    )
    near = jnp.exp((near - highest) * scale)
    far = jnp.exp((far - highest) * scale)
    total = jnp.sum(near, axis=0, keepdims=True) + jnp.sum(far, axis=0, keepdims=True)
    mix = jnp.dot(turned[:, :rows], near.astype(BF), preferred_element_type=F32)
    mix += jnp.dot(turned[:, rows:], far.astype(BF), preferred_element_type=F32)
    mix = (mix / total).T
    mix_ref[...] = mix
    low_ref[...] = mix.astype(BF)
    log_ref[0] = highest * scale + jnp.log(total)


def attend(qkv, kv_far, heads):
    rows, cols = qkv.shape[0], heads * DH
    away = kv_far.shape[0]
    block = min(512, rows)

    def tile(offset):
        return pl.BlockSpec((block, DH), lambda h, i: (i, offset + h))

    def long(count, offset):
        return pl.BlockSpec((count, DH), lambda h, i: (0, offset + h))

    return pl.pallas_call(
        attend_kernel,
        grid=(heads, rows // block),
        out_shape=(
            jax.ShapeDtypeStruct((rows, cols), F32),
            jax.ShapeDtypeStruct((rows, cols), BF),
            jax.ShapeDtypeStruct((heads, 1, rows), F32),
        ),
        in_specs=[
            tile(0),
            long(rows, heads),
            long(rows, 2 * heads),
            long(away, 0),
            long(away, heads),
        ],
        out_specs=(tile(0), tile(0), pl.BlockSpec((1, 1, block), lambda h, i: (h, 0, i))),
        scratch_shapes=[pltpu.VMEM((DH, rows + away), BF)],
        compiler_params=pltpu.CompilerParams(vmem_limit_bytes=52 * MIB),
        cost_estimate=pl.CostEstimate(
            flops=8 * rows * (rows + away) * cols,
            bytes_accessed=20 * rows * cols,
            transcendentals=rows * (rows + away) * heads,
        ),
        name="attend",
    )(qkv, qkv, qkv, kv_far, kv_far)


def share_meanwhile(
    now, count, pieces, back_ref, all_ref, send_sem, recv_sem, local_sem, also=()
):
    me, along_x, along_y, _ = square()
    send = sender(send_sem, recv_sem, False)
    near, far, passed, local = [], [], [], []
    for index, piece in enumerate(pieces):
        ways = (along_x, along_y) if index % 2 == 0 else (along_y, along_x)
        block, own = back_ref.at[piece], all_ref.at[index, me]
        relayed = all_ref.at[index, ways[0]]
        near.append(send(block, own, 3 * index, {"mp": ways[0]}))
        far.append(send(block, own, 3 * index + 1, {"mp": ways[1]}))
        passed.append(send(relayed, relayed, 3 * index + 2, {"mp": ways[1]}))
        local.append(pltpu.make_async_copy(block, own, local_sem.at[index]))

    @pl.when(now == 0)
    def _():
        greet([{"mp": along_x}, {"mp": along_y}, *also])
        for copy in near + far + local:
            copy.start()

    @pl.when(now == count // 4)
    def _():
        for first, second in zip(near, passed):
            first.wait_recv()
            second.start()

    def finish():
        @pl.when(now == count - 1)
        def _():
            for copy in far + passed:
                copy.wait_recv()
            for copy in near + far + passed:
                copy.wait_send()
            for copy in local:
                copy.wait()

    return finish


def meanwhile_scratch(pieces):
    return [
        pltpu.SemaphoreType.DMA((3 * len(pieces),)),
        pltpu.SemaphoreType.DMA((3 * len(pieces),)),
        pltpu.SemaphoreType.DMA((len(pieces),)),
    ]


def feed_back_kernel(
    pieces, members, low_ref, weight_ref, more_ref, pre_ref, turned_ref, back_ref,
    grad_ref, sums_ref, weight_grad_ref, all_ref, send_sem, recv_sem, local_sem,
):
    now, count = pl.program_id(0), pl.num_programs(0)
    finish = share_meanwhile(now, count, pieces, back_ref, all_ref, send_sem, recv_sem, local_sem)
    value = pre_ref[...]
    root = (2 / math.pi) ** 0.5
    square_of = value * value
    bent = jnp.tanh(root * value * (1 + 0.044715 * square_of))
    slope = 0.5 * (1 + bent) + (0.5 * root) * value * (1 - bent * bent) * (
        1 + 3 * 0.044715 * square_of
    )
    narrow = weight_ref.shape[0] // members
    weight = jnp.concatenate(
        [
            half[place * narrow : (place + 1) * narrow]
            for place in range(members)
            for half in (weight_ref, more_ref)
        ],
        axis=0,
    )
    grad = (matmul(low_ref[...], weight) * slope).astype(BF)
    grad_ref[...] = grad
    sums_ref[...] = jnp.sum(grad.astype(F32), axis=0, keepdims=True)
    weight_grad_ref[...] = matmul(turned_ref[...], grad).astype(BF)
    finish()


def feed_back(low, weight, more, inner_pre, turned, layer_back, pieces, members, parts, ident):
    rows, hidden = inner_pre.shape
    width = low.shape[1]
    step = 512
    _, piece, _ = layer_back.shape
    return pl.pallas_call(
        functools.partial(feed_back_kernel, pieces, members),
        grid=(hidden // step,),
        out_shape=(
            jax.ShapeDtypeStruct((rows, hidden), BF),
            jax.ShapeDtypeStruct((1, hidden), F32),
            jax.ShapeDtypeStruct((width, hidden), BF),
            jax.ShapeDtypeStruct((len(pieces), parts, piece, width), BF),
        ),
        in_specs=[
            pl.BlockSpec((rows, width), lambda i: (0, 0)),
            pl.BlockSpec((width // 2, step), lambda i: (0, i)),
            pl.BlockSpec((width // 2, step), lambda i: (0, i)),
            pl.BlockSpec((rows, step), lambda i: (0, i)),
            pl.BlockSpec((width, rows), lambda i: (0, 0)),
            ANY,
        ],
        out_specs=(
            pl.BlockSpec((rows, step), lambda i: (0, i)),
            pl.BlockSpec((1, step), lambda i: (0, i)),
            pl.BlockSpec((width, step), lambda i: (0, i)),
            ANY,
        ),
        scratch_shapes=meanwhile_scratch(pieces),
        compiler_params=pltpu.CompilerParams(
            collective_id=ident, has_side_effects=True, vmem_limit_bytes=58 * MIB
        ),
        cost_estimate=pl.CostEstimate(
            flops=4 * rows * width * hidden, bytes_accessed=40 * MIB, transcendentals=rows * hidden
        ),
        name="feed_back",
    )(low, weight, more, inner_pre, turned, layer_back)


def sibling():
    here = lax.axis_index("seq")
    return {"seq": here + 1 - 2 * lax.rem(here, 2)}


def attend_back_kernel(
    pieces,
    step,
    query_ref,
    key_ref,
    value_ref,
    key_far_ref,
    value_far_ref,
    grad_ref,
    mix_ref,
    log_ref,
    *rest,
):
    sharing = len(pieces) > 0
    if sharing:
        back_ref, *rest = rest
    dquery_ref, dkey_ref, dvalue_ref, *rest = rest
    if sharing:
        in_ref, all_ref, *rest = rest
    else:
        dkey_far_ref, dvalue_far_ref, *rest = rest
    turned, key_sum, value_sum, *rest = rest
    block = pl.program_id(1)
    rows = key_ref.shape[0]
    if sharing:
        away, pair_send, pair_recv, send_sem, recv_sem, local_sem = rest
        now = pl.program_id(0) * pl.num_programs(1) + block
        count = pl.num_programs(0) * pl.num_programs(1)
        finish = share_meanwhile(
            now, count, pieces, back_ref, all_ref, send_sem, recv_sem, local_sem, [sibling()]
        )

        def cross(kind, head):
            return pltpu.make_async_remote_copy(
                src_ref=away.at[kind, head],
                dst_ref=in_ref.at[kind, head],
                send_sem=pair_send.at[kind, head],
                recv_sem=pair_recv.at[kind, head],
                device_id=sibling(),
                device_id_type=MESH,
            )

    @pl.when(block == 0)
    def _():
        turned[:, :rows] = key_ref[...].T
        turned[:, rows:] = key_far_ref[...].T
        key_sum[...] = jnp.zeros_like(key_sum)
        value_sum[...] = jnp.zeros_like(value_sum)

    scale = DH ** (-0.5)
    query, grad = query_ref[...], grad_ref[...]
    terms = jnp.sum((grad.astype(F32) * mix_ref[...]).T, axis=0, keepdims=True)
    logs = log_ref[0]
    dquery = jnp.zeros((DH, query.shape[0]), F32)
    spans = [(key_ref, value_ref, start, start) for start in range(0, rows, step)]
    spans += [
        (key_far_ref, value_far_ref, start, rows + start)
        for start in range(0, key_far_ref.shape[0], step)
    ]
    for keys, values, start, place in spans:
        part = pl.ds(place, step)
        probs = jnp.exp(score_block(keys[pl.ds(start, step)], query) * scale - logs)
        prob_grad = score_block(values[pl.ds(start, step)], grad)
        score_grad = (probs * (prob_grad - terms) * scale).astype(BF)
        value_sum[part] += jnp.dot(probs.astype(BF), grad, preferred_element_type=F32)
        key_sum[part] += jnp.dot(score_grad, query, preferred_element_type=F32)
        dquery += jnp.dot(turned[:, part], score_grad, preferred_element_type=F32)
    dquery_ref[...] = dquery.T.astype(BF)

    @pl.when(block == pl.num_programs(1) - 1)
    def _():
        dkey_ref[...] = key_sum[:rows]
        dvalue_ref[...] = value_sum[:rows]
        if sharing:
            head = pl.program_id(0)
            for kind, total in enumerate((key_sum, value_sum)):
                away[kind, head] = total[rows:].astype(BF)
                cross(kind, head).start()
        else:
            dkey_far_ref[...] = key_sum[rows:].astype(BF)
            dvalue_far_ref[...] = value_sum[rows:].astype(BF)

    if sharing:

        @pl.when(now == count - 1)
        def _():
            for kind in range(2):
                for head in range(away.shape[1]):
                    cross(kind, head).wait()

        finish()


def attend_back(qkv, kv_far, grad, mix, logs, heads, layer_back, pieces, parts, ident):
    rows, cols = qkv.shape[0], heads * DH
    away = kv_far.shape[0]
    block, step = min(512, rows), min(512, rows)
    sharing = len(pieces) > 0
    _, piece, width = layer_back.shape

    def tile(offset):
        return pl.BlockSpec((block, DH), lambda h, i: (i, offset + h))

    def long(count, offset):
        return pl.BlockSpec((count, DH), lambda h, i: (0, offset + h))

    return pl.pallas_call(
        functools.partial(attend_back_kernel, pieces, step),
        grid=(heads, rows // block),
        out_shape=(
            jax.ShapeDtypeStruct((rows, cols), BF),
            jax.ShapeDtypeStruct((rows, cols), F32),
            jax.ShapeDtypeStruct((rows, cols), F32),
        )
        + (
            (
                jax.ShapeDtypeStruct((2, heads, rows, DH), BF),
                jax.ShapeDtypeStruct((len(pieces), parts, piece, width), BF),
            )
            if sharing
            else (jax.ShapeDtypeStruct((away, cols), BF),) * 2
        ),
        in_specs=[
            tile(0),
            long(rows, heads),
            long(rows, 2 * heads),
            long(away, 0),
            long(away, heads),
            tile(0),
            tile(0),
            pl.BlockSpec((1, 1, block), lambda h, i: (h, 0, i)),
        ]
        + ([ANY] if sharing else []),
        out_specs=(tile(0), long(rows, 0), long(rows, 0))
        + ((ANY, ANY) if sharing else (long(away, 0), long(away, 0))),
        scratch_shapes=[
            pltpu.VMEM((DH, rows + away), BF),
            pltpu.VMEM((rows + away, DH), F32),
            pltpu.VMEM((rows + away, DH), F32),
        ]
        + (
            [
                pltpu.VMEM((2, heads, rows, DH), BF),
                pltpu.SemaphoreType.DMA((2, heads)),
                pltpu.SemaphoreType.DMA((2, heads)),
            ]
            + meanwhile_scratch(pieces)
            if sharing
            else []
        ),
        compiler_params=pltpu.CompilerParams(
            vmem_limit_bytes=52 * MIB,
            **(dict(collective_id=ident, has_side_effects=True) if sharing else {}),
        ),
        cost_estimate=pl.CostEstimate(
            flops=20 * rows * (rows + away) * cols,
            bytes_accessed=30 * rows * cols,
            transcendentals=rows * (rows + away) * heads,
        ),
        name="attend_back",
    )(qkv, qkv, qkv, kv_far, kv_far, grad, mix, logs, *([layer_back] if sharing else []))


def from_group_members(block, members, per):
    blocks = []
    for step in range(1, per):
        pairs = [
            (base + place, base + (place - step) % per)
            for base in range(0, members, per)
            for place in range(per)
        ]
        blocks.append(lax.ppermute(block, "seq", pairs))
    return blocks


def to_group_members(total, blocks, members, per):
    for step in range(1, per):
        pairs = [
            (base + place, base + (place + step) % per)
            for base in range(0, members, per)
            for place in range(per)
        ]
        total = total + lax.ppermute(blocks[step - 1], "seq", pairs).astype(F32)
    return total


def last_kernel(
    per, turned_hbm, query_ref, key_ref, value_ref, in_ref, layer_hbm, layer_more_hbm,
    grad_ref, sums_ref, part_ref, layer_ref, turned_ref, made, layer, load_sem, put_sem,
):
    rows, cols = query_ref.shape
    count = load_sem.shape[0] - 2
    step = turned_ref.shape[0] // count
    loads = []
    for place in range(count):
        block = pl.ds(place * step, step)
        loads.append(
            pltpu.make_async_copy(turned_hbm.at[block], turned_ref.at[block], load_sem.at[place])
        )
    groups = layer.shape[0]
    for place, source in enumerate((layer_hbm, layer_more_hbm)):
        block = pl.ds(place * (groups // 2), groups // 2)
        loads.append(pltpu.make_async_copy(source, layer.at[block], load_sem.at[count + place]))
    for copy in loads:
        copy.start()
    puts = []

    def put(source, target):
        copy = pltpu.make_async_copy(source, target, put_sem.at[len(puts)])
        copy.start()
        puts.append(copy)

    for index, (own, far) in enumerate(
        ((query_ref, None), (key_ref, 0), (value_ref, 1))
    ):
        span = pl.ds(index * cols, cols)
        grad = own[...]
        if far is not None:
            far = [in_ref[far, head] for head in range(cols // DH)]
            grad = (grad + jnp.concatenate(far, axis=1).astype(F32)).astype(BF)
        grad_ref[:, span] = grad
        sums_ref[:, span] = jnp.sum(grad.astype(F32), axis=0, keepdims=True)
        for place in range(count):
            block = pl.ds(place * step, step)
            if index == 0:
                loads[place].wait()
            made[index, block] = matmul(turned_ref[block], grad_ref[:, span]).astype(BF)
        put(made.at[index], part_ref.at[:, span])
        if index == 1:
            for copy in loads[count:]:
                copy.wait()
            group = lax.axis_index("seq") // per
            for piece in range(groups):
                put(layer.at[piece], layer_ref.at[lax.rem(group + piece, groups)])
    for copy in puts:
        copy.wait()


def last_gradients(turned, query, key, value, arrived, layer, layer_more, per):
    rows, cols = query.shape
    width = turned.shape[0]
    return pl.pallas_call(
        functools.partial(last_kernel, per),
        out_shape=(
            jax.ShapeDtypeStruct((rows, 3 * cols), BF),
            jax.ShapeDtypeStruct((1, 3 * cols), F32),
            jax.ShapeDtypeStruct((width, 3 * cols), BF),
            jax.ShapeDtypeStruct((2 * layer.shape[0],) + layer.shape[1:], layer.dtype),
        ),
        in_specs=[ANY] + [VMEM] * 4 + [ANY] * 2,
        out_specs=(VMEM, VMEM, ANY, ANY),
        scratch_shapes=[
            pltpu.VMEM(turned.shape, BF),
            pltpu.VMEM((3, width, cols), BF),
            pltpu.VMEM((2 * layer.shape[0],) + layer.shape[1:], BF),
            pltpu.SemaphoreType.DMA((6,)),
            pltpu.SemaphoreType.DMA((3 + 2 * layer.shape[0],)),
        ],
        compiler_params=pltpu.CompilerParams(vmem_limit_bytes=52 * MIB),
        cost_estimate=pl.CostEstimate(
            flops=6 * rows * width * cols, bytes_accessed=32 * MIB, transcendentals=0
        ),
        name="last_gradients",
    )(turned, query, key, value, arrived, layer, layer_more)


def packed(vectors, lines):
    flat = jnp.concatenate(vectors)
    return jnp.pad(flat, (0, lines * 128 - flat.shape[0])).reshape(lines, 128)


def after(value, *others):
    return lax.optimization_barrier((value,) + others)[0]


def on_device(members, parts, *arrays):
    (
        tokens,
        query_weight,
        query_bias,
        key_weight,
        value_weight,
        value_bias,
        proj_weight,
        proj_bias,
        gain_first,
        shift_first,
        inner_weight,
        inner_bias,
        outer_weight,
        outer_bias,
        gain_second,
        shift_second,
        cotangent,
    ) = arrays
    micro, seqs, length, width = tokens.shape
    groups = micro * seqs
    per = members // groups
    assert per * groups == members and (parts != 4 or per == 2)
    piece = length // parts
    rows = groups * length
    quarter = groups * piece
    mine = lax.axis_index("mp")
    group = lax.axis_index("seq") // per

    depth, cols = query_weight.shape
    heads = cols // DH
    first = jnp.concatenate([query_weight, key_weight, value_weight, proj_weight.T], axis=1)
    first = lax.all_gather(first, "seq", axis=0, tiled=True)
    hidden = inner_weight.shape[1]
    fused = parts == 4 and per == 2
    outer_turned = outer_weight.T
    if fused:
        part = depth // 2
        folded = jnp.concatenate(
            [outer_turned[:part, : hidden // 2], outer_turned[:part, hidden // 2 :]], axis=0
        )
        second = jnp.concatenate([inner_weight, folded], axis=1)
        second = lax.all_gather(second, "seq", axis=0, tiled=True)
        w_inner = second[:, :hidden]
        w_outer = lax.all_gather(outer_turned[part:], "seq", axis=0, tiled=True)
    else:
        w_inner = second = lax.all_gather(inner_weight, "seq", axis=0, tiled=True)
        w_outer = lax.all_gather(outer_turned, "seq", axis=0, tiled=True)
    w_qkv = first[:, : 3 * cols]
    w_proj = first[:, 3 * cols :]
    vectors = [
        query_bias,
        value_bias,
        inner_bias,
        proj_bias,
        gain_first,
        shift_first,
        outer_bias,
        gain_second,
        shift_second,
    ]
    sizes = [vector.shape[0] for vector in vectors]
    lines = -(-sum(sizes) // 2048) * 16
    own_vectors = packed(vectors, lines)

    def to_blocks(array):
        array = array.reshape(groups, length, width)
        return [
            lax.dynamic_slice(
                array, (lax.rem(group + k, groups), mine * piece, 0), (1, piece, width)
            )[0]
            for k in range(groups)
        ]

    x_part, all_vectors = swap_groups(
        jnp.stack(to_blocks(tokens)),
        jnp.broadcast_to(own_vectors[None], (members, lines, 128)),
        members,
        parts,
        1,
        1,
    )
    x_part = x_part.reshape(quarter, width)
    x_rows = share_over_mp(x_part, parts, 8).reshape(rows, width)
    all_vectors = all_vectors.reshape(members, -1).astype(F32)
    full = []
    start = 0
    for size in sizes:
        full.append(all_vectors[:, start : start + size].reshape(-1))
        start += size
    b_query, b_value, b_inner, b_proj, gain_one, shift_one, b_outer, gain_two, shift_two = full

    bias = jnp.concatenate([b_query, jnp.zeros_like(b_query), b_value])
    qkv = (matmul(x_rows, w_qkv) + bias).astype(BF)
    kv_far = from_group_members(qkv[:, cols:], members, per)
    kv_far = kv_far[0] if per == 2 else jnp.concatenate(kv_far, axis=0)
    mixture, mixture_low, logs = attend(qkv, kv_far, heads)

    def blocked(array):
        return array.reshape(groups, piece, width)

    first_low, normal_one, inverse_one, x_turned = first_norm(
        over_cols(mixture_low, w_proj).astype(BF),
        blocked(x_part),
        x_rows,
        jnp.stack([b_proj, gain_one, shift_one]),
        parts,
        2,
    )
    first_low = first_low.reshape(rows, width)

    inner_pre = matmul(first_low, w_inner) + b_inner
    active = gelu_tanh(inner_pre).astype(BF)
    done, active_turned, w_outer_half = None, None, None
    if fused:
        done, active_turned, w_outer_half, first_turned = half_sum(
            active, second, first_low, groups, piece, members, parts, 13
        )
    else:
        first_turned = first_low.T
    second_low, second_grad, layer_back, sums, outer_w_part = second_norm(
        active,
        w_outer,
        active_turned,
        done,
        normal_one,
        jnp.stack(to_blocks(cotangent)),
        jnp.stack([gain_one, shift_one, b_outer, gain_two, shift_two]),
        members,
        parts,
        3,
    )
    second_low = second_low.reshape(rows, width)

    outer_w_grad = lax.psum_scatter(outer_w_part, "seq", scatter_dimension=1, tiled=True)
    pieces = list(range(groups)) if fused else []
    early, late = pieces[: groups // 2], pieces[groups // 2 :]
    if fused:
        inner_grad, inner_b_grad, inner_w_part, layer_out = feed_back(
            second_low,
            w_outer_half,
            w_outer,
            inner_pre,
            first_turned,
            layer_back,
            early,
            members,
            parts,
            7,
        )
    else:
        _, pull_gelu = jax.vjp(gelu_tanh, inner_pre)
        inner_grad = pull_gelu(matmul(second_low, w_outer))[0].astype(BF)
        inner_b_grad = jnp.sum(inner_grad.astype(F32), axis=0)
        inner_w_part = matmul(first_turned, inner_grad).astype(BF)
        layer_out = lax.all_gather(jnp.roll(layer_back, group, axis=0), "mp", axis=1)
    inner_w_grad = lax.psum_scatter(inner_w_part, "seq", scatter_dimension=0, tiled=True)
    attn_low, attn_grad, summed_rows = first_back(
        inner_grad,
        second,
        second_grad,
        normal_one,
        inverse_one,
        after(sums, inner_w_part),
        gain_one[None],
        parts,
        4,
    )
    attn_low = after(attn_low.reshape(rows, width), outer_w_grad)
    summed_rows = jnp.sum(summed_rows, axis=0)

    proj_w_part = over_rows(attn_low, mixture_low).astype(BF)
    mixture_grad = matmul(after(attn_low, proj_w_part), w_proj).astype(BF)
    query_grad, key_grad, value_grad, *others = attend_back(
        qkv, kv_far, mixture_grad, mixture, logs, heads, layer_back, late, parts, 5
    )

    def blocks_of(array):
        return [array[i * rows : (i + 1) * rows] for i in range(per - 1)]

    if fused:
        qkv_grad, bias_grad, last_w_part, layer_out = last_gradients(
            x_turned,
            query_grad,
            key_grad,
            value_grad,
            others[0],
            layer_out,
            others[1],
            per,
        )
        bias_grad = bias_grad[0]
    else:
        key_grad = to_group_members(key_grad, blocks_of(others[0]), members, per)
        value_grad = to_group_members(value_grad, blocks_of(others[1]), members, per)
        qkv_grad = jnp.concatenate([query_grad, key_grad.astype(BF), value_grad.astype(BF)], axis=1)
        last_w_part = matmul(x_turned, qkv_grad).astype(BF)
        bias_grad = jnp.sum(qkv_grad.astype(F32), axis=0)
    last_w_grad = lax.psum_scatter(last_w_part, "seq", scatter_dimension=0, tiled=True).astype(F32)
    small = jnp.concatenate(
        [
            bias_grad[:cols].reshape(members, -1),
            bias_grad[2 * cols :].reshape(members, -1),
            inner_b_grad.reshape(members, -1),
        ]
        + [summed_rows[i].reshape(members, -1) for i in (3, 4, 5, 0, 1, 2)],
        axis=1,
    )
    small = jnp.pad(small, ((0, 0), (0, lines * 128 - small.shape[1])))
    input_grad, small, proj_w_grad = input_gradient(
        qkv_grad,
        first,
        attn_grad,
        small.reshape(members, lines, 128),
        proj_w_part,
        members,
        parts,
        6,
    )
    input_grad = after(input_grad, inner_w_grad).astype(F32).reshape(micro, seqs, length, width)
    layer_out = layer_out.reshape(micro, seqs, length, width)
    small = jnp.sum(small, axis=0).reshape(-1)
    pieces = []
    start = 0
    for size in sizes:
        pieces.append(small[start : start + size])
        start += size
    return (
        layer_out,
        input_grad,
        last_w_grad[:, :cols],
        pieces[0],
        last_w_grad[:, cols : 2 * cols],
        last_w_grad[:, 2 * cols : 3 * cols],
        pieces[1],
        proj_w_grad.T,
        pieces[3],
        pieces[4],
        pieces[5],
        inner_w_grad.astype(F32),
        pieces[2],
        outer_w_grad.astype(F32),
        pieces[6],
        pieces[7],
        pieces[8],
    )


def solution(mesh):
    tokens = P(None, None, "seq", None)
    rows_cols, cols_rows, both, seq = P("seq", "mp"), P("mp", "seq"), P(("mp", "seq")), P("seq")
    weights = (
        rows_cols,
        both,
        rows_cols,
        rows_cols,
        both,
        cols_rows,
        seq,
        seq,
        seq,
        rows_cols,
        both,
        cols_rows,
        seq,
        seq,
        seq,
    )
    return jax.shard_map(
        functools.partial(on_device, mesh.shape["seq"], mesh.shape["mp"]),
        mesh=mesh,
        in_specs=(tokens,) + weights + (tokens,),
        out_specs=(tokens, tokens) + weights,
        check_vma=False,
    )
```

```python
import functools
import math

import jax
import jax.numpy as jnp
from jax import lax
from jax.experimental import pallas as pl
from jax.experimental.pallas import tpu as pltpu
from jax.sharding import PartitionSpec as P

DH = 128
EPSILON = 1e-06
BF = jnp.bfloat16
F32 = jnp.float32
MESH = pl.DeviceIdType.MESH
ANY = pl.BlockSpec(memory_space=pl.ANY)
VMEM = pl.BlockSpec(memory_space=pltpu.VMEM)
MIB = 1 << 20


def matmul(left, right):
    return jnp.dot(left, right, preferred_element_type=F32)


def over_rows(left, right):
    return lax.dot_general(left, right, (((0,), (0,)), ((), ())), preferred_element_type=F32)


def over_cols(left, right):
    return lax.dot_general(left, right, (((1,), (1,)), ((), ())), preferred_element_type=F32)


def gelu_tanh(values):
    return jax.nn.gelu(values, approximate=True)


def square():
    me = lax.axis_index("mp")
    return me, me + 1 - 2 * lax.rem(me, 2), lax.rem(me + 2, 4), 3 - me


def greet(devices):
    barrier = pltpu.get_barrier_semaphore()
    for device in devices:
        pl.semaphore_signal(barrier, inc=1, device_id=device, device_id_type=MESH)
    pl.semaphore_wait(barrier, len(devices))


def sender(send_sem, recv_sem, start=True):
    def send(source, target, slot, device):
        copy = pltpu.make_async_remote_copy(
            src_ref=source,
            dst_ref=target,
            send_sem=send_sem.at[slot],
            recv_sem=recv_sem.at[slot],
            device_id=device,
            device_id_type=MESH,
        )
        if start:
            copy.start()
        return copy

    return send


class Exchange:
    def __init__(self, part_ref, landed, relay, send_sem, recv_sem):
        self.me, self.along_x, self.along_y, self.across = square()
        self.parts, self.landed, self.relay = part_ref, landed, relay
        self.send = sender(send_sem, recv_sem)
        self.copies = {}

    def part(self, owner, piece):
        return self.parts.at[row_place(owner, piece, 2 * self.parts.shape[2])]

    def ways(self, index):
        pair = (self.along_x, self.along_y)
        return pair if index % 2 == 0 else pair[::-1]

    def start(self, index, piece):
        near, _ = self.ways(index)
        for kind, owner in enumerate((self.across, near)):
            self.copies[index, kind] = self.send(
                self.part(owner, piece), self.landed.at[index, kind], 6 * index + kind, {"mp": near}
            )

    def pass_on(self, index, piece):
        _, far = self.ways(index)
        self.copies[index, 0].wait_recv()
        self.relay[index] = (
            self.part(far, piece)[...].astype(F32) + self.landed[index, 0].astype(F32)
        ).astype(BF)
        self.copies[index, 2] = self.send(
            self.relay.at[index], self.landed.at[index, 2], 6 * index + 2, {"mp": far}
        )

    def total(self, index, piece):
        self.copies[index, 1].wait_recv()
        self.copies[index, 2].wait_recv()
        return (
            self.part(self.me, piece)[...].astype(F32)
            + self.landed[index, 1].astype(F32)
            + self.landed[index, 2].astype(F32)
        )

    def share(self, index, source, target):
        near, far = self.ways(index)
        self.copies[index, 3] = self.send(source, target(self.me), 6 * index + 3, {"mp": near})
        self.copies[index, 4] = self.send(source, target(self.me), 6 * index + 4, {"mp": far})

    def forward(self, index, target):
        near, far = self.ways(index)
        self.copies[index, 3].wait_recv()
        self.copies[index, 5] = self.send(target(near), target(near), 6 * index + 5, {"mp": far})

    def arrived(self, indices):
        for index in indices:
            self.copies[index, 4].wait_recv()
            self.copies[index, 5].wait_recv()

    def sent(self):
        for copy in self.copies.values():
            copy.wait_send()

    def finish(self, count):
        self.arrived(range(count))
        self.sent()


def row_place(owner, piece, groups):
    half = groups // 2
    return piece // half, owner, piece % half


def planes(groups, per):
    index = lax.axis_index("seq")
    return [{"seq": lax.rem(index + step * per, groups * per)} for step in range(groups)]


def mean_of(values):
    return jnp.mean(values, axis=-1, keepdims=True)


def normed(values):
    centre = values - mean_of(values)
    inverse = lax.rsqrt(mean_of(centre * centre) + EPSILON)
    return centre * inverse, inverse


def norm_back(grad, normal, inverse, gain):
    inner = grad * gain
    return inverse * (inner - mean_of(inner) - normal * mean_of(inner * normal))


def turner(rows_of, turned_ref):
    width, rows = turned_ref.shape
    step = 256

    def fill(part):
        @pl.loop(0, width // (2 * step))
        def _(index):
            span = pl.ds(pl.multiple_of(part * (width // 2) + index * step, step), step)
            turned_ref[span] = rows_of(span).reshape(rows, step).T

    return fill


class Product:
    def __init__(self, exchange, turned, left_ref, weight_ref, weight, rows, load_sem, blocks=None):
        self.exchange, self.turned = exchange, turned
        self.left, self.weight, self.rows = left_ref, weight, rows
        self.left_loads = {}
        width = exchange.parts.shape[-1]
        self.step = min(512, width)
        self.count = width // self.step
        depth = left_ref.shape[-1]
        self.loads, slot = [], 0
        for index in range(self.count):
            span = pl.ds(index * self.step, self.step)
            place = (span, pl.ds(0, depth)) if turned else (pl.ds(0, depth), span)
            pairs = [(weight_ref.at[place], weight.at[place])] if blocks is None else blocks(index)
            copies = []
            for source, target in pairs:
                copy = pltpu.make_async_copy(source, target, load_sem.at[slot])
                copy.start()
                copies.append(copy)
                slot += 1
            self.loads.append(copies)

    def make(self, batch, first=False):
        _, _, half, piece_rows, _ = self.left.shape
        for _, piece in batch:
            if piece // half in self.left_loads:
                self.left_loads.pop(piece // half).wait()
        for place, (owner, piece) in enumerate(batch):
            self.rows[place * piece_rows : (place + 1) * piece_rows] = self.left[
                row_place(owner, piece, 2 * half)
            ]

        def columns(index):
            span = pl.ds(pl.multiple_of(index * self.step, self.step), self.step)
            if self.turned:
                product = over_cols(self.rows[...], self.weight[span])
            else:
                product = matmul(self.rows[...], self.weight[:, span])
            product = product.astype(BF)
            for place, (owner, piece) in enumerate(batch):
                self.exchange.part(owner, piece)[:, span] = product[
                    place * piece_rows : (place + 1) * piece_rows
                ]

        if first:
            for index in range(self.count):
                for copy in self.loads[index]:
                    copy.wait()
                columns(index)
        else:
            pl.loop(0, self.count)(columns)


def run_pieces(exchange, order, work, product=None, fill=None):
    groups = len(order)
    places = list(enumerate(order))
    half = groups // 2
    first, second = places[:half], places[half:]

    def make(half_places, near):
        if product is None:
            return
        batch = []
        for index, piece in half_places:
            ways = exchange.ways(index)
            owners = (exchange.across, ways[0]) if near else (ways[1], exchange.me)
            batch += [(owner, piece) for owner in owners]
        product.make(batch, near and half_places is first)

    make(first, True)
    for index, piece in first:
        exchange.start(index, piece)
    make(first, False)
    if fill is not None:
        fill(0)
    for index, piece in first:
        exchange.pass_on(index, piece)
    make(second, True)
    for index, piece in second:
        exchange.start(index, piece)
    make(second, False)
    if fill is not None:
        fill(1)
    for index, piece in first:
        work(index, piece, exchange.total(index, piece))
    for index, piece in second:
        exchange.pass_on(index, piece)
    return first, second


def first_norm_kernel(
    groups, part_ref, x_ref, all_ref, rows_ref, low_ref, normal_ref, inverse_ref, turned_ref,
    landed, relay, ready, send_sem, recv_sem, local_sem,
):
    exchange = Exchange(part_ref, landed, relay, send_sem, recv_sem)
    greet([{"mp": exchange.along_x}, {"mp": exchange.along_y}])
    local = []

    def target(piece):
        return lambda device: low_ref.at[row_place(device, piece, groups)]

    def work(index, piece, total):
        values = x_ref[piece].astype(F32) + total + rows_ref[0:1]
        normal, inverse = normed(values)
        normal_ref[piece] = normal
        inverse_ref[piece] = inverse
        ready[index] = (normal * rows_ref[1:2] + rows_ref[2:3]).astype(BF)
        exchange.share(index, ready.at[index], target(piece))
        copy = pltpu.make_async_copy(
            ready.at[index], target(piece)(exchange.me), local_sem.at[index]
        )
        copy.start()
        local.append(copy)

    first, second = run_pieces(
        exchange, range(groups), work, None, turner(lambda span: all_ref[:, span], turned_ref)
    )
    for index, piece in first:
        exchange.forward(index, target(piece))
    for index, piece in second:
        work(index, piece, exchange.total(index, piece))
    for index, piece in second:
        exchange.forward(index, target(piece))
    exchange.finish(groups)
    for copy in local:
        copy.wait()


def half_sum_kernel(
    groups, members, left_ref, weight_ref, first_ref, total_ref, turned_ref, weight_out, first_turned_ref,
    landed, relay, part_ref, weight, rows, load_sem, put_sem, send_sem, recv_sem,
):
    exchange = Exchange(part_ref, landed, relay, send_sem, recv_sem)
    width, depth = weight.shape
    narrow, half = width // members, depth // 2
    apart = weight_ref.shape[1] - half

    def blocks(index):
        step = min(512, width)
        for place in range(index * step // narrow, (index + 1) * step // narrow):
            for part in range(2):
                yield (
                    weight_ref.at[pl.ds((2 * place + part) * narrow, narrow), pl.ds(apart, half)],
                    weight.at[pl.ds(place * narrow, narrow), pl.ds(part * half, half)],
                )

    product = Product(exchange, True, left_ref, weight_ref, weight, rows, load_sem, blocks)
    greet([{"mp": exchange.along_x}, {"mp": exchange.along_y}])

    def work(index, piece, total):
        total_ref[piece] = total

    turn_left = turner(lambda span: left_ref[:, :, :, :, span], turned_ref)
    turn_first = turner(lambda span: first_ref[:, span], first_turned_ref)

    def fill(part):
        turn_left(part)
        turn_first(part)

    _, second = run_pieces(exchange, range(groups), work, product, fill)
    put = pltpu.make_async_copy(weight, weight_out, put_sem)
    put.start()
    for index, piece in second:
        work(index, piece, exchange.total(index, piece))
    put.wait()
    exchange.sent()


def second_norm_kernel(
    groups, per, left_hbm, weight_ref, turned_hbm, done_hbm,
    normal_hbm, cotan_ref, rows_ref,
    low_hbm, grad_hbm, back_ref, sums_ref, weight_grad_ref,
    landed, relay, part_ref, weight, rows, load_sem,
    ready, layer, cotan_in, turned_ref, whole, left_ref, done_ref, normal_ref, low_ref, grad_ref,
    put_sem, in_sem, out_sem,
    send_sem, recv_sem, local_sem,
):
    exchange = Exchange(part_ref, landed, relay, send_sem, recv_sem)

    def moved(source, target, sem):
        copy = pltpu.make_async_copy(source, target, sem)
        copy.start()
        return copy

    left_loads = {0: moved(left_hbm.at[0], left_ref.at[0], in_sem.at[0])}
    product = Product(exchange, True, left_ref, weight_ref, weight, rows, load_sem)
    members = groups * per
    narrow = weight.shape[0] // members
    left_loads[1] = moved(left_hbm.at[1], left_ref.at[1], in_sem.at[1])
    product.left_loads = left_loads
    early = [
        moved(cotan_ref.at[0], cotan_in.at[0], in_sem.at[2]),
        moved(normal_hbm, normal_ref, in_sem.at[3]),
        moved(done_hbm, done_ref, in_sem.at[4]),
    ]
    load_turned = moved(turned_hbm, turned_ref, in_sem.at[5])
    outward = []
    peers = planes(groups, per)
    greet([{"mp": exchange.along_x}, {"mp": exchange.along_y}] + peers[1:])
    base = 6 * groups
    arriving = {
        step: exchange.send(cotan_ref.at[step], cotan_in.at[step], base + step, peers[step])
        for step in range(1, groups)
    }
    leaving, local = [], []
    sums_ref[...] = jnp.zeros_like(sums_ref)

    def target(piece):
        return lambda device: low_ref.at[row_place(device, piece, groups)]

    def keep(source, place, slot):
        copy = pltpu.make_async_copy(source, place, local_sem.at[slot])
        copy.start()
        local.append(copy)

    def work(index, piece, total):
        while early:
            early.pop().wait()
        gain_one, shift_one, bias = rows_ref[0:1], rows_ref[1:2], rows_ref[2:3]
        gain, shift = rows_ref[3:4], rows_ref[4:5]
        done = done_ref[piece]
        total = jnp.concatenate(
            [
                half[:, place * narrow : (place + 1) * narrow]
                for place in range(members)
                for half in (done, total)
            ],
            axis=1,
        )
        values = normal_ref[piece] * gain_one + shift_one + total + bias
        normal, inverse = normed(values)
        layer[index] = (normal * gain + shift).astype(BF)
        if piece == 0:
            keep(layer.at[index], back_ref.at[0], groups)
            cotan = cotan_in[0].astype(F32)
        else:
            leaving.append(
                exchange.send(
                    layer.at[index], back_ref.at[piece], base + groups + piece, peers[groups - piece]
                )
            )
            arriving[piece].wait_recv()
            cotan = cotan_in[piece].astype(F32)
        grad = norm_back(cotan, normal, inverse, gain)
        grad_ref[piece] = grad
        ready[index] = grad.astype(BF)
        exchange.share(index, ready.at[index], target(piece))
        keep(ready.at[index], target(piece)(exchange.me), index)
        normal_ref[piece] = normal
        outward.append(moved(grad_ref.at[piece], grad_hbm.at[piece], out_sem.at[2 + index]))

    first, second = run_pieces(exchange, range(groups), work, product)
    for index, piece in first:
        exchange.forward(index, target(piece))
    for index, piece in second:
        work(index, piece, exchange.total(index, piece))
    step = 512
    count = whole.shape[1] // step
    depth = turned_ref.shape[1] // 2

    def columns(index):
        return pl.ds(pl.multiple_of(index * step, step), step)

    def put(index):
        span = columns(index)
        return pltpu.make_async_copy(
            whole.at[:, span], weight_grad_ref.at[:, span], put_sem.at[index]
        )

    def product_of(part, span):
        low = low_ref[part, :, :, :, span].reshape(depth, step)
        return matmul(turned_ref[:, part * depth : (part + 1) * depth], low)

    exchange.arrived([index for index, _ in first])
    load_turned.wait()
    for copy in local[: len(first) + 1]:
        copy.wait()
    outward.append(moved(low_ref.at[0], low_hbm.at[0], out_sem.at[0]))

    def first_product(start, stop):
        @pl.loop(start, stop)
        def _(index):
            span = columns(index)
            whole[:, span] = product_of(0, span).astype(BF)

    for _, piece in first + second:
        cotan = cotan_in[piece].astype(F32)
        sums_ref[0:1] += jnp.sum(grad_ref[piece], axis=0, keepdims=True)
        sums_ref[1:2] += jnp.sum(cotan * normal_ref[piece], axis=0, keepdims=True)
        sums_ref[2:3] += jnp.sum(cotan, axis=0, keepdims=True)

    share_out = count // (2 * len(second))
    done = count // 2
    first_product(0, done)
    for index, piece in second:
        exchange.forward(index, target(piece))
        first_product(done, done + share_out)
        done += share_out
    exchange.arrived([index for index, _ in second])
    for copy in local[len(first) + 1 :]:
        copy.wait()
    outward.append(moved(low_ref.at[1], low_hbm.at[1], out_sem.at[1]))

    @pl.loop(0, count)
    def _(index):
        span = columns(index)
        whole[:, span] = (product_of(1, span) + whole[:, span].astype(F32)).astype(BF)
        put(index).start()

    exchange.sent()
    for copy in outward:
        copy.wait()
    for copy in leaving:
        copy.wait()
    for copy in arriving.values():
        copy.wait_send()
    for index in range(count):
        put(index).wait()


def first_back_kernel(
    groups, left_ref, weight_ref, grad_ref, normal_ref, inverse_ref, sums_in_ref, rows_ref,
    low_ref, out_ref, sums_ref,
    landed, relay, ready, own_sums, part_ref, weight, rows, load_sem,
    send_sem, recv_sem, local_sem,
):
    exchange = Exchange(part_ref, landed, relay, send_sem, recv_sem)
    product = Product(exchange, True, left_ref, weight_ref, weight, rows, load_sem)
    greet([{"mp": exchange.along_x}, {"mp": exchange.along_y}, {"mp": exchange.across}])
    local = []
    own_sums[...] = sums_in_ref[...]

    def target(piece):
        return lambda device: low_ref.at[row_place(device, piece, groups)]

    def keep(source, place, slot):
        copy = pltpu.make_async_copy(source, place, local_sem.at[slot])
        copy.start()
        local.append(copy)

    def work(index, piece, total):
        grad = total + grad_ref[piece]
        normal = normal_ref[piece]
        moved = norm_back(grad, normal, inverse_ref[piece], rows_ref[0:1])
        out_ref[piece] = moved
        ready[index] = moved.astype(BF)
        exchange.share(index, ready.at[index], target(piece))
        keep(ready.at[index], target(piece)(exchange.me), index)
        own_sums[3:4] += jnp.sum(moved, axis=0, keepdims=True)
        own_sums[4:5] += jnp.sum(grad * normal, axis=0, keepdims=True)
        own_sums[5:6] += jnp.sum(grad, axis=0, keepdims=True)

    first, second = run_pieces(exchange, range(groups), work, product)
    for index, piece in first:
        exchange.forward(index, target(piece))
    for index, piece in second:
        work(index, piece, exchange.total(index, piece))
    others = [
        exchange.send(own_sums, sums_ref.at[exchange.me], 6 * groups + slot, {"mp": device})
        for slot, device in enumerate((exchange.along_x, exchange.along_y, exchange.across))
    ]
    keep(own_sums, sums_ref.at[exchange.me], groups)
    for index, piece in second:
        exchange.forward(index, target(piece))
    exchange.finish(groups)
    for copy in others:
        copy.wait()
    for copy in local:
        copy.wait()


def input_order(groups):
    return list(range(1, groups - 1)) + [0, groups - 1]


class LineSum:
    def __init__(
        self, groups, per, blocks_ref, own, other, inbox, line_send, line_recv, pair_send, pair_recv, pair_local
    ):
        self.groups, self.per = groups, per
        here = lax.axis_index("seq")
        self.group, self.place = here // per, lax.rem(here, per)
        self.own, self.other, self.inbox = own, other, inbox
        self.line_send, self.line_recv = line_send, line_recv
        sibling = {"seq": self.group * per + 1 - self.place}
        send = sender(pair_send, pair_recv)
        self.order = sorted(range(groups), key=lambda index: -abs(2 * index - groups + 1))
        self.away, self.near = {}, {}
        for index in self.order:
            self.away[index] = send(
                blocks_ref.at[index, 1 - self.place], other.at[index], index, sibling
            )
            copy = pltpu.make_async_copy(
                blocks_ref.at[index, self.place], own.at[index], pair_local.at[index]
            )
            copy.start()
            self.near[index] = copy

    def seen(self, stream):
        return self.group if stream == 0 else self.groups - 1 - self.group

    def copy(self, stream, to):
        group = to if stream == 0 else self.groups - 1 - to
        ahead = self.group + (1 if stream == 0 else -1)
        slot = stream * self.groups + to
        return pltpu.make_async_remote_copy(
            src_ref=self.own.at[group],
            dst_ref=self.inbox.at[stream, to - 1],
            send_sem=self.line_send.at[slot],
            recv_sem=self.line_recv.at[slot],
            device_id={"seq": ahead * self.per + self.place},
            device_id_type=MESH,
        )

    def first_send(self, to):
        for stream in range(2):

            @pl.when(self.seen(stream) == 0)
            def _(stream=stream):
                self.copy(stream, to).start()

    def pair_sums(self, indices):
        for index in indices:
            self.near[index].wait()
            self.away[index].wait_recv()
            self.own[index] = (
                self.own[index].astype(F32) + self.other[index].astype(F32)
            ).astype(BF)

    def begin(self):
        self.pair_sums(self.order[:2])
        self.first_send(self.groups - 1)

    def go_on(self):
        self.pair_sums(self.order[2:])
        self.first_send(self.groups - 2)

    def hop(self, time):
        if self.groups - 2 - time > 0:
            for stream in range(2):

                @pl.when(self.seen(stream) == 0)
                def _(stream=stream):
                    self.copy(stream, self.groups - time).wait_send()

            self.first_send(self.groups - 2 - time)
        for stream in range(2):
            seen = self.seen(stream)

            @pl.when((seen >= 1) & (seen <= time))
            def _(stream=stream, seen=seen):
                to = self.groups - 1 + seen - time
                group = to if stream == 0 else self.groups - 1 - to
                self.copy(stream, to).wait_recv()
                self.own[group] = (
                    self.own[group].astype(F32) + self.inbox[stream, to - 1].astype(F32)
                ).astype(BF)
                self.copy(stream, to).start()

    def end(self, out_ref):
        out_ref[...] = self.own[self.group].astype(F32)
        for stream in range(2):
            seen = self.seen(stream)

            @pl.when(seen >= 1)
            def _(stream=stream, seen=seen):
                self.copy(stream, seen).wait_recv()
                out_ref[...] += self.inbox[stream, seen - 1].astype(F32)

        for stream in range(2):
            for to in range(1, self.groups):

                seen = self.seen(stream)
                waited = (seen == 0) & (to > 2)

                @pl.when((seen < to) & jnp.logical_not(waited))
                def _(stream=stream, to=to):
                    self.copy(stream, to).wait_send()

        for copy in self.away.values():
            copy.wait_send()


def input_kernel(
    groups, per, left_ref, weight_ref, grad_ref, small_ref, blocks_ref,
    all_ref, small_out, block_out,
    landed, relay, ready, back, part_ref, weight, rows, load_sem,
    own, other, inbox, line_send, line_recv, pair_send, pair_recv, pair_local,
    send_sem, recv_sem, local_sem,
):
    exchange = Exchange(part_ref, landed, relay, send_sem, recv_sem)
    product = Product(exchange, True, left_ref, weight_ref, weight, rows, load_sem)
    peers = planes(groups, per)
    members = groups * per
    here = lax.axis_index("seq")
    group = here // per
    devices = [{"seq": lax.rem(here + step, members)} for step in range(1, members)]
    greet([{"mp": exchange.along_x}, {"mp": exchange.along_y}] + devices)
    line = LineSum(
        groups, per, blocks_ref, own, other, inbox,
        line_send, line_recv, pair_send, pair_recv, pair_local,
    )
    base = 6 * groups
    small = [
        exchange.send(
            small_ref.at[lax.rem(here + step, members)],
            small_out.at[here],
            base + groups + step,
            devices[step - 1],
        )
        for step in range(1, members)
    ]
    crossing, local = {}, []

    def keep(source, place, slot):
        copy = pltpu.make_async_copy(source, place, local_sem.at[slot])
        copy.start()
        local.append(copy)

    keep(small_ref.at[here], small_out.at[here], groups)

    def target(piece):
        sequence = lax.rem(group + piece, groups)
        return lambda device: all_ref.at[sequence, device]

    def work(index, piece, total):
        ready[piece] = (total + grad_ref[piece]).astype(BF)
        if piece > 0:
            crossing[piece] = exchange.send(
                ready.at[piece], back.at[piece], base + piece, peers[groups - piece]
            )

    def share(index, piece):
        source = ready.at[0]
        if piece > 0:
            crossing[piece].wait_recv()
            source = back.at[piece]
        exchange.share(index, source, target(piece))
        keep(source, target(piece)(exchange.me), index)

    def fill(part):
        if part == 0:
            line.begin()
        else:
            line.go_on()

    first, second = run_pieces(exchange, input_order(groups), work, product, fill)
    for index, piece in second:
        work(index, piece, exchange.total(index, piece))
    here_first = [place for place in second if place[1] == 0]
    late = [place for place in second if place[1] > 0]
    line.hop(1)
    for index, piece in here_first + first:
        share(index, piece)
    for index, piece in here_first:
        exchange.forward(index, target(piece))
    for time in range(2, groups - 1):
        line.hop(time)
    for index, piece in late:
        share(index, piece)
    for index, piece in first + late:
        exchange.forward(index, target(piece))
    line.end(block_out)
    exchange.finish(groups)
    for copy in small:
        copy.wait()
    for copy in crossing.values():
        copy.wait_send()
    for copy in local:
        copy.wait()


def product_scratch(parts, groups, piece, width, depth, turned, loads=1):
    return [
        pltpu.VMEM((2, parts, groups // 2, piece, width), BF),
        pltpu.VMEM((width, depth) if turned else (depth, width), BF),
        pltpu.VMEM((groups * piece, depth), BF),
        pltpu.SemaphoreType.DMA((max(width // 512, loads),)),
    ]


def exchange_call(kernel, ident, operands, results, sums, scratch, extra, outside=(), local=True):
    groups, piece, width = sums
    return pl.pallas_call(
        kernel,
        out_shape=tuple(jax.ShapeDtypeStruct(shape, dtype) for shape, dtype, _ in results),
        in_specs=[ANY if place in outside else VMEM for place in range(len(operands))],
        out_specs=tuple(spec for _, _, spec in results),
        scratch_shapes=[
            pltpu.VMEM((groups, 3, piece, width), BF),
            pltpu.VMEM((groups, piece, width), BF),
        ]
        + scratch
        + [
            pltpu.SemaphoreType.DMA((6 * groups + extra,)),
            pltpu.SemaphoreType.DMA((6 * groups + extra,)),
        ]
        + ([pltpu.SemaphoreType.DMA((groups + 1,))] if local else []),
        compiler_params=pltpu.CompilerParams(
            collective_id=ident, has_side_effects=True, vmem_limit_bytes=58 * MIB
        ),
        cost_estimate=pl.CostEstimate(flops=0, bytes_accessed=200 * MIB, transcendentals=0),
        name=f"exchange_{ident}",
    )(*operands)


def first_norm(part, x_part, x_rows, rows, parts, ident):
    groups, piece, width = x_part.shape
    half = groups // 2
    if parts != 4:
        total = lax.psum_scatter(part, "mp", scatter_dimension=0, tiled=True).astype(F32)
        values = x_part.astype(F32) + total.reshape(x_part.shape) + rows[0]
        normal, inverse = normed(values)
        low = lax.all_gather((normal * rows[1] + rows[2]).astype(BF), "mp", axis=0)
        return low, normal, inverse, x_rows.T
    return exchange_call(
        functools.partial(first_norm_kernel, groups),
        ident,
        (part.reshape(2, parts, half, piece, width), x_part, x_rows, rows),
        [
            ((2, parts, half, piece, width), BF, ANY),
            ((groups, piece, width), F32, VMEM),
            ((groups, piece, 1), F32, VMEM),
            ((width, x_rows.shape[0]), BF, VMEM),
        ],
        (groups, piece, width),
        [pltpu.VMEM((groups, piece, width), BF)],
        0,
    )


def half_sum(left, second, first, groups, piece, members, parts, ident):
    rows, depth = left.shape
    width = second.shape[0] // 2
    return exchange_call(
        functools.partial(half_sum_kernel, groups, members),
        ident,
        (left.reshape(2, parts, groups // 2, piece, depth), second, first),
        [
            ((groups, piece, width), F32, VMEM),
            ((depth, rows), BF, VMEM),
            ((width, depth), BF, ANY),
            (first.shape[::-1], BF, VMEM),
        ],
        (groups, piece, width),
        product_scratch(parts, groups, piece, width, depth, True, 2 * members)
        + [pltpu.SemaphoreType.DMA],
        0,
        (1,),
        False,
    )


def second_norm(left, weight, turned, done, normal, cotan, rows, members, parts, ident):
    groups, piece, width = normal.shape
    depth = left.shape[-1]
    half = groups // 2
    if parts != 4:
        part = over_cols(left, weight).astype(BF)
        total = lax.psum_scatter(part, "mp", scatter_dimension=0, tiled=True).astype(F32)
        values = normal * rows[0] + rows[1] + total.reshape(normal.shape) + rows[2]
        normal, inverse = normed(values)
        layer = (normal * rows[3] + rows[4]).astype(BF)
        back = jnp.stack(swap_blocks(layer, members, -1))
        cotan = jnp.stack(swap_blocks(cotan, members, 1)).astype(F32)
        grad = norm_back(cotan, normal, inverse, rows[3])
        sums = [jnp.sum(array, axis=(0, 1)) for array in (grad, cotan * normal, cotan)]
        sums = jnp.stack(sums + [jnp.zeros_like(sums[0])] * 5)
        low = lax.all_gather(grad.astype(BF), "mp", axis=0)
        return low, grad, back, sums, over_rows(left, low.reshape(-1, width)).astype(BF)
    block = pltpu.VMEM((groups, piece, width), BF)
    return exchange_call(
        functools.partial(second_norm_kernel, groups, members // groups),
        ident,
        (
            left.reshape(2, parts, half, piece, depth),
            weight, turned, done, normal, cotan, rows,
        ),
        [
            ((2, parts, half, piece, width), BF, ANY),
            ((groups, piece, width), F32, ANY),
            ((groups, piece, width), BF, ANY),
            ((8, width), F32, VMEM),
            ((depth, width), BF, ANY),
        ],
        (groups, piece, width // 2),
        product_scratch(parts, groups, piece, width // 2, depth, True)
        + [
            block,
            block,
            block,
            pltpu.VMEM(turned.shape, BF),
            pltpu.VMEM((depth, width), BF),
            pltpu.VMEM((2, parts, half, piece, depth), BF),
            pltpu.VMEM(done.shape, F32),
            pltpu.VMEM(normal.shape, F32),
            pltpu.VMEM((2, parts, half, piece, width), BF),
            pltpu.VMEM((groups, piece, width), F32),
            pltpu.SemaphoreType.DMA((width // 256,)),
            pltpu.SemaphoreType.DMA((6,)),
            pltpu.SemaphoreType.DMA((2 + groups,)),
        ],
        2 * groups,
        (0, 1, 2, 3, 4, 5),
    )


def first_back(left, weight, grad, normal, inverse, sums, rows, parts, ident):
    groups, piece, width = normal.shape
    depth = left.shape[-1]
    if parts != 4:
        part = over_cols(left, weight[:, :depth]).astype(BF)
        total = lax.psum_scatter(part, "mp", scatter_dimension=0, tiled=True).astype(F32)
        grad = total.reshape(normal.shape) + grad
        moved = norm_back(grad, normal, inverse, rows[0])
        more = [jnp.sum(array, axis=(0, 1)) for array in (moved, grad * normal, grad)]
        sums = sums.at[3:6].add(jnp.stack(more))
        return (
            lax.all_gather(moved.astype(BF), "mp", axis=0),
            moved,
            lax.all_gather(sums, "mp", axis=0),
        )
    half = groups // 2
    return exchange_call(
        functools.partial(first_back_kernel, groups),
        ident,
        (
            left.reshape(2, parts, half, piece, depth), weight,
            grad, normal, inverse, sums, rows,
        ),
        [
            ((2, parts, half, piece, width), BF, ANY),
            ((groups, piece, width), F32, VMEM),
            ((parts, 8, width), F32, VMEM),
        ],
        (groups, piece, width),
        [pltpu.VMEM((groups, piece, width), BF), pltpu.VMEM((8, width), F32)]
        + product_scratch(parts, groups, piece, width, depth, True),
        3,
        (1,),
    )


def input_gradient(left, weight, grad, small, part, members, parts, ident):
    groups, piece, width = grad.shape
    depth = left.shape[-1]
    if parts != 4:
        summed = lax.psum_scatter(part, "seq", scatter_dimension=0, tiled=True).astype(F32)
        part = over_cols(left, weight[:, :depth]).astype(BF)
        total = lax.psum_scatter(part, "mp", scatter_dimension=0, tiled=True).astype(F32)
        ready = (total.reshape(grad.shape) + grad).astype(BF)
        back = jnp.stack(swap_blocks(ready, members, -1))
        back = jnp.roll(back, lax.axis_index("seq") // (members // groups), axis=0)
        return lax.all_gather(back, "mp", axis=1), lax.all_to_all(small, "seq", 0, 0), summed
    per = members // groups
    block = (part.shape[0] // members, part.shape[1])
    return exchange_call(
        functools.partial(input_kernel, groups, members // groups),
        ident,
        (left.reshape(2, parts, groups // 2, piece, depth), weight, grad, small, part.reshape(groups, per, *block)),
        [
            ((groups, parts, piece, width), BF, ANY),
            (small.shape, F32, VMEM),
            (block, F32, VMEM),
        ],
        (groups, piece, width),
        [pltpu.VMEM((groups, piece, width), BF)] * 2
        + product_scratch(parts, groups, piece, width, depth, True)
        + [
            pltpu.VMEM((groups, *block), BF),
            pltpu.VMEM((groups, *block), BF),
            pltpu.VMEM((2, groups - 1, *block), BF),
        ]
        + [pltpu.SemaphoreType.DMA((2 * groups,))] * 2
        + [pltpu.SemaphoreType.DMA((groups,))] * 3,
        groups + members,
        (1, 4),
    )


def share_kernel(own_ref, all_ref, send_sem, recv_sem, local_sem):
    me, along_x, along_y, _ = square()
    to_x, to_y = {"mp": along_x}, {"mp": along_y}
    greet([to_x, to_y])
    send = sender(send_sem, recv_sem)
    half = own_ref.shape[0] // 2
    upper, lower = pl.ds(0, half), pl.ds(half, half)
    copies = [
        send(own_ref.at[upper], all_ref.at[0, me], 0, to_x),
        send(own_ref.at[lower], all_ref.at[1, me], 1, to_y),
        send(own_ref.at[lower], all_ref.at[1, me], 2, to_x),
        send(own_ref.at[upper], all_ref.at[0, me], 3, to_y),
    ]
    local = [
        pltpu.make_async_copy(own_ref.at[upper], all_ref.at[0, me], local_sem.at[0]),
        pltpu.make_async_copy(own_ref.at[lower], all_ref.at[1, me], local_sem.at[1]),
    ]
    for copy in local:
        copy.start()
    copies[0].wait_recv()
    copies.append(send(all_ref.at[0, along_x], all_ref.at[0, along_x], 4, to_y))
    copies[1].wait_recv()
    copies.append(send(all_ref.at[1, along_y], all_ref.at[1, along_y], 5, to_x))
    for copy in copies[2:]:
        copy.wait_recv()
    for copy in copies:
        copy.wait_send()
    for copy in local:
        copy.wait()


def share_over_mp(own, parts, ident):
    if parts != 4:
        return lax.all_gather(own, "mp", axis=0)
    return pl.pallas_call(
        share_kernel,
        out_shape=jax.ShapeDtypeStruct((2, parts, own.shape[0] // 2, own.shape[1]), own.dtype),
        in_specs=[ANY],
        out_specs=ANY,
        scratch_shapes=[
            pltpu.SemaphoreType.DMA((6,)),
            pltpu.SemaphoreType.DMA((6,)),
            pltpu.SemaphoreType.DMA((2,)),
        ],
        compiler_params=pltpu.CompilerParams(collective_id=ident, has_side_effects=True),
        cost_estimate=pl.CostEstimate(flops=0, bytes_accessed=100 * MIB, transcendentals=0),
        name=f"share_over_mp_{ident}",
    )(own)


def swap_kernel(
    groups, per, sign, block_ref, small_ref, out_ref, small_out, send_sem, recv_sem, local_sem
):
    members = groups * per
    index = lax.axis_index("seq")
    devices = [{"seq": lax.rem(index + step, members)} for step in range(1, members)]
    greet(devices)
    send = sender(send_sem, recv_sem)
    copies = []
    for step in range(1, groups):
        ahead = step if sign > 0 else groups - step
        source = block_ref.at[step]
        copies.append(send(source, out_ref.at[step], step, devices[ahead * per - 1]))
    for step in range(1, members):
        target = lax.rem(index + step, members)
        copies.append(
            send(small_ref.at[target], small_out.at[index], groups + step, devices[step - 1])
        )
    locals_ = [
        pltpu.make_async_copy(block_ref.at[0], out_ref.at[0], local_sem.at[0]),
        pltpu.make_async_copy(small_ref.at[index], small_out.at[index], local_sem.at[1]),
    ]
    for local in locals_:
        local.start()
    for local in locals_:
        local.wait()
    for copy in copies:
        copy.wait()


def shift_pairs(members, ahead):
    return [(index, (index + ahead) % members) for index in range(members)]


def swap_blocks(blocks, members, sign):
    groups = blocks.shape[0]
    per = members // groups
    arrived = [blocks[0]]
    for step in range(1, groups):
        pairs = shift_pairs(members, sign * step * per)
        arrived.append(lax.ppermute(blocks[step], "seq", pairs))
    return arrived


def swap_groups(blocks, small, members, parts, sign, ident):
    groups = blocks.shape[0]
    per = members // groups
    if parts != 4:
        return jnp.stack(swap_blocks(blocks, members, sign)), lax.all_to_all(small, "seq", 0, 0)
    return pl.pallas_call(
        functools.partial(swap_kernel, groups, per, sign),
        out_shape=(
            jax.ShapeDtypeStruct(blocks.shape, blocks.dtype),
            jax.ShapeDtypeStruct(small.shape, small.dtype),
        ),
        in_specs=[ANY, ANY],
        out_specs=(ANY, ANY),
        scratch_shapes=[
            pltpu.SemaphoreType.DMA((groups + members,)),
            pltpu.SemaphoreType.DMA((groups + members,)),
            pltpu.SemaphoreType.DMA((2,)),
        ],
        compiler_params=pltpu.CompilerParams(collective_id=ident, has_side_effects=True),
        cost_estimate=pl.CostEstimate(flops=0, bytes_accessed=60 * MIB, transcendentals=0),
        name=f"swap_groups_{ident}",
    )(blocks, small)


def score_block(keys, queries):
    return lax.dot_general(keys, queries, (((1,), (1,)), ((), ())), preferred_element_type=F32)


def attend_kernel(
    query_ref, key_ref, value_ref, key_far_ref, value_far_ref, mix_ref, low_ref, log_ref, turned
):
    rows = key_ref.shape[0]

    @pl.when(pl.program_id(1) == 0)
    def _():
        turned[:, :rows] = value_ref[...].T
        turned[:, rows:] = value_far_ref[...].T

    scale = DH ** (-0.5)
    near = score_block(key_ref[...], query_ref[...])
    far = score_block(key_far_ref[...], query_ref[...])
    highest = jnp.maximum(
        jnp.max(near, axis=0, keepdims=True), jnp.max(far, axis=0, keepdims=True)
    )
    near = jnp.exp((near - highest) * scale)
    far = jnp.exp((far - highest) * scale)
    total = jnp.sum(near, axis=0, keepdims=True) + jnp.sum(far, axis=0, keepdims=True)
    mix = jnp.dot(turned[:, :rows], near.astype(BF), preferred_element_type=F32)
    mix += jnp.dot(turned[:, rows:], far.astype(BF), preferred_element_type=F32)
    mix = (mix / total).T
    mix_ref[...] = mix
    low_ref[...] = mix.astype(BF)
    log_ref[0] = highest * scale + jnp.log(total)


def attend(qkv, kv_far, heads):
    rows, cols = qkv.shape[0], heads * DH
    away = kv_far.shape[0]
    block = min(512, rows)

    def tile(offset):
        return pl.BlockSpec((block, DH), lambda h, i: (i, offset + h))

    def long(count, offset):
        return pl.BlockSpec((count, DH), lambda h, i: (0, offset + h))

    return pl.pallas_call(
        attend_kernel,
        grid=(heads, rows // block),
        out_shape=(
            jax.ShapeDtypeStruct((rows, cols), F32),
            jax.ShapeDtypeStruct((rows, cols), BF),
            jax.ShapeDtypeStruct((heads, 1, rows), F32),
        ),
        in_specs=[
            tile(0),
            long(rows, heads),
            long(rows, 2 * heads),
            long(away, 0),
            long(away, heads),
        ],
        out_specs=(tile(0), tile(0), pl.BlockSpec((1, 1, block), lambda h, i: (h, 0, i))),
        scratch_shapes=[pltpu.VMEM((DH, rows + away), BF)],
        compiler_params=pltpu.CompilerParams(vmem_limit_bytes=52 * MIB),
        cost_estimate=pl.CostEstimate(
            flops=8 * rows * (rows + away) * cols,
            bytes_accessed=20 * rows * cols,
            transcendentals=rows * (rows + away) * heads,
        ),
        name="attend",
    )(qkv, qkv, qkv, kv_far, kv_far)


def share_meanwhile(
    now, count, pieces, back_ref, all_ref, send_sem, recv_sem, local_sem, also=()
):
    me, along_x, along_y, _ = square()
    send = sender(send_sem, recv_sem, False)
    near, far, passed, local = [], [], [], []
    for index, piece in enumerate(pieces):
        ways = (along_x, along_y) if index % 2 == 0 else (along_y, along_x)
        block, own = back_ref.at[piece], all_ref.at[index, me]
        relayed = all_ref.at[index, ways[0]]
        near.append(send(block, own, 3 * index, {"mp": ways[0]}))
        far.append(send(block, own, 3 * index + 1, {"mp": ways[1]}))
        passed.append(send(relayed, relayed, 3 * index + 2, {"mp": ways[1]}))
        local.append(pltpu.make_async_copy(block, own, local_sem.at[index]))

    @pl.when(now == 0)
    def _():
        greet([{"mp": along_x}, {"mp": along_y}, *also])
        for copy in near + far + local:
            copy.start()

    @pl.when(now == count // 4)
    def _():
        for first, second in zip(near, passed):
            first.wait_recv()
            second.start()

    def finish():
        @pl.when(now == count - 1)
        def _():
            for copy in far + passed:
                copy.wait_recv()
            for copy in near + far + passed:
                copy.wait_send()
            for copy in local:
                copy.wait()

    return finish


def meanwhile_scratch(pieces):
    return [
        pltpu.SemaphoreType.DMA((3 * len(pieces),)),
        pltpu.SemaphoreType.DMA((3 * len(pieces),)),
        pltpu.SemaphoreType.DMA((len(pieces),)),
    ]


def feed_back_kernel(
    pieces, members, low_ref, weight_ref, more_ref, pre_ref, turned_ref, back_ref,
    grad_ref, sums_ref, weight_grad_ref, all_ref, send_sem, recv_sem, local_sem,
):
    now, count = pl.program_id(0), pl.num_programs(0)
    finish = share_meanwhile(now, count, pieces, back_ref, all_ref, send_sem, recv_sem, local_sem)
    value = pre_ref[...]
    root = (2 / math.pi) ** 0.5
    square_of = value * value
    bent = jnp.tanh(root * value * (1 + 0.044715 * square_of))
    slope = 0.5 * (1 + bent) + (0.5 * root) * value * (1 - bent * bent) * (
        1 + 3 * 0.044715 * square_of
    )
    narrow = weight_ref.shape[0] // members
    weight = jnp.concatenate(
        [
            half[place * narrow : (place + 1) * narrow]
            for place in range(members)
            for half in (weight_ref, more_ref)
        ],
        axis=0,
    )
    grad = (matmul(low_ref[...], weight) * slope).astype(BF)
    grad_ref[...] = grad
    sums_ref[...] = jnp.sum(grad.astype(F32), axis=0, keepdims=True)
    weight_grad_ref[...] = matmul(turned_ref[...], grad).astype(BF)
    finish()


def feed_back(low, weight, more, inner_pre, turned, layer_back, pieces, members, parts, ident):
    rows, hidden = inner_pre.shape
    width = low.shape[1]
    step = 512
    _, piece, _ = layer_back.shape
    return pl.pallas_call(
        functools.partial(feed_back_kernel, pieces, members),
        grid=(hidden // step,),
        out_shape=(
            jax.ShapeDtypeStruct((rows, hidden), BF),
            jax.ShapeDtypeStruct((1, hidden), F32),
            jax.ShapeDtypeStruct((width, hidden), BF),
            jax.ShapeDtypeStruct((len(pieces), parts, piece, width), BF),
        ),
        in_specs=[
            pl.BlockSpec((rows, width), lambda i: (0, 0)),
            pl.BlockSpec((width // 2, step), lambda i: (0, i)),
            pl.BlockSpec((width // 2, step), lambda i: (0, i)),
            pl.BlockSpec((rows, step), lambda i: (0, i)),
            pl.BlockSpec((width, rows), lambda i: (0, 0)),
            ANY,
        ],
        out_specs=(
            pl.BlockSpec((rows, step), lambda i: (0, i)),
            pl.BlockSpec((1, step), lambda i: (0, i)),
            pl.BlockSpec((width, step), lambda i: (0, i)),
            ANY,
        ),
        scratch_shapes=meanwhile_scratch(pieces),
        compiler_params=pltpu.CompilerParams(
            collective_id=ident, has_side_effects=True, vmem_limit_bytes=58 * MIB
        ),
        cost_estimate=pl.CostEstimate(
            flops=4 * rows * width * hidden, bytes_accessed=40 * MIB, transcendentals=rows * hidden
        ),
        name="feed_back",
    )(low, weight, more, inner_pre, turned, layer_back)


def sibling():
    here = lax.axis_index("seq")
    return {"seq": here + 1 - 2 * lax.rem(here, 2)}


def attend_back_kernel(
    pieces,
    step,
    query_ref,
    key_ref,
    value_ref,
    key_far_ref,
    value_far_ref,
    grad_ref,
    mix_ref,
    log_ref,
    *rest,
):
    sharing = len(pieces) > 0
    if sharing:
        back_ref, *rest = rest
    dquery_ref, dkey_ref, dvalue_ref, *rest = rest
    if sharing:
        in_ref, all_ref, *rest = rest
    else:
        dkey_far_ref, dvalue_far_ref, *rest = rest
    turned, key_sum, value_sum, *rest = rest
    block = pl.program_id(1)
    rows = key_ref.shape[0]
    if sharing:
        away, pair_send, pair_recv, send_sem, recv_sem, local_sem = rest
        now = pl.program_id(0) * pl.num_programs(1) + block
        count = pl.num_programs(0) * pl.num_programs(1)
        finish = share_meanwhile(
            now, count, pieces, back_ref, all_ref, send_sem, recv_sem, local_sem, [sibling()]
        )

        def cross(kind, head):
            return pltpu.make_async_remote_copy(
                src_ref=away.at[kind, head],
                dst_ref=in_ref.at[kind, head],
                send_sem=pair_send.at[kind, head],
                recv_sem=pair_recv.at[kind, head],
                device_id=sibling(),
                device_id_type=MESH,
            )

    @pl.when(block == 0)
    def _():
        turned[:, :rows] = key_ref[...].T
        turned[:, rows:] = key_far_ref[...].T
        key_sum[...] = jnp.zeros_like(key_sum)
        value_sum[...] = jnp.zeros_like(value_sum)

    scale = DH ** (-0.5)
    query, grad = query_ref[...], grad_ref[...]
    terms = jnp.sum((grad.astype(F32) * mix_ref[...]).T, axis=0, keepdims=True)
    logs = log_ref[0]
    dquery = jnp.zeros((DH, query.shape[0]), F32)
    spans = [(key_ref, value_ref, start, start) for start in range(0, rows, step)]
    spans += [
        (key_far_ref, value_far_ref, start, rows + start)
        for start in range(0, key_far_ref.shape[0], step)
    ]
    for keys, values, start, place in spans:
        part = pl.ds(place, step)
        probs = jnp.exp(score_block(keys[pl.ds(start, step)], query) * scale - logs)
        prob_grad = score_block(values[pl.ds(start, step)], grad)
        score_grad = (probs * (prob_grad - terms) * scale).astype(BF)
        value_sum[part] += jnp.dot(probs.astype(BF), grad, preferred_element_type=F32)
        key_sum[part] += jnp.dot(score_grad, query, preferred_element_type=F32)
        dquery += jnp.dot(turned[:, part], score_grad, preferred_element_type=F32)
    dquery_ref[...] = dquery.T.astype(BF)

    @pl.when(block == pl.num_programs(1) - 1)
    def _():
        dkey_ref[...] = key_sum[:rows]
        dvalue_ref[...] = value_sum[:rows]
        if sharing:
            head = pl.program_id(0)
            for kind, total in enumerate((key_sum, value_sum)):
                away[kind, head] = total[rows:].astype(BF)
                cross(kind, head).start()
        else:
            dkey_far_ref[...] = key_sum[rows:].astype(BF)
            dvalue_far_ref[...] = value_sum[rows:].astype(BF)

    if sharing:

        @pl.when(now == count - 1)
        def _():
            for kind in range(2):
                for head in range(away.shape[1]):
                    cross(kind, head).wait()

        finish()


def attend_back(qkv, kv_far, grad, mix, logs, heads, layer_back, pieces, parts, ident):
    rows, cols = qkv.shape[0], heads * DH
    away = kv_far.shape[0]
    block, step = min(512, rows), min(512, rows)
    sharing = len(pieces) > 0
    _, piece, width = layer_back.shape

    def tile(offset):
        return pl.BlockSpec((block, DH), lambda h, i: (i, offset + h))

    def long(count, offset):
        return pl.BlockSpec((count, DH), lambda h, i: (0, offset + h))

    return pl.pallas_call(
        functools.partial(attend_back_kernel, pieces, step),
        grid=(heads, rows // block),
        out_shape=(
            jax.ShapeDtypeStruct((rows, cols), BF),
            jax.ShapeDtypeStruct((rows, cols), F32),
            jax.ShapeDtypeStruct((rows, cols), F32),
        )
        + (
            (
                jax.ShapeDtypeStruct((2, heads, rows, DH), BF),
                jax.ShapeDtypeStruct((len(pieces), parts, piece, width), BF),
            )
            if sharing
            else (jax.ShapeDtypeStruct((away, cols), BF),) * 2
        ),
        in_specs=[
            tile(0),
            long(rows, heads),
            long(rows, 2 * heads),
            long(away, 0),
            long(away, heads),
            tile(0),
            tile(0),
            pl.BlockSpec((1, 1, block), lambda h, i: (h, 0, i)),
        ]
        + ([ANY] if sharing else []),
        out_specs=(tile(0), long(rows, 0), long(rows, 0))
        + ((ANY, ANY) if sharing else (long(away, 0), long(away, 0))),
        scratch_shapes=[
            pltpu.VMEM((DH, rows + away), BF),
            pltpu.VMEM((rows + away, DH), F32),
            pltpu.VMEM((rows + away, DH), F32),
        ]
        + (
            [
                pltpu.VMEM((2, heads, rows, DH), BF),
                pltpu.SemaphoreType.DMA((2, heads)),
                pltpu.SemaphoreType.DMA((2, heads)),
            ]
            + meanwhile_scratch(pieces)
            if sharing
            else []
        ),
        compiler_params=pltpu.CompilerParams(
            vmem_limit_bytes=52 * MIB,
            **(dict(collective_id=ident, has_side_effects=True) if sharing else {}),
        ),
        cost_estimate=pl.CostEstimate(
            flops=20 * rows * (rows + away) * cols,
            bytes_accessed=30 * rows * cols,
            transcendentals=rows * (rows + away) * heads,
        ),
        name="attend_back",
    )(qkv, qkv, qkv, kv_far, kv_far, grad, mix, logs, *([layer_back] if sharing else []))


def from_group_members(block, members, per):
    blocks = []
    for step in range(1, per):
        pairs = [
            (base + place, base + (place - step) % per)
            for base in range(0, members, per)
            for place in range(per)
        ]
        blocks.append(lax.ppermute(block, "seq", pairs))
    return blocks


def to_group_members(total, blocks, members, per):
    for step in range(1, per):
        pairs = [
            (base + place, base + (place + step) % per)
            for base in range(0, members, per)
            for place in range(per)
        ]
        total = total + lax.ppermute(blocks[step - 1], "seq", pairs).astype(F32)
    return total


def last_kernel(
    per, turned_hbm, query_ref, key_ref, value_ref, in_ref, layer_hbm, layer_more_hbm,
    grad_ref, sums_ref, part_ref, layer_ref, turned_ref, made, layer, load_sem, put_sem,
):
    rows, cols = query_ref.shape
    count = load_sem.shape[0] - 2
    step = turned_ref.shape[0] // count
    loads = []
    for place in range(count):
        block = pl.ds(place * step, step)
        loads.append(
            pltpu.make_async_copy(turned_hbm.at[block], turned_ref.at[block], load_sem.at[place])
        )
    groups = layer.shape[0]
    for place, source in enumerate((layer_hbm, layer_more_hbm)):
        block = pl.ds(place * (groups // 2), groups // 2)
        loads.append(pltpu.make_async_copy(source, layer.at[block], load_sem.at[count + place]))
    for copy in loads:
        copy.start()
    puts = []

    def put(source, target):
        copy = pltpu.make_async_copy(source, target, put_sem.at[len(puts)])
        copy.start()
        puts.append(copy)

    for index, (own, far) in enumerate(
        ((query_ref, None), (key_ref, 0), (value_ref, 1))
    ):
        span = pl.ds(index * cols, cols)
        grad = own[...]
        if far is not None:
            far = [in_ref[far, head] for head in range(cols // DH)]
            grad = (grad + jnp.concatenate(far, axis=1).astype(F32)).astype(BF)
        grad_ref[:, span] = grad
        sums_ref[:, span] = jnp.sum(grad.astype(F32), axis=0, keepdims=True)
        for place in range(count):
            block = pl.ds(place * step, step)
            if index == 0:
                loads[place].wait()
            made[index, block] = matmul(turned_ref[block], grad_ref[:, span]).astype(BF)
        put(made.at[index], part_ref.at[:, span])
        if index == 1:
            for copy in loads[count:]:
                copy.wait()
            group = lax.axis_index("seq") // per
            for piece in range(groups):
                put(layer.at[piece], layer_ref.at[lax.rem(group + piece, groups)])
    for copy in puts:
        copy.wait()


def last_gradients(turned, query, key, value, arrived, layer, layer_more, per):
    rows, cols = query.shape
    width = turned.shape[0]
    return pl.pallas_call(
        functools.partial(last_kernel, per),
        out_shape=(
            jax.ShapeDtypeStruct((rows, 3 * cols), BF),
            jax.ShapeDtypeStruct((1, 3 * cols), F32),
            jax.ShapeDtypeStruct((width, 3 * cols), BF),
            jax.ShapeDtypeStruct((2 * layer.shape[0],) + layer.shape[1:], layer.dtype),
        ),
        in_specs=[ANY] + [VMEM] * 4 + [ANY] * 2,
        out_specs=(VMEM, VMEM, ANY, ANY),
        scratch_shapes=[
            pltpu.VMEM(turned.shape, BF),
            pltpu.VMEM((3, width, cols), BF),
            pltpu.VMEM((2 * layer.shape[0],) + layer.shape[1:], BF),
            pltpu.SemaphoreType.DMA((6,)),
            pltpu.SemaphoreType.DMA((3 + 2 * layer.shape[0],)),
        ],
        compiler_params=pltpu.CompilerParams(vmem_limit_bytes=52 * MIB),
        cost_estimate=pl.CostEstimate(
            flops=6 * rows * width * cols, bytes_accessed=32 * MIB, transcendentals=0
        ),
        name="last_gradients",
    )(turned, query, key, value, arrived, layer, layer_more)


def packed(vectors, lines):
    flat = jnp.concatenate(vectors)
    return jnp.pad(flat, (0, lines * 128 - flat.shape[0])).reshape(lines, 128)


def after(value, *others):
    return lax.optimization_barrier((value,) + others)[0]


def on_device(members, parts, *arrays):
    (
        tokens,
        query_weight,
        query_bias,
        key_weight,
        value_weight,
        value_bias,
        proj_weight,
        proj_bias,
        gain_first,
        shift_first,
        inner_weight,
        inner_bias,
        outer_weight,
        outer_bias,
        gain_second,
        shift_second,
        cotangent,
    ) = arrays
    micro, seqs, length, width = tokens.shape
    groups = micro * seqs
    per = members // groups
    assert per * groups == members and (parts != 4 or per == 2)
    piece = length // parts
    rows = groups * length
    quarter = groups * piece
    mine = lax.axis_index("mp")
    group = lax.axis_index("seq") // per

    depth, cols = query_weight.shape
    heads = cols // DH
    first = jnp.concatenate([query_weight, key_weight, value_weight, proj_weight.T], axis=1)
    first = lax.all_gather(first, "seq", axis=0, tiled=True)
    hidden = inner_weight.shape[1]
    fused = parts == 4 and per == 2
    outer_turned = outer_weight.T
    if fused:
        part = depth // 2
        folded = jnp.concatenate(
            [outer_turned[:part, : hidden // 2], outer_turned[:part, hidden // 2 :]], axis=0
        )
        second = jnp.concatenate([inner_weight, folded], axis=1)
        second = lax.all_gather(second, "seq", axis=0, tiled=True)
        w_inner = second[:, :hidden]
        w_outer = lax.all_gather(outer_turned[part:], "seq", axis=0, tiled=True)
    else:
        w_inner = second = lax.all_gather(inner_weight, "seq", axis=0, tiled=True)
        w_outer = lax.all_gather(outer_turned, "seq", axis=0, tiled=True)
    w_qkv = first[:, : 3 * cols]
    w_proj = first[:, 3 * cols :]
    vectors = [
        query_bias,
        value_bias,
        inner_bias,
        proj_bias,
        gain_first,
        shift_first,
        outer_bias,
        gain_second,
        shift_second,
    ]
    sizes = [vector.shape[0] for vector in vectors]
    lines = -(-sum(sizes) // 2048) * 16
    own_vectors = packed(vectors, lines)

    def to_blocks(array):
        array = array.reshape(groups, length, width)
        return [
            lax.dynamic_slice(
                array, (lax.rem(group + k, groups), mine * piece, 0), (1, piece, width)
            )[0]
            for k in range(groups)
        ]

    x_part, all_vectors = swap_groups(
        jnp.stack(to_blocks(tokens)),
        jnp.broadcast_to(own_vectors[None], (members, lines, 128)),
        members,
        parts,
        1,
        1,
    )
    x_part = x_part.reshape(quarter, width)
    x_rows = share_over_mp(x_part, parts, 8).reshape(rows, width)
    all_vectors = all_vectors.reshape(members, -1).astype(F32)
    full = []
    start = 0
    for size in sizes:
        full.append(all_vectors[:, start : start + size].reshape(-1))
        start += size
    b_query, b_value, b_inner, b_proj, gain_one, shift_one, b_outer, gain_two, shift_two = full

    bias = jnp.concatenate([b_query, jnp.zeros_like(b_query), b_value])
    qkv = (matmul(x_rows, w_qkv) + bias).astype(BF)
    kv_far = from_group_members(qkv[:, cols:], members, per)
    kv_far = kv_far[0] if per == 2 else jnp.concatenate(kv_far, axis=0)
    mixture, mixture_low, logs = attend(qkv, kv_far, heads)

    def blocked(array):
        return array.reshape(groups, piece, width)

    first_low, normal_one, inverse_one, x_turned = first_norm(
        over_cols(mixture_low, w_proj).astype(BF),
        blocked(x_part),
        x_rows,
        jnp.stack([b_proj, gain_one, shift_one]),
        parts,
        2,
    )
    first_low = first_low.reshape(rows, width)

    inner_pre = matmul(first_low, w_inner) + b_inner
    active = gelu_tanh(inner_pre).astype(BF)
    done, active_turned, w_outer_half = None, None, None
    if fused:
        done, active_turned, w_outer_half, first_turned = half_sum(
            active, second, first_low, groups, piece, members, parts, 13
        )
    else:
        first_turned = first_low.T
    second_low, second_grad, layer_back, sums, outer_w_part = second_norm(
        active,
        w_outer,
        active_turned,
        done,
        normal_one,
        jnp.stack(to_blocks(cotangent)),
        jnp.stack([gain_one, shift_one, b_outer, gain_two, shift_two]),
        members,
        parts,
        3,
    )
    second_low = second_low.reshape(rows, width)

    outer_w_grad = lax.psum_scatter(outer_w_part, "seq", scatter_dimension=1, tiled=True)
    pieces = list(range(groups)) if fused else []
    early, late = pieces[: groups // 2], pieces[groups // 2 :]
    if fused:
        inner_grad, inner_b_grad, inner_w_part, layer_out = feed_back(
            second_low,
            w_outer_half,
            w_outer,
            inner_pre,
            first_turned,
            layer_back,
            early,
            members,
            parts,
            7,
        )
    else:
        _, pull_gelu = jax.vjp(gelu_tanh, inner_pre)
        inner_grad = pull_gelu(matmul(second_low, w_outer))[0].astype(BF)
        inner_b_grad = jnp.sum(inner_grad.astype(F32), axis=0)
        inner_w_part = matmul(first_turned, inner_grad).astype(BF)
        layer_out = lax.all_gather(jnp.roll(layer_back, group, axis=0), "mp", axis=1)
    inner_w_grad = lax.psum_scatter(inner_w_part, "seq", scatter_dimension=0, tiled=True)
    attn_low, attn_grad, summed_rows = first_back(
        inner_grad,
        second,
        second_grad,
        normal_one,
        inverse_one,
        after(sums, inner_w_part),
        gain_one[None],
        parts,
        4,
    )
    attn_low = after(attn_low.reshape(rows, width), outer_w_grad)
    summed_rows = jnp.sum(summed_rows, axis=0)

    proj_w_part = over_rows(attn_low, mixture_low).astype(BF)
    mixture_grad = matmul(after(attn_low, proj_w_part), w_proj).astype(BF)
    query_grad, key_grad, value_grad, *others = attend_back(
        qkv, kv_far, mixture_grad, mixture, logs, heads, layer_back, late, parts, 5
    )

    def blocks_of(array):
        return [array[i * rows : (i + 1) * rows] for i in range(per - 1)]

    if fused:
        qkv_grad, bias_grad, last_w_part, layer_out = last_gradients(
            x_turned,
            query_grad,
            key_grad,
            value_grad,
            others[0],
            layer_out,
            others[1],
            per,
        )
        bias_grad = bias_grad[0]
    else:
        key_grad = to_group_members(key_grad, blocks_of(others[0]), members, per)
        value_grad = to_group_members(value_grad, blocks_of(others[1]), members, per)
        qkv_grad = jnp.concatenate([query_grad, key_grad.astype(BF), value_grad.astype(BF)], axis=1)
        last_w_part = matmul(x_turned, qkv_grad).astype(BF)
        bias_grad = jnp.sum(qkv_grad.astype(F32), axis=0)
    last_w_grad = lax.psum_scatter(last_w_part, "seq", scatter_dimension=0, tiled=True).astype(F32)
    small = jnp.concatenate(
        [
            bias_grad[:cols].reshape(members, -1),
            bias_grad[2 * cols :].reshape(members, -1),
            inner_b_grad.reshape(members, -1),
        ]
        + [summed_rows[i].reshape(members, -1) for i in (3, 4, 5, 0, 1, 2)],
        axis=1,
    )
    small = jnp.pad(small, ((0, 0), (0, lines * 128 - small.shape[1])))
    input_grad, small, proj_w_grad = input_gradient(
        qkv_grad,
        first,
        attn_grad,
        small.reshape(members, lines, 128),
        proj_w_part,
        members,
        parts,
        6,
    )
    input_grad = after(input_grad, inner_w_grad).astype(F32).reshape(micro, seqs, length, width)
    layer_out = layer_out.reshape(micro, seqs, length, width)
    small = jnp.sum(small, axis=0).reshape(-1)
    pieces = []
    start = 0
    for size in sizes:
        pieces.append(small[start : start + size])
        start += size
    return (
        layer_out,
        input_grad,
        last_w_grad[:, :cols],
        pieces[0],
        last_w_grad[:, cols : 2 * cols],
        last_w_grad[:, 2 * cols : 3 * cols],
        pieces[1],
        proj_w_grad.T,
        pieces[3],
        pieces[4],
        pieces[5],
        inner_w_grad.astype(F32),
        pieces[2],
        outer_w_grad.astype(F32),
        pieces[6],
        pieces[7],
        pieces[8],
    )


def solution(mesh):
    tokens = P(None, None, "seq", None)
    rows_cols, cols_rows, both, seq = P("seq", "mp"), P("mp", "seq"), P(("mp", "seq")), P("seq")
    weights = (
        rows_cols,
        both,
        rows_cols,
        rows_cols,
        both,
        cols_rows,
        seq,
        seq,
        seq,
        rows_cols,
        both,
        cols_rows,
        seq,
        seq,
        seq,
    )
    return jax.shard_map(
        functools.partial(on_device, mesh.shape["seq"], mesh.shape["mp"]),
        mesh=mesh,
        in_specs=(tokens,) + weights + (tokens,),
        out_specs=(tokens, tokens) + weights,
        check_vma=False,
    )
```
